32 devices in a mesh: blk: 8 (over z, x), head: 4 (over y, core).
Axes of the slice: x: 2, y: 2, z: 4, core: 2. Of those that a mesh axis runs over, the one named last changes fastest.
Arguments:
- token_ids: int32 [4, 1024], P(None, 'blk'), may hold values from 1 to 24, as said below
- targets: int32 [4, 1024], P(None, 'blk'), may hold values from 4 to 23
- masked: int32 [4, 1024], P(None, 'blk'), may hold values from 0 to 1, as said below
- lengths: int32 [4], replicated, may hold values from 512 to 1024, as said below
- family_weight: float32 [4], replicated, may hold values from 0.5 to 2
- embed_table: float32 [1049, 640], P(None, 'blk'), may hold values from -0.625 to 0.625
- w_qkv: float32 [2, 640, 3, 640], P(None, 'blk', None, 'head'), may hold values from -0.25 to 0.25
- w_out: float32 [2, 640, 640], P(None, 'head', 'blk'), may hold values from -2 to 2
- w_up: float32 [2, 640, 5120], P(None, 'blk', 'head'), may hold values from -0.25 to 0.25
- w_down: float32 [2, 5120, 640], P(None, ('head', 'blk')), may hold values from -0.078125 to 0.078125
- norm_params: float32 [5, 2, 640], P(None, None, 'blk'), may hold values from -0.35 to 2.6, as said below
- embed_first: float32 [1049, 640], P(None, 'blk'), may hold values from -1.59783534e-05 to 1.59783534e-05
- qkv_first: float32 [2, 640, 3, 640], P(None, 'blk', None, 'head'), may hold values from -1.66893e-06 to 1.66893e-06
- out_first: float32 [2, 640, 640], P(None, 'head', 'blk'), may hold values from -1.66893e-06 to 1.66893e-06
- up_first: float32 [2, 640, 5120], P(None, 'blk', 'head'), may hold values from -1.66893e-06 to 1.66893e-06
- down_first: float32 [2, 5120, 640], P(None, ('head', 'blk')), may hold values from -1.66893e-06 to 1.66893e-06
- norm_first: float32 [5, 2, 640], P(None, None, 'blk'), may hold values from -1.5258789e-05 to 1.5258789e-05
- embed_second: float32 [1049, 640], P(None, 'blk'), may hold values from 2.93053e-15 to 4.688848e-12, as said below
- qkv_second: float32 [2, 640, 3, 640], P(None, 'blk', None, 'head'), may hold values from 2.93053e-15 to 4.688848e-14
- out_second: float32 [2, 640, 640], P(None, 'head', 'blk'), may hold values from 2.93053e-15 to 4.688848e-14
- up_second: float32 [2, 640, 5120], P(None, 'blk', 'head'), may hold values from 2.93053e-15 to 4.688848e-14
- down_second: float32 [2, 5120, 640], P(None, ('head', 'blk')), may hold values from 2.93053e-15 to 4.688848e-14
- norm_second: float32 [5, 2, 640], P(None, None, 'blk'), may hold values from 2.93053e-13 to 4.688848e-12
Outputs:
- loss_sum: float32 [], replicated
- weight_sum: float32 [], replicated
- grad_norm: float32 [], replicated
- stream_rms: float32 [2, 3], replicated
- embed_first_new: float32 [1049, 640], P(None, 'blk')
- embed_second_new: float32 [1049, 640], P(None, 'blk')
- embed_new: float32 [1049, 640], P(None, 'blk')
- embed_copy: bfloat16 [1049, 640], P(None, 'blk')
- qkv_first_new: float32 [2, 640, 3, 640], P(None, 'blk', None, 'head')
- qkv_second_new: float32 [2, 640, 3, 640], P(None, 'blk', None, 'head')
- qkv_new: float32 [2, 640, 3, 640], P(None, 'blk', None, 'head')
- qkv_copy: bfloat16 [2, 640, 3, 640], P(None, 'blk', None, 'head')
- out_first_new: float32 [2, 640, 640], P(None, 'head', 'blk')
- out_second_new: float32 [2, 640, 640], P(None, 'head', 'blk')
- out_new: float32 [2, 640, 640], P(None, 'head', 'blk')
- out_copy: bfloat16 [2, 640, 640], P(None, 'head', 'blk')
- up_first_new: float32 [2, 640, 5120], P(None, 'blk', 'head')
- up_second_new: float32 [2, 640, 5120], P(None, 'blk', 'head')
- up_new: float32 [2, 640, 5120], P(None, 'blk', 'head')
- up_copy: bfloat16 [2, 640, 5120], P(None, 'blk', 'head')
- down_first_new: float32 [2, 5120, 640], P(None, ('head', 'blk'))
- down_second_new: float32 [2, 5120, 640], P(None, ('head', 'blk'))
- down_new: float32 [2, 5120, 640], P(None, ('head', 'blk'))
- down_copy: bfloat16 [2, 5120, 640], P(None, ('head', 'blk'))
- norm_first_new: float32 [5, 2, 640], P(None, None, 'blk')
- norm_second_new: float32 [5, 2, 640], P(None, None, 'blk')
- norm_new: float32 [5, 2, 640], P(None, None, 'blk')
- norm_copy: bfloat16 [5, 2, 640], P(None, None, 'blk')
The draws below stay inside these ranges and needn't reach their ends.
Inputs may be any that keep to these rules, and one draw needn't show every extreme that they name: `token_ids`: 1 where position >= length, 24 where masked is 1, else equal to targets. `masked`: zero at positions >= length; every sequence has a masked position. `lengths`: one sequence has length 1024. `norm_params`: gains positive. `embed_second`: positive.
All inputs are finite; a program needn't handle non-finite values.
Results may differ from the reference program's by a relative error of at most 0.012.
The reference program's roundings to bfloat16 on the way count: a program that leaves them out, or rounds other values in their place, can miss the bound.
Values may be sent and summed in bfloat16 or wider, within the bound.
A program may use at most 320 MiB of HBM per device.

```python
import math
import jax
import jax.numpy as jnp
from jax import lax

VOCAB = 25
D = 640
HEADS = 20
HEAD_DIM = 32
FF = 5120
LAYERS = 2
STEP = 10
SEQ_LEN = 1024
SEQS = 4
PARAMS = 17061760


def draw_batch(key):
    key_len, key_pick, key_tgt, key_mask, key_force = jax.random.split(key, 5)
    seq_lengths = jax.random.randint(key_len, (SEQS,), SEQ_LEN // 2, SEQ_LEN + 1)
    chosen = jax.random.randint(key_pick, (), 0, SEQS)
    seq_lengths = jnp.where(jnp.arange(SEQS) == chosen, SEQ_LEN, seq_lengths)
    positions = jnp.arange(SEQ_LEN)[None, :]
    live_cells = positions < seq_lengths[:, None]
    target_ids = jax.random.randint(key_tgt, (SEQS, SEQ_LEN), 4, 24)
    levels = jax.random.randint(key_mask, (SEQS, SEQ_LEN), 0, 1000)
    limits = 60 + 300 * positions // SEQ_LEN
    forced = jax.random.randint(key_force, (SEQS, 1), 0, SEQ_LEN // 2)
    mask_cells = ((levels < limits) & live_cells | (positions == forced)).astype(jnp.int32)
    input_ids = jnp.where(live_cells, jnp.where(mask_cells == 1, 24, target_ids), 1)
    return (input_ids.astype(jnp.int32), target_ids.astype(jnp.int32), mask_cells, seq_lengths.astype(jnp.int32))


def draw_token_ids(key, part):
    return draw_batch(key)[0]


def draw_targets(key, part):
    return draw_batch(key)[1]


def draw_masked(key, part):
    return draw_batch(key)[2]


def draw_lengths(key, part):
    return draw_batch(key)[3]


def draw_norm_params(key, part):
    key = jax.random.fold_in(key, 7)
    key_gain, key_shift = jax.random.split(key)
    ramp = jnp.arange(D, dtype=jnp.float32) / D
    gains = (0.6 + 1.2 * ramp) * jax.random.uniform(key_gain, (2 * LAYERS + 1, D), jnp.float32, 0.8, 1.2)
    shifts = jax.random.uniform(key_shift, (2 * LAYERS + 1, D), jnp.float32, -0.25, 0.25)
    return jnp.stack([gains, shifts], axis=1).astype(jnp.float32)


def row_factor(token_value, place_value):
    rows = jnp.arange(VOCAB + SEQ_LEN)[:, None]
    return jnp.where(rows < VOCAB, token_value, place_value).astype(jnp.float32)


def draw_embed_first(key, part):
    key = jax.random.fold_in(key, 11)
    noise = jnp.clip(jax.random.normal(key, (VOCAB + SEQ_LEN, D), jnp.float32), -6.0, 6.0)
    return (noise * row_factor(0.011, 0.0011) / PARAMS ** 0.5).astype(jnp.float32)


def draw_embed_second(key, part):
    key = jax.random.fold_in(key, 13)
    spread = jax.random.uniform(key, (VOCAB + SEQ_LEN, D), jnp.float32, jnp.log(5e-08), jnp.log(8e-07))
    return (jnp.exp(spread) * row_factor(100.0, 1.0) / PARAMS).astype(jnp.float32)


def steps_of(stream_key, dims, pieces, smallest, high):
    def one(axis_at, shards_of):
        steps = jax.random.uniform(jax.random.fold_in(jax.random.fold_in(stream_key, 6), axis_at), (shards_of,), jnp.float32, smallest / len(pieces), high / len(pieces))
        return jnp.repeat(jnp.exp(steps), dims[axis_at] // shards_of).reshape((-1,) + (1,) * (len(dims) - axis_at - 1))

    factor_of = one(*pieces[0])
    for cut in pieces[1:]:
        factor_of = factor_of * one(*cut)
    return factor_of


def normal_values(own_key, dims, width, limit, shards=(), kind=jnp.bfloat16):
    result = width * jax.random.normal(own_key, dims, jnp.float32)
    if shards:
        result = result * steps_of(own_key, dims, shards, -0.22, 0.18)
    return jnp.clip(result, -limit, limit).astype(kind)


def setup_inputs(seed: int = 0) -> dict:
    key_list = jax.random.split(jax.random.key(seed), 24)
    return {
        "token_ids": draw_token_ids(jax.random.fold_in(key_list[23], 71), 0),
        "targets": draw_targets(jax.random.fold_in(key_list[23], 71), 0),
        "masked": draw_masked(jax.random.fold_in(key_list[23], 71), 0),
        "lengths": draw_lengths(jax.random.fold_in(key_list[23], 71), 0),
        "family_weight": jnp.clip(jnp.exp(jax.random.uniform(key_list[4], (SEQS,), jnp.float32, math.log(0.5), math.log(2.0))), 0.5, 2.0),
        "embed_table": normal_values(key_list[5], (VOCAB + SEQ_LEN, D), 100 ** -0.5, 0.625, ((1, 8),), jnp.float32),
        "w_qkv": normal_values(key_list[6], (LAYERS, D, 3, D), D ** -0.5, 0.25, ((1, 8), (3, 4)), jnp.float32),
        "w_out": normal_values(key_list[7], (LAYERS, D, D), (D // 64) ** -0.5, 2.0, ((1, 4), (2, 8)), jnp.float32),
        "w_up": normal_values(key_list[8], (LAYERS, D, FF), D ** -0.5, 0.25, ((1, 8), (2, 4)), jnp.float32),
        "w_down": normal_values(key_list[9], (LAYERS, FF, D), FF ** -0.5, 0.078125, ((1, 32),), jnp.float32),
        "norm_params": draw_norm_params(jax.random.fold_in(key_list[23], 71), 0),
        "embed_first": draw_embed_first(jax.random.fold_in(key_list[23], 71), 0),
        "qkv_first": normal_values(key_list[12], (LAYERS, D, 3, D), (0.0011 / PARAMS ** 0.5), 1.6689300537109375e-06, ((1, 8), (3, 4)), jnp.float32),
        "out_first": normal_values(key_list[13], (LAYERS, D, D), (0.0011 / PARAMS ** 0.5), 1.6689300537109375e-06, ((1, 4), (2, 8)), jnp.float32),
        "up_first": normal_values(key_list[14], (LAYERS, D, FF), (0.0011 / PARAMS ** 0.5), 1.6689300537109375e-06, ((1, 8), (2, 4)), jnp.float32),
        "down_first": normal_values(key_list[15], (LAYERS, FF, D), (0.0011 / PARAMS ** 0.5), 1.6689300537109375e-06, ((1, 32),), jnp.float32),
        "norm_first": normal_values(key_list[16], (2 * LAYERS + 1, 2, D), (0.011 / PARAMS ** 0.5), 1.52587890625e-05, ((2, 8),), jnp.float32),
        "embed_second": draw_embed_second(jax.random.fold_in(key_list[23], 71), 0),
        "qkv_second": jnp.clip(jnp.exp(math.log(4.6888481189085243e-14) - 2.7725887 * jax.random.uniform(key_list[18], (LAYERS, D, 3, D), jnp.float32) ** steps_of(key_list[18], (LAYERS, D, 3, D), ((1, 8), (3, 4)), -0.2, 0.2)), 2.9305300743178277e-15, 4.6888481189085243e-14),
        "out_second": jnp.clip(jnp.exp(math.log(4.6888481189085243e-14) - 2.7725887 * jax.random.uniform(key_list[19], (LAYERS, D, D), jnp.float32) ** steps_of(key_list[19], (LAYERS, D, D), ((1, 4), (2, 8)), -0.2, 0.2)), 2.9305300743178277e-15, 4.6888481189085243e-14),
        "up_second": jnp.clip(jnp.exp(math.log(4.6888481189085243e-14) - 2.7725887 * jax.random.uniform(key_list[20], (LAYERS, D, FF), jnp.float32) ** steps_of(key_list[20], (LAYERS, D, FF), ((1, 8), (2, 4)), -0.2, 0.2)), 2.9305300743178277e-15, 4.6888481189085243e-14),
        "down_second": jnp.clip(jnp.exp(math.log(4.6888481189085243e-14) - 2.7725887 * jax.random.uniform(key_list[21], (LAYERS, FF, D), jnp.float32) ** steps_of(key_list[21], (LAYERS, FF, D), ((1, 32),), -0.2, 0.2)), 2.9305300743178277e-15, 4.6888481189085243e-14),
        "norm_second": jnp.clip(jnp.exp(math.log(4.688847834305454e-12) - 2.7725887 * jax.random.uniform(key_list[22], (2 * LAYERS + 1, 2, D), jnp.float32) ** steps_of(key_list[22], (2 * LAYERS + 1, 2, D), ((2, 8),), -0.2, 0.2)), 2.930529896440909e-13, 4.688847834305454e-12),
    }


NEGATIVE = -1e+30
NORM_EPS = 1e-05
CLIP_NORM = 0.01
BETA_FIRST = 0.9
BETA_SECOND = 0.999
ADAM_EPS = 1e-08
RATES = (0.2, 0.1, 0.5, 0.1, 0.03, 0.5)
DECAYS = (0.1, 0.1, 0.1, 0.1, 0.1, 0.0)
HIGHEST = lax.Precision.HIGHEST

@jax.custom_vjp
def low(v):
    return lax.optimization_barrier(v.astype(jnp.bfloat16)).astype(jnp.float32)

@jax.custom_vjp
def low_back(v):
    return v

def low_keep(v):
    return (low(v), None)

def low_pass(kept, grad):
    return (grad,)

def back_keep(v):
    return (v, None)

def back_low(kept, grad):
    return (low(grad),)
low.defvjp(low_keep, low_pass)
low_back.defvjp(back_keep, back_low)

def layer_norm(inputs, gain_row, shift_row):
    centred = inputs - lax.optimization_barrier(jnp.mean(inputs, axis=-1, keepdims=True))
    spread = lax.optimization_barrier(jnp.mean(centred * centred, axis=-1, keepdims=True))
    return centred * lax.rsqrt(spread + NORM_EPS) * gain_row + shift_row

def matmul(left, right):
    return jnp.dot(left, right, precision=HIGHEST)

def attention(queries, keys_all, values_all, live_keys):
    query_block = math.gcd(512, SEQ_LEN)
    score_scale = HEAD_DIM ** (-0.5)

    def one_block(query_rows):
        scores = low_back(jnp.einsum('the,jhe->htj', query_rows, keys_all, precision=HIGHEST) * score_scale)
        masked_scores = jnp.where(live_keys[None, None, :], scores, NEGATIVE)
        row_peaks = lax.optimization_barrier(jnp.max(masked_scores, axis=-1, keepdims=True))
        exp_scores = jnp.exp(masked_scores - row_peaks)
        attn_probs = exp_scores / lax.optimization_barrier(jnp.sum(exp_scores, axis=-1, keepdims=True))
        return jnp.einsum('htj,jhe->the', low(attn_probs), values_all, precision=HIGHEST)
    blocks = queries.reshape(SEQ_LEN // query_block, query_block, HEADS, HEAD_DIM)
    return lax.map(jax.checkpoint(one_block), blocks).reshape(SEQ_LEN, D)

def sequence_loss(params, token_row, target_row, mask_row, seq_length, family, weight_sum):
    embed_table, w_qkv, w_out, w_up, w_down, norm_params = params
    table_low = low(embed_table)
    token_table = table_low[:VOCAB]
    place_table = table_low[VOCAB:]
    norm_low = low(norm_params)
    live_keys = jnp.arange(SEQ_LEN) < seq_length
    live_rows = live_keys.astype(jnp.float32)[:, None]
    stream = token_table[token_row] + place_table
    squares = []
    for layer_idx in range(LAYERS):
        squares.append(jnp.sum(stream * stream * live_rows))
        normed = low(layer_norm(stream, norm_low[2 * layer_idx, 0], norm_low[2 * layer_idx, 1]))
        packed = low(low_back(matmul(normed, low(w_qkv[layer_idx]).reshape(D, 3 * D))))
        heads_view = packed.reshape(SEQ_LEN, 3, HEADS, HEAD_DIM)
        attended = attention(heads_view[:, 0], heads_view[:, 1], heads_view[:, 2], live_keys)
        attn_out = low_back(matmul(low(low_back(attended)), low(w_out[layer_idx])))
        squares.append(jnp.sum(attn_out * attn_out * live_rows))
        stream = stream + attn_out
        normed_two = low(layer_norm(stream, norm_low[2 * layer_idx + 1, 0], norm_low[2 * layer_idx + 1, 1]))
        hidden_pre = low_back(matmul(normed_two, low(w_up[layer_idx])))
        hidden_act = low(jax.nn.gelu(hidden_pre, approximate=False))
        ffn_out = low_back(matmul(hidden_act, low(w_down[layer_idx])))
        squares.append(jnp.sum(ffn_out * ffn_out * live_rows))
        stream = stream + ffn_out
    final = low(layer_norm(stream, norm_low[2 * LAYERS, 0], norm_low[2 * LAYERS, 1]))
    logits = low_back(matmul(final, token_table.T))
    log_probs = jax.nn.log_softmax(logits, axis=-1)
    token_loss = -jnp.take_along_axis(log_probs, target_row[:, None], axis=1)[:, 0]
    token_weight = mask_row.astype(jnp.float32) * family
    loss_part = jnp.sum(token_weight * token_loss)
    return (loss_part / weight_sum, (loss_part, jnp.stack(squares)))

def adamw_update(weight, first, second, gradient, rate, decay):
    first = BETA_FIRST * first + (1.0 - BETA_FIRST) * gradient
    second = BETA_SECOND * second + (1.0 - BETA_SECOND) * gradient * gradient
    first_hat = first / (1.0 - BETA_FIRST ** STEP)
    second_hat = second / (1.0 - BETA_SECOND ** STEP)
    weight = weight - rate * (first_hat / (jnp.sqrt(second_hat) + ADAM_EPS) + decay * weight)
    return (first, second, weight)

def reference(token_ids, targets, masked, lengths, family_weight, embed_table, w_qkv, w_out, w_up, w_down, norm_params, embed_first, qkv_first, out_first, up_first, down_first, norm_first, embed_second, qkv_second, out_second, up_second, down_second, norm_second):
    params = (embed_table, w_qkv, w_out, w_up, w_down, norm_params)
    firsts = (embed_first, qkv_first, out_first, up_first, down_first, norm_first)
    seconds = (embed_second, qkv_second, out_second, up_second, down_second, norm_second)
    weight_sum = jnp.sum(masked.astype(jnp.float32) * family_weight[:, None])

    def one_sequence(running, seq_items):
        grad_sums, loss_total, square_total = running
        token_row, target_row, mask_row, seq_length, family = seq_items

        def loss_of(param_tuple):
            return sequence_loss(param_tuple, token_row, target_row, mask_row, seq_length, family, weight_sum)
        primal, pullback, aux_pair = jax.vjp(loss_of, params, has_aux=True)
        step_grads, = pullback(jnp.ones_like(primal))
        grad_sums = jax.tree.map(jnp.add, grad_sums, step_grads)
        return ((grad_sums, loss_total + aux_pair[0], square_total + aux_pair[1]), None)
    zero_grads = jax.tree.map(jnp.zeros_like, params)
    start_state = (zero_grads, jnp.zeros((), jnp.float32), jnp.zeros((3 * LAYERS,), jnp.float32))
    (grad_sums, loss_sum, squares), _ = lax.scan(one_sequence, start_state, (token_ids, targets, masked, lengths, family_weight))
    total_squares = sum((jnp.sum(grad_part * grad_part) for grad_part in grad_sums))
    grad_norm = jnp.sqrt(total_squares)
    factor = CLIP_NORM / jnp.maximum(grad_norm, CLIP_NORM)
    stream_rms = jnp.sqrt(squares.reshape(LAYERS, 3) / (jnp.sum(lengths).astype(jnp.float32) * D))
    results = [loss_sum, weight_sum, grad_norm, stream_rms]
    for group_idx in range(6):
        first, second, weight = adamw_update(params[group_idx], firsts[group_idx], seconds[group_idx], grad_sums[group_idx] * factor, RATES[group_idx], DECAYS[group_idx])
        results += [first, second, weight, weight.astype(jnp.bfloat16)]
    return tuple(results)
```

```python
import functools

import jax
import jax.numpy as jnp
from jax import lax
from jax.experimental import pallas as pl
from jax.experimental.pallas import tpu as pltpu
from jax.sharding import PartitionSpec as P

VOCAB = 25
D = 640
HEAD_DIM = 32
LAYERS = 2
STEP = 10


NEGATIVE = -1e30
NORM_EPS = 1e-05
CLIP_NORM = 0.01
BETA_FIRST = 0.9
BETA_SECOND = 0.999
ADAM_EPS = 1e-08
RATES = (0.2, 0.1, 0.5, 0.1, 0.03, 0.5)
DECAYS = (0.1, 0.1, 0.1, 0.1, 0.1, 0.0)
HIGHEST = lax.Precision.HIGHEST


def layer_norm(inputs, gain_row, shift_row):
    centred = inputs - jnp.mean(inputs, axis=-1, keepdims=True)
    spread = jnp.mean(centred * centred, axis=-1, keepdims=True)
    return centred * lax.rsqrt(spread + NORM_EPS) * gain_row + shift_row


def gelu_exact(inputs):
    return jax.nn.gelu(inputs, approximate=False)


def adamw_update(weight, first, second, gradient, rate, decay):
    first = BETA_FIRST * first + (1.0 - BETA_FIRST) * gradient
    second = BETA_SECOND * second + (1.0 - BETA_SECOND) * gradient * gradient
    first_hat = first / (1.0 - BETA_FIRST**STEP)
    second_hat = second / (1.0 - BETA_SECOND**STEP)
    weight = weight - rate * (first_hat / (jnp.sqrt(second_hat) + ADAM_EPS) + decay * weight)
    return (first, second, weight)


def slice_head(tensor, head_index):
    return lax.dynamic_slice_in_dim(tensor, head_index * HEAD_DIM, HEAD_DIM, tensor.ndim - 1)


def join_heads(stacked):
    moved = jnp.moveaxis(stacked, 0, 2)
    return moved.reshape(moved.shape[0], moved.shape[1], -1)


def spread_rows(normed):
    return lax.all_gather(normed, "head", axis=0, tiled=True)


def spread_grads(grad_rows):
    return lax.all_gather(grad_rows, "head", axis=0, tiled=True)


def sum_rows(full_rows, weight, row_share):

    def row_term(row_start, row_count):
        return jnp.dot(full_rows, weight, preferred_element_type=jnp.float32)

    return lax.psum_scatter(
        row_term(jnp.int32(0), row_share * lax.axis_size("head")),
        "head",
        scatter_dimension=0,
        tiled=True,
    )


def sum_grads(full_rows, weight, row_share):

    def row_term(row_start, row_count):
        return jnp.einsum("nc,dc->nd", full_rows, weight, preferred_element_type=jnp.float32)

    return lax.psum_scatter(
        row_term(jnp.int32(0), row_share * lax.axis_size("head")).astype(jnp.bfloat16),
        "head",
        scatter_dimension=0,
        tiled=True,
    ).astype(jnp.float32)


def attend(queries, keys_all, values_all, live_keys):
    local_heads = queries.shape[-1] // HEAD_DIM
    score_scale = HEAD_DIM ** (-0.5)
    live_mask = live_keys[:, None, :]

    def one_head(head_index):
        scores = (
            jnp.einsum(
                "ste,sje->stj",
                slice_head(queries, head_index),
                slice_head(keys_all, head_index),
                preferred_element_type=jnp.float32,
            )
            * score_scale
        )
        masked_scores = jnp.where(live_mask, scores, NEGATIVE)
        row_peak = jnp.max(masked_scores, axis=-1, keepdims=True)
        exp_scores = jnp.exp(masked_scores - row_peak)
        row_total = jnp.sum(exp_scores, axis=-1, keepdims=True)
        attn_probs = (exp_scores / row_total).astype(jnp.bfloat16)
        attended = jnp.einsum(
            "stj,sje->ste",
            attn_probs,
            slice_head(values_all, head_index),
            preferred_element_type=jnp.float32,
        )
        return (attended, (row_peak + jnp.log(row_total))[..., 0])

    outputs, log_totals = lax.map(one_head, jnp.arange(local_heads))
    return (join_heads(outputs), log_totals)


def attend_back(queries, keys_all, values_all, grad_heads, log_totals, live_keys):
    local_heads = queries.shape[-1] // HEAD_DIM
    score_scale = HEAD_DIM ** (-0.5)
    live_mask = live_keys[:, None, :]

    def one_head(head_index):
        query_h = slice_head(queries, head_index)
        key_h = slice_head(keys_all, head_index)
        grad_h = slice_head(grad_heads, head_index)
        scores = (
            jnp.einsum("ste,sje->stj", query_h, key_h, preferred_element_type=jnp.float32)
            * score_scale
        )
        masked_scores = jnp.where(live_mask, scores, NEGATIVE)
        attn_probs = jnp.exp(masked_scores - log_totals[head_index][..., None])
        grad_probs = jnp.einsum(
            "ste,sje->stj",
            grad_h,
            slice_head(values_all, head_index),
            preferred_element_type=jnp.float32,
        )
        row_delta = jnp.sum(attn_probs * grad_probs, axis=-1)
        grad_scores = (attn_probs * (grad_probs - row_delta[..., None])).astype(jnp.bfloat16)
        grad_query = (
            jnp.einsum("stj,sje->ste", grad_scores, key_h, preferred_element_type=jnp.float32)
            * score_scale
        )
        grad_key = (
            jnp.einsum("stj,ste->sje", grad_scores, query_h, preferred_element_type=jnp.float32)
            * score_scale
        )
        grad_value = jnp.einsum(
            "stj,ste->sje",
            attn_probs.astype(jnp.bfloat16),
            grad_h,
            preferred_element_type=jnp.float32,
        )
        return (grad_query, grad_key, grad_value)

    grad_query, grad_key, grad_value = lax.map(one_head, jnp.arange(local_heads))
    grad_key, grad_value = (
        lax.psum_scatter(grad_key, "blk", scatter_dimension=2, tiled=True),
        lax.psum_scatter(grad_value, "blk", scatter_dimension=2, tiled=True),
    )
    return (join_heads(grad_query), join_heads(grad_key), join_heads(grad_value))


def layer_forward(stream, layer_weights, norm_rows, live_keys, row_share):
    w_qkv, w_out, w_up, w_down = layer_weights
    seq_count = live_keys.shape[0]
    normed = layer_norm(stream, norm_rows[0, 0], norm_rows[0, 1]).astype(jnp.bfloat16)
    normed_all = spread_rows(normed)
    packed = jnp.dot(
        normed_all, w_qkv.reshape(w_qkv.shape[0], -1), preferred_element_type=jnp.float32
    ).astype(jnp.bfloat16)
    packed = packed.reshape(seq_count, -1, 3, w_qkv.shape[-1])
    queries, keys_local, values_local = (packed[:, :, 0], packed[:, :, 1], packed[:, :, 2])
    keys_all, values_all = (
        lax.all_gather(keys_local, "blk", axis=1, tiled=True),
        lax.all_gather(values_local, "blk", axis=1, tiled=True),
    )
    attended, log_totals = attend(queries, keys_all, values_all, live_keys)
    attended = attended.astype(jnp.bfloat16).reshape(-1, attended.shape[-1])
    attn_out = sum_rows(attended, w_out, row_share)
    middle = stream + attn_out
    normed_two = layer_norm(middle, norm_rows[1, 0], norm_rows[1, 1]).astype(jnp.bfloat16)
    normed_two_all = spread_rows(normed_two)
    hidden_pre = jnp.dot(normed_two_all, w_up, preferred_element_type=jnp.float32)
    hidden_act = gelu_exact(hidden_pre).astype(jnp.bfloat16)
    ffn_out = sum_rows(hidden_act, w_down, row_share)
    kept = (
        stream,
        middle,
        normed_all,
        queries,
        keys_local,
        values_local,
        keys_all,
        values_all,
        log_totals,
        attended,
        normed_two_all,
        hidden_pre,
    )
    return (middle + ffn_out, attn_out, ffn_out, kept)


def layer_backward(grad_stream, kept, layer_weights, norm_rows, live_keys, row_share):
    (
        stream,
        middle,
        normed_all,
        queries,
        keys_local,
        values_local,
        keys_all,
        values_all,
        log_totals,
        attended,
        normed_two_all,
        hidden_pre,
    ) = kept
    w_qkv, w_out, w_up, w_down = layer_weights
    grad_ffn = spread_grads(grad_stream.astype(jnp.bfloat16))
    hidden_act, gelu_back = jax.vjp(gelu_exact, hidden_pre)
    grad_down = jnp.einsum(
        "nf,nd->fd", hidden_act.astype(jnp.bfloat16), grad_ffn, preferred_element_type=jnp.float32
    )
    grad_act = jnp.einsum("nd,fd->nf", grad_ffn, w_down, preferred_element_type=jnp.float32)
    (grad_pre,) = gelu_back(grad_act)
    grad_pre = grad_pre.astype(jnp.bfloat16)
    grad_up = jnp.einsum("nd,nf->df", normed_two_all, grad_pre, preferred_element_type=jnp.float32)
    grad_normed_two = sum_grads(grad_pre, w_up, row_share)
    _, norm_back_two = jax.vjp(layer_norm, middle, norm_rows[1, 0], norm_rows[1, 1])
    grad_mid, gain_two, shift_two = norm_back_two(grad_normed_two)
    grad_middle = grad_stream + grad_mid
    grad_attn = spread_grads(grad_middle.astype(jnp.bfloat16))
    grad_out_w = jnp.einsum("nf,nd->fd", attended, grad_attn, preferred_element_type=jnp.float32)
    grad_heads = (
        jnp.einsum("nd,fd->nf", grad_attn, w_out, preferred_element_type=jnp.float32)
        .astype(jnp.bfloat16)
        .reshape(queries.shape)
    )
    grad_query, grad_key, grad_value = attend_back(
        queries, keys_all, values_all, grad_heads, log_totals, live_keys
    )
    grad_packed = (
        jnp.stack((grad_query, grad_key, grad_value), axis=2)
        .astype(jnp.bfloat16)
        .reshape(normed_all.shape[0], -1)
    )
    grad_qkv = jnp.einsum(
        "nd,nc->dc", normed_all, grad_packed, preferred_element_type=jnp.float32
    ).reshape(w_qkv.shape)
    grad_normed = sum_grads(grad_packed, w_qkv.reshape(w_qkv.shape[0], -1), row_share)
    _, norm_back_one = jax.vjp(layer_norm, stream, norm_rows[0, 0], norm_rows[0, 1])
    grad_input, gain_one, shift_one = norm_back_one(grad_normed)
    norm_grads = jnp.stack((jnp.stack((gain_one, shift_one)), jnp.stack((gain_two, shift_two))))
    return (grad_middle + grad_input, (grad_qkv, grad_out_w, grad_up, grad_down), norm_grads)


def plain_step(
    token_ids,
    targets,
    masked,
    lengths,
    family_weight,
    embed_table,
    w_qkv,
    w_out,
    w_up,
    w_down,
    norm_params,
):
    blk_count = lax.axis_size("blk")
    head_count = lax.axis_size("head")
    seq_count, blk_tokens = token_ids.shape
    row_share = seq_count * blk_tokens // head_count
    row_first = lax.axis_index("head") * row_share
    blk_start = lax.axis_index("blk") * blk_tokens
    table_all, qkv_all, out_all, up_all, down_all, norm_all = (
        lax.all_gather(embed_table.astype(jnp.bfloat16), "blk", axis=1, tiled=True),
        lax.all_gather(w_qkv.astype(jnp.bfloat16), "blk", axis=1, tiled=True),
        lax.all_gather(w_out.astype(jnp.bfloat16), "blk", axis=2, tiled=True),
        lax.all_gather(w_up.astype(jnp.bfloat16), "blk", axis=1, tiled=True),
        lax.all_gather(w_down.astype(jnp.bfloat16), "blk", axis=1, tiled=True),
        lax.all_gather(norm_params.astype(jnp.bfloat16), "blk", axis=2, tiled=True),
    )
    token_table = table_all[:VOCAB]
    place_rows = lax.dynamic_slice_in_dim(table_all, VOCAB + blk_start, blk_tokens, 0)
    norm_rows = norm_all.astype(jnp.float32)
    live_keys = jnp.arange(blk_tokens * blk_count)[None, :] < lengths[:, None]
    positions = blk_start + jnp.arange(blk_tokens)
    live_local = positions[None, :] < lengths[:, None]
    seq_of_row = (row_first + jnp.arange(row_share)) // blk_tokens
    place_of_row = (row_first + jnp.arange(row_share)) % blk_tokens
    seq_hot = (seq_of_row[:, None] == jnp.arange(seq_count)[None, :]).astype(jnp.float32)
    place_hot = place_of_row[:, None] == jnp.arange(blk_tokens)[None, :]
    row_family = jnp.dot(seq_hot, family_weight, precision=HIGHEST)
    row_live = lax.dynamic_slice_in_dim(live_local.reshape(-1), row_first, row_share, 0).astype(
        jnp.float32
    )[:, None]
    row_ids = lax.dynamic_slice_in_dim(token_ids.reshape(-1), row_first, row_share, 0)
    row_targets = lax.dynamic_slice_in_dim(targets.reshape(-1), row_first, row_share, 0)
    row_masked = lax.dynamic_slice_in_dim(masked.reshape(-1), row_first, row_share, 0)
    token_hot = row_ids[:, None] == jnp.arange(VOCAB)[None, :]
    stream = jnp.dot(
        token_hot.astype(jnp.bfloat16), token_table, preferred_element_type=jnp.float32
    ) + jnp.dot(place_hot.astype(jnp.bfloat16), place_rows, preferred_element_type=jnp.float32)
    layer_stats = []
    kept_all = []
    for layer_idx in range(LAYERS):
        layer_weights = (
            qkv_all[layer_idx],
            out_all[layer_idx],
            up_all[layer_idx],
            down_all[layer_idx],
        )
        layer_stats.append(jnp.sum(stream * stream * row_live))
        stream, attn_out, ffn_out, kept = layer_forward(
            stream,
            layer_weights,
            norm_rows[2 * layer_idx : 2 * layer_idx + 2],
            live_keys,
            row_share,
        )
        layer_stats.append(jnp.sum(attn_out * attn_out * row_live))
        layer_stats.append(jnp.sum(ffn_out * ffn_out * row_live))
        kept_all.append(kept)
    final_low = layer_norm(stream, norm_rows[2 * LAYERS, 0], norm_rows[2 * LAYERS, 1]).astype(
        jnp.bfloat16
    )
    logits = jnp.einsum("nd,vd->nv", final_low, token_table, preferred_element_type=jnp.float32)
    shifted = logits - jnp.max(logits, axis=-1, keepdims=True)
    log_probs = shifted - jnp.log(jnp.sum(jnp.exp(shifted), axis=-1, keepdims=True))
    target_hot = (row_targets[:, None] == jnp.arange(VOCAB)[None, :]).astype(jnp.float32)
    token_loss = -jnp.sum(target_hot * log_probs, axis=1)
    token_weight = row_masked.astype(jnp.float32) * row_family
    loss_sum, weight_sum, squares = lax.psum(
        (jnp.sum(token_weight * token_loss), jnp.sum(token_weight), jnp.stack(layer_stats)),
        ("blk", "head"),
    )
    grad_logits = ((token_weight / weight_sum)[:, None] * (jnp.exp(log_probs) - target_hot)).astype(
        jnp.bfloat16
    )
    grad_final = jnp.einsum(
        "nv,vd->nd", grad_logits, token_table, preferred_element_type=jnp.float32
    )
    grad_table = jnp.einsum("nv,nd->vd", grad_logits, final_low, preferred_element_type=jnp.float32)
    _, final_back = jax.vjp(layer_norm, stream, norm_rows[2 * LAYERS, 0], norm_rows[2 * LAYERS, 1])
    grad_stream, gain_last, shift_last = final_back(grad_final)
    layer_grads = []
    norm_grads = []
    for layer_idx in reversed(range(LAYERS)):
        layer_weights = (
            qkv_all[layer_idx],
            out_all[layer_idx],
            up_all[layer_idx],
            down_all[layer_idx],
        )
        grad_stream, grads_now, norms_now = layer_backward(
            grad_stream,
            kept_all[layer_idx],
            layer_weights,
            norm_rows[2 * layer_idx : 2 * layer_idx + 2],
            live_keys,
            row_share,
        )
        layer_grads.insert(0, grads_now)
        norm_grads.insert(0, norms_now)
    grad_table = grad_table + jnp.dot(
        token_hot.astype(jnp.float32).T, grad_stream, precision=HIGHEST
    )
    grad_place = jnp.dot(place_hot.astype(jnp.float32).T, grad_stream, precision=HIGHEST)
    grad_norms = jnp.concatenate(norm_grads + [jnp.stack((gain_last, shift_last))[None]], axis=0)
    stacked = [
        jnp.stack([layer_entry[slot_idx] for layer_entry in layer_grads]) for slot_idx in range(4)
    ]
    table_sum, place_sum, norm_sum = (
        lax.psum(grad_table.astype(jnp.bfloat16), "head").astype(jnp.float32),
        lax.psum(grad_place.astype(jnp.bfloat16), "head").astype(jnp.float32),
        lax.psum(grad_norms.astype(jnp.bfloat16), "head").astype(jnp.float32),
    )
    place_full = lax.dynamic_update_slice_in_dim(
        jnp.zeros((blk_tokens * blk_count, place_sum.shape[1]), jnp.float32),
        place_sum,
        blk_start,
        0,
    )
    full_table = jnp.concatenate((table_sum, place_full), axis=0)
    reduced = (
        lax.psum_scatter(full_table, "blk", scatter_dimension=1, tiled=True),
        lax.psum_scatter(stacked[0], "blk", scatter_dimension=1, tiled=True),
        lax.psum_scatter(stacked[1], "blk", scatter_dimension=2, tiled=True),
        lax.psum_scatter(stacked[2], "blk", scatter_dimension=1, tiled=True),
        lax.psum_scatter(stacked[3], "blk", scatter_dimension=1, tiled=True),
        lax.psum_scatter(norm_sum, "blk", scatter_dimension=2, tiled=True),
    )
    sharded_squares = sum((jnp.sum(grad_part * grad_part) for grad_part in reduced[1:5]))
    shared_squares = (
        jnp.sum(reduced[0] * reduced[0]) + jnp.sum(reduced[5] * reduced[5])
    ) / head_count
    grad_norm = jnp.sqrt(lax.psum(sharded_squares + shared_squares, ("blk", "head")))
    return loss_sum, weight_sum, grad_norm, squares, reduced


BF16 = jnp.bfloat16
F32 = jnp.float32
MESH = pl.DeviceIdType.MESH
LOG2E = 1.4426950408889634
NORM_LANE = 32


def dot(left, right, left_dim, right_dim):
    return lax.dot_general(
        left, right, (((left_dim,), (right_dim,)), ((), ())), preferred_element_type=F32
    )


class Sizes:
    def __init__(self, blk, head, seqs, blk_tokens, w_qkv, w_up, w_down):
        self.B, self.H, self.S = blk, head, seqs
        self.L = w_qkv[0]
        self.DB = w_qkv[1]
        self.D = self.DB * blk
        self.HC = w_qkv[3]
        self.T = blk_tokens * blk
        self.G = blk // seqs if blk % seqs == 0 else 0
        self.FD = w_down[1]
        if self.G:
            self.NR = self.G * head
            self.R = self.T // self.NR
            self.NC = self.NR // 2
            self.FU = w_up[2] // self.G

    def fused(self, blk_tokens):
        if not self.G or self.H % 2 or self.R != blk_tokens or self.R != 128:
            return False
        if self.FU != self.FD * self.S or 3 * self.S > 16 or VOCAB > NORM_LANE:
            return False
        if NORM_LANE + 2 * (2 * self.L + 1) > 128:
            return False
        if any(n % 16 for n in (self.DB, self.HC, self.FD)) or self.D % 128 or self.FU % 128:
            return False
        weights = self.L * 2 * (4 * self.D * self.HC + 2 * self.D * self.FU)
        kept = self.L * self.T * (6 * self.D + 6 * self.FU + 14 * self.HC)
        return 3 * weights + kept + 16 * self.T * self.D + 8 * self.T * 256 * 4 < (60 << 20)


def step_kernel(
    z,
    lens,
    fam,
    ids,
    tp,
    wq_own,
    wo_own,
    wu_own,
    wd_own,
    scal_out,
    gq_out,
    go_out,
    gu_out,
    gd_out,
    gp_out,
    gs_out,
    idsg,
    tpg,
    etg,
    ptg,
    wq,
    wo,
    wu,
    wd,
    h1,
    h2,
    df,
    da,
    act,
    slope,
    du,
    qt,
    kt,
    vt,
    o32,
    ob,
    dob,
    lse,
    dqkv,
    bias,
    xs,
    xm,
    keep,
    psrc,
    csrc,
    srecv,
    rrecv,
    sg,
    stq,
    sto,
    stu,
    std,
    rq,
    ro,
    ru,
    rd,
    fst,
    frx,
    hrx,
    scg,
    id_s,
    id_r,
    tp_s,
    tp_r,
    wl,
    w_s,
    w_r,
    ag_s,
    ag_r,
    rs_s,
    rs_r,
    g_s,
    g_r,
    f_s,
    f_r,
    hx_s,
    hx_r,
    sc_s,
    sc_r,
):
    B, H, S, G, L, D, DB, HC, R, NC, NR, FU, FD, T = (
        z.B, z.H, z.S, z.G, z.L, z.D, z.DB, z.HC, z.R, z.NC, z.NR, z.FU, z.FD, z.T,
    )
    N_HEADS = HC // HEAD_DIM
    W = 2 * R
    QT = 2
    scale = HEAD_DIM ** (-0.5)
    c2 = scale * LOG2E
    b = lax.axis_index("blk")
    h = lax.axis_index("head")
    s, g = b // G, b % G
    y, c = h // 2, h % 2
    own_row = g * H + h

    def dev(blk_i, head_i):
        return (blk_i, head_i)

    sibling = dev(b, y * 2 + 1 - c)

    def peer(k):
        return dev(s * G + (g + k // 2) % G, ((y + k % 2) % 2) * 2 + c)

    def back(k):
        return ((-(k // 2)) % G) * 2 + k % 2

    waits = []

    def send(src, dst, ssem, rsem, device):
        copy = pltpu.make_async_remote_copy(src, dst, ssem, rsem, device, MESH)
        copy.start()
        return copy

    def arrived(dst, ssem, rsem):
        pltpu.make_async_remote_copy(dst, dst, ssem, rsem, sibling, MESH).wait_recv()

    def over_blk(body):
        def one(k, carry):
            body(lax.rem(b + k, B))
            return carry

        lax.fori_loop(1, B, one, 0)

    def over_seq(body):
        def one(k, carry):
            body(lax.rem(s + k, S))
            return carry

        lax.fori_loop(1, S, one, 0)

    def rows(i, n):
        return pl.ds(pl.multiple_of(i * n, 16), n)

    barrier = pltpu.get_barrier_semaphore()

    def greet(k, carry):
        other = lax.rem(b * H + h + k, B * H)
        pl.semaphore_signal(barrier, inc=1, device_id=dev(other // H, other % H), device_id_type=MESH)
        return carry

    lax.fori_loop(1, B * H, greet, 0)
    pl.semaphore_wait(barrier, B * H - 1)

    def send_tp(other):
        send(tp.at[(other % G) * H + h], tpg.at[b], tp_s.at[other], tp_r.at[b], dev(other, h))
        send(ids, idsg.at[b], id_s.at[other], id_r.at[b], dev(other, h))

    over_blk(send_tp)
    idsg[b] = ids[...]
    tpg[b] = tp[own_row]

    def w_sems(sems, l, kind, i):
        return sems.at[(l * 4 + kind) * B + i]

    def own_copy(l, kind):
        src, dst = {
            0: lambda: (wq_own.at[l], wq.at[l, rows(b, DB)]),
            1: lambda: (wo_own.at[l], wo.at[l, rows(b, DB)]),
            2: lambda: (wu_own.at[l, g], wu.at[l, rows(b, DB)]),
            3: lambda: (wd_own.at[l], wd.at[l, rows(s, FD)]),
        }[kind]()
        return pltpu.make_async_copy(src, dst, wl.at[l * 4 + kind])

    def send_weights(l, kind):
        own_copy(l, kind).start()

        def one(other):
            src, dst = {
                0: lambda: (wq_own.at[l], wq.at[l, rows(b, DB)]),
                1: lambda: (wo_own.at[l], wo.at[l, rows(b, DB)]),
                2: lambda: (wu_own.at[l, other % G], wu.at[l, rows(b, DB)]),
            }[kind]()
            send(src, dst, w_sems(w_s, l, kind, other), w_sems(w_r, l, kind, b), dev(other, h))

        def one_down(other):
            send(
                wd_own.at[l],
                wd.at[l, rows(s, FD)],
                w_sems(w_s, l, 3, other),
                w_sems(w_r, l, 3, s),
                dev(other * G + g, h),
            )

        if kind == 3:
            over_seq(one_down)
        else:
            over_blk(one)

    def weight_blocks(l, kind, other):
        return {
            0: lambda: wq.at[l, rows(other, DB)],
            1: lambda: wo.at[l, rows(other, DB)],
            2: lambda: wu.at[l, rows(other, DB)],
            3: lambda: wd.at[l, rows(other, FD)],
        }[kind]()

    def wait_weights(l, kind):
        own_copy(l, kind).wait()

        def one(other):
            arrived(
                weight_blocks(l, kind, other),
                w_sems(w_s, l, kind, other),
                w_sems(w_r, l, kind, other),
            )

        (over_seq if kind == 3 else over_blk)(one)

    def wait_weights_sent(l, kind):
        def one(other):
            block = weight_blocks(l, kind, other)
            pltpu.make_async_remote_copy(
                block, block, w_sems(w_s, l, kind, other), w_sems(w_r, l, kind, other), sibling, MESH
            ).wait_send()

        (over_seq if kind == 3 else over_blk)(one)

    send_weights(0, 0)
    send_weights(0, 1)

    def ag_sem(sems, use, i):
        return sems.at[use * 2 * NC + i]

    def block(buf, k, half):
        return buf.at[:, k * W + half * R : k * W + half * R + R]

    def spread(buf, use, slots):
        for k in reversed(slots):
            if k:
                waits.append(
                    send(
                        block(buf, 0, 0),
                        block(buf, back(k), 0),
                        ag_sem(ag_s, use, k),
                        ag_sem(ag_r, use, back(k)),
                        peer(k),
                    )
                )
        waits.append(
            send(block(buf, 0, 0), block(buf, 0, 1), ag_sem(ag_s, use, NC), ag_sem(ag_r, use, NC), sibling)
        )

    def hand_on(buf, use, k):
        arrived(block(buf, k, 0), ag_sem(ag_s, use, k), ag_sem(ag_r, use, k))
        waits.append(
            send(
                block(buf, k, 0),
                block(buf, k, 1),
                ag_sem(ag_s, use, NC + k),
                ag_sem(ag_r, use, NC + k),
                sibling,
            )
        )

    def have(buf, use, k):
        arrived(block(buf, k, 1), ag_sem(ag_s, use, NC + k), ag_sem(ag_r, use, NC + k))

    staged = {}

    def rs_sem(sems, use, i):
        return sems.at[use * 2 * NC + i]

    def stage(ref, key, value):
        if key in staged:
            staged.pop(key).wait_send()
        ref[...] = value

    def part(use, k, value):
        keep[k] = value[:, :R]
        stage(psrc.at[k], ("p", k), value[:, R:].astype(BF16))
        staged["p", k] = send(
            psrc.at[k], srecv.at[use, k], rs_sem(rs_s, use, k), rs_sem(rs_r, use, k), sibling
        )

    def pair_sum(use, k):
        arrived(srecv.at[use, k], rs_sem(rs_s, use, k), rs_sem(rs_r, use, k))
        return keep[k] + srecv[use, k].astype(F32)

    def pass_on(use, k):
        stage(csrc.at[k], ("c", k), pair_sum(use, k).astype(BF16))
        staged["c", k] = send(
            csrc.at[k],
            rrecv.at[use, back(k)],
            rs_sem(rs_s, use, NC + k),
            rs_sem(rs_r, use, NC + back(k)),
            peer(k),
        )

    def total(use, slots):
        out = pair_sum(use, 0)
        for k in slots:
            if k:
                arrived(rrecv.at[use, k], rs_sem(rs_s, use, NC + k), rs_sem(rs_r, use, NC + k))
                out = out + rrecv[use, k].astype(F32)
        return out

    def g_sems(sems, l, kind, i):
        return sems.at[(l * 4 + kind) * B + i]

    def grad_refs(l, kind):
        return ((stq, rq), (sto, ro), (stu, ru), (std, rd))[kind]

    def send_grads(l, kind, value):
        src, dst = grad_refs(l, kind)
        if l != L - 1:
            wait_grads_sent(l + 1, kind)
        src[...] = value.astype(BF16)
        n, me = (FD, s) if kind == 3 else (DB, b)
        dst[l, me] = src[rows(me, n)]

        def one(other):
            target = dev(other * G + g, h) if kind == 3 else dev(other, h)
            send(
                src.at[rows(other, n)],
                dst.at[l, me],
                g_sems(g_s, l, kind, other),
                g_sems(g_r, l, kind, me),
                target,
            )

        (over_seq if kind == 3 else over_blk)(one)

    def wait_grads_sent(l, kind):
        src, dst = grad_refs(l, kind)
        n = FD if kind == 3 else DB

        def one(other):
            pltpu.make_async_remote_copy(
                src.at[rows(other, n)],
                dst.at[l, other],
                g_sems(g_s, l, kind, other),
                g_sems(g_r, l, kind, other),
                sibling,
                MESH,
            ).wait_send()

        (over_seq if kind == 3 else over_blk)(one)

    def wait_grads(l, kind):
        _, dst = grad_refs(l, kind)

        def one(other):
            arrived(dst.at[l, other], g_sems(g_s, l, kind, other), g_sems(g_r, l, kind, other))

        (over_seq if kind == 3 else over_blk)(one)

    length = lens[s]
    for k in range(NC):
        for half in range(2):
            core = c if half == 0 else 1 - c
            block_row = ((g + k // 2) % G) * H + ((y + k % 2) % 2) * 2 + core
            place = block_row * R + lax.broadcasted_iota(jnp.int32, (R, 128), 0)
            bias[k * W + half * R : k * W + half * R + R, :] = jnp.where(place < length, 0.0, NEGATIVE)
    lane_place = own_row * R + lax.broadcasted_iota(jnp.int32, (1, R), 1)
    live = jnp.where(lane_place < length, 1.0, 0.0)
    dqkv[0:HC, QT * W :] = jnp.zeros((HC, T - QT * W), BF16)
    sg[...] = jnp.zeros((D, 128), F32)
    lane = lax.broadcasted_iota(jnp.int32, (D, 128), 1)
    row_of = lax.broadcasted_iota(jnp.int32, (128, R), 0)

    def tp_here(other):
        arrived(tpg.at[other], tp_s.at[other], tp_r.at[other])
        arrived(idsg.at[other], id_s.at[other], id_r.at[other])

    over_blk(tp_here)
    for i in range(B):
        etg[i * DB : (i + 1) * DB] = tpg[i, :DB]
        ptg[i * DB : (i + 1) * DB] = tpg[i, DB:]
    token_row = idsg[own_row, pl.ds(s, 1), :]
    target_row = idsg[own_row, pl.ds(S + s, 1), :]
    mask_row = idsg[own_row, pl.ds(2 * S + s, 1), :].astype(F32)
    token_hot = jnp.where(row_of == token_row, 1.0, 0.0).astype(BF16)
    token_weight = mask_row * fam[s]
    weight_sum = jnp.zeros((1, 1), F32)
    for i in range(S):
        counts = jnp.zeros((1, R), F32)
        for j in range(B):
            counts = counts + idsg[j, 2 * S + i : 2 * S + i + 1, :].astype(F32)
        weight_sum = weight_sum + jnp.sum(counts, axis=1, keepdims=True) * fam[i]

    def gain(i):
        return etg[:, NORM_LANE + 2 * i : NORM_LANE + 2 * i + 1].astype(F32)

    def shift(i):
        return etg[:, NORM_LANE + 2 * i + 1 : NORM_LANE + 2 * i + 2].astype(F32)

    def normalize(v):
        centred = v - jnp.mean(v, axis=0, keepdims=True)
        rstd = lax.rsqrt(jnp.mean(centred * centred, axis=0, keepdims=True) + NORM_EPS)
        return centred * rstd, rstd

    def layer_norm_low(v, i):
        hat, _ = normalize(v)
        return (hat * gain(i) + shift(i)).astype(BF16)

    def layer_norm_back(grad, v, i):
        hat, rstd = normalize(v)
        gain_grad = jnp.sum(grad * hat, axis=1, keepdims=True)
        shift_grad = jnp.sum(grad, axis=1, keepdims=True)
        sg[...] += jnp.where(lane == NORM_LANE + 2 * i, gain_grad, 0.0) + jnp.where(
            lane == NORM_LANE + 2 * i + 1, shift_grad, 0.0
        )
        scaled = grad * gain(i)
        mean_one = jnp.mean(scaled, axis=0, keepdims=True)
        mean_two = jnp.mean(scaled * hat, axis=0, keepdims=True)
        return rstd * (scaled - mean_one - hat * mean_two)

    def square_sum(v):
        return jnp.sum(jnp.sum(v * v, axis=0, keepdims=True) * live, axis=1, keepdims=True)

    slots = list(range(NC))
    near = slots[:2]
    far = slots[1:]
    stats = []
    xs[0] = dot(etg[...], token_hot, 1, 0) + ptg[...].astype(F32)

    def cols(k):
        return slice(k * W, (k + 1) * W)

    for l in range(L):
        x = xs[l]
        stats.append(square_sum(x))
        h1[l, :, 0:R] = layer_norm_low(x, 2 * l)
        spread(h1.at[l], 3 * l, slots)
        if l == 0:
            for kind in (2, 3):
                send_weights(0, kind)

        wait_weights(l, 0)

        def project(k):
            if k in near:
                packed = dot(wq[l], h1[l, :, cols(k)], 0, 0).astype(BF16)
                qt[l, :, cols(k)] = packed[0:HC]
                packed = packed[HC:]
            else:
                packed = dot(wq[l, :, :], h1[l, :, cols(k)], 0, 0).astype(BF16)[HC:]
            kt[l, :, cols(k)] = packed[0:HC]
            vt[l, :, cols(k)] = packed[HC:]

        have(h1.at[l], 3 * l, 0)
        project(0)
        for k in far:
            hand_on(h1.at[l], 3 * l, k)
            if k > 1:
                have(h1.at[l], 3 * l, k - 1)
                project(k - 1)
        have(h1.at[l], 3 * l, NC - 1)
        project(NC - 1)
        if l == 0:
            for kind in (0, 1, 2, 3):
                for later in range(1, L):
                    send_weights(later, kind)

        def attend(q, first, last):
            def one(i, carry):
                at = rows(i, HEAD_DIM)
                scores = dot(kt[l, at, :], qt[l, at, cols(q)], 0, 0) + jnp.concatenate([bias[...]] * 2, axis=1)
                peak = jnp.max(scores, axis=0, keepdims=True)
                exps = jnp.exp2((scores - peak) * c2)
                norm = jnp.sum(exps, axis=0, keepdims=True)
                probs = (exps * (1.0 / norm)).astype(BF16)
                out = dot(vt[l, at, :], probs, 1, 0)
                o32[l, at, cols(q)] = out
                ob[l, at, cols(q)] = out.astype(BF16)
                lse[l, pl.ds(pl.multiple_of(i * 8, 8), 8), cols(q)] = jnp.broadcast_to(
                    peak * c2 + jnp.log(norm) * LOG2E, (8, W)
                )
                return carry

            lax.fori_loop(first, last, one, 0)

        attend(1, 0, N_HEADS)
        wait_weights(l, 1)
        part(4 * l, 1, dot(wo[l], ob[l, :, cols(1)], 1, 0))
        attend(0, 0, N_HEADS // 2)
        pass_on(4 * l, 1)
        attend(0, N_HEADS // 2, N_HEADS)
        part(4 * l, 0, dot(wo[l], ob[l, :, cols(0)], 1, 0))
        attn_out = total(4 * l, near)
        stats.append(square_sum(attn_out))
        middle = xs[l] + attn_out
        xm[l] = middle
        h2[l, :, 0:R] = layer_norm_low(middle, 2 * l + 1)
        spread(h2.at[l], 3 * l + 1, slots)
        wait_weights(l, 2)
        wait_weights(l, 3)

        def feed(k):
            pre = dot(wu[l], h2[l, :, cols(k)], 0, 0)
            cdf = 0.5 * (1.0 + lax.erf(pre * (0.5**0.5)))
            low = (pre * cdf).astype(BF16)
            act[l, :, cols(k)] = low
            slope[l, :, cols(k)] = cdf + pre * (jnp.exp(-0.5 * pre * pre) * 0.3989422804014327)
            part(4 * l + 1, k, dot(wd[l], low, 0, 0))

        have(h2.at[l], 3 * l + 1, 0)
        feed(0)
        for k in far:
            hand_on(h2.at[l], 3 * l + 1, k)
            if k > 1:
                have(h2.at[l], 3 * l + 1, k - 1)
                feed(k - 1)
                if k > 2:
                    pass_on(4 * l + 1, k - 2)
        have(h2.at[l], 3 * l + 1, NC - 1)
        feed(NC - 1)
        for k in far[-2:]:
            pass_on(4 * l + 1, k)
        ffn_out = total(4 * l + 1, slots)
        stats.append(square_sum(ffn_out))
        xs[l + 1] = xm[l] + ffn_out

    last = xs[L]
    final_low = layer_norm_low(last, 2 * L)
    logits = dot(etg[...], final_low, 0, 0)[0:NORM_LANE]
    vocab_row = row_of[0:NORM_LANE]
    logits = jnp.where(vocab_row < VOCAB, logits, NEGATIVE)
    shifted = logits - jnp.max(logits, axis=0, keepdims=True)
    log_probs = shifted - jnp.log(jnp.sum(jnp.exp(shifted), axis=0, keepdims=True))
    target_hot = jnp.where(vocab_row == target_row, 1.0, 0.0)
    token_loss = -jnp.sum(target_hot * log_probs, axis=0, keepdims=True)
    loss = jnp.sum(token_weight * token_loss, axis=1, keepdims=True)
    grad_logits = ((token_weight / weight_sum) * (jnp.exp(log_probs) - target_hot)).astype(BF16)
    grad_logits = jnp.concatenate([grad_logits, jnp.zeros((128 - NORM_LANE, R), BF16)], axis=0)
    grad_final = dot(etg[...], grad_logits, 1, 0)
    sg[...] += dot(final_low, grad_logits, 1, 1)
    grad = layer_norm_back(grad_final, last, 2 * L)

    for l in reversed(range(L)):
        df[l, :, 0:R] = grad.astype(BF16)
        xs[l + 1] = grad
        spread(df.at[l], 3 * l + 2, slots)

        def feed_back(k):
            grad_act = dot(wd[l], df[l, :, cols(k)], 1, 0)
            low = (grad_act * slope[l, :, cols(k)]).astype(BF16)
            du[:, cols(k)] = low
            part(4 * l + 2, k, dot(wu[l], low, 1, 0))

        have(df.at[l], 3 * l + 2, 0)
        feed_back(0)
        for k in far:
            hand_on(df.at[l], 3 * l + 2, k)
            if k > 1:
                have(df.at[l], 3 * l + 2, k - 1)
                feed_back(k - 1)
                if k > 2:
                    pass_on(4 * l + 2, k - 2)
        have(df.at[l], 3 * l + 2, NC - 1)
        feed_back(NC - 1)
        for k in far[-2:]:
            pass_on(4 * l + 2, k)
        send_grads(l, 3, dot(act[l], df[l], 1, 1))
        send_grads(l, 2, dot(h2[l], du[...], 1, 1))
        grad_middle = xs[l + 1] + layer_norm_back(total(4 * l + 2, slots), xm[l], 2 * l + 1)
        xm[l] = grad_middle

        da[l, :, 0:R] = grad_middle.astype(BF16)
        spread(da.at[l], 3 * L + l, near)

        def out_back(k):
            dob[:, cols(k)] = dot(wo[l], da[l, :, cols(k)], 0, 0).astype(BF16)

        have(da.at[l], 3 * L + l, 0)
        out_back(0)
        hand_on(da.at[l], 3 * L + l, 1)
        have(da.at[l], 3 * L + l, 1)
        out_back(1)

        def attend_back(i, carry):
            at = rows(i, HEAD_DIM)
            key_h = kt[l, at, :]
            value_h = vt[l, at, :]
            grad_key = jnp.zeros((HEAD_DIM, T), F32)
            grad_value = jnp.zeros((HEAD_DIM, T), F32)
            for q in range(QT):
                query_h = qt[l, at, cols(q)]
                grad_h = dob[at, cols(q)]
                lse_h = lse[l, pl.ds(pl.multiple_of(i * 8, 8), 8), cols(q)][0:1]
                scores = dot(key_h, query_h, 0, 0) + jnp.concatenate([bias[...]] * 2, axis=1)
                probs = jnp.exp2(scores * c2 - lse_h)
                delta = jnp.sum(grad_h.astype(F32) * o32[l, at, cols(q)], axis=0, keepdims=True)
                grad_scores = (probs * (dot(value_h, grad_h, 0, 0) - delta)).astype(BF16)
                dqkv[at, cols(q)] = (dot(key_h, grad_scores, 1, 0) * scale).astype(BF16)
                grad_key = grad_key + dot(query_h, grad_scores, 1, 1)
                grad_value = grad_value + dot(grad_h, probs.astype(BF16), 1, 1)
            dqkv[pl.ds(pl.multiple_of(HC + i * HEAD_DIM, 16), HEAD_DIM), :] = (grad_key * scale).astype(BF16)
            dqkv[pl.ds(pl.multiple_of(2 * HC + i * HEAD_DIM, 16), HEAD_DIM), :] = grad_value.astype(BF16)
            return carry

        lax.fori_loop(0, N_HEADS, attend_back, 0)
        for k in reversed(slots):
            part(4 * l + 3, k, dot(wq[l], dqkv[:, cols(k)], 1, 0))
            if 0 < k + 1 < NC:
                pass_on(4 * l + 3, k + 1)
        send_grads(l, 0, dot(h1[l], dqkv[...], 1, 1))
        send_grads(l, 1, dot(da[l], ob[l], 1, 1))
        grad = xm[l] + layer_norm_back(total(4 * l + 3, slots), xs[l], 2 * l)

    high = grad.astype(BF16)
    low = (grad - high.astype(F32)).astype(BF16)
    small = sg[...] + dot(high, token_hot, 1, 1) + dot(low, token_hot, 1, 1)
    small = small.astype(BF16)
    for i in range(B):
        fst[i, :DB] = small[i * DB : (i + 1) * DB]
        fst[i, DB:] = high[i * DB : (i + 1) * DB]

    def send_table(other):
        send(fst.at[other], frx.at[b], f_s.at[other], f_r.at[b], dev(other, h))

    over_blk(send_table)
    frx[b] = fst[b]

    squares = jnp.zeros((1, 128), F32)

    def lanes_of(v):
        folded = jnp.sum(v * v, axis=0, keepdims=True)
        return jnp.sum(folded, axis=1, keepdims=True) + jnp.zeros((1, 128), F32)

    for l in reversed(range(L)):
        for kind in (3, 2, 1, 0):
            wait_grads(l, kind)
            if kind == 3:
                value = rd[l, 0].astype(F32)
                for i in range(1, S):
                    value = value + rd[l, i].astype(F32)
                gd_out[l] = value
                squares = squares + lanes_of(value)
            elif kind == 2:
                for j in range(G):
                    value = ru[l, j].astype(F32)
                    for i in range(1, S):
                        value = value + ru[l, i * G + j].astype(F32)
                    gu_out[l, j] = value
                    squares = squares + lanes_of(value)
            else:
                src, dst = ((rq, gq_out), (ro, go_out))[kind]
                value = src[l, 0].astype(F32)
                for i in range(1, B):
                    value = value + src[l, i].astype(F32)
                dst[l] = value
                squares = squares + lanes_of(value)

    def table_here(other):
        arrived(frx.at[other], f_s.at[other], f_r.at[other])

    over_blk(table_here)
    for j in range(G):
        value = frx[j, DB:].astype(F32)
        for i in range(1, S):
            value = value + frx[i * G + j, DB:].astype(F32)
        hrx[h, j] = value
        squares = squares + lanes_of(value)
    value = frx[0, :DB].astype(F32)
    for i in range(1, B):
        value = value + frx[i, :DB].astype(F32)
    hrx[h, G] = value

    def send_heads(k, carry):
        other = lax.rem(h + k, H)
        send(hrx.at[h], hrx.at[h], hx_s.at[other], hx_r.at[h], dev(b, other))
        return carry

    lax.fori_loop(1, H, send_heads, 0)

    def heads_here(k, carry):
        other = lax.rem(h + k, H)
        arrived(hrx.at[other], hx_s.at[other], hx_r.at[other])
        return carry

    lax.fori_loop(1, H, heads_here, 0)
    value = hrx[0, G]
    for i in range(1, H):
        value = value + hrx[i, G]
    gs_out[...] = value
    squares = squares + lanes_of(value) * (1.0 / H)

    lane_one = lax.broadcasted_iota(jnp.int32, (1, 128), 1)
    packed = jnp.where(lane_one == 0, loss, 0.0) + jnp.where(lane_one == 1, squares, 0.0)
    for i, stat in enumerate(stats):
        packed = packed + jnp.where(lane_one == 2 + i, stat, 0.0)
    me = b * H + h
    scg[me] = jnp.broadcast_to(packed, (8, 128))

    def send_scalars(k, carry):
        other = lax.rem(me + k, B * H)
        send(scg.at[me], scg.at[me], sc_s.at[other], sc_r.at[me], dev(other // H, other % H))
        return carry

    lax.fori_loop(1, B * H, send_scalars, 0)
    for i in range(H):
        for j in range(G):
            gp_out[j * H + i] = hrx[i, j]

    def scalars_here(k, carry):
        other = lax.rem(me + k, B * H)
        arrived(scg.at[other], sc_s.at[other], sc_r.at[other])
        return carry

    lax.fori_loop(1, B * H, scalars_here, 0)
    out = scg[0]
    for i in range(1, B * H):
        out = out + scg[i]
    lane_eight = lax.broadcasted_iota(jnp.int32, (8, 128), 1)
    out = jnp.where(lane_eight == 1, jnp.sqrt(out), out)
    scal_out[...] = jnp.where(lane_eight == 2 + 3 * L, weight_sum, out)

    for copy in waits:
        copy.wait_send()
    for copy in staged.values():
        copy.wait_send()
    for l in range(L):
        for kind in range(4):
            wait_weights_sent(l, kind)
    for kind in range(4):
        wait_grads_sent(0, kind)

    def sent(other):
        for src, ssem, rsem in ((tpg.at[other], tp_s, tp_r), (idsg.at[other], id_s, id_r), (frx.at[other], f_s, f_r)):
            pltpu.make_async_remote_copy(src, src, ssem.at[other], rsem.at[other], sibling, MESH).wait_send()

    over_blk(sent)

    def heads_sent(k, carry):
        other = lax.rem(h + k, H)
        pltpu.make_async_remote_copy(
            hrx.at[other], hrx.at[other], hx_s.at[other], hx_r.at[other], sibling, MESH
        ).wait_send()
        return carry

    lax.fori_loop(1, H, heads_sent, 0)

    def scalars_sent(k, carry):
        other = lax.rem(me + k, B * H)
        pltpu.make_async_remote_copy(
            scg.at[other], scg.at[other], sc_s.at[other], sc_r.at[other], sibling, MESH
        ).wait_send()
        return carry

    lax.fori_loop(1, B * H, scalars_sent, 0)


def fused_step(z, token_ids, targets, masked, lengths, family_weight, embed_table, w_qkv, w_out, w_up, w_down, norm_params):
    B, H, S, G, L, D, DB, HC, R, NC, NR, FU, FD, T = (
        z.B, z.H, z.S, z.G, z.L, z.D, z.DB, z.HC, z.R, z.NC, z.NR, z.FU, z.FD, z.T,
    )
    W = 2 * R
    ids = jnp.concatenate([token_ids, targets, masked], axis=0)
    ids = jnp.pad(ids, ((0, 16 - 3 * S), (0, 0)))
    table = embed_table.astype(BF16).T
    norms = norm_params.astype(BF16).transpose(2, 0, 1).reshape(DB, -1)
    token_part = jnp.concatenate(
        [
            table[:, :VOCAB],
            jnp.zeros((DB, NORM_LANE - VOCAB), BF16),
            norms,
            jnp.zeros((DB, 128 - NORM_LANE - norms.shape[1]), BF16),
        ],
        axis=1,
    )
    place_part = table[:, VOCAB:].reshape(DB, NR, R).transpose(1, 0, 2)
    tp = jnp.concatenate([jnp.broadcast_to(token_part[None], (NR, DB, 128)), place_part], axis=1)
    wq_own = w_qkv.astype(BF16).reshape(L, DB, 3 * HC)
    wo_own = w_out.astype(BF16).transpose(0, 2, 1)
    wu_own = w_up.astype(BF16).reshape(L, DB, S, G, FD).transpose(0, 3, 1, 2, 4).reshape(L, G, DB, FU)
    wd_own = w_down.astype(BF16)
    smem = pl.BlockSpec(memory_space=pltpu.SMEM)
    vmem = pl.BlockSpec(memory_space=pltpu.VMEM)
    hbm = pl.BlockSpec(memory_space=pl.ANY)
    dma = pltpu.SemaphoreType.DMA
    scratch = [
        pltpu.VMEM((B, 16, R), jnp.int32),
        pltpu.VMEM((B, 2 * DB, 128), BF16),
        pltpu.VMEM((D, 128), BF16),
        pltpu.VMEM((D, R), BF16),
        pltpu.VMEM((L, D, 3 * HC), BF16),
        pltpu.VMEM((L, D, HC), BF16),
        pltpu.VMEM((L, D, FU), BF16),
        pltpu.VMEM((L, FU, D), BF16),
        pltpu.VMEM((L, D, T), BF16),
        pltpu.VMEM((L, D, T), BF16),
        pltpu.VMEM((L, D, T), BF16),
        pltpu.VMEM((L, D, 2 * W), BF16),
        pltpu.VMEM((L, FU, T), BF16),
        pltpu.VMEM((L, FU, T), F32),
        pltpu.VMEM((FU, T), BF16),
        pltpu.VMEM((L, HC, 2 * W), BF16),
        pltpu.VMEM((L, HC, T), BF16),
        pltpu.VMEM((L, HC, T), BF16),
        pltpu.VMEM((L, HC, 2 * W), F32),
        pltpu.VMEM((L, HC, 2 * W), BF16),
        pltpu.VMEM((HC, 2 * W), BF16),
        pltpu.VMEM((L, 8 * (HC // HEAD_DIM), 2 * W), F32),
        pltpu.VMEM((3 * HC, T), BF16),
        pltpu.VMEM((T, 128), F32),
        pltpu.VMEM((L + 1, D, R), F32),
        pltpu.VMEM((L, D, R), F32),
        pltpu.VMEM((NC, D, R), F32),
        pltpu.VMEM((NC, D, R), BF16),
        pltpu.VMEM((NC, D, R), BF16),
        pltpu.VMEM((4 * L, NC, D, R), BF16),
        pltpu.VMEM((4 * L, NC, D, R), BF16),
        pltpu.VMEM((D, 128), F32),
        pltpu.VMEM((D, 3 * HC), BF16),
        pltpu.VMEM((D, HC), BF16),
        pltpu.VMEM((D, FU), BF16),
        pltpu.VMEM((FU, D), BF16),
        pltpu.VMEM((L, B, DB, 3 * HC), BF16),
        pltpu.VMEM((L, B, DB, HC), BF16),
        pltpu.VMEM((L, B, DB, FU), BF16),
        pltpu.VMEM((L, S, FD, D), BF16),
        pltpu.VMEM((B, 2 * DB, 128), BF16),
        pltpu.VMEM((B, 2 * DB, 128), BF16),
        pltpu.VMEM((H, G + 1, DB, 128), F32),
        pltpu.VMEM((B * H, 8, 128), F32),
        dma((B,)),
        dma((B,)),
        dma((B,)),
        dma((B,)),
        dma((4 * L,)),
        dma((4 * L * B,)),
        dma((4 * L * B,)),
        dma((4 * L * 2 * NC,)),
        dma((4 * L * 2 * NC,)),
        dma((4 * L * 2 * NC,)),
        dma((4 * L * 2 * NC,)),
        dma((4 * L * B,)),
        dma((4 * L * B,)),
        dma((B,)),
        dma((B,)),
        dma((H,)),
        dma((H,)),
        dma((B * H,)),
        dma((B * H,)),
    ]
    outs = (
        jax.ShapeDtypeStruct((8, 128), F32),
        jax.ShapeDtypeStruct((L, DB, 3 * HC), F32),
        jax.ShapeDtypeStruct((L, DB, HC), F32),
        jax.ShapeDtypeStruct((L, G, DB, FU), F32),
        jax.ShapeDtypeStruct((L, FD, D), F32),
        jax.ShapeDtypeStruct((NR, DB, R), F32),
        jax.ShapeDtypeStruct((DB, 128), F32),
    )
    scal, gq, go, gu, gd, gp, gs = pl.pallas_call(
        functools.partial(step_kernel, z),
        out_shape=outs,
        in_specs=[smem, smem, vmem, vmem, hbm, hbm, hbm, hbm],
        out_specs=[vmem] * 7,
        scratch_shapes=scratch,
        compiler_params=pltpu.CompilerParams(
            collective_id=0, has_side_effects=True, vmem_limit_bytes=62 << 20
        ),
        name="train_step",
    )(lengths, family_weight, ids, tp, wq_own, wo_own, wu_own, wd_own)
    grads = (
        jnp.concatenate([gs[:, :VOCAB].T, gp.transpose(0, 2, 1).reshape(T, DB)], axis=0),
        gq.reshape(L, DB, 3, HC),
        go.transpose(0, 2, 1),
        gu.reshape(L, G, DB, S, FD).transpose(0, 2, 3, 1, 4).reshape(L, DB, S * G * FD),
        gd,
        gs[:, NORM_LANE : NORM_LANE + 2 * (2 * L + 1)].T.reshape(2 * L + 1, 2, DB),
    )
    return scal[0], grads


def local(
    token_ids,
    targets,
    masked,
    lengths,
    family_weight,
    embed_table,
    w_qkv,
    w_out,
    w_up,
    w_down,
    norm_params,
    embed_first,
    qkv_first,
    out_first,
    up_first,
    down_first,
    norm_first,
    embed_second,
    qkv_second,
    out_second,
    up_second,
    down_second,
    norm_second,
):
    z = Sizes(
        lax.axis_size("blk"),
        lax.axis_size("head"),
        token_ids.shape[0],
        token_ids.shape[1],
        w_qkv.shape,
        w_up.shape,
        w_down.shape,
    )
    masters = (embed_table, w_qkv, w_out, w_up, w_down, norm_params)
    firsts = (embed_first, qkv_first, out_first, up_first, down_first, norm_first)
    seconds = (embed_second, qkv_second, out_second, up_second, down_second, norm_second)
    tokens = (token_ids, targets, masked, lengths, family_weight)
    if z.fused(token_ids.shape[1]):
        scal, grads = fused_step(z, *tokens, *masters)
        loss_sum, weight_sum, grad_norm = (scal[0], scal[2 + 3 * LAYERS], scal[1])
        squares = scal[2 : 2 + 3 * LAYERS]
    else:
        loss_sum, weight_sum, grad_norm, squares, grads = plain_step(*tokens, *masters)
    factor = CLIP_NORM / jnp.maximum(grad_norm, CLIP_NORM)
    stream_rms = jnp.sqrt(squares.reshape(LAYERS, 3) / (jnp.sum(lengths).astype(jnp.float32) * D))
    results = [loss_sum, weight_sum, grad_norm, stream_rms]
    for group_idx in range(6):
        first, second, weight = adamw_update(
            masters[group_idx],
            firsts[group_idx],
            seconds[group_idx],
            grads[group_idx] * factor,
            RATES[group_idx],
            DECAYS[group_idx],
        )
        results += [first, second, weight, weight.astype(jnp.bfloat16)]
    return tuple(results)


def solution(mesh):
    return jax.shard_map(
        local,
        mesh=mesh,
        in_specs=(
            P(None, "blk"),
            P(None, "blk"),
            P(None, "blk"),
            P(),
            P(),
            P(None, "blk"),
            P(None, "blk", None, "head"),
            P(None, "head", "blk"),
            P(None, "blk", "head"),
            P(None, ("head", "blk"), None),
            P(None, None, "blk"),
            P(None, "blk"),
            P(None, "blk", None, "head"),
            P(None, "head", "blk"),
            P(None, "blk", "head"),
            P(None, ("head", "blk"), None),
            P(None, None, "blk"),
            P(None, "blk"),
            P(None, "blk", None, "head"),
            P(None, "head", "blk"),
            P(None, "blk", "head"),
            P(None, ("head", "blk"), None),
            P(None, None, "blk"),
        ),
        out_specs=(
            P(),
            P(),
            P(),
            P(),
            P(None, "blk"),
            P(None, "blk"),
            P(None, "blk"),
            P(None, "blk"),
            P(None, "blk", None, "head"),
            P(None, "blk", None, "head"),
            P(None, "blk", None, "head"),
            P(None, "blk", None, "head"),
            P(None, "head", "blk"),
            P(None, "head", "blk"),
            P(None, "head", "blk"),
            P(None, "head", "blk"),
            P(None, "blk", "head"),
            P(None, "blk", "head"),
            P(None, "blk", "head"),
            P(None, "blk", "head"),
            P(None, ("head", "blk"), None),
            P(None, ("head", "blk"), None),
            P(None, ("head", "blk"), None),
            P(None, ("head", "blk"), None),
            P(None, None, "blk"),
            P(None, None, "blk"),
            P(None, None, "blk"),
            P(None, None, "blk"),
        ),
        check_vma=False,
    )
```

```python
import functools

import jax
import jax.numpy as jnp
from jax import lax
from jax.experimental import pallas as pl
from jax.experimental.pallas import tpu as pltpu
from jax.sharding import PartitionSpec as P

VOCAB = 25
D = 640
HEAD_DIM = 32
LAYERS = 2
STEP = 10


NEGATIVE = -1e30
NORM_EPS = 1e-05
CLIP_NORM = 0.01
BETA_FIRST = 0.9
BETA_SECOND = 0.999
ADAM_EPS = 1e-08
RATES = (0.2, 0.1, 0.5, 0.1, 0.03, 0.5)
DECAYS = (0.1, 0.1, 0.1, 0.1, 0.1, 0.0)
HIGHEST = lax.Precision.HIGHEST


def layer_norm(inputs, gain_row, shift_row):
    centred = inputs - jnp.mean(inputs, axis=-1, keepdims=True)
    spread = jnp.mean(centred * centred, axis=-1, keepdims=True)
    return centred * lax.rsqrt(spread + NORM_EPS) * gain_row + shift_row


def gelu_exact(inputs):
    return jax.nn.gelu(inputs, approximate=False)


def adamw_update(weight, first, second, gradient, rate, decay):
    first = BETA_FIRST * first + (1.0 - BETA_FIRST) * gradient
    second = BETA_SECOND * second + (1.0 - BETA_SECOND) * gradient * gradient
    first_hat = first / (1.0 - BETA_FIRST**STEP)
    second_hat = second / (1.0 - BETA_SECOND**STEP)
    weight = weight - rate * (first_hat / (jnp.sqrt(second_hat) + ADAM_EPS) + decay * weight)
    return (first, second, weight)


def slice_head(tensor, head_index):
    return lax.dynamic_slice_in_dim(tensor, head_index * HEAD_DIM, HEAD_DIM, tensor.ndim - 1)


def join_heads(stacked):
    moved = jnp.moveaxis(stacked, 0, 2)
    return moved.reshape(moved.shape[0], moved.shape[1], -1)


def spread_rows(normed):
    return lax.all_gather(normed, "head", axis=0, tiled=True)


def spread_grads(grad_rows):
    return lax.all_gather(grad_rows, "head", axis=0, tiled=True)


def sum_rows(full_rows, weight, row_share):

    def row_term(row_start, row_count):
        return jnp.dot(full_rows, weight, preferred_element_type=jnp.float32)

    return lax.psum_scatter(
        row_term(jnp.int32(0), row_share * lax.axis_size("head")),
        "head",
        scatter_dimension=0,
        tiled=True,
    )


def sum_grads(full_rows, weight, row_share):

    def row_term(row_start, row_count):
        return jnp.einsum("nc,dc->nd", full_rows, weight, preferred_element_type=jnp.float32)

    return lax.psum_scatter(
        row_term(jnp.int32(0), row_share * lax.axis_size("head")).astype(jnp.bfloat16),
        "head",
        scatter_dimension=0,
        tiled=True,
    ).astype(jnp.float32)


def attend(queries, keys_all, values_all, live_keys):
    local_heads = queries.shape[-1] // HEAD_DIM
    score_scale = HEAD_DIM ** (-0.5)
    live_mask = live_keys[:, None, :]

    def one_head(head_index):
        scores = (
            jnp.einsum(
                "ste,sje->stj",
                slice_head(queries, head_index),
                slice_head(keys_all, head_index),
                preferred_element_type=jnp.float32,
            )
            * score_scale
        )
        masked_scores = jnp.where(live_mask, scores, NEGATIVE)
        row_peak = jnp.max(masked_scores, axis=-1, keepdims=True)
        exp_scores = jnp.exp(masked_scores - row_peak)
        row_total = jnp.sum(exp_scores, axis=-1, keepdims=True)
        attn_probs = (exp_scores / row_total).astype(jnp.bfloat16)
        attended = jnp.einsum(
            "stj,sje->ste",
            attn_probs,
            slice_head(values_all, head_index),
            preferred_element_type=jnp.float32,
        )
        return (attended, (row_peak + jnp.log(row_total))[..., 0])

    outputs, log_totals = lax.map(one_head, jnp.arange(local_heads))
    return (join_heads(outputs), log_totals)


def attend_back(queries, keys_all, values_all, grad_heads, log_totals, live_keys):
    local_heads = queries.shape[-1] // HEAD_DIM
    score_scale = HEAD_DIM ** (-0.5)
    live_mask = live_keys[:, None, :]

    def one_head(head_index):
        query_h = slice_head(queries, head_index)
        key_h = slice_head(keys_all, head_index)
        grad_h = slice_head(grad_heads, head_index)
        scores = (
            jnp.einsum("ste,sje->stj", query_h, key_h, preferred_element_type=jnp.float32)
            * score_scale
        )
        masked_scores = jnp.where(live_mask, scores, NEGATIVE)
        attn_probs = jnp.exp(masked_scores - log_totals[head_index][..., None])
        grad_probs = jnp.einsum(
            "ste,sje->stj",
            grad_h,
            slice_head(values_all, head_index),
            preferred_element_type=jnp.float32,
        )
        row_delta = jnp.sum(attn_probs * grad_probs, axis=-1)
        grad_scores = (attn_probs * (grad_probs - row_delta[..., None])).astype(jnp.bfloat16)
        grad_query = (
            jnp.einsum("stj,sje->ste", grad_scores, key_h, preferred_element_type=jnp.float32)
            * score_scale
        )
        grad_key = (
            jnp.einsum("stj,ste->sje", grad_scores, query_h, preferred_element_type=jnp.float32)
            * score_scale
        )
        grad_value = jnp.einsum(
            "stj,ste->sje",
            attn_probs.astype(jnp.bfloat16),
            grad_h,
            preferred_element_type=jnp.float32,
        )
        return (grad_query, grad_key, grad_value)

    grad_query, grad_key, grad_value = lax.map(one_head, jnp.arange(local_heads))
    grad_key, grad_value = (
        lax.psum_scatter(grad_key, "blk", scatter_dimension=2, tiled=True),
        lax.psum_scatter(grad_value, "blk", scatter_dimension=2, tiled=True),
    )
    return (join_heads(grad_query), join_heads(grad_key), join_heads(grad_value))


def layer_forward(stream, layer_weights, norm_rows, live_keys, row_share):
    w_qkv, w_out, w_up, w_down = layer_weights
    seq_count = live_keys.shape[0]
    normed = layer_norm(stream, norm_rows[0, 0], norm_rows[0, 1]).astype(jnp.bfloat16)
    normed_all = spread_rows(normed)
    packed = jnp.dot(
        normed_all, w_qkv.reshape(w_qkv.shape[0], -1), preferred_element_type=jnp.float32
    ).astype(jnp.bfloat16)
    packed = packed.reshape(seq_count, -1, 3, w_qkv.shape[-1])
    queries, keys_local, values_local = (packed[:, :, 0], packed[:, :, 1], packed[:, :, 2])
    keys_all, values_all = (
        lax.all_gather(keys_local, "blk", axis=1, tiled=True),
        lax.all_gather(values_local, "blk", axis=1, tiled=True),
    )
    attended, log_totals = attend(queries, keys_all, values_all, live_keys)
    attended = attended.astype(jnp.bfloat16).reshape(-1, attended.shape[-1])
    attn_out = sum_rows(attended, w_out, row_share)
    middle = stream + attn_out
    normed_two = layer_norm(middle, norm_rows[1, 0], norm_rows[1, 1]).astype(jnp.bfloat16)
    normed_two_all = spread_rows(normed_two)
    hidden_pre = jnp.dot(normed_two_all, w_up, preferred_element_type=jnp.float32)
    hidden_act = gelu_exact(hidden_pre).astype(jnp.bfloat16)
    ffn_out = sum_rows(hidden_act, w_down, row_share)
    kept = (
        stream,
        middle,
        normed_all,
        queries,
        keys_local,
        values_local,
        keys_all,
        values_all,
        log_totals,
        attended,
        normed_two_all,
        hidden_pre,
    )
    return (middle + ffn_out, attn_out, ffn_out, kept)


def layer_backward(grad_stream, kept, layer_weights, norm_rows, live_keys, row_share):
    (
        stream,
        middle,
        normed_all,
        queries,
        keys_local,
        values_local,
        keys_all,
        values_all,
        log_totals,
        attended,
        normed_two_all,
        hidden_pre,
    ) = kept
    w_qkv, w_out, w_up, w_down = layer_weights
    grad_ffn = spread_grads(grad_stream.astype(jnp.bfloat16))
    hidden_act, gelu_back = jax.vjp(gelu_exact, hidden_pre)
    grad_down = jnp.einsum(
        "nf,nd->fd", hidden_act.astype(jnp.bfloat16), grad_ffn, preferred_element_type=jnp.float32
    )
    grad_act = jnp.einsum("nd,fd->nf", grad_ffn, w_down, preferred_element_type=jnp.float32)
    (grad_pre,) = gelu_back(grad_act)
    grad_pre = grad_pre.astype(jnp.bfloat16)
    grad_up = jnp.einsum("nd,nf->df", normed_two_all, grad_pre, preferred_element_type=jnp.float32)
    grad_normed_two = sum_grads(grad_pre, w_up, row_share)
    _, norm_back_two = jax.vjp(layer_norm, middle, norm_rows[1, 0], norm_rows[1, 1])
    grad_mid, gain_two, shift_two = norm_back_two(grad_normed_two)
    grad_middle = grad_stream + grad_mid
    grad_attn = spread_grads(grad_middle.astype(jnp.bfloat16))
    grad_out_w = jnp.einsum("nf,nd->fd", attended, grad_attn, preferred_element_type=jnp.float32)
    grad_heads = (
        jnp.einsum("nd,fd->nf", grad_attn, w_out, preferred_element_type=jnp.float32)
        .astype(jnp.bfloat16)
        .reshape(queries.shape)
    )
    grad_query, grad_key, grad_value = attend_back(
        queries, keys_all, values_all, grad_heads, log_totals, live_keys
    )
    grad_packed = (
        jnp.stack((grad_query, grad_key, grad_value), axis=2)
        .astype(jnp.bfloat16)
        .reshape(normed_all.shape[0], -1)
    )
    grad_qkv = jnp.einsum(
        "nd,nc->dc", normed_all, grad_packed, preferred_element_type=jnp.float32
    ).reshape(w_qkv.shape)
    grad_normed = sum_grads(grad_packed, w_qkv.reshape(w_qkv.shape[0], -1), row_share)
    _, norm_back_one = jax.vjp(layer_norm, stream, norm_rows[0, 0], norm_rows[0, 1])
    grad_input, gain_one, shift_one = norm_back_one(grad_normed)
    norm_grads = jnp.stack((jnp.stack((gain_one, shift_one)), jnp.stack((gain_two, shift_two))))
    return (grad_middle + grad_input, (grad_qkv, grad_out_w, grad_up, grad_down), norm_grads)


def plain_step(
    token_ids,
    targets,
    masked,
    lengths,
    family_weight,
    embed_table,
    w_qkv,
    w_out,
    w_up,
    w_down,
    norm_params,
):
    blk_count = lax.axis_size("blk")
    head_count = lax.axis_size("head")
    seq_count, blk_tokens = token_ids.shape
    row_share = seq_count * blk_tokens // head_count
    row_first = lax.axis_index("head") * row_share
    blk_start = lax.axis_index("blk") * blk_tokens
    table_all, qkv_all, out_all, up_all, down_all, norm_all = (
        lax.all_gather(embed_table.astype(jnp.bfloat16), "blk", axis=1, tiled=True),
        lax.all_gather(w_qkv.astype(jnp.bfloat16), "blk", axis=1, tiled=True),
        lax.all_gather(w_out.astype(jnp.bfloat16), "blk", axis=2, tiled=True),
        lax.all_gather(w_up.astype(jnp.bfloat16), "blk", axis=1, tiled=True),
        lax.all_gather(w_down.astype(jnp.bfloat16), "blk", axis=1, tiled=True),
        lax.all_gather(norm_params.astype(jnp.bfloat16), "blk", axis=2, tiled=True),
    )
    token_table = table_all[:VOCAB]
    place_rows = lax.dynamic_slice_in_dim(table_all, VOCAB + blk_start, blk_tokens, 0)
    norm_rows = norm_all.astype(jnp.float32)
    live_keys = jnp.arange(blk_tokens * blk_count)[None, :] < lengths[:, None]
    positions = blk_start + jnp.arange(blk_tokens)
    live_local = positions[None, :] < lengths[:, None]
    seq_of_row = (row_first + jnp.arange(row_share)) // blk_tokens
    place_of_row = (row_first + jnp.arange(row_share)) % blk_tokens
    seq_hot = (seq_of_row[:, None] == jnp.arange(seq_count)[None, :]).astype(jnp.float32)
    place_hot = place_of_row[:, None] == jnp.arange(blk_tokens)[None, :]
    row_family = jnp.dot(seq_hot, family_weight, precision=HIGHEST)
    row_live = lax.dynamic_slice_in_dim(live_local.reshape(-1), row_first, row_share, 0).astype(
        jnp.float32
    )[:, None]
    row_ids = lax.dynamic_slice_in_dim(token_ids.reshape(-1), row_first, row_share, 0)
    row_targets = lax.dynamic_slice_in_dim(targets.reshape(-1), row_first, row_share, 0)
    row_masked = lax.dynamic_slice_in_dim(masked.reshape(-1), row_first, row_share, 0)
    token_hot = row_ids[:, None] == jnp.arange(VOCAB)[None, :]
    stream = jnp.dot(
        token_hot.astype(jnp.bfloat16), token_table, preferred_element_type=jnp.float32
    ) + jnp.dot(place_hot.astype(jnp.bfloat16), place_rows, preferred_element_type=jnp.float32)
    layer_stats = []
    kept_all = []
    for layer_idx in range(LAYERS):
        layer_weights = (
            qkv_all[layer_idx],
            out_all[layer_idx],
            up_all[layer_idx],
            down_all[layer_idx],
        )
        layer_stats.append(jnp.sum(stream * stream * row_live))
        stream, attn_out, ffn_out, kept = layer_forward(
            stream,
            layer_weights,
            norm_rows[2 * layer_idx : 2 * layer_idx + 2],
            live_keys,
            row_share,
        )
        layer_stats.append(jnp.sum(attn_out * attn_out * row_live))
        layer_stats.append(jnp.sum(ffn_out * ffn_out * row_live))
        kept_all.append(kept)
    final_low = layer_norm(stream, norm_rows[2 * LAYERS, 0], norm_rows[2 * LAYERS, 1]).astype(
        jnp.bfloat16
    )
    logits = jnp.einsum("nd,vd->nv", final_low, token_table, preferred_element_type=jnp.float32)
    shifted = logits - jnp.max(logits, axis=-1, keepdims=True)
    log_probs = shifted - jnp.log(jnp.sum(jnp.exp(shifted), axis=-1, keepdims=True))
    target_hot = (row_targets[:, None] == jnp.arange(VOCAB)[None, :]).astype(jnp.float32)
    token_loss = -jnp.sum(target_hot * log_probs, axis=1)
    token_weight = row_masked.astype(jnp.float32) * row_family
    loss_sum, weight_sum, squares = lax.psum(
        (jnp.sum(token_weight * token_loss), jnp.sum(token_weight), jnp.stack(layer_stats)),
        ("blk", "head"),
    )
    grad_logits = ((token_weight / weight_sum)[:, None] * (jnp.exp(log_probs) - target_hot)).astype(
        jnp.bfloat16
    )
    grad_final = jnp.einsum(
        "nv,vd->nd", grad_logits, token_table, preferred_element_type=jnp.float32
    )
    grad_table = jnp.einsum("nv,nd->vd", grad_logits, final_low, preferred_element_type=jnp.float32)
    _, final_back = jax.vjp(layer_norm, stream, norm_rows[2 * LAYERS, 0], norm_rows[2 * LAYERS, 1])
    grad_stream, gain_last, shift_last = final_back(grad_final)
    layer_grads = []
    norm_grads = []
    for layer_idx in reversed(range(LAYERS)):
        layer_weights = (
            qkv_all[layer_idx],
            out_all[layer_idx],
            up_all[layer_idx],
            down_all[layer_idx],
        )
        grad_stream, grads_now, norms_now = layer_backward(
            grad_stream,
            kept_all[layer_idx],
            layer_weights,
            norm_rows[2 * layer_idx : 2 * layer_idx + 2],
            live_keys,
            row_share,
        )
        layer_grads.insert(0, grads_now)
        norm_grads.insert(0, norms_now)
    grad_table = grad_table + jnp.dot(
        token_hot.astype(jnp.float32).T, grad_stream, precision=HIGHEST
    )
    grad_place = jnp.dot(place_hot.astype(jnp.float32).T, grad_stream, precision=HIGHEST)
    grad_norms = jnp.concatenate(norm_grads + [jnp.stack((gain_last, shift_last))[None]], axis=0)
    stacked = [
        jnp.stack([layer_entry[slot_idx] for layer_entry in layer_grads]) for slot_idx in range(4)
    ]
    table_sum, place_sum, norm_sum = (
        lax.psum(grad_table.astype(jnp.bfloat16), "head").astype(jnp.float32),
        lax.psum(grad_place.astype(jnp.bfloat16), "head").astype(jnp.float32),
        lax.psum(grad_norms.astype(jnp.bfloat16), "head").astype(jnp.float32),
    )
    place_full = lax.dynamic_update_slice_in_dim(
        jnp.zeros((blk_tokens * blk_count, place_sum.shape[1]), jnp.float32),
        place_sum,
        blk_start,
        0,
    )
    full_table = jnp.concatenate((table_sum, place_full), axis=0)
    reduced = (
        lax.psum_scatter(full_table, "blk", scatter_dimension=1, tiled=True),
        lax.psum_scatter(stacked[0], "blk", scatter_dimension=1, tiled=True),
        lax.psum_scatter(stacked[1], "blk", scatter_dimension=2, tiled=True),
        lax.psum_scatter(stacked[2], "blk", scatter_dimension=1, tiled=True),
        lax.psum_scatter(stacked[3], "blk", scatter_dimension=1, tiled=True),
        lax.psum_scatter(norm_sum, "blk", scatter_dimension=2, tiled=True),
    )
    sharded_squares = sum((jnp.sum(grad_part * grad_part) for grad_part in reduced[1:5]))
    shared_squares = (
        jnp.sum(reduced[0] * reduced[0]) + jnp.sum(reduced[5] * reduced[5])
    ) / head_count
    grad_norm = jnp.sqrt(lax.psum(sharded_squares + shared_squares, ("blk", "head")))
    return loss_sum, weight_sum, grad_norm, squares, reduced


BF16 = jnp.bfloat16
F32 = jnp.float32
MESH = pl.DeviceIdType.MESH
LOG2E = 1.4426950408889634
NORM_LANE = 32


def dot(left, right, left_dim, right_dim):
    return lax.dot_general(
        left, right, (((left_dim,), (right_dim,)), ((), ())), preferred_element_type=F32
    )


class Sizes:
    def __init__(self, blk, head, seqs, blk_tokens, w_qkv, w_up, w_down):
        self.B, self.H, self.S = blk, head, seqs
        self.L = w_qkv[0]
        self.DB = w_qkv[1]
        self.D = self.DB * blk
        self.HC = w_qkv[3]
        self.T = blk_tokens * blk
        self.G = blk // seqs if blk % seqs == 0 else 0
        self.FD = w_down[1]
        if self.G:
            self.NR = self.G * head
            self.R = self.T // self.NR
            self.NC = self.NR // 2
            self.FU = w_up[2] // self.G

    def fused(self, blk_tokens):
        if self.G != 2 or self.S != 4 or self.H % 2 or self.R != blk_tokens or self.R != 128:
            return False
        if self.FU != self.FD * self.S or 3 * self.S > 16 or VOCAB > NORM_LANE:
            return False
        if NORM_LANE + 2 * (2 * self.L + 1) > 128:
            return False
        if any(n % 16 for n in (self.DB, self.HC, self.FD)) or self.D % 128 or self.FU % 128:
            return False
        weights = self.L * 2 * (4 * self.D * self.HC + 2 * self.D * self.FU)
        kept = self.L * self.T * (6 * self.D + 6 * self.FU + 14 * self.HC)
        return 3 * weights + kept + 16 * self.T * self.D + 8 * self.T * 256 * 4 < (60 << 20)


def step_kernel(
    z,
    lens,
    fam,
    ids,
    tp,
    wq_own,
    wo_own,
    wu_own,
    wd_own,
    scal_out,
    gq_out,
    go_out,
    gu_out,
    gd_out,
    gp_out,
    gs_out,
    idsg,
    tpg,
    etg,
    ptg,
    wq,
    wo,
    wu,
    wd,
    h1,
    h2,
    df,
    da,
    act,
    slope,
    du,
    qt,
    kt,
    vt,
    o32,
    ob,
    dob,
    lse,
    dqkv,
    bias,
    xs,
    xm,
    keep,
    psrc,
    csrc,
    srecv,
    rrecv,
    sg,
    stq,
    sto,
    stu,
    std,
    rq,
    ro,
    ru,
    rd,
    rc,
    tq,
    to,
    tu,
    td,
    tc,
    fst,
    frx,
    hrx,
    scg,
    id_s,
    id_r,
    tp_s,
    tp_r,
    wl,
    w_s,
    w_r,
    ag_s,
    ag_r,
    rs_s,
    rs_r,
    g_s,
    g_r,
    f_s,
    f_r,
    hx_s,
    hx_r,
    sc_s,
    sc_r,
):
    B, H, S, G, L, D, DB, HC, R, NC, NR, FU, FD, T = (
        z.B, z.H, z.S, z.G, z.L, z.D, z.DB, z.HC, z.R, z.NC, z.NR, z.FU, z.FD, z.T,
    )
    N_HEADS = HC // HEAD_DIM
    W = 2 * R
    QT = 2
    scale = HEAD_DIM ** (-0.5)
    c2 = scale * LOG2E
    b = lax.axis_index("blk")
    h = lax.axis_index("head")
    s, g = b // G, b % G
    y, c = h // 2, h % 2
    own_row = g * H + h
    s1 = s + 1 - 2 * (s % 2)
    s2 = (s + 2) % S
    s3 = (s1 + 2) % S

    def dev(blk_i, head_i):
        return (blk_i, head_i)

    sibling = dev(b, y * 2 + 1 - c)

    def peer(k):
        return dev(s * G + (g + k // 2) % G, ((y + k % 2) % 2) * 2 + c)

    def back(k):
        return ((-(k // 2)) % G) * 2 + k % 2

    waits = []

    def send(src, dst, ssem, rsem, device):
        copy = pltpu.make_async_remote_copy(src, dst, ssem, rsem, device, MESH)
        copy.start()
        return copy

    def arrived(dst, ssem, rsem):
        pltpu.make_async_remote_copy(dst, dst, ssem, rsem, sibling, MESH).wait_recv()

    def over_blk(body):
        def one(k, carry):
            body(lax.rem(b + k, B))
            return carry

        lax.fori_loop(1, B, one, 0)

    def rows(i, n):
        return pl.ds(pl.multiple_of(i * n, 16), n)

    barrier = pltpu.get_barrier_semaphore()

    def greet(k, carry):
        other = lax.rem(b * H + h + k, B * H)
        pl.semaphore_signal(barrier, inc=1, device_id=dev(other // H, other % H), device_id_type=MESH)
        return carry

    lax.fori_loop(1, B * H, greet, 0)
    pl.semaphore_wait(barrier, B * H - 1)

    def send_tp(other):
        send(tp.at[(other % G) * H + h], tpg.at[b], tp_s.at[other], tp_r.at[b], dev(other, h))
        send(ids, idsg.at[b], id_s.at[other], id_r.at[b], dev(other, h))

    over_blk(send_tp)
    idsg[b] = ids[...]
    tpg[b] = tp[own_row]

    def w_sem(sems, l, kind, m):
        return sems.at[(l * 4 + kind) * 8 + m]

    def w_ref(l, kind, at):
        return (wq, wo, wu, wd)[kind].at[l, at]

    def shard_rows(kind, plane, column=None):
        if kind == 3:
            return rows(plane, FD)
        return rows(plane * G + (g if column is None else column), DB)

    def w_send(l, kind, m, src, at, device):
        waits.append(
            send(src, w_ref(l, kind, at), w_sem(w_s, l, kind, m), w_sem(w_r, l, kind, m), device)
        )

    def w_arrived(l, kind, m, at):
        arrived(w_ref(l, kind, at), w_sem(w_s, l, kind, m), w_sem(w_r, l, kind, m))

    def own_copy(l, kind):
        src = (wq_own.at[l], wo_own.at[l], wu_own.at[l, g], wd_own.at[l])[kind]
        return pltpu.make_async_copy(src, w_ref(l, kind, shard_rows(kind, s)), wl.at[l * 4 + kind])

    def send_weights(l, kind):
        own_copy(l, kind).start()
        at = shard_rows(kind, s)
        if kind == 2:
            w_send(l, 2, 1, wu_own.at[l, g], at, dev(s2 * G + g, h))
            w_send(l, 2, 2, wu_own.at[l, 1 - g], at, dev(s2 * G + 1 - g, h))
            w_send(l, 2, 0, wu_own.at[l, 1 - g], at, dev(s * G + 1 - g, h))
            w_send(l, 2, 3, wu_own.at[l, g], at, dev(s1 * G + g, h))
            w_send(l, 2, 4, wu_own.at[l, 1 - g], at, dev(s1 * G + 1 - g, h))
            return
        src = (wq_own, wo_own, None, wd_own)[kind].at[l]
        w_send(l, kind, 0, src, at, dev(s2 * G + g, h))
        w_send(l, kind, 1, src, at, dev(s1 * G + g, h))
        if kind < 2:
            w_send(l, kind, 3, src, at, dev(s * G + 1 - g, h))

    def relay_weights(l, kind):
        if kind == 2:
            w_arrived(l, 2, 1, shard_rows(2, s2))
            w_arrived(l, 2, 2, shard_rows(2, s2, 1 - g))
            both = rows(s2, G * DB)
            w_send(l, 2, 5, w_ref(l, 2, both), both, dev(s1 * G + g, h))
            return
        at = shard_rows(kind, s2)
        w_arrived(l, kind, 0, at)
        w_send(l, kind, 2, w_ref(l, kind, at), at, dev(s1 * G + g, h))
        if kind < 2:
            w_send(l, kind, 4, w_ref(l, kind, at), at, dev(s * G + 1 - g, h))

    def cross_weights(l, kind):
        for m, plane in ((1, s1), (2, s3)):
            at = shard_rows(kind, plane)
            w_arrived(l, kind, m, at)
            w_send(l, kind, m + 4, w_ref(l, kind, at), at, dev(s * G + 1 - g, h))

    def wait_weights(l, kind):
        own_copy(l, kind).wait()
        if kind < 2:
            for m, plane in ((3, s), (4, s2), (5, s1), (6, s3)):
                w_arrived(l, kind, m, shard_rows(kind, plane, 1 - g))
        elif kind == 2:
            w_arrived(l, 2, 0, shard_rows(2, s, 1 - g))
            w_arrived(l, 2, 3, shard_rows(2, s1))
            w_arrived(l, 2, 4, shard_rows(2, s1, 1 - g))
            w_arrived(l, 2, 5, rows(s3, G * DB))
        else:
            w_arrived(l, 3, 1, shard_rows(3, s1))
            w_arrived(l, 3, 2, shard_rows(3, s3))

    for kind in range(4):
        send_weights(0, kind)

    def ag_sem(sems, use, i):
        return sems.at[use * 2 * NC + i]

    def block(buf, k, half):
        return buf.at[:, k * W + half * R : k * W + half * R + R]

    def spread(buf, use, slots):
        for k in reversed(slots):
            if k:
                waits.append(
                    send(
                        block(buf, 0, 0),
                        block(buf, back(k), 0),
                        ag_sem(ag_s, use, k),
                        ag_sem(ag_r, use, back(k)),
                        peer(k),
                    )
                )
        waits.append(
            send(block(buf, 0, 0), block(buf, 0, 1), ag_sem(ag_s, use, NC), ag_sem(ag_r, use, NC), sibling)
        )

    def hand_on(buf, use, k):
        arrived(block(buf, k, 0), ag_sem(ag_s, use, k), ag_sem(ag_r, use, k))
        waits.append(
            send(
                block(buf, k, 0),
                block(buf, k, 1),
                ag_sem(ag_s, use, NC + k),
                ag_sem(ag_r, use, NC + k),
                sibling,
            )
        )

    def have(buf, use, k):
        arrived(block(buf, k, 1), ag_sem(ag_s, use, NC + k), ag_sem(ag_r, use, NC + k))

    staged = {}

    def rs_sem(sems, use, i):
        return sems.at[use * 2 * NC + i]

    def stage(ref, key, value):
        if key in staged:
            staged.pop(key)[0].wait_send()
        ref[...] = value

    def part(use, k, value):
        keep[k] = value[:, :R]
        stage(psrc.at[k], ("p", k), value[:, R:].astype(BF16))
        staged["p", k] = [
            send(psrc.at[k], srecv.at[use, k], rs_sem(rs_s, use, k), rs_sem(rs_r, use, k), sibling)
        ]

    def pair_sum(use, k):
        arrived(srecv.at[use, k], rs_sem(rs_s, use, k), rs_sem(rs_r, use, k))
        return keep[k] + srecv[use, k].astype(F32)

    def pass_on(use, k):
        stage(csrc.at[k], ("c", k), pair_sum(use, k).astype(BF16))
        staged["c", k] = [
            send(
                csrc.at[k],
                rrecv.at[use, back(k)],
                rs_sem(rs_s, use, NC + k),
                rs_sem(rs_r, use, NC + back(k)),
                peer(k),
            )
        ]

    def total(use, slots):
        out = pair_sum(use, 0)
        for k in slots:
            if k:
                arrived(rrecv.at[use, k], rs_sem(rs_s, use, NC + k), rs_sem(rs_r, use, NC + k))
                out = out + rrecv[use, k].astype(F32)
        return out

    def g_sem(sems, l, kind, m):
        return sems.at[(l * 4 + kind) * 8 + m]

    def g_send(l, kind, m, src, dst, device):
        return send(src, dst, g_sem(g_s, l, kind, m), g_sem(g_r, l, kind, m), device)

    def g_arrived(l, kind, m, dst):
        arrived(dst, g_sem(g_s, l, kind, m), g_sem(g_r, l, kind, m))

    def g_stage(key, ref, value):
        for copy in staged.pop(key, ()):
            copy.wait_send()
        ref[...] = value.astype(BF16)

    def g_first(l, kind, value):
        src, dst = ((stq, rq), (sto, ro), (stu, ru), (std, rd))[kind]
        g_stage(("g", kind), src, value)
        if kind < 2:
            staged["g", kind] = [
                g_send(
                    l, kind, i, src.at[rows(i * G + 1 - g, DB)], dst.at[l, i], dev(s * G + 1 - g, h)
                )
                for i in range(S)
            ]
            return
        n = G * DB if kind == 2 else FD
        dst[l, 0] = src[rows(s, n)]
        staged["g", kind] = [
            g_send(l, kind, i, src.at[rows(plane, n)], dst.at[l, 1 + i], dev(s1 * G + g, h))
            for i, plane in ((1, s3), (0, s1))
        ]

    def g_column(l, kind, plane):
        src, dst = ((stq, rq), (sto, ro))[kind]
        return src[rows(plane * G + g, DB)].astype(F32) + dst[l, plane].astype(F32)

    def g_mid(l, kind):
        src, dst, tmp = ((stq, rq, tq), (sto, ro, to))[kind]
        for i in range(S):
            g_arrived(l, kind, i, dst.at[l, i])
        g_stage(("m", kind, 1), tmp.at[1], g_column(l, kind, s3))
        one = g_send(l, kind, 5, tmp.at[1], dst.at[l, S + 1], dev(s1 * G + g, h))
        g_stage(("m", kind, 0), tmp.at[0], g_column(l, kind, s1))
        two = g_send(l, kind, 4, tmp.at[0], dst.at[l, S], dev(s1 * G + g, h))
        staged["m", kind, 1] = [one]
        staged["m", kind, 0] = [two]

    def g_second(l, kind):
        if kind < 2:
            src, dst, tmp = ((stq, rq, tq), (sto, ro, to))[kind]
            g_arrived(l, kind, 5, dst.at[l, S + 1])
            g_stage(("s", kind), tmp.at[2], g_column(l, kind, s2) + dst[l, S + 1].astype(F32))
            staged["s", kind] = [g_send(l, kind, 6, tmp.at[2], dst.at[l, S + 2], dev(s2 * G + g, h))]
            return
        src, dst, tmp, n = ((stu, ru, tu, G * DB), (std, rd, td, FD))[kind - 2]
        g_arrived(l, kind, 1, dst.at[l, 2])
        g_stage(("s", kind), tmp, src[rows(s2, n)].astype(F32) + dst[l, 2].astype(F32))
        staged["s", kind] = [g_send(l, kind, 2, tmp, dst.at[l, 3], dev(s2 * G + g, h))]

    def g_third(l):
        g_arrived(l, 2, 0, ru.at[l, 1])
        g_arrived(l, 2, 2, ru.at[l, 3])

        def summed(column):
            at = rows(column, DB)
            return sum(ru[l, i, at, :].astype(F32) for i in (0, 1, 3))

        g_stage(("t", 2), tc, summed(1 - g))
        staged["t", 2] = [g_send(l, 2, 3, tc, rc.at[l], dev(s * G + 1 - g, h))]
        gu_out[l, g] = summed(g)

    def lanes_of(v):
        folded = jnp.sum(v * v, axis=0, keepdims=True)
        return jnp.sum(folded, axis=1, keepdims=True) + jnp.zeros((1, 128), F32)

    def g_final(l, kind):
        if kind < 2:
            dst, out = ((rq, gq_out), (ro, go_out))[kind]
            g_arrived(l, kind, 4, dst.at[l, S])
            g_arrived(l, kind, 6, dst.at[l, S + 2])
            value = g_column(l, kind, s) + dst[l, S].astype(F32) + dst[l, S + 2].astype(F32)
            out[l] = value
        elif kind == 2:
            g_arrived(l, 2, 3, rc.at[l])
            value = rc[l].astype(F32)
            gu_out[l, 1 - g] = value
            return lanes_of(value) + lanes_of(gu_out[l, g])
        else:
            g_arrived(l, 3, 0, rd.at[l, 1])
            g_arrived(l, 3, 2, rd.at[l, 3])
            value = sum(rd[l, i].astype(F32) for i in (0, 1, 3))
            gd_out[l] = value
        return lanes_of(value)

    squares = jnp.zeros((1, 128), F32)

    length = lens[s]
    for k in range(NC):
        for half in range(2):
            core = c if half == 0 else 1 - c
            block_row = ((g + k // 2) % G) * H + ((y + k % 2) % 2) * 2 + core
            place = block_row * R + lax.broadcasted_iota(jnp.int32, (R, 128), 0)
            bias[k * W + half * R : k * W + half * R + R, :] = jnp.where(place < length, 0.0, NEGATIVE)
    lane_place = own_row * R + lax.broadcasted_iota(jnp.int32, (1, R), 1)
    live = jnp.where(lane_place < length, 1.0, 0.0)
    dqkv[0:HC, QT * W :] = jnp.zeros((HC, T - QT * W), BF16)
    sg[...] = jnp.zeros((D, 128), F32)
    lane = lax.broadcasted_iota(jnp.int32, (D, 128), 1)
    row_of = lax.broadcasted_iota(jnp.int32, (128, R), 0)

    def tp_here(other):
        arrived(tpg.at[other], tp_s.at[other], tp_r.at[other])
        arrived(idsg.at[other], id_s.at[other], id_r.at[other])

    over_blk(tp_here)
    for i in range(B):
        etg[i * DB : (i + 1) * DB] = tpg[i, :DB]
        ptg[i * DB : (i + 1) * DB] = tpg[i, DB:]
    token_row = idsg[own_row, pl.ds(s, 1), :]
    target_row = idsg[own_row, pl.ds(S + s, 1), :]
    mask_row = idsg[own_row, pl.ds(2 * S + s, 1), :].astype(F32)
    token_hot = jnp.where(row_of == token_row, 1.0, 0.0).astype(BF16)
    token_weight = mask_row * fam[s]
    weight_sum = jnp.zeros((1, 1), F32)
    for i in range(S):
        counts = jnp.zeros((1, R), F32)
        for j in range(B):
            counts = counts + idsg[j, 2 * S + i : 2 * S + i + 1, :].astype(F32)
        weight_sum = weight_sum + jnp.sum(counts, axis=1, keepdims=True) * fam[i]

    def gain(i):
        return etg[:, NORM_LANE + 2 * i : NORM_LANE + 2 * i + 1].astype(F32)

    def shift(i):
        return etg[:, NORM_LANE + 2 * i + 1 : NORM_LANE + 2 * i + 2].astype(F32)

    def normalize(v):
        centred = v - jnp.mean(v, axis=0, keepdims=True)
        rstd = lax.rsqrt(jnp.mean(centred * centred, axis=0, keepdims=True) + NORM_EPS)
        return centred * rstd, rstd

    def layer_norm_low(v, i):
        hat, _ = normalize(v)
        return (hat * gain(i) + shift(i)).astype(BF16)

    def layer_norm_back(grad, v, i):
        hat, rstd = normalize(v)
        gain_grad = jnp.sum(grad * hat, axis=1, keepdims=True)
        shift_grad = jnp.sum(grad, axis=1, keepdims=True)
        sg[...] += jnp.where(lane == NORM_LANE + 2 * i, gain_grad, 0.0) + jnp.where(
            lane == NORM_LANE + 2 * i + 1, shift_grad, 0.0
        )
        scaled = grad * gain(i)
        mean_one = jnp.mean(scaled, axis=0, keepdims=True)
        mean_two = jnp.mean(scaled * hat, axis=0, keepdims=True)
        return rstd * (scaled - mean_one - hat * mean_two)

    def square_sum(v):
        return jnp.sum(jnp.sum(v * v, axis=0, keepdims=True) * live, axis=1, keepdims=True)

    slots = list(range(NC))
    near = slots[:2]
    far = slots[1:]
    stats = []
    relay_weights(0, 0)
    relay_weights(0, 1)
    xs[0] = dot(etg[...], token_hot, 1, 0) + ptg[...].astype(F32)

    def cols(k):
        return slice(k * W, (k + 1) * W)

    for l in range(L):
        x = xs[l]
        stats.append(square_sum(x))
        h1[l, :, 0:R] = layer_norm_low(x, 2 * l)
        spread(h1.at[l], 3 * l, slots)
        cross_weights(l, 0)
        cross_weights(l, 1)
        wait_weights(l, 0)

        def project(k):
            if k in near:
                packed = dot(wq[l], h1[l, :, cols(k)], 0, 0).astype(BF16)
                qt[l, :, cols(k)] = packed[0:HC]
                packed = packed[HC:]
            else:
                packed = dot(wq[l, :, :], h1[l, :, cols(k)], 0, 0).astype(BF16)[HC:]
            kt[l, :, cols(k)] = packed[0:HC]
            vt[l, :, cols(k)] = packed[HC:]

        have(h1.at[l], 3 * l, 0)
        project(0)
        for k in far:
            hand_on(h1.at[l], 3 * l, k)
            if k > 1:
                have(h1.at[l], 3 * l, k - 1)
                project(k - 1)
        have(h1.at[l], 3 * l, NC - 1)
        project(NC - 1)
        relay_weights(l, 2)
        relay_weights(l, 3)
        if l + 1 < L:
            for kind in range(4):
                send_weights(l + 1, kind)

        def attend(q, first, last):
            def one(i, carry):
                at = rows(i, HEAD_DIM)
                scores = dot(kt[l, at, :], qt[l, at, cols(q)], 0, 0) + jnp.concatenate([bias[...]] * 2, axis=1)
                peak = jnp.max(scores, axis=0, keepdims=True)
                exps = jnp.exp2((scores - peak) * c2)
                norm = jnp.sum(exps, axis=0, keepdims=True)
                probs = (exps * (1.0 / norm)).astype(BF16)
                out = dot(vt[l, at, :], probs, 1, 0)
                o32[l, at, cols(q)] = out
                ob[l, at, cols(q)] = out.astype(BF16)
                lse[l, pl.ds(pl.multiple_of(i * 8, 8), 8), cols(q)] = jnp.broadcast_to(
                    peak * c2 + jnp.log(norm) * LOG2E, (8, W)
                )
                return carry

            lax.fori_loop(first, last, one, 0)

        attend(1, 0, N_HEADS)
        wait_weights(l, 1)
        part(4 * l, 1, dot(wo[l], ob[l, :, cols(1)], 1, 0))
        attend(0, 0, N_HEADS // 2)
        pass_on(4 * l, 1)
        attend(0, N_HEADS // 2, N_HEADS)
        part(4 * l, 0, dot(wo[l], ob[l, :, cols(0)], 1, 0))
        attn_out = total(4 * l, near)
        stats.append(square_sum(attn_out))
        middle = xs[l] + attn_out
        xm[l] = middle
        h2[l, :, 0:R] = layer_norm_low(middle, 2 * l + 1)
        spread(h2.at[l], 3 * l + 1, slots)
        wait_weights(l, 2)
        wait_weights(l, 3)

        def feed(k):
            pre = dot(wu[l], h2[l, :, cols(k)], 0, 0)
            cdf = 0.5 * (1.0 + lax.erf(pre * (0.5**0.5)))
            low = (pre * cdf).astype(BF16)
            act[l, :, cols(k)] = low
            slope[l, :, cols(k)] = cdf + pre * (jnp.exp(-0.5 * pre * pre) * 0.3989422804014327)
            part(4 * l + 1, k, dot(wd[l], low, 0, 0))

        have(h2.at[l], 3 * l + 1, 0)
        feed(0)
        for k in far:
            hand_on(h2.at[l], 3 * l + 1, k)
            if k > 1:
                have(h2.at[l], 3 * l + 1, k - 1)
                feed(k - 1)
                if k > 2:
                    pass_on(4 * l + 1, k - 2)
        have(h2.at[l], 3 * l + 1, NC - 1)
        feed(NC - 1)
        for k in far[-2:]:
            pass_on(4 * l + 1, k)
        if l + 1 < L:
            relay_weights(l + 1, 0)
            relay_weights(l + 1, 1)
        ffn_out = total(4 * l + 1, slots)
        stats.append(square_sum(ffn_out))
        xs[l + 1] = xm[l] + ffn_out

    last = xs[L]
    final_low = layer_norm_low(last, 2 * L)
    logits = dot(etg[...], final_low, 0, 0)[0:NORM_LANE]
    vocab_row = row_of[0:NORM_LANE]
    logits = jnp.where(vocab_row < VOCAB, logits, NEGATIVE)
    shifted = logits - jnp.max(logits, axis=0, keepdims=True)
    log_probs = shifted - jnp.log(jnp.sum(jnp.exp(shifted), axis=0, keepdims=True))
    target_hot = jnp.where(vocab_row == target_row, 1.0, 0.0)
    token_loss = -jnp.sum(target_hot * log_probs, axis=0, keepdims=True)
    loss = jnp.sum(token_weight * token_loss, axis=1, keepdims=True)
    grad_logits = ((token_weight / weight_sum) * (jnp.exp(log_probs) - target_hot)).astype(BF16)
    grad_logits = jnp.concatenate([grad_logits, jnp.zeros((128 - NORM_LANE, R), BF16)], axis=0)
    grad_final = dot(etg[...], grad_logits, 1, 0)
    sg[...] += dot(final_low, grad_logits, 1, 1)
    grad = layer_norm_back(grad_final, last, 2 * L)

    for l in reversed(range(L)):
        df[l, :, 0:R] = grad.astype(BF16)
        xs[l + 1] = grad
        spread(df.at[l], 3 * l + 2, slots)
        if l + 1 < L:
            g_mid(l + 1, 0)
            g_mid(l + 1, 1)
            g_third(l + 1)

        def feed_back(k):
            grad_act = dot(wd[l], df[l, :, cols(k)], 1, 0)
            low = (grad_act * slope[l, :, cols(k)]).astype(BF16)
            du[:, cols(k)] = low
            part(4 * l + 2, k, dot(wu[l], low, 1, 0))

        have(df.at[l], 3 * l + 2, 0)
        feed_back(0)
        for k in far:
            hand_on(df.at[l], 3 * l + 2, k)
            if k > 1:
                have(df.at[l], 3 * l + 2, k - 1)
                feed_back(k - 1)
                if k > 2:
                    pass_on(4 * l + 2, k - 2)
        have(df.at[l], 3 * l + 2, NC - 1)
        feed_back(NC - 1)
        for k in far[-2:]:
            pass_on(4 * l + 2, k)
        if l + 1 < L:
            g_second(l + 1, 0)
            g_second(l + 1, 1)
        g_first(l, 3, dot(act[l], df[l], 1, 1))
        g_first(l, 2, dot(h2[l], du[...], 1, 1))
        grad_middle = xs[l + 1] + layer_norm_back(total(4 * l + 2, slots), xm[l], 2 * l + 1)
        xm[l] = grad_middle

        da[l, :, 0:R] = grad_middle.astype(BF16)
        spread(da.at[l], 3 * L + l, near)
        if l + 1 < L:
            for kind in range(4):
                squares = squares + g_final(l + 1, kind)

        def out_back(k):
            dob[:, cols(k)] = dot(wo[l], da[l, :, cols(k)], 0, 0).astype(BF16)

        have(da.at[l], 3 * L + l, 0)
        out_back(0)
        hand_on(da.at[l], 3 * L + l, 1)
        have(da.at[l], 3 * L + l, 1)
        out_back(1)

        g_second(l, 3)

        def attend_back(i, carry):
            at = rows(i, HEAD_DIM)
            key_h = kt[l, at, :]
            value_h = vt[l, at, :]
            grad_key = jnp.zeros((HEAD_DIM, T), F32)
            grad_value = jnp.zeros((HEAD_DIM, T), F32)
            for q in range(QT):
                query_h = qt[l, at, cols(q)]
                grad_h = dob[at, cols(q)]
                lse_h = lse[l, pl.ds(pl.multiple_of(i * 8, 8), 8), cols(q)][0:1]
                scores = dot(key_h, query_h, 0, 0) + jnp.concatenate([bias[...]] * 2, axis=1)
                probs = jnp.exp2(scores * c2 - lse_h)
                delta = jnp.sum(grad_h.astype(F32) * o32[l, at, cols(q)], axis=0, keepdims=True)
                grad_scores = (probs * (dot(value_h, grad_h, 0, 0) - delta)).astype(BF16)
                dqkv[at, cols(q)] = (dot(key_h, grad_scores, 1, 0) * scale).astype(BF16)
                grad_key = grad_key + dot(query_h, grad_scores, 1, 1)
                grad_value = grad_value + dot(grad_h, probs.astype(BF16), 1, 1)
            dqkv[pl.ds(pl.multiple_of(HC + i * HEAD_DIM, 16), HEAD_DIM), :] = (grad_key * scale).astype(BF16)
            dqkv[pl.ds(pl.multiple_of(2 * HC + i * HEAD_DIM, 16), HEAD_DIM), :] = grad_value.astype(BF16)
            return carry

        lax.fori_loop(0, N_HEADS, attend_back, 0)
        g_second(l, 2)
        for k in reversed(slots):
            part(4 * l + 3, k, dot(wq[l], dqkv[:, cols(k)], 1, 0))
            if 0 < k + 1 < NC:
                pass_on(4 * l + 3, k + 1)
        g_first(l, 0, dot(h1[l], dqkv[...], 1, 1))
        g_first(l, 1, dot(da[l], ob[l], 1, 1))
        grad = xm[l] + layer_norm_back(total(4 * l + 3, slots), xs[l], 2 * l)

    high = grad.astype(BF16)
    low = (grad - high.astype(F32)).astype(BF16)
    small = sg[...] + dot(high, token_hot, 1, 1) + dot(low, token_hot, 1, 1)
    small = small.astype(BF16)
    for i in range(B):
        fst[i, :DB] = small[i * DB : (i + 1) * DB]
        fst[i, DB:] = high[i * DB : (i + 1) * DB]

    def send_table(other):
        send(fst.at[other], frx.at[b], f_s.at[other], f_r.at[b], dev(other, h))

    over_blk(send_table)
    frx[b] = fst[b]

    g_mid(0, 0)
    g_mid(0, 1)
    g_third(0)
    squares = squares + g_final(0, 3)
    g_second(0, 0)
    g_second(0, 1)
    squares = squares + g_final(0, 2)
    def table_here(other):
        arrived(frx.at[other], f_s.at[other], f_r.at[other])

    over_blk(table_here)
    for j in range(G):
        value = frx[j, DB:].astype(F32)
        for i in range(1, S):
            value = value + frx[i * G + j, DB:].astype(F32)
        hrx[h, j] = value
        squares = squares + lanes_of(value)
    value = frx[0, :DB].astype(F32)
    for i in range(1, B):
        value = value + frx[i, :DB].astype(F32)
    hrx[h, G] = value

    def send_heads(k, carry):
        other = lax.rem(h + k, H)
        send(hrx.at[h], hrx.at[h], hx_s.at[other], hx_r.at[h], dev(b, other))
        return carry

    lax.fori_loop(1, H, send_heads, 0)

    def heads_here(k, carry):
        other = lax.rem(h + k, H)
        arrived(hrx.at[other], hx_s.at[other], hx_r.at[other])
        return carry

    for kind in (0, 1):
        squares = squares + g_final(0, kind)
    lax.fori_loop(1, H, heads_here, 0)
    value = hrx[0, G]
    for i in range(1, H):
        value = value + hrx[i, G]
    gs_out[...] = value
    squares = squares + lanes_of(value) * (1.0 / H)

    lane_one = lax.broadcasted_iota(jnp.int32, (1, 128), 1)
    packed = jnp.where(lane_one == 0, loss, 0.0) + jnp.where(lane_one == 1, squares, 0.0)
    for i, stat in enumerate(stats):
        packed = packed + jnp.where(lane_one == 2 + i, stat, 0.0)
    me = b * H + h
    scg[me] = jnp.broadcast_to(packed, (8, 128))

    def send_scalars(k, carry):
        other = lax.rem(me + k, B * H)
        send(scg.at[me], scg.at[me], sc_s.at[other], sc_r.at[me], dev(other // H, other % H))
        return carry

    lax.fori_loop(1, B * H, send_scalars, 0)
    for i in range(H):
        for j in range(G):
            gp_out[j * H + i] = hrx[i, j]

    def scalars_here(k, carry):
        other = lax.rem(me + k, B * H)
        arrived(scg.at[other], sc_s.at[other], sc_r.at[other])
        return carry

    lax.fori_loop(1, B * H, scalars_here, 0)
    out = scg[0]
    for i in range(1, B * H):
        out = out + scg[i]
    lane_eight = lax.broadcasted_iota(jnp.int32, (8, 128), 1)
    out = jnp.where(lane_eight == 1, jnp.sqrt(out), out)
    scal_out[...] = jnp.where(lane_eight == 2 + 3 * L, weight_sum, out)

    for copy in waits:
        copy.wait_send()
    for copies in staged.values():
        for copy in copies:
            copy.wait_send()

    def sent(other):
        for src, ssem, rsem in ((tpg.at[other], tp_s, tp_r), (idsg.at[other], id_s, id_r), (frx.at[other], f_s, f_r)):
            pltpu.make_async_remote_copy(src, src, ssem.at[other], rsem.at[other], sibling, MESH).wait_send()

    over_blk(sent)

    def heads_sent(k, carry):
        other = lax.rem(h + k, H)
        pltpu.make_async_remote_copy(
            hrx.at[other], hrx.at[other], hx_s.at[other], hx_r.at[other], sibling, MESH
        ).wait_send()
        return carry

    lax.fori_loop(1, H, heads_sent, 0)

    def scalars_sent(k, carry):
        other = lax.rem(me + k, B * H)
        pltpu.make_async_remote_copy(
            scg.at[other], scg.at[other], sc_s.at[other], sc_r.at[other], sibling, MESH
        ).wait_send()
        return carry

    lax.fori_loop(1, B * H, scalars_sent, 0)


def fused_step(z, token_ids, targets, masked, lengths, family_weight, embed_table, w_qkv, w_out, w_up, w_down, norm_params):
    B, H, S, G, L, D, DB, HC, R, NC, NR, FU, FD, T = (
        z.B, z.H, z.S, z.G, z.L, z.D, z.DB, z.HC, z.R, z.NC, z.NR, z.FU, z.FD, z.T,
    )
    W = 2 * R
    ids = jnp.concatenate([token_ids, targets, masked], axis=0)
    ids = jnp.pad(ids, ((0, 16 - 3 * S), (0, 0)))
    table = embed_table.astype(BF16).T
    norms = norm_params.astype(BF16).transpose(2, 0, 1).reshape(DB, -1)
    token_part = jnp.concatenate(
        [
            table[:, :VOCAB],
            jnp.zeros((DB, NORM_LANE - VOCAB), BF16),
            norms,
            jnp.zeros((DB, 128 - NORM_LANE - norms.shape[1]), BF16),
        ],
        axis=1,
    )
    place_part = table[:, VOCAB:].reshape(DB, NR, R).transpose(1, 0, 2)
    tp = jnp.concatenate([jnp.broadcast_to(token_part[None], (NR, DB, 128)), place_part], axis=1)
    wq_own = w_qkv.astype(BF16).reshape(L, DB, 3 * HC)
    wo_own = w_out.astype(BF16).transpose(0, 2, 1)
    wu_own = w_up.astype(BF16).reshape(L, DB, S, G, FD).transpose(0, 3, 1, 2, 4).reshape(L, G, DB, FU)
    wd_own = w_down.astype(BF16)
    smem = pl.BlockSpec(memory_space=pltpu.SMEM)
    vmem = pl.BlockSpec(memory_space=pltpu.VMEM)
    hbm = pl.BlockSpec(memory_space=pl.ANY)
    dma = pltpu.SemaphoreType.DMA
    scratch = [
        pltpu.VMEM((B, 16, R), jnp.int32),
        pltpu.VMEM((B, 2 * DB, 128), BF16),
        pltpu.VMEM((D, 128), BF16),
        pltpu.VMEM((D, R), BF16),
        pltpu.VMEM((L, D, 3 * HC), BF16),
        pltpu.VMEM((L, D, HC), BF16),
        pltpu.VMEM((L, D, FU), BF16),
        pltpu.VMEM((L, FU, D), BF16),
        pltpu.VMEM((L, D, T), BF16),
        pltpu.VMEM((L, D, T), BF16),
        pltpu.VMEM((L, D, T), BF16),
        pltpu.VMEM((L, D, 2 * W), BF16),
        pltpu.VMEM((L, FU, T), BF16),
        pltpu.VMEM((L, FU, T), F32),
        pltpu.VMEM((FU, T), BF16),
        pltpu.VMEM((L, HC, 2 * W), BF16),
        pltpu.VMEM((L, HC, T), BF16),
        pltpu.VMEM((L, HC, T), BF16),
        pltpu.VMEM((L, HC, 2 * W), F32),
        pltpu.VMEM((L, HC, 2 * W), BF16),
        pltpu.VMEM((HC, 2 * W), BF16),
        pltpu.VMEM((L, 8 * (HC // HEAD_DIM), 2 * W), F32),
        pltpu.VMEM((3 * HC, T), BF16),
        pltpu.VMEM((T, 128), F32),
        pltpu.VMEM((L + 1, D, R), F32),
        pltpu.VMEM((L, D, R), F32),
        pltpu.VMEM((NC, D, R), F32),
        pltpu.VMEM((NC, D, R), BF16),
        pltpu.VMEM((NC, D, R), BF16),
        pltpu.VMEM((4 * L, NC, D, R), BF16),
        pltpu.VMEM((4 * L, NC, D, R), BF16),
        pltpu.VMEM((D, 128), F32),
        pltpu.VMEM((D, 3 * HC), BF16),
        pltpu.VMEM((D, HC), BF16),
        pltpu.VMEM((D, FU), BF16),
        pltpu.VMEM((FU, D), BF16),
        pltpu.VMEM((L, S + 3, DB, 3 * HC), BF16),
        pltpu.VMEM((L, S + 3, DB, HC), BF16),
        pltpu.VMEM((L, S, G * DB, FU), BF16),
        pltpu.VMEM((L, S, FD, D), BF16),
        pltpu.VMEM((L, DB, FU), BF16),
        pltpu.VMEM((3, DB, 3 * HC), BF16),
        pltpu.VMEM((3, DB, HC), BF16),
        pltpu.VMEM((G * DB, FU), BF16),
        pltpu.VMEM((FD, D), BF16),
        pltpu.VMEM((DB, FU), BF16),
        pltpu.VMEM((B, 2 * DB, 128), BF16),
        pltpu.VMEM((B, 2 * DB, 128), BF16),
        pltpu.VMEM((H, G + 1, DB, 128), F32),
        pltpu.VMEM((B * H, 8, 128), F32),
        dma((B,)),
        dma((B,)),
        dma((B,)),
        dma((B,)),
        dma((4 * L,)),
        dma((4 * L * 8,)),
        dma((4 * L * 8,)),
        dma((4 * L * 2 * NC,)),
        dma((4 * L * 2 * NC,)),
        dma((4 * L * 2 * NC,)),
        dma((4 * L * 2 * NC,)),
        dma((4 * L * 8,)),
        dma((4 * L * 8,)),
        dma((B,)),
        dma((B,)),
        dma((H,)),
        dma((H,)),
        dma((B * H,)),
        dma((B * H,)),
    ]
    outs = (
        jax.ShapeDtypeStruct((8, 128), F32),
        jax.ShapeDtypeStruct((L, DB, 3 * HC), F32),
        jax.ShapeDtypeStruct((L, DB, HC), F32),
        jax.ShapeDtypeStruct((L, G, DB, FU), F32),
        jax.ShapeDtypeStruct((L, FD, D), F32),
        jax.ShapeDtypeStruct((NR, DB, R), F32),
        jax.ShapeDtypeStruct((DB, 128), F32),
    )
    scal, gq, go, gu, gd, gp, gs = pl.pallas_call(
        functools.partial(step_kernel, z),
        out_shape=outs,
        in_specs=[smem, smem, vmem, vmem, hbm, hbm, hbm, hbm],
        out_specs=[vmem] * 7,
        scratch_shapes=scratch,
        compiler_params=pltpu.CompilerParams(
            collective_id=0, has_side_effects=True, vmem_limit_bytes=62 << 20
        ),
        name="train_step",
    )(lengths, family_weight, ids, tp, wq_own, wo_own, wu_own, wd_own)
    grads = (
        jnp.concatenate([gs[:, :VOCAB].T, gp.transpose(0, 2, 1).reshape(T, DB)], axis=0),
        gq.reshape(L, DB, 3, HC),
        go.transpose(0, 2, 1),
        gu.reshape(L, G, DB, S, FD).transpose(0, 2, 3, 1, 4).reshape(L, DB, S * G * FD),
        gd,
        gs[:, NORM_LANE : NORM_LANE + 2 * (2 * L + 1)].T.reshape(2 * L + 1, 2, DB),
    )
    return scal[0], grads


def local(
    token_ids,
    targets,
    masked,
    lengths,
    family_weight,
    embed_table,
    w_qkv,
    w_out,
    w_up,
    w_down,
    norm_params,
    embed_first,
    qkv_first,
    out_first,
    up_first,
    down_first,
    norm_first,
    embed_second,
    qkv_second,
    out_second,
    up_second,
    down_second,
    norm_second,
):
    z = Sizes(
        lax.axis_size("blk"),
        lax.axis_size("head"),
        token_ids.shape[0],
        token_ids.shape[1],
        w_qkv.shape,
        w_up.shape,
        w_down.shape,
    )
    masters = (embed_table, w_qkv, w_out, w_up, w_down, norm_params)
    firsts = (embed_first, qkv_first, out_first, up_first, down_first, norm_first)
    seconds = (embed_second, qkv_second, out_second, up_second, down_second, norm_second)
    tokens = (token_ids, targets, masked, lengths, family_weight)
    if z.fused(token_ids.shape[1]):
        scal, grads = fused_step(z, *tokens, *masters)
        loss_sum, weight_sum, grad_norm = (scal[0], scal[2 + 3 * LAYERS], scal[1])
        squares = scal[2 : 2 + 3 * LAYERS]
    else:
        loss_sum, weight_sum, grad_norm, squares, grads = plain_step(*tokens, *masters)
    factor = CLIP_NORM / jnp.maximum(grad_norm, CLIP_NORM)
    stream_rms = jnp.sqrt(squares.reshape(LAYERS, 3) / (jnp.sum(lengths).astype(jnp.float32) * D))
    results = [loss_sum, weight_sum, grad_norm, stream_rms]
    for group_idx in range(6):
        first, second, weight = adamw_update(
            masters[group_idx],
            firsts[group_idx],
            seconds[group_idx],
            grads[group_idx] * factor,
            RATES[group_idx],
            DECAYS[group_idx],
        )
        results += [first, second, weight, weight.astype(jnp.bfloat16)]
    return tuple(results)


def solution(mesh):
    return jax.shard_map(
        local,
        mesh=mesh,
        in_specs=(
            P(None, "blk"),
            P(None, "blk"),
            P(None, "blk"),
            P(),
            P(),
            P(None, "blk"),
            P(None, "blk", None, "head"),
            P(None, "head", "blk"),
            P(None, "blk", "head"),
            P(None, ("head", "blk"), None),
            P(None, None, "blk"),
            P(None, "blk"),
            P(None, "blk", None, "head"),
            P(None, "head", "blk"),
            P(None, "blk", "head"),
            P(None, ("head", "blk"), None),
            P(None, None, "blk"),
            P(None, "blk"),
            P(None, "blk", None, "head"),
            P(None, "head", "blk"),
            P(None, "blk", "head"),
            P(None, ("head", "blk"), None),
            P(None, None, "blk"),
        ),
        out_specs=(
            P(),
            P(),
            P(),
            P(),
            P(None, "blk"),
            P(None, "blk"),
            P(None, "blk"),
            P(None, "blk"),
            P(None, "blk", None, "head"),
            P(None, "blk", None, "head"),
            P(None, "blk", None, "head"),
            P(None, "blk", None, "head"),
            P(None, "head", "blk"),
            P(None, "head", "blk"),
            P(None, "head", "blk"),
            P(None, "head", "blk"),
            P(None, "blk", "head"),
            P(None, "blk", "head"),
            P(None, "blk", "head"),
            P(None, "blk", "head"),
            P(None, ("head", "blk"), None),
            P(None, ("head", "blk"), None),
            P(None, ("head", "blk"), None),
            P(None, ("head", "blk"), None),
            P(None, None, "blk"),
            P(None, None, "blk"),
            P(None, None, "blk"),
            P(None, None, "blk"),
        ),
        check_vma=False,
    )
```

```python
import functools

import jax
import jax.numpy as jnp
from jax import lax
from jax.experimental import pallas as pl
from jax.experimental.pallas import tpu as pltpu
from jax.sharding import PartitionSpec as P

VOCAB = 25
D = 640
HEAD_DIM = 32
LAYERS = 2
STEP = 10


NEGATIVE = -1e30
NORM_EPS = 1e-05
CLIP_NORM = 0.01
BETA_FIRST = 0.9
BETA_SECOND = 0.999
ADAM_EPS = 1e-08
RATES = (0.2, 0.1, 0.5, 0.1, 0.03, 0.5)
DECAYS = (0.1, 0.1, 0.1, 0.1, 0.1, 0.0)
HIGHEST = lax.Precision.HIGHEST


def layer_norm(inputs, gain_row, shift_row):
    centred = inputs - jnp.mean(inputs, axis=-1, keepdims=True)
    spread = jnp.mean(centred * centred, axis=-1, keepdims=True)
    return centred * lax.rsqrt(spread + NORM_EPS) * gain_row + shift_row


def gelu_exact(inputs):
    return jax.nn.gelu(inputs, approximate=False)


def adamw_update(weight, first, second, gradient, rate, decay):
    first = BETA_FIRST * first + (1.0 - BETA_FIRST) * gradient
    second = BETA_SECOND * second + (1.0 - BETA_SECOND) * gradient * gradient
    first_hat = first / (1.0 - BETA_FIRST**STEP)
    second_hat = second / (1.0 - BETA_SECOND**STEP)
    weight = weight - rate * (first_hat / (jnp.sqrt(second_hat) + ADAM_EPS) + decay * weight)
    return (first, second, weight)


def slice_head(tensor, head_index):
    return lax.dynamic_slice_in_dim(tensor, head_index * HEAD_DIM, HEAD_DIM, tensor.ndim - 1)


def join_heads(stacked):
    moved = jnp.moveaxis(stacked, 0, 2)
    return moved.reshape(moved.shape[0], moved.shape[1], -1)


def spread_rows(normed):
    return lax.all_gather(normed, "head", axis=0, tiled=True)


def spread_grads(grad_rows):
    return lax.all_gather(grad_rows, "head", axis=0, tiled=True)


def sum_rows(full_rows, weight, row_share):

    def row_term(row_start, row_count):
        return jnp.dot(full_rows, weight, preferred_element_type=jnp.float32)

    return lax.psum_scatter(
        row_term(jnp.int32(0), row_share * lax.axis_size("head")),
        "head",
        scatter_dimension=0,
        tiled=True,
    )


def sum_grads(full_rows, weight, row_share):

    def row_term(row_start, row_count):
        return jnp.einsum("nc,dc->nd", full_rows, weight, preferred_element_type=jnp.float32)

    return lax.psum_scatter(
        row_term(jnp.int32(0), row_share * lax.axis_size("head")).astype(jnp.bfloat16),
        "head",
        scatter_dimension=0,
        tiled=True,
    ).astype(jnp.float32)


def attend(queries, keys_all, values_all, live_keys):
    local_heads = queries.shape[-1] // HEAD_DIM
    score_scale = HEAD_DIM ** (-0.5)
    live_mask = live_keys[:, None, :]

    def one_head(head_index):
        scores = (
            jnp.einsum(
                "ste,sje->stj",
                slice_head(queries, head_index),
                slice_head(keys_all, head_index),
                preferred_element_type=jnp.float32,
            )
            * score_scale
        )
        masked_scores = jnp.where(live_mask, scores, NEGATIVE)
        row_peak = jnp.max(masked_scores, axis=-1, keepdims=True)
        exp_scores = jnp.exp(masked_scores - row_peak)
        row_total = jnp.sum(exp_scores, axis=-1, keepdims=True)
        attn_probs = (exp_scores / row_total).astype(jnp.bfloat16)
        attended = jnp.einsum(
            "stj,sje->ste",
            attn_probs,
            slice_head(values_all, head_index),
            preferred_element_type=jnp.float32,
        )
        return (attended, (row_peak + jnp.log(row_total))[..., 0])

    outputs, log_totals = lax.map(one_head, jnp.arange(local_heads))
    return (join_heads(outputs), log_totals)


def attend_back(queries, keys_all, values_all, grad_heads, log_totals, live_keys):
    local_heads = queries.shape[-1] // HEAD_DIM
    score_scale = HEAD_DIM ** (-0.5)
    live_mask = live_keys[:, None, :]

    def one_head(head_index):
        query_h = slice_head(queries, head_index)
        key_h = slice_head(keys_all, head_index)
        grad_h = slice_head(grad_heads, head_index)
        scores = (
            jnp.einsum("ste,sje->stj", query_h, key_h, preferred_element_type=jnp.float32)
            * score_scale
        )
        masked_scores = jnp.where(live_mask, scores, NEGATIVE)
        attn_probs = jnp.exp(masked_scores - log_totals[head_index][..., None])
        grad_probs = jnp.einsum(
            "ste,sje->stj",
            grad_h,
            slice_head(values_all, head_index),
            preferred_element_type=jnp.float32,
        )
        row_delta = jnp.sum(attn_probs * grad_probs, axis=-1)
        grad_scores = (attn_probs * (grad_probs - row_delta[..., None])).astype(jnp.bfloat16)
        grad_query = (
            jnp.einsum("stj,sje->ste", grad_scores, key_h, preferred_element_type=jnp.float32)
            * score_scale
        )
        grad_key = (
            jnp.einsum("stj,ste->sje", grad_scores, query_h, preferred_element_type=jnp.float32)
            * score_scale
        )
        grad_value = jnp.einsum(
            "stj,ste->sje",
            attn_probs.astype(jnp.bfloat16),
            grad_h,
            preferred_element_type=jnp.float32,
        )
        return (grad_query, grad_key, grad_value)

    grad_query, grad_key, grad_value = lax.map(one_head, jnp.arange(local_heads))
    grad_key, grad_value = (
        lax.psum_scatter(grad_key, "blk", scatter_dimension=2, tiled=True),
        lax.psum_scatter(grad_value, "blk", scatter_dimension=2, tiled=True),
    )
    return (join_heads(grad_query), join_heads(grad_key), join_heads(grad_value))


def layer_forward(stream, layer_weights, norm_rows, live_keys, row_share):
    w_qkv, w_out, w_up, w_down = layer_weights
    seq_count = live_keys.shape[0]
    normed = layer_norm(stream, norm_rows[0, 0], norm_rows[0, 1]).astype(jnp.bfloat16)
    normed_all = spread_rows(normed)
    packed = jnp.dot(
        normed_all, w_qkv.reshape(w_qkv.shape[0], -1), preferred_element_type=jnp.float32
    ).astype(jnp.bfloat16)
    packed = packed.reshape(seq_count, -1, 3, w_qkv.shape[-1])
    queries, keys_local, values_local = (packed[:, :, 0], packed[:, :, 1], packed[:, :, 2])
    keys_all, values_all = (
        lax.all_gather(keys_local, "blk", axis=1, tiled=True),
        lax.all_gather(values_local, "blk", axis=1, tiled=True),
    )
    attended, log_totals = attend(queries, keys_all, values_all, live_keys)
    attended = attended.astype(jnp.bfloat16).reshape(-1, attended.shape[-1])
    attn_out = sum_rows(attended, w_out, row_share)
    middle = stream + attn_out
    normed_two = layer_norm(middle, norm_rows[1, 0], norm_rows[1, 1]).astype(jnp.bfloat16)
    normed_two_all = spread_rows(normed_two)
    hidden_pre = jnp.dot(normed_two_all, w_up, preferred_element_type=jnp.float32)
    hidden_act = gelu_exact(hidden_pre).astype(jnp.bfloat16)
    ffn_out = sum_rows(hidden_act, w_down, row_share)
    kept = (
        stream,
        middle,
        normed_all,
        queries,
        keys_local,
        values_local,
        keys_all,
        values_all,
        log_totals,
        attended,
        normed_two_all,
        hidden_pre,
    )
    return (middle + ffn_out, attn_out, ffn_out, kept)


def layer_backward(grad_stream, kept, layer_weights, norm_rows, live_keys, row_share):
    (
        stream,
        middle,
        normed_all,
        queries,
        keys_local,
        values_local,
        keys_all,
        values_all,
        log_totals,
        attended,
        normed_two_all,
        hidden_pre,
    ) = kept
    w_qkv, w_out, w_up, w_down = layer_weights
    grad_ffn = spread_grads(grad_stream.astype(jnp.bfloat16))
    hidden_act, gelu_back = jax.vjp(gelu_exact, hidden_pre)
    grad_down = jnp.einsum(
        "nf,nd->fd", hidden_act.astype(jnp.bfloat16), grad_ffn, preferred_element_type=jnp.float32
    )
    grad_act = jnp.einsum("nd,fd->nf", grad_ffn, w_down, preferred_element_type=jnp.float32)
    (grad_pre,) = gelu_back(grad_act)
    grad_pre = grad_pre.astype(jnp.bfloat16)
    grad_up = jnp.einsum("nd,nf->df", normed_two_all, grad_pre, preferred_element_type=jnp.float32)
    grad_normed_two = sum_grads(grad_pre, w_up, row_share)
    _, norm_back_two = jax.vjp(layer_norm, middle, norm_rows[1, 0], norm_rows[1, 1])
    grad_mid, gain_two, shift_two = norm_back_two(grad_normed_two)
    grad_middle = grad_stream + grad_mid
    grad_attn = spread_grads(grad_middle.astype(jnp.bfloat16))
    grad_out_w = jnp.einsum("nf,nd->fd", attended, grad_attn, preferred_element_type=jnp.float32)
    grad_heads = (
        jnp.einsum("nd,fd->nf", grad_attn, w_out, preferred_element_type=jnp.float32)
        .astype(jnp.bfloat16)
        .reshape(queries.shape)
    )
    grad_query, grad_key, grad_value = attend_back(
        queries, keys_all, values_all, grad_heads, log_totals, live_keys
    )
    grad_packed = (
        jnp.stack((grad_query, grad_key, grad_value), axis=2)
        .astype(jnp.bfloat16)
        .reshape(normed_all.shape[0], -1)
    )
    grad_qkv = jnp.einsum(
        "nd,nc->dc", normed_all, grad_packed, preferred_element_type=jnp.float32
    ).reshape(w_qkv.shape)
    grad_normed = sum_grads(grad_packed, w_qkv.reshape(w_qkv.shape[0], -1), row_share)
    _, norm_back_one = jax.vjp(layer_norm, stream, norm_rows[0, 0], norm_rows[0, 1])
    grad_input, gain_one, shift_one = norm_back_one(grad_normed)
    norm_grads = jnp.stack((jnp.stack((gain_one, shift_one)), jnp.stack((gain_two, shift_two))))
    return (grad_middle + grad_input, (grad_qkv, grad_out_w, grad_up, grad_down), norm_grads)


def plain_step(
    token_ids,
    targets,
    masked,
    lengths,
    family_weight,
    embed_table,
    w_qkv,
    w_out,
    w_up,
    w_down,
    norm_params,
):
    blk_count = lax.axis_size("blk")
    head_count = lax.axis_size("head")
    seq_count, blk_tokens = token_ids.shape
    row_share = seq_count * blk_tokens // head_count
    row_first = lax.axis_index("head") * row_share
    blk_start = lax.axis_index("blk") * blk_tokens
    table_all, qkv_all, out_all, up_all, down_all, norm_all = (
        lax.all_gather(embed_table.astype(jnp.bfloat16), "blk", axis=1, tiled=True),
        lax.all_gather(w_qkv.astype(jnp.bfloat16), "blk", axis=1, tiled=True),
        lax.all_gather(w_out.astype(jnp.bfloat16), "blk", axis=2, tiled=True),
        lax.all_gather(w_up.astype(jnp.bfloat16), "blk", axis=1, tiled=True),
        lax.all_gather(w_down.astype(jnp.bfloat16), "blk", axis=1, tiled=True),
        lax.all_gather(norm_params.astype(jnp.bfloat16), "blk", axis=2, tiled=True),
    )
    token_table = table_all[:VOCAB]
    place_rows = lax.dynamic_slice_in_dim(table_all, VOCAB + blk_start, blk_tokens, 0)
    norm_rows = norm_all.astype(jnp.float32)
    live_keys = jnp.arange(blk_tokens * blk_count)[None, :] < lengths[:, None]
    positions = blk_start + jnp.arange(blk_tokens)
    live_local = positions[None, :] < lengths[:, None]
    seq_of_row = (row_first + jnp.arange(row_share)) // blk_tokens
    place_of_row = (row_first + jnp.arange(row_share)) % blk_tokens
    seq_hot = (seq_of_row[:, None] == jnp.arange(seq_count)[None, :]).astype(jnp.float32)
    place_hot = place_of_row[:, None] == jnp.arange(blk_tokens)[None, :]
    row_family = jnp.dot(seq_hot, family_weight, precision=HIGHEST)
    row_live = lax.dynamic_slice_in_dim(live_local.reshape(-1), row_first, row_share, 0).astype(
        jnp.float32
    )[:, None]
    row_ids = lax.dynamic_slice_in_dim(token_ids.reshape(-1), row_first, row_share, 0)
    row_targets = lax.dynamic_slice_in_dim(targets.reshape(-1), row_first, row_share, 0)
    row_masked = lax.dynamic_slice_in_dim(masked.reshape(-1), row_first, row_share, 0)
    token_hot = row_ids[:, None] == jnp.arange(VOCAB)[None, :]
    stream = jnp.dot(
        token_hot.astype(jnp.bfloat16), token_table, preferred_element_type=jnp.float32
    ) + jnp.dot(place_hot.astype(jnp.bfloat16), place_rows, preferred_element_type=jnp.float32)
    layer_stats = []
    kept_all = []
    for layer_idx in range(LAYERS):
        layer_weights = (
            qkv_all[layer_idx],
            out_all[layer_idx],
            up_all[layer_idx],
            down_all[layer_idx],
        )
        layer_stats.append(jnp.sum(stream * stream * row_live))
        stream, attn_out, ffn_out, kept = layer_forward(
            stream,
            layer_weights,
            norm_rows[2 * layer_idx : 2 * layer_idx + 2],
            live_keys,
            row_share,
        )
        layer_stats.append(jnp.sum(attn_out * attn_out * row_live))
        layer_stats.append(jnp.sum(ffn_out * ffn_out * row_live))
        kept_all.append(kept)
    final_low = layer_norm(stream, norm_rows[2 * LAYERS, 0], norm_rows[2 * LAYERS, 1]).astype(
        jnp.bfloat16
    )
    logits = jnp.einsum("nd,vd->nv", final_low, token_table, preferred_element_type=jnp.float32)
    shifted = logits - jnp.max(logits, axis=-1, keepdims=True)
    log_probs = shifted - jnp.log(jnp.sum(jnp.exp(shifted), axis=-1, keepdims=True))
    target_hot = (row_targets[:, None] == jnp.arange(VOCAB)[None, :]).astype(jnp.float32)
    token_loss = -jnp.sum(target_hot * log_probs, axis=1)
    token_weight = row_masked.astype(jnp.float32) * row_family
    loss_sum, weight_sum, squares = lax.psum(
        (jnp.sum(token_weight * token_loss), jnp.sum(token_weight), jnp.stack(layer_stats)),
        ("blk", "head"),
    )
    grad_logits = ((token_weight / weight_sum)[:, None] * (jnp.exp(log_probs) - target_hot)).astype(
        jnp.bfloat16
    )
    grad_final = jnp.einsum(
        "nv,vd->nd", grad_logits, token_table, preferred_element_type=jnp.float32
    )
    grad_table = jnp.einsum("nv,nd->vd", grad_logits, final_low, preferred_element_type=jnp.float32)
    _, final_back = jax.vjp(layer_norm, stream, norm_rows[2 * LAYERS, 0], norm_rows[2 * LAYERS, 1])
    grad_stream, gain_last, shift_last = final_back(grad_final)
    layer_grads = []
    norm_grads = []
    for layer_idx in reversed(range(LAYERS)):
        layer_weights = (
            qkv_all[layer_idx],
            out_all[layer_idx],
            up_all[layer_idx],
            down_all[layer_idx],
        )
        grad_stream, grads_now, norms_now = layer_backward(
            grad_stream,
            kept_all[layer_idx],
            layer_weights,
            norm_rows[2 * layer_idx : 2 * layer_idx + 2],
            live_keys,
            row_share,
        )
        layer_grads.insert(0, grads_now)
        norm_grads.insert(0, norms_now)
    grad_table = grad_table + jnp.dot(
        token_hot.astype(jnp.float32).T, grad_stream, precision=HIGHEST
    )
    grad_place = jnp.dot(place_hot.astype(jnp.float32).T, grad_stream, precision=HIGHEST)
    grad_norms = jnp.concatenate(norm_grads + [jnp.stack((gain_last, shift_last))[None]], axis=0)
    stacked = [
        jnp.stack([layer_entry[slot_idx] for layer_entry in layer_grads]) for slot_idx in range(4)
    ]
    table_sum, place_sum, norm_sum = (
        lax.psum(grad_table.astype(jnp.bfloat16), "head").astype(jnp.float32),
        lax.psum(grad_place.astype(jnp.bfloat16), "head").astype(jnp.float32),
        lax.psum(grad_norms.astype(jnp.bfloat16), "head").astype(jnp.float32),
    )
    place_full = lax.dynamic_update_slice_in_dim(
        jnp.zeros((blk_tokens * blk_count, place_sum.shape[1]), jnp.float32),
        place_sum,
        blk_start,
        0,
    )
    full_table = jnp.concatenate((table_sum, place_full), axis=0)
    reduced = (
        lax.psum_scatter(full_table, "blk", scatter_dimension=1, tiled=True),
        lax.psum_scatter(stacked[0], "blk", scatter_dimension=1, tiled=True),
        lax.psum_scatter(stacked[1], "blk", scatter_dimension=2, tiled=True),
        lax.psum_scatter(stacked[2], "blk", scatter_dimension=1, tiled=True),
        lax.psum_scatter(stacked[3], "blk", scatter_dimension=1, tiled=True),
        lax.psum_scatter(norm_sum, "blk", scatter_dimension=2, tiled=True),
    )
    sharded_squares = sum((jnp.sum(grad_part * grad_part) for grad_part in reduced[1:5]))
    shared_squares = (
        jnp.sum(reduced[0] * reduced[0]) + jnp.sum(reduced[5] * reduced[5])
    ) / head_count
    grad_norm = jnp.sqrt(lax.psum(sharded_squares + shared_squares, ("blk", "head")))
    return loss_sum, weight_sum, grad_norm, squares, reduced


BF16 = jnp.bfloat16
F32 = jnp.float32
MESH = pl.DeviceIdType.MESH
LOG2E = 1.4426950408889634
NORM_LANE = 32


def dot(left, right, left_dim, right_dim):
    return lax.dot_general(
        left, right, (((left_dim,), (right_dim,)), ((), ())), preferred_element_type=F32
    )


class Sizes:
    def __init__(self, blk, head, seqs, blk_tokens, w_qkv, w_up, w_down):
        self.B, self.H, self.S = blk, head, seqs
        self.L = w_qkv[0]
        self.DB = w_qkv[1]
        self.D = self.DB * blk
        self.HC = w_qkv[3]
        self.T = blk_tokens * blk
        self.G = blk // seqs if blk % seqs == 0 else 0
        self.FD = w_down[1]
        if self.G:
            self.NR = self.G * head
            self.R = self.T // self.NR
            self.NC = self.NR // 2
            self.FU = w_up[2] // self.G

    def fused(self, blk_tokens):
        if self.G != 2 or self.S != 4 or self.H % 2 or self.R != blk_tokens or self.R != 128:
            return False
        if self.FU != self.FD * self.S or 3 * self.S > 16 or VOCAB > NORM_LANE:
            return False
        if NORM_LANE + 2 * (2 * self.L + 1) > 128:
            return False
        if any(n % 16 for n in (self.DB, self.HC, self.FD)) or self.D % 128 or self.FU % 128:
            return False
        weights = self.L * 2 * (4 * self.D * self.HC + 2 * self.D * self.FU)
        kept = self.L * self.T * (6 * self.D + 6 * self.FU + 14 * self.HC)
        return 3 * weights + kept + 16 * self.T * self.D + 8 * self.T * 256 * 4 < (60 << 20)


def step_kernel(
    z,
    lens,
    fam,
    tok_in,
    tgt_in,
    msk_in,
    emb_in,
    wq_in,
    wo_in,
    wu_in,
    wd_in,
    norm_in,
    scal_out,
    ge_out,
    gq_out,
    go_out,
    gu_out,
    gd_out,
    gn_out,
    ids,
    tp,
    wq_own,
    wo_own,
    wu_own,
    wd_own,
    gu_sum,
    idsg,
    tpg,
    etg,
    ptg,
    wq,
    wo,
    wu,
    wd,
    h1,
    h2,
    df,
    da,
    act,
    slope,
    du,
    qt,
    kt,
    vt,
    o32,
    ob,
    dob,
    lse,
    dqkv,
    bias,
    xs,
    xm,
    keep,
    psrc,
    csrc,
    srecv,
    rrecv,
    sg,
    stq,
    sto,
    stu,
    std,
    rq,
    ro,
    ru,
    rd,
    rc,
    tq,
    to,
    tu,
    td,
    tc,
    fst,
    frx,
    hrx,
    scg,
    id_s,
    id_r,
    tp_s,
    tp_r,
    w_s,
    w_r,
    ag_s,
    ag_r,
    rs_s,
    rs_r,
    g_s,
    g_r,
    f_s,
    f_r,
    hx_s,
    hx_r,
    sc_s,
    sc_r,
):
    B, H, S, G, L, D, DB, HC, R, NC, NR, FU, FD, T = (
        z.B, z.H, z.S, z.G, z.L, z.D, z.DB, z.HC, z.R, z.NC, z.NR, z.FU, z.FD, z.T,
    )
    N_HEADS = HC // HEAD_DIM
    W = 2 * R
    QT = 2
    scale = HEAD_DIM ** (-0.5)
    c2 = scale * LOG2E
    b = lax.axis_index("blk")
    h = lax.axis_index("head")
    s, g = b // G, b % G
    y, c = h // 2, h % 2
    own_row = g * H + h
    s1 = s + 1 - 2 * (s % 2)
    s2 = (s + 2) % S
    s3 = (s1 + 2) % S

    def dev(blk_i, head_i):
        return (blk_i, head_i)

    sibling = dev(b, y * 2 + 1 - c)

    def peer(k):
        return dev(s * G + (g + k // 2) % G, ((y + k % 2) % 2) * 2 + c)

    def back(k):
        return ((-(k // 2)) % G) * 2 + k % 2

    waits = []

    def send(src, dst, ssem, rsem, device):
        copy = pltpu.make_async_remote_copy(src, dst, ssem, rsem, device, MESH)
        copy.start()
        return copy

    def arrived(dst, ssem, rsem):
        pltpu.make_async_remote_copy(dst, dst, ssem, rsem, sibling, MESH).wait_recv()

    def over_blk(body):
        def one(k, carry):
            body(lax.rem(b + k, B))
            return carry

        lax.fori_loop(1, B, one, 0)

    def rows(i, n):
        return pl.ds(pl.multiple_of(i * n, 16), n)

    barrier = pltpu.get_barrier_semaphore()

    def greet(k, carry):
        other = lax.rem(b * H + h + k, B * H)
        pl.semaphore_signal(barrier, inc=1, device_id=dev(other // H, other % H), device_id_type=MESH)
        return carry

    lax.fori_loop(1, B * H, greet, 0)

    table = emb_in[...]
    ids[...] = jnp.zeros((16, R), jnp.int32)
    ids[0:S] = tok_in[...]
    ids[S : 2 * S] = tgt_in[...]
    ids[2 * S : 3 * S] = msk_in[...]
    sg[...] = jnp.zeros((D, 128), F32)
    for i in range(2 * L + 1):
        sg[NORM_LANE + 2 * i : NORM_LANE + 2 * i + 2, 0:DB] = norm_in[i]
    lane_small = lax.broadcasted_iota(jnp.int32, (DB, 128), 1)
    token_part = jnp.where(lane_small < VOCAB, table[:, 0:128], sg[0:128, :].T[0:DB]).astype(BF16)
    for i in range(NR):
        tp[i, 0:DB] = token_part
        tp[i, DB:] = table[:, VOCAB + i * R : VOCAB + (i + 1) * R].astype(BF16)
    pl.semaphore_wait(barrier, B * H - 1)

    def send_tp(other):
        send(tp.at[(other % G) * H + h], tpg.at[b], tp_s.at[other], tp_r.at[b], dev(other, h))
        send(ids, idsg.at[b], id_s.at[other], id_r.at[b], dev(other, h))

    over_blk(send_tp)
    idsg[b] = ids[...]
    tpg[b] = tp[own_row]

    def w_sem(sems, l, kind, m):
        return sems.at[(l * 4 + kind) * 8 + m]

    def w_ref(l, kind, at):
        return (wq, wo, wu, wd)[kind].at[l, at]

    def shard_rows(kind, plane, column=None):
        if kind == 3:
            return rows(plane, FD)
        return rows(plane * G + (g if column is None else column), DB)

    def w_send(l, kind, m, src, at, device):
        waits.append(
            send(src, w_ref(l, kind, at), w_sem(w_s, l, kind, m), w_sem(w_r, l, kind, m), device)
        )

    def w_arrived(l, kind, m, at):
        arrived(w_ref(l, kind, at), w_sem(w_s, l, kind, m), w_sem(w_r, l, kind, m))

    def round_weights(l, kind):
        at = shard_rows(kind, s)
        if kind == 0:
            wq_own[l] = jnp.concatenate([wq_in[l, i] for i in range(3)], axis=1).astype(BF16)
            wq[l, at] = wq_own[l]
        elif kind == 1:
            wo_own[l] = wo_in[l].T.astype(BF16)
            wo[l, at] = wo_own[l]
        elif kind == 2:
            up = wu_in[l]
            for j in range(G):
                parts = [up[:, (i * G + j) * FD : (i * G + j + 1) * FD] for i in range(S)]
                wu_own[l, j] = jnp.concatenate(parts, axis=1).astype(BF16)
            wu[l, at] = wu_own[l, g]
        else:
            wd_own[l] = wd_in[l].astype(BF16)
            wd[l, at] = wd_own[l]

    def send_weights(l, kind):
        round_weights(l, kind)
        at = shard_rows(kind, s)
        if kind == 2:
            w_send(l, 2, 1, wu_own.at[l, g], at, dev(s2 * G + g, h))
            w_send(l, 2, 2, wu_own.at[l, 1 - g], at, dev(s2 * G + 1 - g, h))
            w_send(l, 2, 0, wu_own.at[l, 1 - g], at, dev(s * G + 1 - g, h))
            w_send(l, 2, 3, wu_own.at[l, g], at, dev(s1 * G + g, h))
            w_send(l, 2, 4, wu_own.at[l, 1 - g], at, dev(s1 * G + 1 - g, h))
            return
        src = (wq_own, wo_own, None, wd_own)[kind].at[l]
        w_send(l, kind, 0, src, at, dev(s2 * G + g, h))
        w_send(l, kind, 1, src, at, dev(s1 * G + g, h))
        if kind < 2:
            w_send(l, kind, 3, src, at, dev(s * G + 1 - g, h))

    def relay_weights(l, kind):
        if kind == 2:
            w_arrived(l, 2, 1, shard_rows(2, s2))
            w_arrived(l, 2, 2, shard_rows(2, s2, 1 - g))
            both = rows(s2, G * DB)
            w_send(l, 2, 5, w_ref(l, 2, both), both, dev(s1 * G + g, h))
            return
        at = shard_rows(kind, s2)
        w_arrived(l, kind, 0, at)
        w_send(l, kind, 2, w_ref(l, kind, at), at, dev(s1 * G + g, h))
        if kind < 2:
            w_send(l, kind, 4, w_ref(l, kind, at), at, dev(s * G + 1 - g, h))

    def cross_weights(l, kind):
        for m, plane in ((1, s1), (2, s3)):
            at = shard_rows(kind, plane)
            w_arrived(l, kind, m, at)
            w_send(l, kind, m + 4, w_ref(l, kind, at), at, dev(s * G + 1 - g, h))

    def wait_weights(l, kind):
        if kind < 2:
            for m, plane in ((3, s), (4, s2), (5, s1), (6, s3)):
                w_arrived(l, kind, m, shard_rows(kind, plane, 1 - g))
        elif kind == 2:
            w_arrived(l, 2, 0, shard_rows(2, s, 1 - g))
            w_arrived(l, 2, 3, shard_rows(2, s1))
            w_arrived(l, 2, 4, shard_rows(2, s1, 1 - g))
            w_arrived(l, 2, 5, rows(s3, G * DB))
        else:
            w_arrived(l, 3, 1, shard_rows(3, s1))
            w_arrived(l, 3, 2, shard_rows(3, s3))

    for kind in range(4):
        send_weights(0, kind)

    def ag_sem(sems, use, i):
        return sems.at[use * 2 * NC + i]

    def block(buf, k, half):
        return buf.at[:, k * W + half * R : k * W + half * R + R]

    def spread(buf, use, slots):
        for k in reversed(slots):
            if k:
                waits.append(
                    send(
                        block(buf, 0, 0),
                        block(buf, back(k), 0),
                        ag_sem(ag_s, use, k),
                        ag_sem(ag_r, use, back(k)),
                        peer(k),
                    )
                )
        waits.append(
            send(block(buf, 0, 0), block(buf, 0, 1), ag_sem(ag_s, use, NC), ag_sem(ag_r, use, NC), sibling)
        )

    def hand_on(buf, use, k):
        arrived(block(buf, k, 0), ag_sem(ag_s, use, k), ag_sem(ag_r, use, k))
        waits.append(
            send(
                block(buf, k, 0),
                block(buf, k, 1),
                ag_sem(ag_s, use, NC + k),
                ag_sem(ag_r, use, NC + k),
                sibling,
            )
        )

    def have(buf, use, k):
        arrived(block(buf, k, 1), ag_sem(ag_s, use, NC + k), ag_sem(ag_r, use, NC + k))

    staged = {}

    def rs_sem(sems, use, i):
        return sems.at[use * 2 * NC + i]

    def stage(ref, key, value):
        if key in staged:
            staged.pop(key)[0].wait_send()
        ref[...] = value

    def part(use, k, value):
        keep[k] = value[:, :R]
        stage(psrc.at[k], ("p", k), value[:, R:].astype(BF16))
        staged["p", k] = [
            send(psrc.at[k], srecv.at[use % 4, k], rs_sem(rs_s, use, k), rs_sem(rs_r, use, k), sibling)
        ]

    def pair_sum(use, k):
        arrived(srecv.at[use % 4, k], rs_sem(rs_s, use, k), rs_sem(rs_r, use, k))
        return keep[k] + srecv[use % 4, k].astype(F32)

    def pass_on(use, k):
        stage(csrc.at[k], ("c", k), pair_sum(use, k).astype(BF16))
        staged["c", k] = [
            send(
                csrc.at[k],
                rrecv.at[use % 4, back(k)],
                rs_sem(rs_s, use, NC + k),
                rs_sem(rs_r, use, NC + back(k)),
                peer(k),
            )
        ]

    def total(use, slots):
        out = pair_sum(use, 0)
        for k in slots:
            if k:
                arrived(rrecv.at[use % 4, k], rs_sem(rs_s, use, NC + k), rs_sem(rs_r, use, NC + k))
                out = out + rrecv[use % 4, k].astype(F32)
        return out

    def g_sem(sems, l, kind, m):
        return sems.at[(l * 4 + kind) * 8 + m]

    def g_send(l, kind, m, src, dst, device):
        return send(src, dst, g_sem(g_s, l, kind, m), g_sem(g_r, l, kind, m), device)

    def g_arrived(l, kind, m, dst):
        arrived(dst, g_sem(g_s, l, kind, m), g_sem(g_r, l, kind, m))

    def g_stage(key, ref, value):
        for copy in staged.pop(key, ()):
            copy.wait_send()
        ref[...] = value.astype(BF16)

    def g_first(l, kind, value):
        src, dst = ((stq, rq), (sto, ro), (stu, ru), (std, rd))[kind]
        g_stage(("g", kind), src, value)
        if kind < 2:
            staged["g", kind] = [
                g_send(
                    l, kind, i, src.at[rows(i * G + 1 - g, DB)], dst.at[l, i], dev(s * G + 1 - g, h)
                )
                for i in range(S)
            ]
            return
        n = G * DB if kind == 2 else FD
        dst[l, 0] = src[rows(s, n)]
        staged["g", kind] = [
            g_send(l, kind, i, src.at[rows(plane, n)], dst.at[l, 1 + i], dev(s1 * G + g, h))
            for i, plane in ((1, s3), (0, s1))
        ]

    def g_column(l, kind, plane):
        src, dst = ((stq, rq), (sto, ro))[kind]
        return src[rows(plane * G + g, DB)].astype(F32) + dst[l, plane].astype(F32)

    def g_mid(l, kind):
        src, dst, tmp = ((stq, rq, tq), (sto, ro, to))[kind]
        for i in range(S):
            g_arrived(l, kind, i, dst.at[l, i])
        g_stage(("m", kind, 1), tmp.at[1], g_column(l, kind, s3))
        one = g_send(l, kind, 5, tmp.at[1], dst.at[l, S + 1], dev(s1 * G + g, h))
        g_stage(("m", kind, 0), tmp.at[0], g_column(l, kind, s1))
        two = g_send(l, kind, 4, tmp.at[0], dst.at[l, S], dev(s1 * G + g, h))
        staged["m", kind, 1] = [one]
        staged["m", kind, 0] = [two]

    def g_second(l, kind):
        if kind < 2:
            src, dst, tmp = ((stq, rq, tq), (sto, ro, to))[kind]
            g_arrived(l, kind, 5, dst.at[l, S + 1])
            g_stage(("s", kind), tmp.at[2], g_column(l, kind, s2) + dst[l, S + 1].astype(F32))
            staged["s", kind] = [g_send(l, kind, 6, tmp.at[2], dst.at[l, S + 2], dev(s2 * G + g, h))]
            return
        src, dst, tmp, n = ((stu, ru, tu, G * DB), (std, rd, td, FD))[kind - 2]
        g_arrived(l, kind, 1, dst.at[l, 2])
        g_stage(("s", kind), tmp, src[rows(s2, n)].astype(F32) + dst[l, 2].astype(F32))
        staged["s", kind] = [g_send(l, kind, 2, tmp, dst.at[l, 3], dev(s2 * G + g, h))]

    def g_third(l):
        g_arrived(l, 2, 0, ru.at[l, 1])
        g_arrived(l, 2, 2, ru.at[l, 3])

        def summed(column):
            at = rows(column, DB)
            return sum(ru[l, i, at, :].astype(F32) for i in (0, 1, 3))

        g_stage(("t", 2), tc, summed(1 - g))
        staged["t", 2] = [g_send(l, 2, 3, tc, rc.at[l], dev(s * G + 1 - g, h))]
        gu_sum[g] = summed(g)

    def lanes_of(v):
        folded = jnp.sum(v * v, axis=0, keepdims=True)
        return jnp.sum(folded, axis=1, keepdims=True) + jnp.zeros((1, 128), F32)

    def g_final(l, kind):
        if kind < 2:
            dst, out = ((rq, gq_out), (ro, go_out))[kind]
            g_arrived(l, kind, 4, dst.at[l, S])
            g_arrived(l, kind, 6, dst.at[l, S + 2])
            value = g_column(l, kind, s) + dst[l, S].astype(F32) + dst[l, S + 2].astype(F32)
            if kind == 0:
                for i in range(3):
                    out[l, i] = value[:, i * HC : (i + 1) * HC]
            else:
                out[l] = value.T
        elif kind == 2:
            g_arrived(l, 2, 3, rc.at[l])
            value = rc[l].astype(F32)
            gu_sum[1 - g] = value
            parts = [gu_sum[j, :, i * FD : (i + 1) * FD] for i in range(S) for j in range(G)]
            gu_out[l] = jnp.concatenate(parts, axis=1)
            return lanes_of(gu_sum[0]) + lanes_of(gu_sum[1])
        else:
            g_arrived(l, 3, 0, rd.at[l, 1])
            g_arrived(l, 3, 2, rd.at[l, 3])
            value = sum(rd[l, i].astype(F32) for i in (0, 1, 3))
            gd_out[l] = value
        return lanes_of(value)

    squares = jnp.zeros((1, 128), F32)

    length = lens[s]
    for k in range(NC):
        for half in range(2):
            core = c if half == 0 else 1 - c
            block_row = ((g + k // 2) % G) * H + ((y + k % 2) % 2) * 2 + core
            place = block_row * R + lax.broadcasted_iota(jnp.int32, (R, 128), 0)
            bias[k * W + half * R : k * W + half * R + R, :] = jnp.where(place < length, 0.0, NEGATIVE)
    lane_place = own_row * R + lax.broadcasted_iota(jnp.int32, (1, R), 1)
    live = jnp.where(lane_place < length, 1.0, 0.0)
    dqkv[0:HC, QT * W :] = jnp.zeros((HC, T - QT * W), BF16)
    sg[...] = jnp.zeros((D, 128), F32)
    lane = lax.broadcasted_iota(jnp.int32, (D, 128), 1)
    row_of = lax.broadcasted_iota(jnp.int32, (128, R), 0)

    def tp_here(other):
        arrived(tpg.at[other], tp_s.at[other], tp_r.at[other])
        arrived(idsg.at[other], id_s.at[other], id_r.at[other])

    over_blk(tp_here)
    for i in range(B):
        etg[i * DB : (i + 1) * DB] = tpg[i, :DB]
        ptg[i * DB : (i + 1) * DB] = tpg[i, DB:]
    token_row = idsg[own_row, pl.ds(s, 1), :]
    target_row = idsg[own_row, pl.ds(S + s, 1), :]
    mask_row = idsg[own_row, pl.ds(2 * S + s, 1), :].astype(F32)
    token_hot = jnp.where(row_of == token_row, 1.0, 0.0).astype(BF16)
    token_weight = mask_row * fam[s]
    weight_sum = jnp.zeros((1, 1), F32)
    for i in range(S):
        counts = jnp.zeros((1, R), F32)
        for j in range(B):
            counts = counts + idsg[j, 2 * S + i : 2 * S + i + 1, :].astype(F32)
        weight_sum = weight_sum + jnp.sum(counts, axis=1, keepdims=True) * fam[i]

    def gain(i):
        return etg[:, NORM_LANE + 2 * i : NORM_LANE + 2 * i + 1].astype(F32)

    def shift(i):
        return etg[:, NORM_LANE + 2 * i + 1 : NORM_LANE + 2 * i + 2].astype(F32)

    def normalize(v):
        centred = v - jnp.mean(v, axis=0, keepdims=True)
        rstd = lax.rsqrt(jnp.mean(centred * centred, axis=0, keepdims=True) + NORM_EPS)
        return centred * rstd, rstd

    def layer_norm_low(v, i):
        hat, _ = normalize(v)
        return (hat * gain(i) + shift(i)).astype(BF16)

    def layer_norm_back(grad, v, i):
        hat, rstd = normalize(v)
        gain_grad = jnp.sum(grad * hat, axis=1, keepdims=True)
        shift_grad = jnp.sum(grad, axis=1, keepdims=True)
        sg[...] += jnp.where(lane == NORM_LANE + 2 * i, gain_grad, 0.0) + jnp.where(
            lane == NORM_LANE + 2 * i + 1, shift_grad, 0.0
        )
        scaled = grad * gain(i)
        mean_one = jnp.mean(scaled, axis=0, keepdims=True)
        mean_two = jnp.mean(scaled * hat, axis=0, keepdims=True)
        return rstd * (scaled - mean_one - hat * mean_two)

    def square_sum(v):
        return jnp.sum(jnp.sum(v * v, axis=0, keepdims=True) * live, axis=1, keepdims=True)

    slots = list(range(NC))
    near = slots[:2]
    far = slots[1:]
    stats = []
    relay_weights(0, 0)
    relay_weights(0, 1)
    xs[0] = dot(etg[...], token_hot, 1, 0) + ptg[...].astype(F32)

    def cols(k):
        return slice(k * W, (k + 1) * W)

    for l in range(L):
        x = xs[l]
        stats.append(square_sum(x))
        h1[l, :, 0:R] = layer_norm_low(x, 2 * l)
        spread(h1.at[l], 3 * l, slots)
        cross_weights(l, 0)
        cross_weights(l, 1)
        wait_weights(l, 0)

        def project(k):
            if k in near:
                packed = dot(wq[l], h1[l, :, cols(k)], 0, 0).astype(BF16)
                qt[l, :, cols(k)] = packed[0:HC]
                packed = packed[HC:]
            else:
                packed = dot(wq[l, :, :], h1[l, :, cols(k)], 0, 0).astype(BF16)[HC:]
            kt[l, :, cols(k)] = packed[0:HC]
            vt[l, :, cols(k)] = packed[HC:]

        have(h1.at[l], 3 * l, 0)
        project(0)
        for k in far:
            hand_on(h1.at[l], 3 * l, k)
            if k > 1:
                have(h1.at[l], 3 * l, k - 1)
                project(k - 1)
        have(h1.at[l], 3 * l, NC - 1)
        project(NC - 1)
        relay_weights(l, 2)
        relay_weights(l, 3)
        if l + 1 < L:
            for kind in range(4):
                send_weights(l + 1, kind)

        def attend(q, first, last):
            def one(i, carry):
                at = rows(i, HEAD_DIM)
                scores = dot(kt[l, at, :], qt[l, at, cols(q)], 0, 0) + jnp.concatenate([bias[...]] * 2, axis=1)
                peak = jnp.max(scores, axis=0, keepdims=True)
                exps = jnp.exp2((scores - peak) * c2)
                norm = jnp.sum(exps, axis=0, keepdims=True)
                probs = (exps * (1.0 / norm)).astype(BF16)
                out = dot(vt[l, at, :], probs, 1, 0)
                o32[l, at, cols(q)] = out
                ob[l, at, cols(q)] = out.astype(BF16)
                lse[l, pl.ds(pl.multiple_of(i * 8, 8), 8), cols(q)] = jnp.broadcast_to(
                    peak * c2 + jnp.log(norm) * LOG2E, (8, W)
                )
                return carry

            lax.fori_loop(first, last, one, 0)

        attend(1, 0, N_HEADS)
        wait_weights(l, 1)
        part(4 * l, 1, dot(wo[l], ob[l, :, cols(1)], 1, 0))
        attend(0, 0, N_HEADS // 2)
        pass_on(4 * l, 1)
        attend(0, N_HEADS // 2, N_HEADS)
        part(4 * l, 0, dot(wo[l], ob[l, :, cols(0)], 1, 0))
        attn_out = total(4 * l, near)
        stats.append(square_sum(attn_out))
        middle = xs[l] + attn_out
        xm[l] = middle
        h2[l, :, 0:R] = layer_norm_low(middle, 2 * l + 1)
        spread(h2.at[l], 3 * l + 1, slots)
        wait_weights(l, 2)
        wait_weights(l, 3)

        def feed(k):
            pre = dot(wu[l], h2[l, :, cols(k)], 0, 0)
            cdf = 0.5 * (1.0 + lax.erf(pre * (0.5**0.5)))
            low = (pre * cdf).astype(BF16)
            act[l, :, cols(k)] = low
            slope[l, :, cols(k)] = cdf + pre * (jnp.exp(-0.5 * pre * pre) * 0.3989422804014327)
            part(4 * l + 1, k, dot(wd[l], low, 0, 0))

        have(h2.at[l], 3 * l + 1, 0)
        feed(0)
        for k in far:
            hand_on(h2.at[l], 3 * l + 1, k)
            if k > 1:
                have(h2.at[l], 3 * l + 1, k - 1)
                feed(k - 1)
                if k > 2:
                    pass_on(4 * l + 1, k - 2)
        have(h2.at[l], 3 * l + 1, NC - 1)
        feed(NC - 1)
        for k in far[-2:]:
            pass_on(4 * l + 1, k)
        if l + 1 < L:
            relay_weights(l + 1, 0)
            relay_weights(l + 1, 1)
        ffn_out = total(4 * l + 1, slots)
        stats.append(square_sum(ffn_out))
        xs[l + 1] = xm[l] + ffn_out

    last = xs[L]
    final_low = layer_norm_low(last, 2 * L)
    logits = dot(etg[...], final_low, 0, 0)[0:NORM_LANE]
    vocab_row = row_of[0:NORM_LANE]
    logits = jnp.where(vocab_row < VOCAB, logits, NEGATIVE)
    shifted = logits - jnp.max(logits, axis=0, keepdims=True)
    log_probs = shifted - jnp.log(jnp.sum(jnp.exp(shifted), axis=0, keepdims=True))
    target_hot = jnp.where(vocab_row == target_row, 1.0, 0.0)
    token_loss = -jnp.sum(target_hot * log_probs, axis=0, keepdims=True)
    loss = jnp.sum(token_weight * token_loss, axis=1, keepdims=True)
    grad_logits = ((token_weight / weight_sum) * (jnp.exp(log_probs) - target_hot)).astype(BF16)
    grad_logits = jnp.concatenate([grad_logits, jnp.zeros((128 - NORM_LANE, R), BF16)], axis=0)
    grad_final = dot(etg[...], grad_logits, 1, 0)
    sg[...] += dot(final_low, grad_logits, 1, 1)
    grad = layer_norm_back(grad_final, last, 2 * L)

    for l in reversed(range(L)):
        df[l, :, 0:R] = grad.astype(BF16)
        xs[l + 1] = grad
        spread(df.at[l], 3 * l + 2, slots)
        if l + 1 < L:
            g_mid(l + 1, 0)
            g_mid(l + 1, 1)
            g_third(l + 1)

        def feed_back(k):
            grad_act = dot(wd[l], df[l, :, cols(k)], 1, 0)
            low = (grad_act * slope[l, :, cols(k)]).astype(BF16)
            du[:, cols(k)] = low
            part(4 * l + 2, k, dot(wu[l], low, 1, 0))

        have(df.at[l], 3 * l + 2, 0)
        feed_back(0)
        for k in far:
            hand_on(df.at[l], 3 * l + 2, k)
            if k > 1:
                have(df.at[l], 3 * l + 2, k - 1)
                feed_back(k - 1)
                if k > 2:
                    pass_on(4 * l + 2, k - 2)
        have(df.at[l], 3 * l + 2, NC - 1)
        feed_back(NC - 1)
        for k in far[-2:]:
            pass_on(4 * l + 2, k)
        if l + 1 < L:
            g_second(l + 1, 0)
            g_second(l + 1, 1)
        g_first(l, 3, dot(act[l], df[l], 1, 1))
        g_first(l, 2, dot(h2[l], du[...], 1, 1))
        grad_middle = xs[l + 1] + layer_norm_back(total(4 * l + 2, slots), xm[l], 2 * l + 1)
        xm[l] = grad_middle

        da[l, :, 0:R] = grad_middle.astype(BF16)
        spread(da.at[l], 3 * L + l, near)
        if l + 1 < L:
            for kind in range(4):
                squares = squares + g_final(l + 1, kind)

        def out_back(k):
            dob[:, cols(k)] = dot(wo[l], da[l, :, cols(k)], 0, 0).astype(BF16)

        have(da.at[l], 3 * L + l, 0)
        out_back(0)
        hand_on(da.at[l], 3 * L + l, 1)
        have(da.at[l], 3 * L + l, 1)
        out_back(1)

        g_second(l, 3)

        def attend_back(i, carry):
            at = rows(i, HEAD_DIM)
            key_h = kt[l, at, :]
            value_h = vt[l, at, :]
            grad_key = jnp.zeros((HEAD_DIM, T), F32)
            grad_value = jnp.zeros((HEAD_DIM, T), F32)
            for q in range(QT):
                query_h = qt[l, at, cols(q)]
                grad_h = dob[at, cols(q)]
                lse_h = lse[l, pl.ds(pl.multiple_of(i * 8, 8), 8), cols(q)][0:1]
                scores = dot(key_h, query_h, 0, 0) + jnp.concatenate([bias[...]] * 2, axis=1)
                probs = jnp.exp2(scores * c2 - lse_h)
                delta = jnp.sum(grad_h.astype(F32) * o32[l, at, cols(q)], axis=0, keepdims=True)
                grad_scores = (probs * (dot(value_h, grad_h, 0, 0) - delta)).astype(BF16)
                dqkv[at, cols(q)] = (dot(key_h, grad_scores, 1, 0) * scale).astype(BF16)
                grad_key = grad_key + dot(query_h, grad_scores, 1, 1)
                grad_value = grad_value + dot(grad_h, probs.astype(BF16), 1, 1)
            dqkv[pl.ds(pl.multiple_of(HC + i * HEAD_DIM, 16), HEAD_DIM), :] = (grad_key * scale).astype(BF16)
            dqkv[pl.ds(pl.multiple_of(2 * HC + i * HEAD_DIM, 16), HEAD_DIM), :] = grad_value.astype(BF16)
            return carry

        lax.fori_loop(0, N_HEADS, attend_back, 0)
        g_second(l, 2)
        for k in reversed(slots):
            part(4 * l + 3, k, dot(wq[l], dqkv[:, cols(k)], 1, 0))
            if 0 < k + 1 < NC:
                pass_on(4 * l + 3, k + 1)
        g_first(l, 0, dot(h1[l], dqkv[...], 1, 1))
        g_first(l, 1, dot(da[l], ob[l], 1, 1))
        grad = xm[l] + layer_norm_back(total(4 * l + 3, slots), xs[l], 2 * l)

    high = grad.astype(BF16)
    low = (grad - high.astype(F32)).astype(BF16)
    small = sg[...] + dot(high, token_hot, 1, 1) + dot(low, token_hot, 1, 1)
    small = small.astype(BF16)
    for i in range(B):
        fst[i, :DB] = small[i * DB : (i + 1) * DB]
        fst[i, DB:] = high[i * DB : (i + 1) * DB]

    def send_table(other):
        send(fst.at[other], frx.at[b], f_s.at[other], f_r.at[b], dev(other, h))

    over_blk(send_table)
    frx[b] = fst[b]

    g_mid(0, 0)
    g_mid(0, 1)
    g_third(0)
    squares = squares + g_final(0, 3)
    g_second(0, 0)
    g_second(0, 1)
    squares = squares + g_final(0, 2)
    def table_here(other):
        arrived(frx.at[other], f_s.at[other], f_r.at[other])

    over_blk(table_here)
    for j in range(G):
        value = frx[j, DB:].astype(F32)
        for i in range(1, S):
            value = value + frx[i * G + j, DB:].astype(F32)
        hrx[h, j] = value
        squares = squares + lanes_of(value)
    value = frx[0, :DB].astype(F32)
    for i in range(1, B):
        value = value + frx[i, :DB].astype(F32)
    hrx[h, G] = value

    def send_heads(k, carry):
        other = lax.rem(h + k, H)
        send(hrx.at[h], hrx.at[h], hx_s.at[other], hx_r.at[h], dev(b, other))
        return carry

    lax.fori_loop(1, H, send_heads, 0)

    def heads_here(k, carry):
        other = lax.rem(h + k, H)
        arrived(hrx.at[other], hx_s.at[other], hx_r.at[other])
        return carry

    for kind in (0, 1):
        squares = squares + g_final(0, kind)
    lax.fori_loop(1, H, heads_here, 0)
    value = hrx[0, G]
    for i in range(1, H):
        value = value + hrx[i, G]
    squares = squares + lanes_of(value) * (1.0 / H)
    small_sum = value

    lane_one = lax.broadcasted_iota(jnp.int32, (1, 128), 1)
    packed = jnp.where(lane_one == 0, loss, 0.0) + jnp.where(lane_one == 1, squares, 0.0)
    for i, stat in enumerate(stats):
        packed = packed + jnp.where(lane_one == 2 + i, stat, 0.0)
    me = b * H + h
    scg[me] = jnp.broadcast_to(packed, (8, 128))

    def send_scalars(k, carry):
        other = lax.rem(me + k, B * H)
        send(scg.at[me], scg.at[me], sc_s.at[other], sc_r.at[me], dev(other // H, other % H))
        return carry

    lax.fori_loop(1, B * H, send_scalars, 0)
    ge_out[...] = jnp.concatenate(
        [small_sum[:, :VOCAB]] + [hrx[i, j] for j in range(G) for i in range(H)], axis=1
    )
    norm_rows = small_sum.T
    for i in range(2 * L + 1):
        gn_out[i] = norm_rows[NORM_LANE + 2 * i : NORM_LANE + 2 * i + 2]

    def scalars_here(k, carry):
        other = lax.rem(me + k, B * H)
        arrived(scg.at[other], sc_s.at[other], sc_r.at[other])
        return carry

    lax.fori_loop(1, B * H, scalars_here, 0)
    out = scg[0]
    for i in range(1, B * H):
        out = out + scg[i]
    lane_eight = lax.broadcasted_iota(jnp.int32, (8, 128), 1)
    tokens = lens[0]
    for i in range(1, S):
        tokens = tokens + lens[i]
    roots = jnp.sqrt(jnp.where(lane_eight == 1, out, out / (tokens.astype(F32) * D)))
    out = jnp.where(lane_eight == 0, out, roots)
    scal_out[...] = jnp.where(lane_eight == 2 + 3 * L, weight_sum, out)

    for copy in waits:
        copy.wait_send()
    for copies in staged.values():
        for copy in copies:
            copy.wait_send()

    def sent(other):
        for src, ssem, rsem in ((tpg.at[other], tp_s, tp_r), (idsg.at[other], id_s, id_r), (frx.at[other], f_s, f_r)):
            pltpu.make_async_remote_copy(src, src, ssem.at[other], rsem.at[other], sibling, MESH).wait_send()

    over_blk(sent)

    def heads_sent(k, carry):
        other = lax.rem(h + k, H)
        pltpu.make_async_remote_copy(
            hrx.at[other], hrx.at[other], hx_s.at[other], hx_r.at[other], sibling, MESH
        ).wait_send()
        return carry

    lax.fori_loop(1, H, heads_sent, 0)

    def scalars_sent(k, carry):
        other = lax.rem(me + k, B * H)
        pltpu.make_async_remote_copy(
            scg.at[other], scg.at[other], sc_s.at[other], sc_r.at[other], sibling, MESH
        ).wait_send()
        return carry

    lax.fori_loop(1, B * H, scalars_sent, 0)


def fused_step(z, token_ids, targets, masked, lengths, family_weight, embed_table, w_qkv, w_out, w_up, w_down, norm_params):
    B, H, S, G, L, D, DB, HC, R, NC, NR, FU, FD, T = (
        z.B, z.H, z.S, z.G, z.L, z.D, z.DB, z.HC, z.R, z.NC, z.NR, z.FU, z.FD, z.T,
    )
    W = 2 * R
    smem = pl.BlockSpec(memory_space=pltpu.SMEM)
    vmem = pl.BlockSpec(memory_space=pltpu.VMEM)
    dma = pltpu.SemaphoreType.DMA
    scratch = [
        pltpu.VMEM((16, R), jnp.int32),
        pltpu.VMEM((NR, 2 * DB, 128), BF16),
        pltpu.VMEM((L, DB, 3 * HC), BF16),
        pltpu.VMEM((L, DB, HC), BF16),
        pltpu.VMEM((L, G, DB, FU), BF16),
        pltpu.VMEM((L, FD, D), BF16),
        pltpu.VMEM((G, DB, FU), F32),
        pltpu.VMEM((B, 16, R), jnp.int32),
        pltpu.VMEM((B, 2 * DB, 128), BF16),
        pltpu.VMEM((D, 128), BF16),
        pltpu.VMEM((D, R), BF16),
        pltpu.VMEM((L, D, 3 * HC), BF16),
        pltpu.VMEM((L, D, HC), BF16),
        pltpu.VMEM((L, D, FU), BF16),
        pltpu.VMEM((L, FU, D), BF16),
        pltpu.VMEM((L, D, T), BF16),
        pltpu.VMEM((L, D, T), BF16),
        pltpu.VMEM((L, D, T), BF16),
        pltpu.VMEM((L, D, 2 * W), BF16),
        pltpu.VMEM((L, FU, T), BF16),
        pltpu.VMEM((L, FU, T), F32),
        pltpu.VMEM((FU, T), BF16),
        pltpu.VMEM((L, HC, 2 * W), BF16),
        pltpu.VMEM((L, HC, T), BF16),
        pltpu.VMEM((L, HC, T), BF16),
        pltpu.VMEM((L, HC, 2 * W), F32),
        pltpu.VMEM((L, HC, 2 * W), BF16),
        pltpu.VMEM((HC, 2 * W), BF16),
        pltpu.VMEM((L, 8 * (HC // HEAD_DIM), 2 * W), F32),
        pltpu.VMEM((3 * HC, T), BF16),
        pltpu.VMEM((T, 128), F32),
        pltpu.VMEM((L + 1, D, R), F32),
        pltpu.VMEM((L, D, R), F32),
        pltpu.VMEM((NC, D, R), F32),
        pltpu.VMEM((NC, D, R), BF16),
        pltpu.VMEM((NC, D, R), BF16),
        pltpu.VMEM((4, NC, D, R), BF16),
        pltpu.VMEM((4, NC, D, R), BF16),
        pltpu.VMEM((D, 128), F32),
        pltpu.VMEM((D, 3 * HC), BF16),
        pltpu.VMEM((D, HC), BF16),
        pltpu.VMEM((D, FU), BF16),
        pltpu.VMEM((FU, D), BF16),
        pltpu.VMEM((L, S + 3, DB, 3 * HC), BF16),
        pltpu.VMEM((L, S + 3, DB, HC), BF16),
        pltpu.VMEM((L, S, G * DB, FU), BF16),
        pltpu.VMEM((L, S, FD, D), BF16),
        pltpu.VMEM((L, DB, FU), BF16),
        pltpu.VMEM((3, DB, 3 * HC), BF16),
        pltpu.VMEM((3, DB, HC), BF16),
        pltpu.VMEM((G * DB, FU), BF16),
        pltpu.VMEM((FD, D), BF16),
        pltpu.VMEM((DB, FU), BF16),
        pltpu.VMEM((B, 2 * DB, 128), BF16),
        pltpu.VMEM((B, 2 * DB, 128), BF16),
        pltpu.VMEM((H, G + 1, DB, 128), F32),
        pltpu.VMEM((B * H, 8, 128), F32),
        dma((B,)),
        dma((B,)),
        dma((B,)),
        dma((B,)),
        dma((4 * L * 8,)),
        dma((4 * L * 8,)),
        dma((4 * L * 2 * NC,)),
        dma((4 * L * 2 * NC,)),
        dma((4 * L * 2 * NC,)),
        dma((4 * L * 2 * NC,)),
        dma((4 * L * 8,)),
        dma((4 * L * 8,)),
        dma((B,)),
        dma((B,)),
        dma((H,)),
        dma((H,)),
        dma((B * H,)),
        dma((B * H,)),
    ]
    outs = (
        jax.ShapeDtypeStruct((8, 128), F32),
        jax.ShapeDtypeStruct((DB, VOCAB + T), F32),
        jax.ShapeDtypeStruct((L, 3, DB, HC), F32),
        jax.ShapeDtypeStruct((L, HC, DB), F32),
        jax.ShapeDtypeStruct((L, DB, S * G * FD), F32),
        jax.ShapeDtypeStruct((L, FD, D), F32),
        jax.ShapeDtypeStruct((2 * L + 1, 2, DB), F32),
    )
    scal, ge, gq, go, gu, gd, gn = pl.pallas_call(
        functools.partial(step_kernel, z),
        out_shape=outs,
        in_specs=[smem, smem] + [vmem] * 9,
        out_specs=[vmem] * 7,
        scratch_shapes=scratch,
        compiler_params=pltpu.CompilerParams(
            collective_id=0, has_side_effects=True, vmem_limit_bytes=62 << 20
        ),
        name="train_step",
    )(
        lengths,
        family_weight,
        token_ids,
        targets,
        masked,
        embed_table.T,
        w_qkv.transpose(0, 2, 1, 3),
        w_out,
        w_up,
        w_down,
        norm_params,
    )
    return scal[0], (ge.T, gq.transpose(0, 2, 1, 3), go, gu, gd, gn)


def local(
    token_ids,
    targets,
    masked,
    lengths,
    family_weight,
    embed_table,
    w_qkv,
    w_out,
    w_up,
    w_down,
    norm_params,
    embed_first,
    qkv_first,
    out_first,
    up_first,
    down_first,
    norm_first,
    embed_second,
    qkv_second,
    out_second,
    up_second,
    down_second,
    norm_second,
):
    z = Sizes(
        lax.axis_size("blk"),
        lax.axis_size("head"),
        token_ids.shape[0],
        token_ids.shape[1],
        w_qkv.shape,
        w_up.shape,
        w_down.shape,
    )
    masters = (embed_table, w_qkv, w_out, w_up, w_down, norm_params)
    firsts = (embed_first, qkv_first, out_first, up_first, down_first, norm_first)
    seconds = (embed_second, qkv_second, out_second, up_second, down_second, norm_second)
    tokens = (token_ids, targets, masked, lengths, family_weight)
    if z.fused(token_ids.shape[1]):
        scal, grads = fused_step(z, *tokens, *masters)
        loss_sum, weight_sum, grad_norm = (scal[0], scal[2 + 3 * LAYERS], scal[1])
        stream_rms = scal[2 : 2 + 3 * LAYERS].reshape(LAYERS, 3)
    else:
        loss_sum, weight_sum, grad_norm, squares, grads = plain_step(*tokens, *masters)
        stream_rms = jnp.sqrt(
            squares.reshape(LAYERS, 3) / (jnp.sum(lengths).astype(jnp.float32) * D)
        )
    factor = CLIP_NORM / jnp.maximum(grad_norm, CLIP_NORM)
    results = [loss_sum, weight_sum, grad_norm, stream_rms]
    for group_idx in range(6):
        first, second, weight = adamw_update(
            masters[group_idx],
            firsts[group_idx],
            seconds[group_idx],
            grads[group_idx] * factor,
            RATES[group_idx],
            DECAYS[group_idx],
        )
        results += [first, second, weight, weight.astype(jnp.bfloat16)]
    return tuple(results)


def solution(mesh):
    return jax.shard_map(
        local,
        mesh=mesh,
        in_specs=(
            P(None, "blk"),
            P(None, "blk"),
            P(None, "blk"),
            P(),
            P(),
            P(None, "blk"),
            P(None, "blk", None, "head"),
            P(None, "head", "blk"),
            P(None, "blk", "head"),
            P(None, ("head", "blk"), None),
            P(None, None, "blk"),
            P(None, "blk"),
            P(None, "blk", None, "head"),
            P(None, "head", "blk"),
            P(None, "blk", "head"),
            P(None, ("head", "blk"), None),
            P(None, None, "blk"),
            P(None, "blk"),
            P(None, "blk", None, "head"),
            P(None, "head", "blk"),
            P(None, "blk", "head"),
            P(None, ("head", "blk"), None),
            P(None, None, "blk"),
        ),
        out_specs=(
            P(),
            P(),
            P(),
            P(),
            P(None, "blk"),
            P(None, "blk"),
            P(None, "blk"),
            P(None, "blk"),
            P(None, "blk", None, "head"),
            P(None, "blk", None, "head"),
            P(None, "blk", None, "head"),
            P(None, "blk", None, "head"),
            P(None, "head", "blk"),
            P(None, "head", "blk"),
            P(None, "head", "blk"),
            P(None, "head", "blk"),
            P(None, "blk", "head"),
            P(None, "blk", "head"),
            P(None, "blk", "head"),
            P(None, "blk", "head"),
            P(None, ("head", "blk"), None),
            P(None, ("head", "blk"), None),
            P(None, ("head", "blk"), None),
            P(None, ("head", "blk"), None),
            P(None, None, "blk"),
            P(None, None, "blk"),
            P(None, None, "blk"),
            P(None, None, "blk"),
        ),
        check_vma=False,
    )
```

```python
import functools

import jax
import jax.numpy as jnp
from jax import lax
from jax.experimental import pallas as pl
from jax.experimental.pallas import tpu as pltpu
from jax.sharding import PartitionSpec as P

VOCAB = 25
D = 640
HEAD_DIM = 32
LAYERS = 2
STEP = 10


NEGATIVE = -1e30
NORM_EPS = 1e-05
CLIP_NORM = 0.01
BETA_FIRST = 0.9
BETA_SECOND = 0.999
ADAM_EPS = 1e-08
RATES = (0.2, 0.1, 0.5, 0.1, 0.03, 0.5)
DECAYS = (0.1, 0.1, 0.1, 0.1, 0.1, 0.0)
HIGHEST = lax.Precision.HIGHEST


def layer_norm(inputs, gain_row, shift_row):
    centred = inputs - jnp.mean(inputs, axis=-1, keepdims=True)
    spread = jnp.mean(centred * centred, axis=-1, keepdims=True)
    return centred * lax.rsqrt(spread + NORM_EPS) * gain_row + shift_row


def gelu_exact(inputs):
    return jax.nn.gelu(inputs, approximate=False)


def adamw_update(weight, first, second, gradient, rate, decay):
    first = BETA_FIRST * first + (1.0 - BETA_FIRST) * gradient
    second = BETA_SECOND * second + (1.0 - BETA_SECOND) * gradient * gradient
    first_hat = first / (1.0 - BETA_FIRST**STEP)
    second_hat = second / (1.0 - BETA_SECOND**STEP)
    weight = weight - rate * (first_hat / (jnp.sqrt(second_hat) + ADAM_EPS) + decay * weight)
    return (first, second, weight)


def slice_head(tensor, head_index):
    return lax.dynamic_slice_in_dim(tensor, head_index * HEAD_DIM, HEAD_DIM, tensor.ndim - 1)


def join_heads(stacked):
    moved = jnp.moveaxis(stacked, 0, 2)
    return moved.reshape(moved.shape[0], moved.shape[1], -1)


def spread_rows(normed):
    return lax.all_gather(normed, "head", axis=0, tiled=True)


def spread_grads(grad_rows):
    return lax.all_gather(grad_rows, "head", axis=0, tiled=True)


def sum_rows(full_rows, weight, row_share):

    def row_term(row_start, row_count):
        return jnp.dot(full_rows, weight, preferred_element_type=jnp.float32)

    return lax.psum_scatter(
        row_term(jnp.int32(0), row_share * lax.axis_size("head")),
        "head",
        scatter_dimension=0,
        tiled=True,
    )


def sum_grads(full_rows, weight, row_share):

    def row_term(row_start, row_count):
        return jnp.einsum("nc,dc->nd", full_rows, weight, preferred_element_type=jnp.float32)

    return lax.psum_scatter(
        row_term(jnp.int32(0), row_share * lax.axis_size("head")).astype(jnp.bfloat16),
        "head",
        scatter_dimension=0,
        tiled=True,
    ).astype(jnp.float32)


def attend(queries, keys_all, values_all, live_keys):
    local_heads = queries.shape[-1] // HEAD_DIM
    score_scale = HEAD_DIM ** (-0.5)
    live_mask = live_keys[:, None, :]

    def one_head(head_index):
        scores = (
            jnp.einsum(
                "ste,sje->stj",
                slice_head(queries, head_index),
                slice_head(keys_all, head_index),
                preferred_element_type=jnp.float32,
            )
            * score_scale
        )
        masked_scores = jnp.where(live_mask, scores, NEGATIVE)
        row_peak = jnp.max(masked_scores, axis=-1, keepdims=True)
        exp_scores = jnp.exp(masked_scores - row_peak)
        row_total = jnp.sum(exp_scores, axis=-1, keepdims=True)
        attn_probs = (exp_scores / row_total).astype(jnp.bfloat16)
        attended = jnp.einsum(
            "stj,sje->ste",
            attn_probs,
            slice_head(values_all, head_index),
            preferred_element_type=jnp.float32,
        )
        return (attended, (row_peak + jnp.log(row_total))[..., 0])

    outputs, log_totals = lax.map(one_head, jnp.arange(local_heads))
    return (join_heads(outputs), log_totals)


def attend_back(queries, keys_all, values_all, grad_heads, log_totals, live_keys):
    local_heads = queries.shape[-1] // HEAD_DIM
    score_scale = HEAD_DIM ** (-0.5)
    live_mask = live_keys[:, None, :]

    def one_head(head_index):
        query_h = slice_head(queries, head_index)
        key_h = slice_head(keys_all, head_index)
        grad_h = slice_head(grad_heads, head_index)
        scores = (
            jnp.einsum("ste,sje->stj", query_h, key_h, preferred_element_type=jnp.float32)
            * score_scale
        )
        masked_scores = jnp.where(live_mask, scores, NEGATIVE)
        attn_probs = jnp.exp(masked_scores - log_totals[head_index][..., None])
        grad_probs = jnp.einsum(
            "ste,sje->stj",
            grad_h,
            slice_head(values_all, head_index),
            preferred_element_type=jnp.float32,
        )
        row_delta = jnp.sum(attn_probs * grad_probs, axis=-1)
        grad_scores = (attn_probs * (grad_probs - row_delta[..., None])).astype(jnp.bfloat16)
        grad_query = (
            jnp.einsum("stj,sje->ste", grad_scores, key_h, preferred_element_type=jnp.float32)
            * score_scale
        )
        grad_key = (
            jnp.einsum("stj,ste->sje", grad_scores, query_h, preferred_element_type=jnp.float32)
            * score_scale
        )
        grad_value = jnp.einsum(
            "stj,ste->sje",
            attn_probs.astype(jnp.bfloat16),
            grad_h,
            preferred_element_type=jnp.float32,
        )
        return (grad_query, grad_key, grad_value)

    grad_query, grad_key, grad_value = lax.map(one_head, jnp.arange(local_heads))
    grad_key, grad_value = (
        lax.psum_scatter(grad_key, "blk", scatter_dimension=2, tiled=True),
        lax.psum_scatter(grad_value, "blk", scatter_dimension=2, tiled=True),
    )
    return (join_heads(grad_query), join_heads(grad_key), join_heads(grad_value))


def layer_forward(stream, layer_weights, norm_rows, live_keys, row_share):
    w_qkv, w_out, w_up, w_down = layer_weights
    seq_count = live_keys.shape[0]
    normed = layer_norm(stream, norm_rows[0, 0], norm_rows[0, 1]).astype(jnp.bfloat16)
    normed_all = spread_rows(normed)
    packed = jnp.dot(
        normed_all, w_qkv.reshape(w_qkv.shape[0], -1), preferred_element_type=jnp.float32
    ).astype(jnp.bfloat16)
    packed = packed.reshape(seq_count, -1, 3, w_qkv.shape[-1])
    queries, keys_local, values_local = (packed[:, :, 0], packed[:, :, 1], packed[:, :, 2])
    keys_all, values_all = (
        lax.all_gather(keys_local, "blk", axis=1, tiled=True),
        lax.all_gather(values_local, "blk", axis=1, tiled=True),
    )
    attended, log_totals = attend(queries, keys_all, values_all, live_keys)
    attended = attended.astype(jnp.bfloat16).reshape(-1, attended.shape[-1])
    attn_out = sum_rows(attended, w_out, row_share)
    middle = stream + attn_out
    normed_two = layer_norm(middle, norm_rows[1, 0], norm_rows[1, 1]).astype(jnp.bfloat16)
    normed_two_all = spread_rows(normed_two)
    hidden_pre = jnp.dot(normed_two_all, w_up, preferred_element_type=jnp.float32)
    hidden_act = gelu_exact(hidden_pre).astype(jnp.bfloat16)
    ffn_out = sum_rows(hidden_act, w_down, row_share)
    kept = (
        stream,
        middle,
        normed_all,
        queries,
        keys_local,
        values_local,
        keys_all,
        values_all,
        log_totals,
        attended,
        normed_two_all,
        hidden_pre,
    )
    return (middle + ffn_out, attn_out, ffn_out, kept)


def layer_backward(grad_stream, kept, layer_weights, norm_rows, live_keys, row_share):
    (
        stream,
        middle,
        normed_all,
        queries,
        keys_local,
        values_local,
        keys_all,
        values_all,
        log_totals,
        attended,
        normed_two_all,
        hidden_pre,
    ) = kept
    w_qkv, w_out, w_up, w_down = layer_weights
    grad_ffn = spread_grads(grad_stream.astype(jnp.bfloat16))
    hidden_act, gelu_back = jax.vjp(gelu_exact, hidden_pre)
    grad_down = jnp.einsum(
        "nf,nd->fd", hidden_act.astype(jnp.bfloat16), grad_ffn, preferred_element_type=jnp.float32
    )
    grad_act = jnp.einsum("nd,fd->nf", grad_ffn, w_down, preferred_element_type=jnp.float32)
    (grad_pre,) = gelu_back(grad_act)
    grad_pre = grad_pre.astype(jnp.bfloat16)
    grad_up = jnp.einsum("nd,nf->df", normed_two_all, grad_pre, preferred_element_type=jnp.float32)
    grad_normed_two = sum_grads(grad_pre, w_up, row_share)
    _, norm_back_two = jax.vjp(layer_norm, middle, norm_rows[1, 0], norm_rows[1, 1])
    grad_mid, gain_two, shift_two = norm_back_two(grad_normed_two)
    grad_middle = grad_stream + grad_mid
    grad_attn = spread_grads(grad_middle.astype(jnp.bfloat16))
    grad_out_w = jnp.einsum("nf,nd->fd", attended, grad_attn, preferred_element_type=jnp.float32)
    grad_heads = (
        jnp.einsum("nd,fd->nf", grad_attn, w_out, preferred_element_type=jnp.float32)
        .astype(jnp.bfloat16)
        .reshape(queries.shape)
    )
    grad_query, grad_key, grad_value = attend_back(
        queries, keys_all, values_all, grad_heads, log_totals, live_keys
    )
    grad_packed = (
        jnp.stack((grad_query, grad_key, grad_value), axis=2)
        .astype(jnp.bfloat16)
        .reshape(normed_all.shape[0], -1)
    )
    grad_qkv = jnp.einsum(
        "nd,nc->dc", normed_all, grad_packed, preferred_element_type=jnp.float32
    ).reshape(w_qkv.shape)
    grad_normed = sum_grads(grad_packed, w_qkv.reshape(w_qkv.shape[0], -1), row_share)
    _, norm_back_one = jax.vjp(layer_norm, stream, norm_rows[0, 0], norm_rows[0, 1])
    grad_input, gain_one, shift_one = norm_back_one(grad_normed)
    norm_grads = jnp.stack((jnp.stack((gain_one, shift_one)), jnp.stack((gain_two, shift_two))))
    return (grad_middle + grad_input, (grad_qkv, grad_out_w, grad_up, grad_down), norm_grads)


def plain_step(
    token_ids,
    targets,
    masked,
    lengths,
    family_weight,
    embed_table,
    w_qkv,
    w_out,
    w_up,
    w_down,
    norm_params,
):
    blk_count = lax.axis_size("blk")
    head_count = lax.axis_size("head")
    seq_count, blk_tokens = token_ids.shape
    row_share = seq_count * blk_tokens // head_count
    row_first = lax.axis_index("head") * row_share
    blk_start = lax.axis_index("blk") * blk_tokens
    table_all, qkv_all, out_all, up_all, down_all, norm_all = (
        lax.all_gather(embed_table.astype(jnp.bfloat16), "blk", axis=1, tiled=True),
        lax.all_gather(w_qkv.astype(jnp.bfloat16), "blk", axis=1, tiled=True),
        lax.all_gather(w_out.astype(jnp.bfloat16), "blk", axis=2, tiled=True),
        lax.all_gather(w_up.astype(jnp.bfloat16), "blk", axis=1, tiled=True),
        lax.all_gather(w_down.astype(jnp.bfloat16), "blk", axis=1, tiled=True),
        lax.all_gather(norm_params.astype(jnp.bfloat16), "blk", axis=2, tiled=True),
    )
    token_table = table_all[:VOCAB]
    place_rows = lax.dynamic_slice_in_dim(table_all, VOCAB + blk_start, blk_tokens, 0)
    norm_rows = norm_all.astype(jnp.float32)
    live_keys = jnp.arange(blk_tokens * blk_count)[None, :] < lengths[:, None]
    positions = blk_start + jnp.arange(blk_tokens)
    live_local = positions[None, :] < lengths[:, None]
    seq_of_row = (row_first + jnp.arange(row_share)) // blk_tokens
    place_of_row = (row_first + jnp.arange(row_share)) % blk_tokens
    seq_hot = (seq_of_row[:, None] == jnp.arange(seq_count)[None, :]).astype(jnp.float32)
    place_hot = place_of_row[:, None] == jnp.arange(blk_tokens)[None, :]
    row_family = jnp.dot(seq_hot, family_weight, precision=HIGHEST)
    row_live = lax.dynamic_slice_in_dim(live_local.reshape(-1), row_first, row_share, 0).astype(
        jnp.float32
    )[:, None]
    row_ids = lax.dynamic_slice_in_dim(token_ids.reshape(-1), row_first, row_share, 0)
    row_targets = lax.dynamic_slice_in_dim(targets.reshape(-1), row_first, row_share, 0)
    row_masked = lax.dynamic_slice_in_dim(masked.reshape(-1), row_first, row_share, 0)
    token_hot = row_ids[:, None] == jnp.arange(VOCAB)[None, :]
    stream = jnp.dot(
        token_hot.astype(jnp.bfloat16), token_table, preferred_element_type=jnp.float32
    ) + jnp.dot(place_hot.astype(jnp.bfloat16), place_rows, preferred_element_type=jnp.float32)
    layer_stats = []
    kept_all = []
    for layer_idx in range(LAYERS):
        layer_weights = (
            qkv_all[layer_idx],
            out_all[layer_idx],
            up_all[layer_idx],
            down_all[layer_idx],
        )
        layer_stats.append(jnp.sum(stream * stream * row_live))
        stream, attn_out, ffn_out, kept = layer_forward(
            stream,
            layer_weights,
            norm_rows[2 * layer_idx : 2 * layer_idx + 2],
            live_keys,
            row_share,
        )
        layer_stats.append(jnp.sum(attn_out * attn_out * row_live))
        layer_stats.append(jnp.sum(ffn_out * ffn_out * row_live))
        kept_all.append(kept)
    final_low = layer_norm(stream, norm_rows[2 * LAYERS, 0], norm_rows[2 * LAYERS, 1]).astype(
        jnp.bfloat16
    )
    logits = jnp.einsum("nd,vd->nv", final_low, token_table, preferred_element_type=jnp.float32)
    shifted = logits - jnp.max(logits, axis=-1, keepdims=True)
    log_probs = shifted - jnp.log(jnp.sum(jnp.exp(shifted), axis=-1, keepdims=True))
    target_hot = (row_targets[:, None] == jnp.arange(VOCAB)[None, :]).astype(jnp.float32)
    token_loss = -jnp.sum(target_hot * log_probs, axis=1)
    token_weight = row_masked.astype(jnp.float32) * row_family
    loss_sum, weight_sum, squares = lax.psum(
        (jnp.sum(token_weight * token_loss), jnp.sum(token_weight), jnp.stack(layer_stats)),
        ("blk", "head"),
    )
    grad_logits = ((token_weight / weight_sum)[:, None] * (jnp.exp(log_probs) - target_hot)).astype(
        jnp.bfloat16
    )
    grad_final = jnp.einsum(
        "nv,vd->nd", grad_logits, token_table, preferred_element_type=jnp.float32
    )
    grad_table = jnp.einsum("nv,nd->vd", grad_logits, final_low, preferred_element_type=jnp.float32)
    _, final_back = jax.vjp(layer_norm, stream, norm_rows[2 * LAYERS, 0], norm_rows[2 * LAYERS, 1])
    grad_stream, gain_last, shift_last = final_back(grad_final)
    layer_grads = []
    norm_grads = []
    for layer_idx in reversed(range(LAYERS)):
        layer_weights = (
            qkv_all[layer_idx],
            out_all[layer_idx],
            up_all[layer_idx],
            down_all[layer_idx],
        )
        grad_stream, grads_now, norms_now = layer_backward(
            grad_stream,
            kept_all[layer_idx],
            layer_weights,
            norm_rows[2 * layer_idx : 2 * layer_idx + 2],
            live_keys,
            row_share,
        )
        layer_grads.insert(0, grads_now)
        norm_grads.insert(0, norms_now)
    grad_table = grad_table + jnp.dot(
        token_hot.astype(jnp.float32).T, grad_stream, precision=HIGHEST
    )
    grad_place = jnp.dot(place_hot.astype(jnp.float32).T, grad_stream, precision=HIGHEST)
    grad_norms = jnp.concatenate(norm_grads + [jnp.stack((gain_last, shift_last))[None]], axis=0)
    stacked = [
        jnp.stack([layer_entry[slot_idx] for layer_entry in layer_grads]) for slot_idx in range(4)
    ]
    table_sum, place_sum, norm_sum = (
        lax.psum(grad_table.astype(jnp.bfloat16), "head").astype(jnp.float32),
        lax.psum(grad_place.astype(jnp.bfloat16), "head").astype(jnp.float32),
        lax.psum(grad_norms.astype(jnp.bfloat16), "head").astype(jnp.float32),
    )
    place_full = lax.dynamic_update_slice_in_dim(
        jnp.zeros((blk_tokens * blk_count, place_sum.shape[1]), jnp.float32),
        place_sum,
        blk_start,
        0,
    )
    full_table = jnp.concatenate((table_sum, place_full), axis=0)
    reduced = (
        lax.psum_scatter(full_table, "blk", scatter_dimension=1, tiled=True),
        lax.psum_scatter(stacked[0], "blk", scatter_dimension=1, tiled=True),
        lax.psum_scatter(stacked[1], "blk", scatter_dimension=2, tiled=True),
        lax.psum_scatter(stacked[2], "blk", scatter_dimension=1, tiled=True),
        lax.psum_scatter(stacked[3], "blk", scatter_dimension=1, tiled=True),
        lax.psum_scatter(norm_sum, "blk", scatter_dimension=2, tiled=True),
    )
    sharded_squares = sum((jnp.sum(grad_part * grad_part) for grad_part in reduced[1:5]))
    shared_squares = (
        jnp.sum(reduced[0] * reduced[0]) + jnp.sum(reduced[5] * reduced[5])
    ) / head_count
    grad_norm = jnp.sqrt(lax.psum(sharded_squares + shared_squares, ("blk", "head")))
    return loss_sum, weight_sum, grad_norm, squares, reduced


BF16 = jnp.bfloat16
F32 = jnp.float32
MESH = pl.DeviceIdType.MESH
LOG2E = 1.4426950408889634
NORM_LANE = 32


def dot(left, right, left_dim, right_dim):
    return lax.dot_general(
        left, right, (((left_dim,), (right_dim,)), ((), ())), preferred_element_type=F32
    )


class Sizes:
    def __init__(self, blk, head, seqs, blk_tokens, w_qkv, w_up, w_down):
        self.B, self.H, self.S = blk, head, seqs
        self.L = w_qkv[0]
        self.DB = w_qkv[1]
        self.D = self.DB * blk
        self.HC = w_qkv[3]
        self.T = blk_tokens * blk
        self.G = blk // seqs if blk % seqs == 0 else 0
        self.FD = w_down[1]
        if self.G:
            self.NR = self.G * head
            self.R = self.T // self.NR
            self.NC = self.NR // 2
            self.FU = w_up[2] // self.G

    def fused(self, blk_tokens):
        if self.G != 2 or self.S != 4 or self.H % 2 or self.R != blk_tokens or self.R != 128:
            return False
        if self.FU != self.FD * self.S or 3 * self.S > 16 or VOCAB > NORM_LANE:
            return False
        if NORM_LANE + 2 * (2 * self.L + 1) > 128:
            return False
        if any(n % 16 for n in (self.DB, self.HC, self.FD)) or self.D % 128 or self.FU % 128:
            return False
        weights = self.L * 2 * (4 * self.D * self.HC + 2 * self.D * self.FU)
        kept = self.L * self.T * (6 * self.D + 6 * self.FU + 14 * self.HC)
        return 3 * weights + kept + 16 * self.T * self.D + 8 * self.T * 256 * 4 < (60 << 20)


def step_kernel(
    z,
    lens,
    fam,
    tok_in,
    tgt_in,
    msk_in,
    emb_in,
    wq_in,
    wo_in,
    wu_in,
    wd_in,
    norm_in,
    scal_out,
    ge_out,
    gq_out,
    go_out,
    gu_out,
    gd_out,
    gn_out,
    ids,
    wq_own,
    wo_own,
    wu_own,
    wd_own,
    gu_sum,
    idsg,
    tg,
    wq,
    wo,
    wu,
    wd,
    h1,
    h2,
    df,
    da,
    act,
    slope,
    du,
    qt,
    kt,
    vt,
    o32,
    ob,
    dob,
    lse,
    dqkv,
    bias,
    sbuf,
    pbuf,
    xs,
    xm,
    keep,
    psrc,
    csrc,
    srecv,
    rrecv,
    sg,
    stq,
    sto,
    stu,
    std,
    rq,
    ro,
    ru,
    rd,
    rc,
    tq,
    to,
    tu,
    td,
    tc,
    fst,
    frx,
    hrs,
    hrx,
    scg,
    id_s,
    id_r,
    tp_s,
    tp_r,
    w_s,
    w_r,
    ag_s,
    ag_r,
    rs_s,
    rs_r,
    g_s,
    g_r,
    f_s,
    f_r,
    hx_s,
    hx_r,
    sc_s,
    sc_r,
):
    B, H, S, G, L, D, DB, HC, R, NC, NR, FU, FD, T = (
        z.B, z.H, z.S, z.G, z.L, z.D, z.DB, z.HC, z.R, z.NC, z.NR, z.FU, z.FD, z.T,
    )
    N_HEADS = HC // HEAD_DIM
    W = 2 * R
    QT = 2
    scale = HEAD_DIM ** (-0.5)
    c2 = scale * LOG2E
    b = lax.axis_index("blk")
    h = lax.axis_index("head")
    s, g = b // G, b % G
    y, c = h // 2, h % 2
    own_row = g * H + h
    s1 = s + 1 - 2 * (s % 2)
    s2 = (s + 2) % S
    s3 = (s1 + 2) % S

    def dev(blk_i, head_i):
        return (blk_i, head_i)

    sibling = dev(b, y * 2 + 1 - c)

    def peer(k):
        return dev(s * G + (g + k // 2) % G, ((y + k % 2) % 2) * 2 + c)

    waits = []

    def send(src, dst, ssem, rsem, device):
        copy = pltpu.make_async_remote_copy(src, dst, ssem, rsem, device, MESH)
        copy.start()
        return copy

    def arrived(dst, ssem, rsem):
        pltpu.make_async_remote_copy(dst, dst, ssem, rsem, sibling, MESH).wait_recv()

    def over_blk(body):
        def one(k, carry):
            body(lax.rem(b + k, B))
            return carry

        lax.fori_loop(1, B, one, 0)

    def rows(i, n):
        return pl.ds(pl.multiple_of(i * n, 16), n)

    barrier = pltpu.get_barrier_semaphore()

    def greet(k, carry):
        other = lax.rem(b * H + h + k, B * H)
        pl.semaphore_signal(barrier, inc=1, device_id=dev(other // H, other % H), device_id_type=MESH)
        return carry

    lax.fori_loop(1, B * H, greet, 0)

    table = emb_in[...]
    ids[...] = jnp.zeros((16, R), jnp.int32)
    ids[0:S] = tok_in[...]
    ids[S : 2 * S] = tgt_in[...]
    ids[2 * S : 3 * S] = msk_in[...]
    sg[...] = jnp.zeros((D, 128), F32)
    for i in range(2 * L + 1):
        sg[NORM_LANE + 2 * i : NORM_LANE + 2 * i + 2, 0:DB] = norm_in[i]
    lane_small = lax.broadcasted_iota(jnp.int32, (DB, 128), 1)
    token_part = jnp.where(lane_small < VOCAB, table[:, 0:128], sg[0:128, :].T[0:DB]).astype(BF16)
    own_rows = rows(b, DB)
    tg[own_rows, 0:128] = token_part
    tg[own_rows, 128:] = table[:, VOCAB:].astype(BF16)
    pl.semaphore_wait(barrier, B * H - 1)

    def send_ids(other):
        send(ids, idsg.at[b], id_s.at[other], id_r.at[b], dev(other, h))

    over_blk(send_ids)
    idsg[b] = ids[...]

    lanes_in = pl.ds(pl.multiple_of(c * 512, 128), T + 128 - 512)
    lanes_out = pl.ds(pl.multiple_of(c * (T + 128 - 512), 128), 512)
    lanes_back = pl.ds(pl.multiple_of((1 - c) * (T + 128 - 512), 128), 512)

    def t_send(m, at, cut, device):
        block = tg.at[at, cut]
        waits.append(send(block, block, tp_s.at[m], tp_r.at[m], device))

    def t_here(m, at, cut):
        arrived(tg.at[at, cut], tp_s.at[m], tp_r.at[m])

    def plane_rows(plane, column):
        return rows(plane * G + column, DB)

    t_send(0, own_rows, lanes_in, dev(s2 * G + g, h))
    t_send(1, own_rows, lanes_in, dev(s1 * G + g, h))
    t_send(3, own_rows, lanes_in, dev(s * G + 1 - g, h))

    def w_sem(sems, l, kind, m):
        return sems.at[(l * 4 + kind) * 8 + m]

    def w_ref(l, kind, at):
        return (wq, wo, wu, wd)[kind].at[l, at]

    def shard_rows(kind, plane, column=None):
        if kind == 3:
            return rows(plane, FD)
        return rows(plane * G + (g if column is None else column), DB)

    def w_send(l, kind, m, src, at, device):
        waits.append(
            send(src, w_ref(l, kind, at), w_sem(w_s, l, kind, m), w_sem(w_r, l, kind, m), device)
        )

    def w_arrived(l, kind, m, at):
        arrived(w_ref(l, kind, at), w_sem(w_s, l, kind, m), w_sem(w_r, l, kind, m))

    def round_weights(l, kind):
        at = shard_rows(kind, s)
        if kind == 0:
            wq_own[l] = jnp.concatenate([wq_in[l, i] for i in range(3)], axis=1).astype(BF16)
            wq[l, at] = wq_own[l]
        elif kind == 1:
            wo_own[l] = wo_in[l].T.astype(BF16)
            wo[l, at] = wo_own[l]
        elif kind == 2:
            up = wu_in[l]
            for j in range(G):
                parts = [up[:, (i * G + j) * FD : (i * G + j + 1) * FD] for i in range(S)]
                wu_own[l, j] = jnp.concatenate(parts, axis=1).astype(BF16)
            wu[l, at] = wu_own[l, g]
        else:
            wd_own[l] = wd_in[l].astype(BF16)
            wd[l, at] = wd_own[l]

    def plane_block(kind, plane):
        return rows(plane, FD) if kind == 3 else rows(plane, G * DB)

    def send_weights(l, kind):
        round_weights(l, kind)
        at = shard_rows(kind, s)
        if kind == 2:
            w_send(l, 2, 0, wu_own.at[l, 1 - g], at, dev(s * G + 1 - g, h))
            return
        src = (wq_own, wo_own, None, wd_own)[kind].at[l]
        w_send(l, kind, 1, src, at, dev(s2 * G + g, h))
        w_send(l, kind, 2, src, at, dev(s1 * G + g, h))

    def push_weights(l):
        w_arrived(l, 2, 0, shard_rows(2, s, 1 - g))
        at = plane_block(2, s)
        w_send(l, 2, 1, w_ref(l, 2, at), at, dev(s2 * G + g, h))
        w_send(l, 2, 2, w_ref(l, 2, at), at, dev(s1 * G + g, h))

    def relay_weights(l, kind):
        at = shard_rows(kind, s2) if kind < 2 else plane_block(kind, s2)
        w_arrived(l, kind, 1, at)
        w_send(l, kind, 3, w_ref(l, kind, at), at, dev(s1 * G + g, h))

    def cross_weights(l, kind, planes):
        for m, plane, known in ((4, s, True), (5, s2, True), (6, s1, False), (7, s3, False)):
            if m - 4 in planes:
                at = shard_rows(kind, plane)
                if not known:
                    w_arrived(l, kind, m - 4, at)
                w_send(l, kind, m, w_ref(l, kind, at), at, dev(s * G + 1 - g, h))

    def wait_weights(l, kind):
        if kind < 2:
            for m, plane in ((4, s), (5, s2), (6, s1), (7, s3)):
                w_arrived(l, kind, m, shard_rows(kind, plane, 1 - g))
        else:
            w_arrived(l, kind, 2, plane_block(kind, s1))
            w_arrived(l, kind, 3, plane_block(kind, s3))

    for kind in range(2):
        send_weights(0, kind)
        cross_weights(0, kind, (0,))
    at = plane_rows(s2, g)
    t_here(0, at, lanes_in)
    t_send(2, at, lanes_in, dev(s1 * G + g, h))
    t_send(4, at, lanes_in, dev(s * G + 1 - g, h))
    for m, plane in ((1, s1), (2, s3)):
        at = plane_rows(plane, g)
        t_here(m, at, lanes_in)
        t_send(m + 4, at, lanes_in, dev(s * G + 1 - g, h))
    send_weights(0, 2)
    for kind in range(2):
        relay_weights(0, kind)
        cross_weights(0, kind, (1,))
    send_weights(0, 3)
    push_weights(0)

    half_rows = (slice(0, D // 2), slice(D // 2, D))

    def ag_send(use, m, src, dst, device):
        waits.append(send(src, dst, ag_s.at[use * 12 + m], ag_r.at[use * 12 + m], device))

    def ag_here(use, m, dst):
        arrived(dst, ag_s.at[use * 12 + m], ag_r.at[use * 12 + m])

    def block(buf, k, half):
        return buf.at[:, k * W + half * R : k * W + half * R + R]

    def block_half(buf, k, half, i):
        return buf.at[half_rows[i], k * W + half * R : k * W + half * R + R]

    def spread(buf, use):
        ag_send(use, 0, block_half(buf, 0, 0, 0), block_half(buf, 1, 0, 0), peer(1))
        ag_send(use, 1, block_half(buf, 0, 0, 1), block_half(buf, 2, 0, 1), peer(2))
        ag_send(use, 2, block_half(buf, 0, 0, 1), block_half(buf, 1, 0, 1), peer(1))
        ag_send(use, 3, block_half(buf, 0, 0, 0), block_half(buf, 2, 0, 0), peer(2))
        ag_send(use, 4, block(buf, 0, 0), block(buf, 0, 1), sibling)

    def relay_near(buf, use):
        ag_here(use, 0, block_half(buf, 1, 0, 0))
        ag_send(use, 5, block_half(buf, 1, 0, 0), block_half(buf, 3, 0, 0), peer(2))
        ag_here(use, 1, block_half(buf, 2, 0, 1))
        ag_send(use, 6, block_half(buf, 2, 0, 1), block_half(buf, 3, 0, 1), peer(1))
        ag_here(use, 2, block_half(buf, 1, 0, 1))
        ag_send(use, 7, block(buf, 1, 0), block(buf, 1, 1), sibling)
        ag_here(use, 3, block_half(buf, 2, 0, 0))
        ag_send(use, 8, block(buf, 2, 0), block(buf, 2, 1), sibling)

    def relay_far(buf, use):
        for i in range(2):
            ag_here(use, 5 + i, block_half(buf, 3, 0, i))
            ag_send(use, 9 + i, block_half(buf, 3, 0, i), block_half(buf, 3, 1, i), sibling)

    def have(buf, use, k):
        if k == 0:
            ag_here(use, 4, block(buf, 0, 1))
        elif k < 3:
            ag_here(use, 6 + k, block(buf, k, 1))
        else:
            for i in range(2):
                ag_here(use, 9 + i, block_half(buf, 3, 1, i))

    def spread_column(buf, use):
        ag_send(use, 0, block(buf, 0, 0), block(buf, 1, 0), peer(1))
        ag_send(use, 4, block(buf, 0, 0), block(buf, 0, 1), sibling)

    def relay_column(buf, use):
        ag_here(use, 0, block(buf, 1, 0))
        ag_send(use, 7, block(buf, 1, 0), block(buf, 1, 1), sibling)

    staged = {}
    summed_pairs = set()
    half_of = (slice(0, D // 2), slice(D // 2, D))

    def stage(ref, key, value):
        for copy in staged.pop(key, ()):
            copy.wait_send()
        ref[...] = value

    def rs_send(use, m, src, dst, device):
        return [send(src, dst, rs_s.at[use * 12 + m], rs_r.at[use * 12 + m], device)]

    def rs_here(use, m, dst):
        arrived(dst, rs_s.at[use * 12 + m], rs_r.at[use * 12 + m])

    def part(use, k, value):
        keep[k] = value[:, :R]
        stage(psrc.at[k], ("p", k), value[:, R:].astype(BF16))
        staged["p", k] = rs_send(use, k, psrc.at[k], srecv.at[use % 4, k], sibling)

    def pair_sum(use, k, at=slice(0, D)):
        if (use, k) not in summed_pairs:
            summed_pairs.add((use, k))
            rs_here(use, k, srecv.at[use % 4, k])
        return keep[k, at] + srecv[use % 4, k, at].astype(F32)

    def pass_half(use, m, k, i, value, slot, device):
        stage(csrc.at[k, half_of[i]], ("c", k, i), value.astype(BF16))
        staged["c", k, i] = rs_send(
            use, m, csrc.at[k, half_of[i]], rrecv.at[use % 4, slot, half_of[i]], device
        )

    def pass_across(use):
        pass_half(use, 4, 3, 0, pair_sum(use, 3, half_of[0]), 0, peer(1))
        pass_half(use, 5, 3, 1, pair_sum(use, 3, half_of[1]), 0, peer(2))

    def pass_near(use):
        pass_half(use, 6, 1, 0, pair_sum(use, 1, half_of[0]), 1, peer(1))
        pass_half(use, 7, 2, 1, pair_sum(use, 2, half_of[1]), 2, peer(2))

    def pass_joined(use):
        for i, k in ((0, 2), (1, 1)):
            rs_here(use, 4 + i, rrecv.at[use % 4, 0, half_of[i]])
            value = pair_sum(use, k, half_of[i]) + rrecv[use % 4, 0, half_of[i]].astype(F32)
            pass_half(use, 8 + i, k, i, value, k, peer(k))

    def total(use):
        out = pair_sum(use, 0)
        for m, k, i in ((6, 1, 0), (7, 2, 1), (8, 2, 0), (9, 1, 1)):
            rs_here(use, m, rrecv.at[use % 4, k, half_of[i]])
        return out + rrecv[use % 4, 1].astype(F32) + rrecv[use % 4, 2].astype(F32)

    def pass_column(use):
        for i in range(2):
            pass_half(use, 6 + i, 1, i, pair_sum(use, 1, half_of[i]), 1, peer(1))

    def total_column(use):
        out = pair_sum(use, 0)
        for i in range(2):
            rs_here(use, 6 + i, rrecv.at[use % 4, 1, half_of[i]])
        return out + rrecv[use % 4, 1].astype(F32)

    def g_sem(sems, l, kind, m):
        return sems.at[(l * 4 + kind) * 8 + m]

    def g_send(l, kind, m, src, dst, device):
        return send(src, dst, g_sem(g_s, l, kind, m), g_sem(g_r, l, kind, m), device)

    def g_arrived(l, kind, m, dst):
        arrived(dst, g_sem(g_s, l, kind, m), g_sem(g_r, l, kind, m))

    def g_stage(key, ref, value):
        for copy in staged.pop(key, ()):
            copy.wait_send()
        ref[...] = value.astype(BF16)

    def g_first(l, kind, value):
        src, dst = ((stq, rq), (sto, ro), (stu, ru), (std, rd))[kind]
        g_stage(("g", kind), src, value)
        if kind < 2:
            staged["g", kind] = []
            g_cross(l, kind, ((0, s3), (1, s1)))
            return
        n = G * DB if kind == 2 else FD
        dst[l, 0] = src[rows(s, n)]
        staged["g", kind] = [
            g_send(l, kind, i, src.at[rows(plane, n)], dst.at[l, 1 + i], dev(s1 * G + g, h))
            for i, plane in ((1, s3), (0, s1))
        ]

    def g_cross(l, kind, planes):
        src, dst = ((stq, rq), (sto, ro))[kind]
        for m, plane in planes:
            staged["g", kind].append(
                g_send(
                    l, kind, m, src.at[rows(plane * G + 1 - g, DB)], dst.at[l, m], dev(s * G + 1 - g, h)
                )
            )

    def g_column(l, kind, m, plane):
        src, dst = ((stq, rq), (sto, ro))[kind]
        return src[rows(plane * G + g, DB)].astype(F32) + dst[l, m].astype(F32)

    def g_mid(l, kind):
        src, dst, tmp = ((stq, rq, tq), (sto, ro, to))[kind]
        g_arrived(l, kind, 0, dst.at[l, 0])
        g_stage(("m", kind, 1), tmp.at[1], g_column(l, kind, 0, s3))
        one = g_send(l, kind, 5, tmp.at[1], dst.at[l, S + 1], dev(s1 * G + g, h))
        g_arrived(l, kind, 1, dst.at[l, 1])
        g_stage(("m", kind, 0), tmp.at[0], g_column(l, kind, 1, s1))
        two = g_send(l, kind, 4, tmp.at[0], dst.at[l, S], dev(s1 * G + g, h))
        staged["m", kind, 1] = [one]
        staged["m", kind, 0] = [two]

    def g_second(l, kind):
        if kind < 2:
            src, dst, tmp = ((stq, rq, tq), (sto, ro, to))[kind]
            g_arrived(l, kind, 2, dst.at[l, 2])
            g_arrived(l, kind, 5, dst.at[l, S + 1])
            g_stage(("s", kind), tmp.at[2], g_column(l, kind, 2, s2) + dst[l, S + 1].astype(F32))
            staged["s", kind] = [g_send(l, kind, 6, tmp.at[2], dst.at[l, S + 2], dev(s2 * G + g, h))]
            return
        src, dst, tmp, n = ((stu, ru, tu, G * DB), (std, rd, td, FD))[kind - 2]
        g_arrived(l, kind, 1, dst.at[l, 2])
        g_stage(("s", kind), tmp, src[rows(s2, n)].astype(F32) + dst[l, 2].astype(F32))
        staged["s", kind] = [g_send(l, kind, 2, tmp, dst.at[l, 3], dev(s2 * G + g, h))]

    def g_third(l):
        g_arrived(l, 2, 0, ru.at[l, 1])
        g_arrived(l, 2, 2, ru.at[l, 3])

        def summed(column):
            at = rows(column, DB)
            return sum(ru[l, i, at, :].astype(F32) for i in (0, 1, 3))

        g_stage(("t", 2), tc, summed(1 - g))
        staged["t", 2] = [g_send(l, 2, 3, tc, rc.at[l], dev(s * G + 1 - g, h))]
        gu_sum[g] = summed(g)

    def lanes_of(v):
        folded = jnp.sum(v * v, axis=0, keepdims=True)
        return jnp.sum(folded, axis=1, keepdims=True) + jnp.zeros((1, 128), F32)

    def g_final(l, kind):
        if kind < 2:
            dst, out = ((rq, gq_out), (ro, go_out))[kind]
            g_arrived(l, kind, 3, dst.at[l, 3])
            g_arrived(l, kind, 4, dst.at[l, S])
            g_arrived(l, kind, 6, dst.at[l, S + 2])
            value = g_column(l, kind, 3, s) + dst[l, S].astype(F32) + dst[l, S + 2].astype(F32)
            if kind == 0:
                for i in range(3):
                    out[l, i] = value[:, i * HC : (i + 1) * HC]
            else:
                out[l] = value.T
        elif kind == 2:
            g_arrived(l, 2, 3, rc.at[l])
            value = rc[l].astype(F32)
            gu_sum[1 - g] = value
            parts = [gu_sum[j, :, i * FD : (i + 1) * FD] for i in range(S) for j in range(G)]
            gu_out[l] = jnp.concatenate(parts, axis=1)
            return lanes_of(gu_sum[0]) + lanes_of(gu_sum[1])
        else:
            g_arrived(l, 3, 0, rd.at[l, 1])
            g_arrived(l, 3, 2, rd.at[l, 3])
            value = sum(rd[l, i].astype(F32) for i in (0, 1, 3))
            gd_out[l] = value
        return lanes_of(value)

    squares = jnp.zeros((1, 128), F32)

    length = lens[s]
    for k in range(NC):
        for half in range(2):
            core = c if half == 0 else 1 - c
            block_row = ((g + k // 2) % G) * H + ((y + k % 2) % 2) * 2 + core
            place = block_row * R + lax.broadcasted_iota(jnp.int32, (R, 128), 0)
            bias[k * W + half * R : k * W + half * R + R, :] = jnp.where(place < length, 0.0, NEGATIVE)
    lane_place = own_row * R + lax.broadcasted_iota(jnp.int32, (1, R), 1)
    live = jnp.where(lane_place < length, 1.0, 0.0)
    dqkv[0:HC, QT * W :] = jnp.zeros((HC, T - QT * W), BF16)
    sg[...] = jnp.zeros((D, 128), F32)
    lane = lax.broadcasted_iota(jnp.int32, (D, 128), 1)
    row_of = lax.broadcasted_iota(jnp.int32, (128, R), 0)

    def ids_here(other):
        arrived(idsg.at[other], id_s.at[other], id_r.at[other])

    over_blk(ids_here)
    t_here(3, plane_rows(s, 1 - g), lanes_in)
    t_send(7, plane_rows(s, 1 - g), lanes_out, sibling)
    for m, plane in ((4, s2), (5, s1), (6, s3)):
        t_here(m, plane_rows(plane, 1 - g), lanes_in)
        t_send(m + 4, rows(plane, G * DB), lanes_out, sibling)
    t_here(7, plane_rows(s, 1 - g), lanes_back)
    for m, plane in ((8, s2), (9, s1), (10, s3)):
        t_here(m, rows(plane, G * DB), lanes_back)
    etg = tg.at[:, 0:128]
    target_row = idsg[own_row, pl.ds(S + s, 1), :]
    mask_row = idsg[own_row, pl.ds(2 * S + s, 1), :].astype(F32)
    token_weight = mask_row * fam[s]
    weight_sum = jnp.zeros((1, 1), F32)
    for i in range(S):
        counts = jnp.zeros((1, R), F32)
        for j in range(B):
            counts = counts + idsg[j, 2 * S + i : 2 * S + i + 1, :].astype(F32)
        weight_sum = weight_sum + jnp.sum(counts, axis=1, keepdims=True) * fam[i]

    def gain(i):
        return etg[:, NORM_LANE + 2 * i : NORM_LANE + 2 * i + 1].astype(F32)

    def shift(i):
        return etg[:, NORM_LANE + 2 * i + 1 : NORM_LANE + 2 * i + 2].astype(F32)

    def normalize(v):
        centred = v - jnp.mean(v, axis=0, keepdims=True)
        rstd = lax.rsqrt(jnp.mean(centred * centred, axis=0, keepdims=True) + NORM_EPS)
        return centred * rstd, rstd

    def layer_norm_low(v, i):
        hat, _ = normalize(v)
        return (hat * gain(i) + shift(i)).astype(BF16)

    def layer_norm_back(grad, v, i):
        hat, rstd = normalize(v)
        gain_grad = jnp.sum(grad * hat, axis=1, keepdims=True)
        shift_grad = jnp.sum(grad, axis=1, keepdims=True)
        sg[...] += jnp.where(lane == NORM_LANE + 2 * i, gain_grad, 0.0) + jnp.where(
            lane == NORM_LANE + 2 * i + 1, shift_grad, 0.0
        )
        scaled = grad * gain(i)
        mean_one = jnp.mean(scaled, axis=0, keepdims=True)
        mean_two = jnp.mean(scaled * hat, axis=0, keepdims=True)
        return rstd * (scaled - mean_one - hat * mean_two)

    def square_sum(v):
        return jnp.sum(jnp.sum(v * v, axis=0, keepdims=True) * live, axis=1, keepdims=True)

    slots = list(range(NC))
    near = slots[:2]
    stats = []
    for k in slots:
        for half in range(2):
            core = c if half == 0 else 1 - c
            block_row = ((g + k // 2) % G) * H + ((y + k % 2) % 2) * 2 + core
            hot = jnp.where(row_of == idsg[block_row, pl.ds(s, 1), :], 1.0, 0.0).astype(BF16)
            place = tg[:, pl.ds(pl.multiple_of(128 + block_row * R, 128), R)]
            start = dot(etg[...], hot, 1, 0) + place.astype(F32)
            h1[0, :, k * W + half * R : k * W + half * R + R] = layer_norm_low(start, 0)
            if k == 0 and half == 0:
                xs[0] = start
                token_hot = hot

    def cols(k):
        return slice(k * W, (k + 1) * W)

    for l in range(L):
        x = xs[l]
        stats.append(square_sum(x))
        if l:
            h1[l, :, 0:R] = layer_norm_low(x, 2 * l)
            spread(h1.at[l], 3 * l)
        else:
            for kind in range(2):
                cross_weights(0, kind, (2, 3))
        wait_weights(l, 0)

        def project(k):
            if k in near:
                packed = dot(wq[l], h1[l, :, cols(k)], 0, 0).astype(BF16)
                qt[l, :, cols(k)] = packed[0:HC]
                packed = packed[HC:]
            else:
                packed = dot(wq[l, :, :], h1[l, :, cols(k)], 0, 0).astype(BF16)[HC:]
            kt[l, :, cols(k)] = packed[0:HC]
            vt[l, :, cols(k)] = packed[HC:]

        if l:
            have(h1.at[l], 3 * l, 0)
            project(0)
            relay_near(h1.at[l], 3 * l)
            have(h1.at[l], 3 * l, 1)
            project(1)
            relay_far(h1.at[l], 3 * l)
            have(h1.at[l], 3 * l, 2)
            project(2)
            have(h1.at[l], 3 * l, 3)
            project(3)
        else:
            for k in slots:
                project(k)

        tiles = [(q, i) for q in (1, 0) for i in range(N_HEADS)]
        chunk = W
        peaks, norms, outs = {}, {}, {}

        def head_rows(i):
            return slice(i * HEAD_DIM, (i + 1) * HEAD_DIM)

        def score(n, j):
            q, i = tiles[n]
            keys = slice(j * chunk, (j + 1) * chunk)
            scores = dot(kt[l, head_rows(i), keys], qt[l, head_rows(i), cols(q)], 0, 0)
            scores = scores + jnp.concatenate([bias[keys, :]] * 2, axis=1)
            sbuf[n % 2, keys, :] = scores
            peak = jnp.max(scores, axis=0, keepdims=True)
            peaks[n] = jnp.maximum(peaks[n], peak) if j else peak

        def weigh(n, j):
            keys = slice(j * chunk, (j + 1) * chunk)
            exps = jnp.exp2((sbuf[n % 2, keys, :] - peaks[n]) * c2)
            norm = jnp.sum(exps, axis=0, keepdims=True)
            norms[n] = norms[n] + norm if j else norm
            pbuf[n % 2, keys, :] = exps.astype(BF16)

        def gather_values(n, j):
            q, i = tiles[n]
            keys = slice(j * chunk, (j + 1) * chunk)
            out = dot(vt[l, head_rows(i), keys], pbuf[n % 2, keys, :], 1, 0)
            outs[n] = outs[n] + out if j else out

        def attended(n):
            q, i = tiles[n]
            out = outs[n] * (1.0 / norms[n])
            o32[l, head_rows(i), cols(q)] = out
            ob[l, head_rows(i), cols(q)] = out.astype(BF16)
            lse[l, i * 8 : i * 8 + 8, cols(q)] = jnp.broadcast_to(
                peaks[n] * c2 + jnp.log(norms[n]) * LOG2E, (8, W)
            )

        for j in range(T // chunk):
            score(0, j)
        for n in range(len(tiles) + 1):
            for j in range(T // chunk):
                if n + 1 < len(tiles):
                    score(n + 1, j)
                if n:
                    gather_values(n - 1, j)
                if n < len(tiles):
                    weigh(n, j)
            if n:
                attended(n - 1)
            if n == N_HEADS:
                wait_weights(l, 1)
                part(4 * l, 1, dot(wo[l], ob[l, :, cols(1)], 1, 0))
                relay_weights(l, 3)
                relay_weights(l, 2)
                if l + 1 < L:
                    for kind in range(3):
                        send_weights(l + 1, kind)
            if n == N_HEADS + 2:
                pass_column(4 * l)
        part(4 * l, 0, dot(wo[l], ob[l, :, cols(0)], 1, 0))
        attn_out = total_column(4 * l)
        stats.append(square_sum(attn_out))
        middle = xs[l] + attn_out
        xm[l] = middle
        h2[l, :, 0:R] = layer_norm_low(middle, 2 * l + 1)
        spread(h2.at[l], 3 * l + 1)
        wait_weights(l, 2)
        wait_weights(l, 3)

        def feed(k):
            pre = dot(wu[l], h2[l, :, cols(k)], 0, 0)
            cdf = 0.5 * (1.0 + lax.erf(pre * (0.5**0.5)))
            low = (pre * cdf).astype(BF16)
            act[l, :, cols(k)] = low
            slope[l, :, cols(k)] = cdf + pre * (jnp.exp(-0.5 * pre * pre) * 0.3989422804014327)
            part(4 * l + 1, k, dot(wd[l], low, 0, 0))

        have(h2.at[l], 3 * l + 1, 0)
        feed(0)
        relay_near(h2.at[l], 3 * l + 1)
        have(h2.at[l], 3 * l + 1, 1)
        feed(1)
        if l + 1 < L:
            for kind in range(2):
                relay_weights(l + 1, kind)
                cross_weights(l + 1, kind, (0, 1))
            send_weights(l + 1, 3)
            push_weights(l + 1)
        relay_far(h2.at[l], 3 * l + 1)
        have(h2.at[l], 3 * l + 1, 2)
        feed(2)
        pass_near(4 * l + 1)
        have(h2.at[l], 3 * l + 1, 3)
        feed(3)
        pass_across(4 * l + 1)
        pass_joined(4 * l + 1)
        if l + 1 < L:
            for kind in range(2):
                cross_weights(l + 1, kind, (2, 3))
        ffn_out = total(4 * l + 1)
        stats.append(square_sum(ffn_out))
        xs[l + 1] = xm[l] + ffn_out

    last = xs[L]
    final_low = layer_norm_low(last, 2 * L)
    logits = dot(etg[...], final_low, 0, 0)[0:NORM_LANE]
    vocab_row = row_of[0:NORM_LANE]
    logits = jnp.where(vocab_row < VOCAB, logits, NEGATIVE)
    shifted = logits - jnp.max(logits, axis=0, keepdims=True)
    log_probs = shifted - jnp.log(jnp.sum(jnp.exp(shifted), axis=0, keepdims=True))
    target_hot = jnp.where(vocab_row == target_row, 1.0, 0.0)
    token_loss = -jnp.sum(target_hot * log_probs, axis=0, keepdims=True)
    loss = jnp.sum(token_weight * token_loss, axis=1, keepdims=True)
    grad_logits = ((token_weight / weight_sum) * (jnp.exp(log_probs) - target_hot)).astype(BF16)
    grad_logits = jnp.concatenate([grad_logits, jnp.zeros((128 - NORM_LANE, R), BF16)], axis=0)
    grad_final = dot(etg[...], grad_logits, 1, 0)
    sg[...] += dot(final_low, grad_logits, 1, 1)
    grad = layer_norm_back(grad_final, last, 2 * L)

    for l in reversed(range(L)):
        df[l, :, 0:R] = grad.astype(BF16)
        xs[l + 1] = grad
        spread(df.at[l], 3 * l + 2)

        def feed_back(k):
            grad_act = dot(wd[l], df[l, :, cols(k)], 1, 0)
            low = (grad_act * slope[l, :, cols(k)]).astype(BF16)
            du[:, cols(k)] = low
            part(4 * l + 2, k, dot(wu[l], low, 1, 0))

        have(df.at[l], 3 * l + 2, 0)
        feed_back(0)
        relay_near(df.at[l], 3 * l + 2)
        if l + 1 < L:
            for kind in range(2):
                g_cross(l + 1, kind, ((2, s2), (3, s)))
        have(df.at[l], 3 * l + 2, 1)
        feed_back(1)
        relay_far(df.at[l], 3 * l + 2)
        have(df.at[l], 3 * l + 2, 2)
        feed_back(2)
        pass_near(4 * l + 2)
        if l + 1 < L:
            g_mid(l + 1, 0)
            g_mid(l + 1, 1)
            g_third(l + 1)
        have(df.at[l], 3 * l + 2, 3)
        feed_back(3)
        pass_across(4 * l + 2)
        g_first(l, 3, dot(act[l], df[l], 1, 1))
        pass_joined(4 * l + 2)
        if l + 1 < L:
            g_second(l + 1, 0)
            g_second(l + 1, 1)
        g_first(l, 2, dot(h2[l], du[...], 1, 1))
        grad_middle = xs[l + 1] + layer_norm_back(total(4 * l + 2), xm[l], 2 * l + 1)
        xm[l] = grad_middle

        da[l, :, 0:R] = grad_middle.astype(BF16)
        spread_column(da.at[l], 3 * L + l)
        if l + 1 < L:
            for kind in range(4):
                squares = squares + g_final(l + 1, kind)

        def out_back(k):
            dob[:, cols(k)] = dot(wo[l], da[l, :, cols(k)], 0, 0).astype(BF16)

        have(da.at[l], 3 * L + l, 0)
        out_back(0)
        relay_column(da.at[l], 3 * L + l)
        have(da.at[l], 3 * L + l, 1)
        out_back(1)

        steps = [(i, q, j) for i in range(N_HEADS) for q in range(QT) for j in range(T // chunk)]
        grad_q, grad_k, grad_v = {}, {}, {}

        def back_scores(n):
            i, q, j = steps[n]
            keys = slice(j * chunk, (j + 1) * chunk)
            sbuf[n % 2, 0:chunk, :] = dot(kt[l, head_rows(i), keys], qt[l, head_rows(i), cols(q)], 0, 0)
            sbuf[n % 2, chunk : 2 * chunk, :] = dot(vt[l, head_rows(i), keys], dob[head_rows(i), cols(q)], 0, 0)

        def back_weigh(n):
            i, q, j = steps[n]
            keys = slice(j * chunk, (j + 1) * chunk)
            delta = jnp.sum(
                dob[head_rows(i), cols(q)].astype(F32) * o32[l, head_rows(i), cols(q)],
                axis=0,
                keepdims=True,
            )
            scores = sbuf[n % 2, 0:chunk, :] + jnp.concatenate([bias[keys, :]] * 2, axis=1)
            probs = jnp.exp2(scores * c2 - lse[l, i * 8 : i * 8 + 1, cols(q)])
            pbuf[n % 2, 0:chunk, :] = probs.astype(BF16)
            pbuf[n % 2, chunk : 2 * chunk, :] = (probs * (sbuf[n % 2, chunk : 2 * chunk, :] - delta)).astype(BF16)

        def back_products(n):
            i, q, j = steps[n]
            keys = slice(j * chunk, (j + 1) * chunk)
            probs = pbuf[n % 2, 0:chunk, :]
            grad_scores = pbuf[n % 2, chunk : 2 * chunk, :]
            term = dot(kt[l, head_rows(i), keys], grad_scores, 1, 0)
            grad_q[i, q] = grad_q[i, q] + term if j else term
            term_k = dot(qt[l, head_rows(i), cols(q)], grad_scores, 1, 1)
            term_v = dot(dob[head_rows(i), cols(q)], probs, 1, 1)
            grad_k[i, j] = grad_k[i, j] + term_k if q else term_k
            grad_v[i, j] = grad_v[i, j] + term_v if q else term_v
            if j == T // chunk - 1:
                dqkv[head_rows(i), cols(q)] = (grad_q[i, q] * scale).astype(BF16)
            if q == QT - 1:
                first = HC + i * HEAD_DIM
                dqkv[first : first + HEAD_DIM, keys] = (grad_k[i, j] * scale).astype(BF16)
                first = 2 * HC + i * HEAD_DIM
                dqkv[first : first + HEAD_DIM, keys] = grad_v[i, j].astype(BF16)

        back_scores(0)
        for n in range(len(steps) + 1):
            if n + 1 < len(steps):
                back_scores(n + 1)
            if n:
                back_products(n - 1)
            if n < len(steps):
                back_weigh(n)
            if n == len(steps) // 2:
                g_second(l, 3)
        def project_back(k):
            part(4 * l + 3, k, dot(wq[l], dqkv[:, cols(k)], 1, 0))

        project_back(3)
        project_back(1)
        pass_across(4 * l + 3)
        project_back(2)
        pass_near(4 * l + 3)
        project_back(0)
        g_second(l, 2)
        g_first(l, 0, dot(h1[l], dqkv[...], 1, 1))
        pass_joined(4 * l + 3)
        g_first(l, 1, dot(da[l], ob[l], 1, 1))
        if l == 0:
            for kind in range(2):
                g_cross(0, kind, ((2, s2), (3, s)))
        grad = xm[l] + layer_norm_back(total(4 * l + 3), xs[l], 2 * l)

    high = grad.astype(BF16)
    low = (grad - high.astype(F32)).astype(BF16)
    small = sg[...] + dot(high, token_hot, 1, 1) + dot(low, token_hot, 1, 1)
    small = small.astype(BF16)
    for i in range(B):
        fst[i, :DB] = small[i * DB : (i + 1) * DB]
        fst[i, DB:] = high[i * DB : (i + 1) * DB]

    def send_table(other):
        send(fst.at[other], frx.at[b], f_s.at[other], f_r.at[b], dev(other, h))

    over_blk(send_table)
    frx[b] = fst[b]

    g_mid(0, 0)
    g_mid(0, 1)
    g_third(0)
    squares = squares + g_final(0, 3)
    g_second(0, 0)
    g_second(0, 1)
    squares = squares + g_final(0, 2)
    def table_here(other):
        arrived(frx.at[other], f_s.at[other], f_r.at[other])

    over_blk(table_here)
    value = frx[0, :DB].astype(F32)
    for i in range(1, B):
        value = value + frx[i, :DB].astype(F32)
    hrs[h] = value

    def send_small(k, carry):
        other = lax.rem(h + k, H)
        send(hrs.at[h], hrs.at[h], hx_s.at[other], hx_r.at[h], dev(b, other))
        return carry

    lax.fori_loop(1, H, send_small, 0)
    for j in range(G):
        value = frx[j, DB:].astype(F32)
        for i in range(1, S):
            value = value + frx[i * G + j, DB:].astype(F32)
        hrx[h, j] = value
        squares = squares + lanes_of(value)

    def send_places(k, carry):
        other = lax.rem(h + k, H)
        send(hrx.at[h], hrx.at[h], hx_s.at[H + other], hx_r.at[H + h], dev(b, other))
        return carry

    lax.fori_loop(1, H, send_places, 0)

    def small_here(k, carry):
        other = lax.rem(h + k, H)
        arrived(hrs.at[other], hx_s.at[other], hx_r.at[other])
        return carry

    def places_here(k, carry):
        other = lax.rem(h + k, H)
        arrived(hrx.at[other], hx_s.at[H + other], hx_r.at[H + other])
        return carry

    for kind in (0, 1):
        squares = squares + g_final(0, kind)
    lax.fori_loop(1, H, small_here, 0)
    value = hrs[0]
    for i in range(1, H):
        value = value + hrs[i]
    squares = squares + lanes_of(value) * (1.0 / H)
    small_sum = value

    lane_one = lax.broadcasted_iota(jnp.int32, (1, 128), 1)
    packed = jnp.where(lane_one == 0, loss, 0.0) + jnp.where(lane_one == 1, squares, 0.0)
    for i, stat in enumerate(stats):
        packed = packed + jnp.where(lane_one == 2 + i, stat, 0.0)
    me = b * H + h
    scg[me] = jnp.broadcast_to(packed, (8, 128))

    def send_scalars(k, carry):
        other = lax.rem(me + k, B * H)
        send(scg.at[me], scg.at[me], sc_s.at[other], sc_r.at[me], dev(other // H, other % H))
        return carry

    lax.fori_loop(1, B * H, send_scalars, 0)
    lax.fori_loop(1, H, places_here, 0)
    ge_out[...] = jnp.concatenate(
        [small_sum[:, :VOCAB]] + [hrx[i, j] for j in range(G) for i in range(H)], axis=1
    )
    norm_rows = small_sum.T
    for i in range(2 * L + 1):
        gn_out[i] = norm_rows[NORM_LANE + 2 * i : NORM_LANE + 2 * i + 2]

    def scalars_here(k, carry):
        other = lax.rem(me + k, B * H)
        arrived(scg.at[other], sc_s.at[other], sc_r.at[other])
        return carry

    lax.fori_loop(1, B * H, scalars_here, 0)
    out = scg[0]
    for i in range(1, B * H):
        out = out + scg[i]
    lane_eight = lax.broadcasted_iota(jnp.int32, (8, 128), 1)
    tokens = lens[0]
    for i in range(1, S):
        tokens = tokens + lens[i]
    roots = jnp.sqrt(jnp.where(lane_eight == 1, out, out / (tokens.astype(F32) * D)))
    out = jnp.where(lane_eight == 0, out, roots)
    scal_out[...] = jnp.where(lane_eight == 2 + 3 * L, weight_sum, out)

    for copy in waits:
        copy.wait_send()
    for copies in staged.values():
        for copy in copies:
            copy.wait_send()

    def sent(other):
        for src, ssem, rsem in ((idsg.at[other], id_s, id_r), (frx.at[other], f_s, f_r)):
            pltpu.make_async_remote_copy(src, src, ssem.at[other], rsem.at[other], sibling, MESH).wait_send()

    over_blk(sent)

    def heads_sent(k, carry):
        other = lax.rem(h + k, H)
        for src, m in ((hrs.at[other], other), (hrx.at[other], H + other)):
            pltpu.make_async_remote_copy(src, src, hx_s.at[m], hx_r.at[m], sibling, MESH).wait_send()
        return carry

    lax.fori_loop(1, H, heads_sent, 0)

    def scalars_sent(k, carry):
        other = lax.rem(me + k, B * H)
        pltpu.make_async_remote_copy(
            scg.at[other], scg.at[other], sc_s.at[other], sc_r.at[other], sibling, MESH
        ).wait_send()
        return carry

    lax.fori_loop(1, B * H, scalars_sent, 0)


def fused_step(z, token_ids, targets, masked, lengths, family_weight, embed_table, w_qkv, w_out, w_up, w_down, norm_params):
    B, H, S, G, L, D, DB, HC, R, NC, NR, FU, FD, T = (
        z.B, z.H, z.S, z.G, z.L, z.D, z.DB, z.HC, z.R, z.NC, z.NR, z.FU, z.FD, z.T,
    )
    W = 2 * R
    smem = pl.BlockSpec(memory_space=pltpu.SMEM)
    vmem = pl.BlockSpec(memory_space=pltpu.VMEM)
    dma = pltpu.SemaphoreType.DMA
    scratch = [
        pltpu.VMEM((16, R), jnp.int32),
        pltpu.VMEM((L, DB, 3 * HC), BF16),
        pltpu.VMEM((L, DB, HC), BF16),
        pltpu.VMEM((L, G, DB, FU), BF16),
        pltpu.VMEM((L, FD, D), BF16),
        pltpu.VMEM((G, DB, FU), F32),
        pltpu.VMEM((B, 16, R), jnp.int32),
        pltpu.VMEM((D, 128 + T), BF16),
        pltpu.VMEM((L, D, 3 * HC), BF16),
        pltpu.VMEM((L, D, HC), BF16),
        pltpu.VMEM((L, D, FU), BF16),
        pltpu.VMEM((L, FU, D), BF16),
        pltpu.VMEM((L, D, T), BF16),
        pltpu.VMEM((L, D, T), BF16),
        pltpu.VMEM((L, D, T), BF16),
        pltpu.VMEM((L, D, 2 * W), BF16),
        pltpu.VMEM((L, FU, T), BF16),
        pltpu.VMEM((L, FU, T), F32),
        pltpu.VMEM((FU, T), BF16),
        pltpu.VMEM((L, HC, 2 * W), BF16),
        pltpu.VMEM((L, HC, T), BF16),
        pltpu.VMEM((L, HC, T), BF16),
        pltpu.VMEM((L, HC, 2 * W), F32),
        pltpu.VMEM((L, HC, 2 * W), BF16),
        pltpu.VMEM((HC, 2 * W), BF16),
        pltpu.VMEM((L, 8 * (HC // HEAD_DIM), 2 * W), F32),
        pltpu.VMEM((3 * HC, T), BF16),
        pltpu.VMEM((T, 128), F32),
        pltpu.VMEM((2, T, W), F32),
        pltpu.VMEM((2, T, W), BF16),
        pltpu.VMEM((L + 1, D, R), F32),
        pltpu.VMEM((L, D, R), F32),
        pltpu.VMEM((NC, D, R), F32),
        pltpu.VMEM((NC, D, R), BF16),
        pltpu.VMEM((NC, D, R), BF16),
        pltpu.VMEM((4, NC, D, R), BF16),
        pltpu.VMEM((4, NC, D, R), BF16),
        pltpu.VMEM((D, 128), F32),
        pltpu.VMEM((D, 3 * HC), BF16),
        pltpu.VMEM((D, HC), BF16),
        pltpu.VMEM((D, FU), BF16),
        pltpu.VMEM((FU, D), BF16),
        pltpu.VMEM((L, S + 3, DB, 3 * HC), BF16),
        pltpu.VMEM((L, S + 3, DB, HC), BF16),
        pltpu.VMEM((L, S, G * DB, FU), BF16),
        pltpu.VMEM((L, S, FD, D), BF16),
        pltpu.VMEM((L, DB, FU), BF16),
        pltpu.VMEM((3, DB, 3 * HC), BF16),
        pltpu.VMEM((3, DB, HC), BF16),
        pltpu.VMEM((G * DB, FU), BF16),
        pltpu.VMEM((FD, D), BF16),
        pltpu.VMEM((DB, FU), BF16),
        pltpu.VMEM((B, 2 * DB, 128), BF16),
        pltpu.VMEM((B, 2 * DB, 128), BF16),
        pltpu.VMEM((H, DB, 128), F32),
        pltpu.VMEM((H, G, DB, 128), F32),
        pltpu.VMEM((B * H, 8, 128), F32),
        dma((B,)),
        dma((B,)),
        dma((16,)),
        dma((16,)),
        dma((4 * L * 8,)),
        dma((4 * L * 8,)),
        dma((4 * L * 12,)),
        dma((4 * L * 12,)),
        dma((4 * L * 12,)),
        dma((4 * L * 12,)),
        dma((4 * L * 8,)),
        dma((4 * L * 8,)),
        dma((B,)),
        dma((B,)),
        dma((2 * H,)),
        dma((2 * H,)),
        dma((B * H,)),
        dma((B * H,)),
    ]
    outs = (
        jax.ShapeDtypeStruct((8, 128), F32),
        jax.ShapeDtypeStruct((DB, VOCAB + T), F32),
        jax.ShapeDtypeStruct((L, 3, DB, HC), F32),
        jax.ShapeDtypeStruct((L, HC, DB), F32),
        jax.ShapeDtypeStruct((L, DB, S * G * FD), F32),
        jax.ShapeDtypeStruct((L, FD, D), F32),
        jax.ShapeDtypeStruct((2 * L + 1, 2, DB), F32),
    )
    scal, ge, gq, go, gu, gd, gn = pl.pallas_call(
        functools.partial(step_kernel, z),
        out_shape=outs,
        in_specs=[smem, smem] + [vmem] * 9,
        out_specs=[vmem] * 7,
        scratch_shapes=scratch,
        compiler_params=pltpu.CompilerParams(
            collective_id=0, has_side_effects=True, vmem_limit_bytes=62 << 20
        ),
        name="train_step",
    )(
        lengths,
        family_weight,
        token_ids,
        targets,
        masked,
        embed_table.T,
        w_qkv.transpose(0, 2, 1, 3),
        w_out,
        w_up,
        w_down,
        norm_params,
    )
    return scal[0], (ge.T, gq.transpose(0, 2, 1, 3), go, gu, gd, gn)


def local(
    token_ids,
    targets,
    masked,
    lengths,
    family_weight,
    embed_table,
    w_qkv,
    w_out,
    w_up,
    w_down,
    norm_params,
    embed_first,
    qkv_first,
    out_first,
    up_first,
    down_first,
    norm_first,
    embed_second,
    qkv_second,
    out_second,
    up_second,
    down_second,
    norm_second,
):
    z = Sizes(
        lax.axis_size("blk"),
        lax.axis_size("head"),
        token_ids.shape[0],
        token_ids.shape[1],
        w_qkv.shape,
        w_up.shape,
        w_down.shape,
    )
    masters = (embed_table, w_qkv, w_out, w_up, w_down, norm_params)
    firsts = (embed_first, qkv_first, out_first, up_first, down_first, norm_first)
    seconds = (embed_second, qkv_second, out_second, up_second, down_second, norm_second)
    tokens = (token_ids, targets, masked, lengths, family_weight)
    if z.fused(token_ids.shape[1]):
        scal, grads = fused_step(z, *tokens, *masters)
        loss_sum, weight_sum, grad_norm = (scal[0], scal[2 + 3 * LAYERS], scal[1])
        stream_rms = scal[2 : 2 + 3 * LAYERS].reshape(LAYERS, 3)
    else:
        loss_sum, weight_sum, grad_norm, squares, grads = plain_step(*tokens, *masters)
        stream_rms = jnp.sqrt(
            squares.reshape(LAYERS, 3) / (jnp.sum(lengths).astype(jnp.float32) * D)
        )
    factor = CLIP_NORM / jnp.maximum(grad_norm, CLIP_NORM)
    results = [loss_sum, weight_sum, grad_norm, stream_rms]
    for group_idx in range(6):
        first, second, weight = adamw_update(
            masters[group_idx],
            firsts[group_idx],
            seconds[group_idx],
            grads[group_idx] * factor,
            RATES[group_idx],
            DECAYS[group_idx],
        )
        results += [first, second, weight, weight.astype(jnp.bfloat16)]
    return tuple(results)


def solution(mesh):
    return jax.shard_map(
        local,
        mesh=mesh,
        in_specs=(
            P(None, "blk"),
            P(None, "blk"),
            P(None, "blk"),
            P(),
            P(),
            P(None, "blk"),
            P(None, "blk", None, "head"),
            P(None, "head", "blk"),
            P(None, "blk", "head"),
            P(None, ("head", "blk"), None),
            P(None, None, "blk"),
            P(None, "blk"),
            P(None, "blk", None, "head"),
            P(None, "head", "blk"),
            P(None, "blk", "head"),
            P(None, ("head", "blk"), None),
            P(None, None, "blk"),
            P(None, "blk"),
            P(None, "blk", None, "head"),
            P(None, "head", "blk"),
            P(None, "blk", "head"),
            P(None, ("head", "blk"), None),
            P(None, None, "blk"),
        ),
        out_specs=(
            P(),
            P(),
            P(),
            P(),
            P(None, "blk"),
            P(None, "blk"),
            P(None, "blk"),
            P(None, "blk"),
            P(None, "blk", None, "head"),
            P(None, "blk", None, "head"),
            P(None, "blk", None, "head"),
            P(None, "blk", None, "head"),
            P(None, "head", "blk"),
            P(None, "head", "blk"),
            P(None, "head", "blk"),
            P(None, "head", "blk"),
            P(None, "blk", "head"),
            P(None, "blk", "head"),
            P(None, "blk", "head"),
            P(None, "blk", "head"),
            P(None, ("head", "blk"), None),
            P(None, ("head", "blk"), None),
            P(None, ("head", "blk"), None),
            P(None, ("head", "blk"), None),
            P(None, None, "blk"),
            P(None, None, "blk"),
            P(None, None, "blk"),
            P(None, None, "blk"),
        ),
        check_vma=False,
    )
```

```python
import functools

import jax
import jax.numpy as jnp
from jax import lax
from jax.experimental import pallas as pl
from jax.experimental.pallas import tpu as pltpu
from jax.sharding import PartitionSpec as P

VOCAB = 25
D = 640
HEAD_DIM = 32
LAYERS = 2
STEP = 10


NEGATIVE = -1e30
NORM_EPS = 1e-05
CLIP_NORM = 0.01
BETA_FIRST = 0.9
BETA_SECOND = 0.999
ADAM_EPS = 1e-08
RATES = (0.2, 0.1, 0.5, 0.1, 0.03, 0.5)
DECAYS = (0.1, 0.1, 0.1, 0.1, 0.1, 0.0)
HIGHEST = lax.Precision.HIGHEST


def layer_norm(inputs, gain_row, shift_row):
    centred = inputs - jnp.mean(inputs, axis=-1, keepdims=True)
    spread = jnp.mean(centred * centred, axis=-1, keepdims=True)
    return centred * lax.rsqrt(spread + NORM_EPS) * gain_row + shift_row


def gelu_exact(inputs):
    return jax.nn.gelu(inputs, approximate=False)


def adamw_update(weight, first, second, gradient, rate, decay):
    first = BETA_FIRST * first + (1.0 - BETA_FIRST) * gradient
    second = BETA_SECOND * second + (1.0 - BETA_SECOND) * gradient * gradient
    first_hat = first / (1.0 - BETA_FIRST**STEP)
    second_hat = second / (1.0 - BETA_SECOND**STEP)
    weight = weight - rate * (first_hat / (jnp.sqrt(second_hat) + ADAM_EPS) + decay * weight)
    return (first, second, weight)


def slice_head(tensor, head_index):
    return lax.dynamic_slice_in_dim(tensor, head_index * HEAD_DIM, HEAD_DIM, tensor.ndim - 1)


def join_heads(stacked):
    moved = jnp.moveaxis(stacked, 0, 2)
    return moved.reshape(moved.shape[0], moved.shape[1], -1)


def spread_rows(normed):
    return lax.all_gather(normed, "head", axis=0, tiled=True)


def spread_grads(grad_rows):
    return lax.all_gather(grad_rows, "head", axis=0, tiled=True)


def sum_rows(full_rows, weight, row_share):

    def row_term(row_start, row_count):
        return jnp.dot(full_rows, weight, preferred_element_type=jnp.float32)

    return lax.psum_scatter(
        row_term(jnp.int32(0), row_share * lax.axis_size("head")),
        "head",
        scatter_dimension=0,
        tiled=True,
    )


def sum_grads(full_rows, weight, row_share):

    def row_term(row_start, row_count):
        return jnp.einsum("nc,dc->nd", full_rows, weight, preferred_element_type=jnp.float32)

    return lax.psum_scatter(
        row_term(jnp.int32(0), row_share * lax.axis_size("head")).astype(jnp.bfloat16),
        "head",
        scatter_dimension=0,
        tiled=True,
    ).astype(jnp.float32)


def attend(queries, keys_all, values_all, live_keys):
    local_heads = queries.shape[-1] // HEAD_DIM
    score_scale = HEAD_DIM ** (-0.5)
    live_mask = live_keys[:, None, :]

    def one_head(head_index):
        scores = (
            jnp.einsum(
                "ste,sje->stj",
                slice_head(queries, head_index),
                slice_head(keys_all, head_index),
                preferred_element_type=jnp.float32,
            )
            * score_scale
        )
        masked_scores = jnp.where(live_mask, scores, NEGATIVE)
        row_peak = jnp.max(masked_scores, axis=-1, keepdims=True)
        exp_scores = jnp.exp(masked_scores - row_peak)
        row_total = jnp.sum(exp_scores, axis=-1, keepdims=True)
        attn_probs = (exp_scores / row_total).astype(jnp.bfloat16)
        attended = jnp.einsum(
            "stj,sje->ste",
            attn_probs,
            slice_head(values_all, head_index),
            preferred_element_type=jnp.float32,
        )
        return (attended, (row_peak + jnp.log(row_total))[..., 0])

    outputs, log_totals = lax.map(one_head, jnp.arange(local_heads))
    return (join_heads(outputs), log_totals)


def attend_back(queries, keys_all, values_all, grad_heads, log_totals, live_keys):
    local_heads = queries.shape[-1] // HEAD_DIM
    score_scale = HEAD_DIM ** (-0.5)
    live_mask = live_keys[:, None, :]

    def one_head(head_index):
        query_h = slice_head(queries, head_index)
        key_h = slice_head(keys_all, head_index)
        grad_h = slice_head(grad_heads, head_index)
        scores = (
            jnp.einsum("ste,sje->stj", query_h, key_h, preferred_element_type=jnp.float32)
            * score_scale
        )
        masked_scores = jnp.where(live_mask, scores, NEGATIVE)
        attn_probs = jnp.exp(masked_scores - log_totals[head_index][..., None])
        grad_probs = jnp.einsum(
            "ste,sje->stj",
            grad_h,
            slice_head(values_all, head_index),
            preferred_element_type=jnp.float32,
        )
        row_delta = jnp.sum(attn_probs * grad_probs, axis=-1)
        grad_scores = (attn_probs * (grad_probs - row_delta[..., None])).astype(jnp.bfloat16)
        grad_query = (
            jnp.einsum("stj,sje->ste", grad_scores, key_h, preferred_element_type=jnp.float32)
            * score_scale
        )
        grad_key = (
            jnp.einsum("stj,ste->sje", grad_scores, query_h, preferred_element_type=jnp.float32)
            * score_scale
        )
        grad_value = jnp.einsum(
            "stj,ste->sje",
            attn_probs.astype(jnp.bfloat16),
            grad_h,
            preferred_element_type=jnp.float32,
        )
        return (grad_query, grad_key, grad_value)

    grad_query, grad_key, grad_value = lax.map(one_head, jnp.arange(local_heads))
    grad_key, grad_value = (
        lax.psum_scatter(grad_key, "blk", scatter_dimension=2, tiled=True),
        lax.psum_scatter(grad_value, "blk", scatter_dimension=2, tiled=True),
    )
    return (join_heads(grad_query), join_heads(grad_key), join_heads(grad_value))


def layer_forward(stream, layer_weights, norm_rows, live_keys, row_share):
    w_qkv, w_out, w_up, w_down = layer_weights
    seq_count = live_keys.shape[0]
    normed = layer_norm(stream, norm_rows[0, 0], norm_rows[0, 1]).astype(jnp.bfloat16)
    normed_all = spread_rows(normed)
    packed = jnp.dot(
        normed_all, w_qkv.reshape(w_qkv.shape[0], -1), preferred_element_type=jnp.float32
    ).astype(jnp.bfloat16)
    packed = packed.reshape(seq_count, -1, 3, w_qkv.shape[-1])
    queries, keys_local, values_local = (packed[:, :, 0], packed[:, :, 1], packed[:, :, 2])
    keys_all, values_all = (
        lax.all_gather(keys_local, "blk", axis=1, tiled=True),
        lax.all_gather(values_local, "blk", axis=1, tiled=True),
    )
    attended, log_totals = attend(queries, keys_all, values_all, live_keys)
    attended = attended.astype(jnp.bfloat16).reshape(-1, attended.shape[-1])
    attn_out = sum_rows(attended, w_out, row_share)
    middle = stream + attn_out
    normed_two = layer_norm(middle, norm_rows[1, 0], norm_rows[1, 1]).astype(jnp.bfloat16)
    normed_two_all = spread_rows(normed_two)
    hidden_pre = jnp.dot(normed_two_all, w_up, preferred_element_type=jnp.float32)
    hidden_act = gelu_exact(hidden_pre).astype(jnp.bfloat16)
    ffn_out = sum_rows(hidden_act, w_down, row_share)
    kept = (
        stream,
        middle,
        normed_all,
        queries,
        keys_local,
        values_local,
        keys_all,
        values_all,
        log_totals,
        attended,
        normed_two_all,
        hidden_pre,
    )
    return (middle + ffn_out, attn_out, ffn_out, kept)


def layer_backward(grad_stream, kept, layer_weights, norm_rows, live_keys, row_share):
    (
        stream,
        middle,
        normed_all,
        queries,
        keys_local,
        values_local,
        keys_all,
        values_all,
        log_totals,
        attended,
        normed_two_all,
        hidden_pre,
    ) = kept
    w_qkv, w_out, w_up, w_down = layer_weights
    grad_ffn = spread_grads(grad_stream.astype(jnp.bfloat16))
    hidden_act, gelu_back = jax.vjp(gelu_exact, hidden_pre)
    grad_down = jnp.einsum(
        "nf,nd->fd", hidden_act.astype(jnp.bfloat16), grad_ffn, preferred_element_type=jnp.float32
    )
    grad_act = jnp.einsum("nd,fd->nf", grad_ffn, w_down, preferred_element_type=jnp.float32)
    (grad_pre,) = gelu_back(grad_act)
    grad_pre = grad_pre.astype(jnp.bfloat16)
    grad_up = jnp.einsum("nd,nf->df", normed_two_all, grad_pre, preferred_element_type=jnp.float32)
    grad_normed_two = sum_grads(grad_pre, w_up, row_share)
    _, norm_back_two = jax.vjp(layer_norm, middle, norm_rows[1, 0], norm_rows[1, 1])
    grad_mid, gain_two, shift_two = norm_back_two(grad_normed_two)
    grad_middle = grad_stream + grad_mid
    grad_attn = spread_grads(grad_middle.astype(jnp.bfloat16))
    grad_out_w = jnp.einsum("nf,nd->fd", attended, grad_attn, preferred_element_type=jnp.float32)
    grad_heads = (
        jnp.einsum("nd,fd->nf", grad_attn, w_out, preferred_element_type=jnp.float32)
        .astype(jnp.bfloat16)
        .reshape(queries.shape)
    )
    grad_query, grad_key, grad_value = attend_back(
        queries, keys_all, values_all, grad_heads, log_totals, live_keys
    )
    grad_packed = (
        jnp.stack((grad_query, grad_key, grad_value), axis=2)
        .astype(jnp.bfloat16)
        .reshape(normed_all.shape[0], -1)
    )
    grad_qkv = jnp.einsum(
        "nd,nc->dc", normed_all, grad_packed, preferred_element_type=jnp.float32
    ).reshape(w_qkv.shape)
    grad_normed = sum_grads(grad_packed, w_qkv.reshape(w_qkv.shape[0], -1), row_share)
    _, norm_back_one = jax.vjp(layer_norm, stream, norm_rows[0, 0], norm_rows[0, 1])
    grad_input, gain_one, shift_one = norm_back_one(grad_normed)
    norm_grads = jnp.stack((jnp.stack((gain_one, shift_one)), jnp.stack((gain_two, shift_two))))
    return (grad_middle + grad_input, (grad_qkv, grad_out_w, grad_up, grad_down), norm_grads)


def plain_step(
    token_ids,
    targets,
    masked,
    lengths,
    family_weight,
    embed_table,
    w_qkv,
    w_out,
    w_up,
    w_down,
    norm_params,
):
    blk_count = lax.axis_size("blk")
    head_count = lax.axis_size("head")
    seq_count, blk_tokens = token_ids.shape
    row_share = seq_count * blk_tokens // head_count
    row_first = lax.axis_index("head") * row_share
    blk_start = lax.axis_index("blk") * blk_tokens
    table_all, qkv_all, out_all, up_all, down_all, norm_all = (
        lax.all_gather(embed_table.astype(jnp.bfloat16), "blk", axis=1, tiled=True),
        lax.all_gather(w_qkv.astype(jnp.bfloat16), "blk", axis=1, tiled=True),
        lax.all_gather(w_out.astype(jnp.bfloat16), "blk", axis=2, tiled=True),
        lax.all_gather(w_up.astype(jnp.bfloat16), "blk", axis=1, tiled=True),
        lax.all_gather(w_down.astype(jnp.bfloat16), "blk", axis=1, tiled=True),
        lax.all_gather(norm_params.astype(jnp.bfloat16), "blk", axis=2, tiled=True),
    )
    token_table = table_all[:VOCAB]
    place_rows = lax.dynamic_slice_in_dim(table_all, VOCAB + blk_start, blk_tokens, 0)
    norm_rows = norm_all.astype(jnp.float32)
    live_keys = jnp.arange(blk_tokens * blk_count)[None, :] < lengths[:, None]
    positions = blk_start + jnp.arange(blk_tokens)
    live_local = positions[None, :] < lengths[:, None]
    seq_of_row = (row_first + jnp.arange(row_share)) // blk_tokens
    place_of_row = (row_first + jnp.arange(row_share)) % blk_tokens
    seq_hot = (seq_of_row[:, None] == jnp.arange(seq_count)[None, :]).astype(jnp.float32)
    place_hot = place_of_row[:, None] == jnp.arange(blk_tokens)[None, :]
    row_family = jnp.dot(seq_hot, family_weight, precision=HIGHEST)
    row_live = lax.dynamic_slice_in_dim(live_local.reshape(-1), row_first, row_share, 0).astype(
        jnp.float32
    )[:, None]
    row_ids = lax.dynamic_slice_in_dim(token_ids.reshape(-1), row_first, row_share, 0)
    row_targets = lax.dynamic_slice_in_dim(targets.reshape(-1), row_first, row_share, 0)
    row_masked = lax.dynamic_slice_in_dim(masked.reshape(-1), row_first, row_share, 0)
    token_hot = row_ids[:, None] == jnp.arange(VOCAB)[None, :]
    stream = jnp.dot(
        token_hot.astype(jnp.bfloat16), token_table, preferred_element_type=jnp.float32
    ) + jnp.dot(place_hot.astype(jnp.bfloat16), place_rows, preferred_element_type=jnp.float32)
    layer_stats = []
    kept_all = []
    for layer_idx in range(LAYERS):
        layer_weights = (
            qkv_all[layer_idx],
            out_all[layer_idx],
            up_all[layer_idx],
            down_all[layer_idx],
        )
        layer_stats.append(jnp.sum(stream * stream * row_live))
        stream, attn_out, ffn_out, kept = layer_forward(
            stream,
            layer_weights,
            norm_rows[2 * layer_idx : 2 * layer_idx + 2],
            live_keys,
            row_share,
        )
        layer_stats.append(jnp.sum(attn_out * attn_out * row_live))
        layer_stats.append(jnp.sum(ffn_out * ffn_out * row_live))
        kept_all.append(kept)
    final_low = layer_norm(stream, norm_rows[2 * LAYERS, 0], norm_rows[2 * LAYERS, 1]).astype(
        jnp.bfloat16
    )
    logits = jnp.einsum("nd,vd->nv", final_low, token_table, preferred_element_type=jnp.float32)
    shifted = logits - jnp.max(logits, axis=-1, keepdims=True)
    log_probs = shifted - jnp.log(jnp.sum(jnp.exp(shifted), axis=-1, keepdims=True))
    target_hot = (row_targets[:, None] == jnp.arange(VOCAB)[None, :]).astype(jnp.float32)
    token_loss = -jnp.sum(target_hot * log_probs, axis=1)
    token_weight = row_masked.astype(jnp.float32) * row_family
    loss_sum, weight_sum, squares = lax.psum(
        (jnp.sum(token_weight * token_loss), jnp.sum(token_weight), jnp.stack(layer_stats)),
        ("blk", "head"),
    )
    grad_logits = ((token_weight / weight_sum)[:, None] * (jnp.exp(log_probs) - target_hot)).astype(
        jnp.bfloat16
    )
    grad_final = jnp.einsum(
        "nv,vd->nd", grad_logits, token_table, preferred_element_type=jnp.float32
    )
    grad_table = jnp.einsum("nv,nd->vd", grad_logits, final_low, preferred_element_type=jnp.float32)
    _, final_back = jax.vjp(layer_norm, stream, norm_rows[2 * LAYERS, 0], norm_rows[2 * LAYERS, 1])
    grad_stream, gain_last, shift_last = final_back(grad_final)
    layer_grads = []
    norm_grads = []
    for layer_idx in reversed(range(LAYERS)):
        layer_weights = (
            qkv_all[layer_idx],
            out_all[layer_idx],
            up_all[layer_idx],
            down_all[layer_idx],
        )
        grad_stream, grads_now, norms_now = layer_backward(
            grad_stream,
            kept_all[layer_idx],
            layer_weights,
            norm_rows[2 * layer_idx : 2 * layer_idx + 2],
            live_keys,
            row_share,
        )
        layer_grads.insert(0, grads_now)
        norm_grads.insert(0, norms_now)
    grad_table = grad_table + jnp.dot(
        token_hot.astype(jnp.float32).T, grad_stream, precision=HIGHEST
    )
    grad_place = jnp.dot(place_hot.astype(jnp.float32).T, grad_stream, precision=HIGHEST)
    grad_norms = jnp.concatenate(norm_grads + [jnp.stack((gain_last, shift_last))[None]], axis=0)
    stacked = [
        jnp.stack([layer_entry[slot_idx] for layer_entry in layer_grads]) for slot_idx in range(4)
    ]
    table_sum, place_sum, norm_sum = (
        lax.psum(grad_table.astype(jnp.bfloat16), "head").astype(jnp.float32),
        lax.psum(grad_place.astype(jnp.bfloat16), "head").astype(jnp.float32),
        lax.psum(grad_norms.astype(jnp.bfloat16), "head").astype(jnp.float32),
    )
    place_full = lax.dynamic_update_slice_in_dim(
        jnp.zeros((blk_tokens * blk_count, place_sum.shape[1]), jnp.float32),
        place_sum,
        blk_start,
        0,
    )
    full_table = jnp.concatenate((table_sum, place_full), axis=0)
    reduced = (
        lax.psum_scatter(full_table, "blk", scatter_dimension=1, tiled=True),
        lax.psum_scatter(stacked[0], "blk", scatter_dimension=1, tiled=True),
        lax.psum_scatter(stacked[1], "blk", scatter_dimension=2, tiled=True),
        lax.psum_scatter(stacked[2], "blk", scatter_dimension=1, tiled=True),
        lax.psum_scatter(stacked[3], "blk", scatter_dimension=1, tiled=True),
        lax.psum_scatter(norm_sum, "blk", scatter_dimension=2, tiled=True),
    )
    sharded_squares = sum((jnp.sum(grad_part * grad_part) for grad_part in reduced[1:5]))
    shared_squares = (
        jnp.sum(reduced[0] * reduced[0]) + jnp.sum(reduced[5] * reduced[5])
    ) / head_count
    grad_norm = jnp.sqrt(lax.psum(sharded_squares + shared_squares, ("blk", "head")))
    return loss_sum, weight_sum, grad_norm, squares, reduced


BF16 = jnp.bfloat16
F32 = jnp.float32
MESH = pl.DeviceIdType.MESH
LOG2E = 1.4426950408889634
NORM_LANE = 32


def dot(left, right, left_dim, right_dim):
    return lax.dot_general(
        left, right, (((left_dim,), (right_dim,)), ((), ())), preferred_element_type=F32
    )


class Sizes:
    def __init__(self, blk, head, seqs, blk_tokens, w_qkv, w_up, w_down):
        self.B, self.H, self.S = blk, head, seqs
        self.L = w_qkv[0]
        self.DB = w_qkv[1]
        self.D = self.DB * blk
        self.HC = w_qkv[3]
        self.T = blk_tokens * blk
        self.G = blk // seqs if blk % seqs == 0 else 0
        self.FD = w_down[1]
        if self.G:
            self.NR = self.G * head
            self.R = self.T // self.NR
            self.NC = self.NR // 2
            self.FU = w_up[2] // self.G

    def fused(self, blk_tokens):
        if self.G != 2 or self.S != 4 or self.H % 2 or self.R != blk_tokens or self.R != 128:
            return False
        if self.FU != self.FD * self.S or 3 * self.S > 16 or VOCAB > NORM_LANE:
            return False
        if NORM_LANE + 2 * (2 * self.L + 1) > 128:
            return False
        if any(n % 16 for n in (self.DB, self.HC, self.FD)) or self.D % 128 or self.FU % 128:
            return False
        weights = self.L * 2 * (4 * self.D * self.HC + 2 * self.D * self.FU)
        kept = self.L * self.T * (6 * self.D + 6 * self.FU + 14 * self.HC)
        return 3 * weights + kept + 16 * self.T * self.D + 8 * self.T * 256 * 4 < (60 << 20)


def step_kernel(
    z,
    lens,
    fam,
    tok_in,
    tgt_in,
    msk_in,
    emb_in,
    wq_in,
    wo_in,
    wu_in,
    wd_in,
    norm_in,
    scal_out,
    ge_out,
    gq_out,
    go_out,
    gu_out,
    gd_out,
    gn_out,
    ids,
    wq_own,
    wo_own,
    wu_own,
    wd_own,
    gu_sum,
    idsg,
    tg,
    wq,
    wo,
    wu,
    wd,
    h1,
    h2,
    df,
    da,
    act,
    slope,
    du,
    qt,
    kt,
    vt,
    o32,
    ob,
    dob,
    lse,
    dqkv,
    bias,
    sbuf,
    pbuf,
    xs,
    xm,
    keep,
    psrc,
    csrc,
    srecv,
    rrecv,
    sg,
    stq,
    sto,
    stu,
    std,
    rq,
    ro,
    ru,
    rd,
    rc,
    tq,
    to,
    tu,
    td,
    tc,
    fst,
    frx,
    hrs,
    hrx,
    scg,
    id_s,
    id_r,
    tp_s,
    tp_r,
    w_s,
    w_r,
    ag_s,
    ag_r,
    rs_s,
    rs_r,
    g_s,
    g_r,
    f_s,
    f_r,
    hx_s,
    hx_r,
    sc_s,
    sc_r,
):
    B, H, S, G, L, D, DB, HC, R, NC, NR, FU, FD, T = (
        z.B, z.H, z.S, z.G, z.L, z.D, z.DB, z.HC, z.R, z.NC, z.NR, z.FU, z.FD, z.T,
    )
    N_HEADS = HC // HEAD_DIM
    W = 2 * R
    QT = 2
    scale = HEAD_DIM ** (-0.5)
    c2 = scale * LOG2E
    b = lax.axis_index("blk")
    h = lax.axis_index("head")
    s, g = b // G, b % G
    y, c = h // 2, h % 2
    own_row = g * H + h
    s1 = s + 1 - 2 * (s % 2)
    s2 = (s + 2) % S
    s3 = (s1 + 2) % S

    def dev(blk_i, head_i):
        return (blk_i, head_i)

    sibling = dev(b, y * 2 + 1 - c)

    def peer(k):
        return dev(s * G + (g + k // 2) % G, ((y + k % 2) % 2) * 2 + c)

    waits = []

    def send(src, dst, ssem, rsem, device):
        copy = pltpu.make_async_remote_copy(src, dst, ssem, rsem, device, MESH)
        copy.start()
        return copy

    def arrived(dst, ssem, rsem):
        pltpu.make_async_remote_copy(dst, dst, ssem, rsem, sibling, MESH).wait_recv()

    def over_blk(body):
        def one(k, carry):
            body(lax.rem(b + k, B))
            return carry

        lax.fori_loop(1, B, one, 0)

    def rows(i, n):
        return pl.ds(pl.multiple_of(i * n, 16), n)

    barrier = pltpu.get_barrier_semaphore()

    def greet_blk(other):
        pl.semaphore_signal(barrier, inc=1, device_id=dev(other, h), device_id_type=MESH)

    def greet_head(k, carry):
        pl.semaphore_signal(
            barrier, inc=1, device_id=dev(b, lax.rem(h + k, H)), device_id_type=MESH
        )
        return carry

    over_blk(greet_blk)
    lax.fori_loop(1, H, greet_head, 0)

    table = emb_in[...]
    ids[...] = jnp.zeros((16, R), jnp.int32)
    ids[0:S] = tok_in[...]
    ids[S : 2 * S] = tgt_in[...]
    ids[2 * S : 3 * S] = msk_in[...]
    sg[...] = jnp.zeros((D, 128), F32)
    for i in range(2 * L + 1):
        sg[NORM_LANE + 2 * i : NORM_LANE + 2 * i + 2, 0:DB] = norm_in[i]
    lane_small = lax.broadcasted_iota(jnp.int32, (DB, 128), 1)
    token_part = jnp.where(lane_small < VOCAB, table[:, 0:128], sg[0:128, :].T[0:DB]).astype(BF16)
    own_rows = rows(b, DB)
    tg[own_rows, 0:128] = token_part
    tg[own_rows, 128:] = table[:, VOCAB:].astype(BF16)
    pl.semaphore_wait(barrier, B + H - 2)

    def send_ids(other):
        send(ids, idsg.at[b], id_s.at[other], id_r.at[b], dev(other, h))

    over_blk(send_ids)
    idsg[b] = ids[...]

    lanes_in = pl.ds(pl.multiple_of(c * 512, 128), T + 128 - 512)
    lanes_out = pl.ds(pl.multiple_of(c * (T + 128 - 512), 128), 512)
    lanes_back = pl.ds(pl.multiple_of((1 - c) * (T + 128 - 512), 128), 512)

    def t_send(m, at, cut, device):
        block = tg.at[at, cut]
        waits.append(send(block, block, tp_s.at[m], tp_r.at[m], device))

    def t_here(m, at, cut):
        arrived(tg.at[at, cut], tp_s.at[m], tp_r.at[m])

    def plane_rows(plane, column):
        return rows(plane * G + column, DB)

    t_send(0, own_rows, lanes_in, dev(s2 * G + g, h))
    t_send(1, own_rows, lanes_in, dev(s1 * G + g, h))
    t_send(3, own_rows, lanes_in, dev(s * G + 1 - g, h))

    def w_sem(sems, l, kind, m):
        return sems.at[l * 21 + (-1, 6, 14, 17)[kind] + m]

    def w_ref(l, kind, at):
        return (wq, wo, wu, wd)[kind].at[l, at]

    def shard_rows(kind, plane, column=None):
        if kind == 3:
            return rows(plane, FD)
        return rows(plane * G + (g if column is None else column), DB)

    def w_send(l, kind, m, src, at, device):
        waits.append(
            send(src, w_ref(l, kind, at), w_sem(w_s, l, kind, m), w_sem(w_r, l, kind, m), device)
        )

    def w_arrived(l, kind, m, at):
        arrived(w_ref(l, kind, at), w_sem(w_s, l, kind, m), w_sem(w_r, l, kind, m))

    def round_weights(l, kind):
        at = shard_rows(kind, s)
        if kind == 0:
            wq_own[l] = jnp.concatenate([wq_in[l, i] for i in range(3)], axis=1).astype(BF16)
            wq[l, at] = wq_own[l]
        elif kind == 1:
            wo_own[l] = wo_in[l].T.astype(BF16)
            wo[l, at] = wo_own[l]
        elif kind == 2:
            up = wu_in[l]
            for j in range(G):
                parts = [up[:, (i * G + j) * FD : (i * G + j + 1) * FD] for i in range(S)]
                wu_own[l, j] = jnp.concatenate(parts, axis=1).astype(BF16)
            wu[l, at] = wu_own[l, g]
        else:
            wd_own[l] = wd_in[l].astype(BF16)
            wd[l, at] = wd_own[l]

    def plane_block(kind, plane):
        return rows(plane, FD) if kind == 3 else rows(plane, G * DB)

    def send_weights(l, kind):
        round_weights(l, kind)
        at = shard_rows(kind, s)
        if kind == 2:
            w_send(l, 2, 0, wu_own.at[l, 1 - g], at, dev(s * G + 1 - g, h))
            return
        src = (wq_own, wo_own, None, wd_own)[kind].at[l]
        w_send(l, kind, 1, src, at, dev(s2 * G + g, h))
        w_send(l, kind, 2, src, at, dev(s1 * G + g, h))

    def push_weights(l):
        w_arrived(l, 2, 0, shard_rows(2, s, 1 - g))
        at = plane_block(2, s)
        w_send(l, 2, 1, w_ref(l, 2, at), at, dev(s2 * G + g, h))
        w_send(l, 2, 2, w_ref(l, 2, at), at, dev(s1 * G + g, h))

    def relay_weights(l, kind):
        at = shard_rows(kind, s2) if kind < 2 else plane_block(kind, s2)
        w_arrived(l, kind, 1, at)
        w_send(l, kind, 3, w_ref(l, kind, at), at, dev(s1 * G + g, h))

    def cross_weights(l, kind, planes):
        for m, plane, known in ((4, s, True), (5, s2, True), (6, s1, False), (7, s3, False)):
            if m - 4 in planes:
                at = shard_rows(kind, plane)
                if not known:
                    w_arrived(l, kind, m - 4, at)
                w_send(l, kind, m, w_ref(l, kind, at), at, dev(s * G + 1 - g, h))

    def wait_weights(l, kind):
        if kind < 2:
            for m, plane in ((4, s), (5, s2), (6, s1), (7, s3)):
                w_arrived(l, kind, m, shard_rows(kind, plane, 1 - g))
        else:
            w_arrived(l, kind, 2, plane_block(kind, s1))
            w_arrived(l, kind, 3, plane_block(kind, s3))

    for kind in range(2):
        send_weights(0, kind)
        cross_weights(0, kind, (0,))
    at = plane_rows(s2, g)
    t_here(0, at, lanes_in)
    t_send(2, at, lanes_in, dev(s1 * G + g, h))
    t_send(4, at, lanes_in, dev(s * G + 1 - g, h))
    for m, plane in ((1, s1), (2, s3)):
        at = plane_rows(plane, g)
        t_here(m, at, lanes_in)
        t_send(m + 4, at, lanes_in, dev(s * G + 1 - g, h))
    send_weights(0, 2)
    for kind in range(2):
        relay_weights(0, kind)
        cross_weights(0, kind, (1,))
    send_weights(0, 3)
    push_weights(0)

    half_rows = (slice(0, D // 2), slice(D // 2, D))

    ag_sent = []

    def ag_send(m, src, dst, device):
        ag_sent.append(send(src, dst, ag_s.at[m], ag_r.at[m], device))

    def ag_here(m, dst):
        arrived(dst, ag_s.at[m], ag_r.at[m])

    def ag_left():
        for copy in ag_sent:
            copy.wait_send()
        ag_sent.clear()

    def block(buf, k, half):
        return buf.at[:, k * W + half * R : k * W + half * R + R]

    def block_half(buf, k, half, i):
        return buf.at[half_rows[i], k * W + half * R : k * W + half * R + R]

    def spread(buf, base=0):
        ag_left()
        ag_send(base + 0, block_half(buf, 0, 0, 0), block_half(buf, 1, 0, 0), peer(1))
        ag_send(base + 1, block_half(buf, 0, 0, 1), block_half(buf, 2, 0, 1), peer(2))
        ag_send(base + 2, block_half(buf, 0, 0, 1), block_half(buf, 1, 0, 1), peer(1))
        ag_send(base + 3, block_half(buf, 0, 0, 0), block_half(buf, 2, 0, 0), peer(2))
        ag_send(base + 4, block(buf, 0, 0), block(buf, 0, 1), sibling)

    def relay_near(buf, base=0):
        ag_here(base + 0, block_half(buf, 1, 0, 0))
        ag_send(base + 5, block_half(buf, 1, 0, 0), block_half(buf, 3, 0, 0), peer(2))
        ag_here(base + 1, block_half(buf, 2, 0, 1))
        ag_send(base + 6, block_half(buf, 2, 0, 1), block_half(buf, 3, 0, 1), peer(1))
        ag_here(base + 2, block_half(buf, 1, 0, 1))
        ag_send(base + 7, block(buf, 1, 0), block(buf, 1, 1), sibling)
        ag_here(base + 3, block_half(buf, 2, 0, 0))
        ag_send(base + 8, block(buf, 2, 0), block(buf, 2, 1), sibling)

    def relay_far(buf, base=0):
        for i in range(2):
            ag_here(base + 5 + i, block_half(buf, 3, 0, i))
            ag_send(base + 9 + i, block_half(buf, 3, 0, i), block_half(buf, 3, 1, i), sibling)

    def have(buf, k, base=0):
        if k == 0:
            ag_here(base + 4, block(buf, 0, 1))
        elif k < 3:
            ag_here(base + 6 + k, block(buf, k, 1))
        else:
            for i in range(2):
                ag_here(base + 9 + i, block_half(buf, 3, 1, i))

    def spread_column(buf):
        ag_left()
        ag_send(0, block(buf, 0, 0), block(buf, 1, 0), peer(1))
        ag_send(4, block(buf, 0, 0), block(buf, 0, 1), sibling)

    def relay_column(buf):
        ag_here(0, block(buf, 1, 0))
        ag_send(7, block(buf, 1, 0), block(buf, 1, 1), sibling)

    staged = {}
    summed_pairs = set()
    half_of = (slice(0, D // 2), slice(D // 2, D))

    def stage(ref, key, value):
        for copy in staged.pop(key, ()):
            copy.wait_send()
        ref[...] = value

    def rs_set(use, m):
        return m + 10 * (use % 4 == 3)

    def rs_send(use, m, src, dst, device):
        n = rs_set(use, m)
        return [send(src, dst, rs_s.at[n], rs_r.at[n], device)]

    def rs_here(use, m, dst):
        n = rs_set(use, m)
        arrived(dst, rs_s.at[n], rs_r.at[n])

    def part(use, k, value):
        keep[k] = value[:, :R]
        stage(psrc.at[k], ("p", k), value[:, R:].astype(BF16))
        staged["p", k] = rs_send(use, k, psrc.at[k], srecv.at[use % 4, k], sibling)

    def pair_sum(use, k, at=slice(0, D)):
        if (use, k) not in summed_pairs:
            summed_pairs.add((use, k))
            rs_here(use, k, srecv.at[use % 4, k])
        return keep[k, at] + srecv[use % 4, k, at].astype(F32)

    def pass_half(use, m, k, i, value, slot, device):
        stage(csrc.at[k, half_of[i]], ("c", k, i), value.astype(BF16))
        staged["c", k, i] = rs_send(
            use, m, csrc.at[k, half_of[i]], rrecv.at[use % 4, slot, half_of[i]], device
        )

    def pass_across(use):
        pass_half(use, 4, 3, 0, pair_sum(use, 3, half_of[0]), 0, peer(1))
        pass_half(use, 5, 3, 1, pair_sum(use, 3, half_of[1]), 0, peer(2))

    def pass_near(use):
        pass_half(use, 6, 1, 0, pair_sum(use, 1, half_of[0]), 1, peer(1))
        pass_half(use, 7, 2, 1, pair_sum(use, 2, half_of[1]), 2, peer(2))

    def pass_joined(use):
        for i, k in ((0, 2), (1, 1)):
            rs_here(use, 4 + i, rrecv.at[use % 4, 0, half_of[i]])
            value = pair_sum(use, k, half_of[i]) + rrecv[use % 4, 0, half_of[i]].astype(F32)
            pass_half(use, 8 + i, k, i, value, k, peer(k))

    def total(use):
        out = pair_sum(use, 0)
        for m, k, i in ((6, 1, 0), (7, 2, 1), (8, 2, 0), (9, 1, 1)):
            rs_here(use, m, rrecv.at[use % 4, k, half_of[i]])
        return out + rrecv[use % 4, 1].astype(F32) + rrecv[use % 4, 2].astype(F32)

    def pass_column(use):
        for i in range(2):
            pass_half(use, 6 + 3 * i, 1, i, pair_sum(use, 1, half_of[i]), 1, peer(1))

    def total_column(use):
        out = pair_sum(use, 0)
        for i in range(2):
            rs_here(use, 6 + 3 * i, rrecv.at[use % 4, 1, half_of[i]])
        return out + rrecv[use % 4, 1].astype(F32)

    def g_sem(sems, l, kind, m):
        return sems.at[l * 21 + (0, 7, 14, 18)[kind] + m]

    def g_send(l, kind, m, src, dst, device):
        return send(src, dst, g_sem(g_s, l, kind, m), g_sem(g_r, l, kind, m), device)

    def g_arrived(l, kind, m, dst):
        arrived(dst, g_sem(g_s, l, kind, m), g_sem(g_r, l, kind, m))

    def g_stage(key, ref, value):
        for copy in staged.pop(key, ()):
            copy.wait_send()
        ref[...] = value.astype(BF16)

    def g_first(l, kind, value):
        src, dst = ((stq, rq), (sto, ro), (stu, ru), (std, rd))[kind]
        g_stage(("g", kind), src, value)
        if kind < 2:
            staged["g", kind] = []
            g_cross(l, kind, ((0, s3), (1, s1)))
            return
        n = G * DB if kind == 2 else FD
        dst[l, 0] = src[rows(s, n)]
        staged["g", kind] = [
            g_send(l, kind, i, src.at[rows(plane, n)], dst.at[l, 1 + i], dev(s1 * G + g, h))
            for i, plane in ((1, s3), (0, s1))
        ]

    def g_cross(l, kind, planes):
        src, dst = ((stq, rq), (sto, ro))[kind]
        for m, plane in planes:
            staged["g", kind].append(
                g_send(
                    l, kind, m, src.at[rows(plane * G + 1 - g, DB)], dst.at[l, m], dev(s * G + 1 - g, h)
                )
            )

    def g_column(l, kind, m, plane):
        src, dst = ((stq, rq), (sto, ro))[kind]
        return src[rows(plane * G + g, DB)].astype(F32) + dst[l, m].astype(F32)

    def g_mid(l, kind):
        src, dst, tmp = ((stq, rq, tq), (sto, ro, to))[kind]
        g_arrived(l, kind, 0, dst.at[l, 0])
        g_stage(("m", kind, 1), tmp.at[1], g_column(l, kind, 0, s3))
        one = g_send(l, kind, 5, tmp.at[1], dst.at[l, S + 1], dev(s1 * G + g, h))
        g_arrived(l, kind, 1, dst.at[l, 1])
        g_stage(("m", kind, 0), tmp.at[0], g_column(l, kind, 1, s1))
        two = g_send(l, kind, 4, tmp.at[0], dst.at[l, S], dev(s1 * G + g, h))
        staged["m", kind, 1] = [one]
        staged["m", kind, 0] = [two]

    def g_second(l, kind):
        if kind < 2:
            src, dst, tmp = ((stq, rq, tq), (sto, ro, to))[kind]
            g_arrived(l, kind, 2, dst.at[l, 2])
            g_arrived(l, kind, 5, dst.at[l, S + 1])
            g_stage(("s", kind), tmp.at[2], g_column(l, kind, 2, s2) + dst[l, S + 1].astype(F32))
            staged["s", kind] = [g_send(l, kind, 6, tmp.at[2], dst.at[l, S + 2], dev(s2 * G + g, h))]
            return
        src, dst, tmp, n = ((stu, ru, tu, G * DB), (std, rd, td, FD))[kind - 2]
        g_arrived(l, kind, 1, dst.at[l, 2])
        g_stage(("s", kind), tmp, src[rows(s2, n)].astype(F32) + dst[l, 2].astype(F32))
        staged["s", kind] = [g_send(l, kind, 2, tmp, dst.at[l, 3], dev(s2 * G + g, h))]

    def g_third(l):
        g_arrived(l, 2, 0, ru.at[l, 1])
        g_arrived(l, 2, 2, ru.at[l, 3])

        def summed(column):
            at = rows(column, DB)
            return sum(ru[l, i, at, :].astype(F32) for i in (0, 1, 3))

        g_stage(("t", 2), tc, summed(1 - g))
        staged["t", 2] = [g_send(l, 2, 3, tc, rc.at[l], dev(s * G + 1 - g, h))]
        gu_sum[g] = summed(g)

    def lanes_of(v):
        folded = jnp.sum(v * v, axis=0, keepdims=True)
        return jnp.sum(folded, axis=1, keepdims=True) + jnp.zeros((1, 128), F32)

    def g_final(l, kind):
        if kind < 2:
            dst, out = ((rq, gq_out), (ro, go_out))[kind]
            g_arrived(l, kind, 3, dst.at[l, 3])
            g_arrived(l, kind, 4, dst.at[l, S])
            g_arrived(l, kind, 6, dst.at[l, S + 2])
            value = g_column(l, kind, 3, s) + dst[l, S].astype(F32) + dst[l, S + 2].astype(F32)
            if kind == 0:
                for i in range(3):
                    out[l, i] = value[:, i * HC : (i + 1) * HC]
            else:
                out[l] = value.T
        elif kind == 2:
            g_arrived(l, 2, 3, rc.at[l])
            value = rc[l].astype(F32)
            gu_sum[1 - g] = value
            parts = [gu_sum[j, :, i * FD : (i + 1) * FD] for i in range(S) for j in range(G)]
            gu_out[l] = jnp.concatenate(parts, axis=1)
            return lanes_of(gu_sum[0]) + lanes_of(gu_sum[1])
        else:
            g_arrived(l, 3, 0, rd.at[l, 1])
            g_arrived(l, 3, 2, rd.at[l, 3])
            value = sum(rd[l, i].astype(F32) for i in (0, 1, 3))
            gd_out[l] = value
        return lanes_of(value)

    squares = jnp.zeros((1, 128), F32)

    length = lens[s]
    for k in range(NC):
        for half in range(2):
            core = c if half == 0 else 1 - c
            block_row = ((g + k // 2) % G) * H + ((y + k % 2) % 2) * 2 + core
            place = block_row * R + lax.broadcasted_iota(jnp.int32, (R, 128), 0)
            bias[k * W + half * R : k * W + half * R + R, :] = jnp.where(place < length, 0.0, NEGATIVE)
    lane_place = own_row * R + lax.broadcasted_iota(jnp.int32, (1, R), 1)
    live = jnp.where(lane_place < length, 1.0, 0.0)
    dqkv[0:HC, QT * W :] = jnp.zeros((HC, T - QT * W), BF16)
    sg[...] = jnp.zeros((D, 128), F32)
    lane = lax.broadcasted_iota(jnp.int32, (D, 128), 1)
    row_of = lax.broadcasted_iota(jnp.int32, (128, R), 0)

    def ids_here(other):
        arrived(idsg.at[other], id_s.at[other], id_r.at[other])

    over_blk(ids_here)
    t_here(3, plane_rows(s, 1 - g), lanes_in)
    t_send(7, plane_rows(s, 1 - g), lanes_out, sibling)
    for m, plane in ((4, s2), (5, s1), (6, s3)):
        t_here(m, plane_rows(plane, 1 - g), lanes_in)
        t_send(m + 4, rows(plane, G * DB), lanes_out, sibling)
    t_here(7, plane_rows(s, 1 - g), lanes_back)
    for m, plane in ((8, s2), (9, s1), (10, s3)):
        t_here(m, rows(plane, G * DB), lanes_back)
    etg = tg.at[:, 0:128]
    target_row = idsg[own_row, pl.ds(S + s, 1), :]
    mask_row = idsg[own_row, pl.ds(2 * S + s, 1), :].astype(F32)
    token_weight = mask_row * fam[s]
    weight_sum = jnp.zeros((1, 1), F32)
    for i in range(S):
        counts = jnp.zeros((1, R), F32)
        for j in range(B):
            counts = counts + idsg[j, 2 * S + i : 2 * S + i + 1, :].astype(F32)
        weight_sum = weight_sum + jnp.sum(counts, axis=1, keepdims=True) * fam[i]

    def gain(i):
        return etg[:, NORM_LANE + 2 * i : NORM_LANE + 2 * i + 1].astype(F32)

    def shift(i):
        return etg[:, NORM_LANE + 2 * i + 1 : NORM_LANE + 2 * i + 2].astype(F32)

    def normalize(v):
        centred = v - jnp.mean(v, axis=0, keepdims=True)
        rstd = lax.rsqrt(jnp.mean(centred * centred, axis=0, keepdims=True) + NORM_EPS)
        return centred * rstd, rstd

    def layer_norm_low(v, i):
        hat, _ = normalize(v)
        return (hat * gain(i) + shift(i)).astype(BF16)

    later = []

    def run_later():
        for work in later:
            work()
        later.clear()

    def norm_grads(grad, hat, i):
        gain_grad = jnp.sum(grad * hat, axis=1, keepdims=True)
        shift_grad = jnp.sum(grad, axis=1, keepdims=True)
        sg[...] += jnp.where(lane == NORM_LANE + 2 * i, gain_grad, 0.0) + jnp.where(
            lane == NORM_LANE + 2 * i + 1, shift_grad, 0.0
        )

    def layer_norm_back(grad, v, i):
        hat, rstd = normalize(v)
        later.append(lambda: norm_grads(grad, hat, i))
        scaled = grad * gain(i)
        mean_one = jnp.mean(scaled, axis=0, keepdims=True)
        mean_two = jnp.mean(scaled * hat, axis=0, keepdims=True)
        return rstd * (scaled - mean_one - hat * mean_two)

    def square_sum(v, l, i):
        later.append(lambda: stats.__setitem__(3 * l + i, squares_of(v)))

    def squares_of(v):
        return jnp.sum(jnp.sum(v * v, axis=0, keepdims=True) * live, axis=1, keepdims=True)

    slots = list(range(NC))
    near = slots[:2]
    stats = {}
    for k in slots:
        for half in range(2):
            core = c if half == 0 else 1 - c
            block_row = ((g + k // 2) % G) * H + ((y + k % 2) % 2) * 2 + core
            hot = jnp.where(row_of == idsg[block_row, pl.ds(s, 1), :], 1.0, 0.0).astype(BF16)
            place = tg[:, pl.ds(pl.multiple_of(128 + block_row * R, 128), R)]
            start = dot(etg[...], hot, 1, 0) + place.astype(F32)
            h1[0, :, k * W + half * R : k * W + half * R + R] = layer_norm_low(start, 0)
            if k == 0 and half == 0:
                xs[0] = start
                token_hot = hot

    def cols(k):
        return slice(k * W, (k + 1) * W)

    for l in range(L):
        x = xs[l]
        square_sum(x, l, 0)
        if l:
            h1[l, :, 0:R] = layer_norm_low(x, 2 * l)
            spread(h1.at[l], 11)
            run_later()
        else:
            for kind in range(2):
                cross_weights(0, kind, (2, 3))
        wait_weights(l, 0)

        def project(k):
            if k in near:
                packed = dot(wq[l], h1[l, :, cols(k)], 0, 0).astype(BF16)
                qt[l, :, cols(k)] = packed[0:HC]
                packed = packed[HC:]
            else:
                packed = dot(wq[l, :, :], h1[l, :, cols(k)], 0, 0).astype(BF16)[HC:]
            kt[l, :, cols(k)] = packed[0:HC]
            vt[l, :, cols(k)] = packed[HC:]

        if l:
            have(h1.at[l], 0, 11)
            project(0)
            relay_near(h1.at[l], 11)
            have(h1.at[l], 1, 11)
            project(1)
            relay_far(h1.at[l], 11)
            have(h1.at[l], 2, 11)
            project(2)
            have(h1.at[l], 3, 11)
            project(3)
        else:
            for k in slots:
                project(k)

        tiles = [(q, i) for q in (1, 0) for i in range(N_HEADS)]
        chunk = W
        peaks, norms, outs = {}, {}, {}

        def head_rows(i):
            return slice(i * HEAD_DIM, (i + 1) * HEAD_DIM)

        def score(n, j):
            q, i = tiles[n]
            keys = slice(j * chunk, (j + 1) * chunk)
            scores = dot(kt[l, head_rows(i), keys], qt[l, head_rows(i), cols(q)], 0, 0)
            scores = scores + jnp.concatenate([bias[keys, :]] * 2, axis=1)
            sbuf[n % 2, keys, :] = scores
            peak = jnp.max(scores, axis=0, keepdims=True)
            peaks[n] = jnp.maximum(peaks[n], peak) if j else peak

        def weigh(n, j):
            keys = slice(j * chunk, (j + 1) * chunk)
            exps = jnp.exp2((sbuf[n % 2, keys, :] - peaks[n]) * c2)
            norm = jnp.sum(exps, axis=0, keepdims=True)
            norms[n] = norms[n] + norm if j else norm
            pbuf[n % 2, keys, :] = exps.astype(BF16)

        def gather_values(n, j):
            q, i = tiles[n]
            keys = slice(j * chunk, (j + 1) * chunk)
            out = dot(vt[l, head_rows(i), keys], pbuf[n % 2, keys, :], 1, 0)
            outs[n] = outs[n] + out if j else out

        def attended(n):
            q, i = tiles[n]
            out = outs[n] * (1.0 / norms[n])
            o32[l, head_rows(i), cols(q)] = out
            ob[l, head_rows(i), cols(q)] = out.astype(BF16)
            lse[l, i * 8 : i * 8 + 8, cols(q)] = jnp.broadcast_to(
                peaks[n] * c2 + jnp.log(norms[n]) * LOG2E, (8, W)
            )

        for j in range(T // chunk):
            score(0, j)
        for n in range(len(tiles) + 1):
            for j in range(T // chunk):
                if n + 1 < len(tiles):
                    score(n + 1, j)
                if n:
                    gather_values(n - 1, j)
                if n < len(tiles):
                    weigh(n, j)
            if n:
                attended(n - 1)
            if n == N_HEADS:
                wait_weights(l, 1)
                part(4 * l, 1, dot(wo[l], ob[l, :, cols(1)], 1, 0))
                relay_weights(l, 3)
                relay_weights(l, 2)
                if l + 1 < L:
                    for kind in range(3):
                        send_weights(l + 1, kind)
            if n == N_HEADS + 2:
                pass_column(4 * l)
        part(4 * l, 0, dot(wo[l], ob[l, :, cols(0)], 1, 0))
        attn_out = total_column(4 * l)
        square_sum(attn_out, l, 1)
        middle = xs[l] + attn_out
        xm[l] = middle
        h2[l, :, 0:R] = layer_norm_low(middle, 2 * l + 1)
        spread(h2.at[l])
        run_later()
        wait_weights(l, 2)
        wait_weights(l, 3)

        def feed(k):
            pre = dot(wu[l], h2[l, :, cols(k)], 0, 0)
            cdf = 0.5 * (1.0 + lax.erf(pre * (0.5**0.5)))
            low = (pre * cdf).astype(BF16)
            act[l, :, cols(k)] = low
            slope[l, :, cols(k)] = cdf + pre * (jnp.exp(-0.5 * pre * pre) * 0.3989422804014327)
            part(4 * l + 1, k, dot(wd[l], low, 0, 0))

        have(h2.at[l], 0)
        feed(0)
        relay_near(h2.at[l])
        have(h2.at[l], 1)
        feed(1)
        if l + 1 < L:
            for kind in range(2):
                relay_weights(l + 1, kind)
                cross_weights(l + 1, kind, (0, 1))
            send_weights(l + 1, 3)
            push_weights(l + 1)
        relay_far(h2.at[l])
        have(h2.at[l], 2)
        feed(2)
        pass_near(4 * l + 1)
        have(h2.at[l], 3)
        feed(3)
        pass_across(4 * l + 1)
        pass_joined(4 * l + 1)
        if l + 1 < L:
            for kind in range(2):
                cross_weights(l + 1, kind, (2, 3))
        ffn_out = total(4 * l + 1)
        square_sum(ffn_out, l, 2)
        xs[l + 1] = xm[l] + ffn_out

    last = xs[L]
    final_low = layer_norm_low(last, 2 * L)
    logits = dot(etg[...], final_low, 0, 0)[0:NORM_LANE]
    vocab_row = row_of[0:NORM_LANE]
    logits = jnp.where(vocab_row < VOCAB, logits, NEGATIVE)
    shifted = logits - jnp.max(logits, axis=0, keepdims=True)
    log_probs = shifted - jnp.log(jnp.sum(jnp.exp(shifted), axis=0, keepdims=True))
    target_hot = jnp.where(vocab_row == target_row, 1.0, 0.0)
    token_loss = -jnp.sum(target_hot * log_probs, axis=0, keepdims=True)
    loss = jnp.sum(token_weight * token_loss, axis=1, keepdims=True)
    grad_logits = ((token_weight / weight_sum) * (jnp.exp(log_probs) - target_hot)).astype(BF16)
    grad_logits = jnp.concatenate([grad_logits, jnp.zeros((128 - NORM_LANE, R), BF16)], axis=0)
    grad_final = dot(etg[...], grad_logits, 1, 0)
    sg[...] += dot(final_low, grad_logits, 1, 1)
    grad = layer_norm_back(grad_final, last, 2 * L)

    for l in reversed(range(L)):
        df[l, :, 0:R] = grad.astype(BF16)
        xs[l + 1] = grad
        spread(df.at[l])
        run_later()

        def feed_back(k):
            grad_act = dot(wd[l], df[l, :, cols(k)], 1, 0)
            low = (grad_act * slope[l, :, cols(k)]).astype(BF16)
            du[:, cols(k)] = low
            part(4 * l + 2, k, dot(wu[l], low, 1, 0))

        have(df.at[l], 0)
        feed_back(0)
        relay_near(df.at[l])
        if l + 1 < L:
            for kind in range(2):
                g_cross(l + 1, kind, ((2, s2), (3, s)))
        have(df.at[l], 1)
        feed_back(1)
        relay_far(df.at[l])
        have(df.at[l], 2)
        feed_back(2)
        pass_near(4 * l + 2)
        if l + 1 < L:
            g_mid(l + 1, 0)
            g_mid(l + 1, 1)
            g_third(l + 1)
        have(df.at[l], 3)
        feed_back(3)
        pass_across(4 * l + 2)
        g_first(l, 3, dot(act[l], df[l], 1, 1))
        pass_joined(4 * l + 2)
        if l + 1 < L:
            g_second(l + 1, 0)
            g_second(l + 1, 1)
        g_first(l, 2, dot(h2[l], du[...], 1, 1))
        grad_middle = xs[l + 1] + layer_norm_back(total(4 * l + 2), xm[l], 2 * l + 1)
        xm[l] = grad_middle

        da[l, :, 0:R] = grad_middle.astype(BF16)
        spread_column(da.at[l])
        run_later()
        if l + 1 < L:
            for kind in range(4):
                squares = squares + g_final(l + 1, kind)

        def out_back(k):
            dob[:, cols(k)] = dot(wo[l], da[l, :, cols(k)], 0, 0).astype(BF16)

        have(da.at[l], 0)
        out_back(0)
        relay_column(da.at[l])
        have(da.at[l], 1)
        out_back(1)

        steps = [(i, q, j) for i in range(N_HEADS) for q in range(QT) for j in range(T // chunk)]
        grad_q, grad_k, grad_v = {}, {}, {}

        def back_scores(n):
            i, q, j = steps[n]
            keys = slice(j * chunk, (j + 1) * chunk)
            sbuf[n % 2, 0:chunk, :] = dot(kt[l, head_rows(i), keys], qt[l, head_rows(i), cols(q)], 0, 0)
            sbuf[n % 2, chunk : 2 * chunk, :] = dot(vt[l, head_rows(i), keys], dob[head_rows(i), cols(q)], 0, 0)

        def back_weigh(n):
            i, q, j = steps[n]
            keys = slice(j * chunk, (j + 1) * chunk)
            delta = jnp.sum(
                dob[head_rows(i), cols(q)].astype(F32) * o32[l, head_rows(i), cols(q)],
                axis=0,
                keepdims=True,
            )
            scores = sbuf[n % 2, 0:chunk, :] + jnp.concatenate([bias[keys, :]] * 2, axis=1)
            probs = jnp.exp2(scores * c2 - lse[l, i * 8 : i * 8 + 1, cols(q)])
            pbuf[n % 2, 0:chunk, :] = probs.astype(BF16)
            pbuf[n % 2, chunk : 2 * chunk, :] = (probs * (sbuf[n % 2, chunk : 2 * chunk, :] - delta)).astype(BF16)

        def back_products(n):
            i, q, j = steps[n]
            keys = slice(j * chunk, (j + 1) * chunk)
            probs = pbuf[n % 2, 0:chunk, :]
            grad_scores = pbuf[n % 2, chunk : 2 * chunk, :]
            term = dot(kt[l, head_rows(i), keys], grad_scores, 1, 0)
            grad_q[i, q] = grad_q[i, q] + term if j else term
            term_k = dot(qt[l, head_rows(i), cols(q)], grad_scores, 1, 1)
            term_v = dot(dob[head_rows(i), cols(q)], probs, 1, 1)
            grad_k[i, j] = grad_k[i, j] + term_k if q else term_k
            grad_v[i, j] = grad_v[i, j] + term_v if q else term_v
            if j == T // chunk - 1:
                dqkv[head_rows(i), cols(q)] = (grad_q[i, q] * scale).astype(BF16)
            if q == QT - 1:
                first = HC + i * HEAD_DIM
                dqkv[first : first + HEAD_DIM, keys] = (grad_k[i, j] * scale).astype(BF16)
                first = 2 * HC + i * HEAD_DIM
                dqkv[first : first + HEAD_DIM, keys] = grad_v[i, j].astype(BF16)

        back_scores(0)
        for n in range(len(steps) + 1):
            if n + 1 < len(steps):
                back_scores(n + 1)
            if n:
                back_products(n - 1)
            if n < len(steps):
                back_weigh(n)
            if n == len(steps) // 2:
                g_second(l, 3)
        def project_back(k):
            part(4 * l + 3, k, dot(wq[l], dqkv[:, cols(k)], 1, 0))

        project_back(3)
        project_back(1)
        pass_across(4 * l + 3)
        project_back(2)
        pass_near(4 * l + 3)
        project_back(0)
        g_second(l, 2)
        g_first(l, 0, dot(h1[l], dqkv[...], 1, 1))
        pass_joined(4 * l + 3)
        g_first(l, 1, dot(da[l], ob[l], 1, 1))
        if l == 0:
            for kind in range(2):
                g_cross(0, kind, ((2, s2), (3, s)))
        grad = xm[l] + layer_norm_back(total(4 * l + 3), xs[l], 2 * l)

    run_later()
    high = grad.astype(BF16)
    low = (grad - high.astype(F32)).astype(BF16)
    small = sg[...] + dot(high, token_hot, 1, 1) + dot(low, token_hot, 1, 1)
    small = small.astype(BF16)
    for i in range(B):
        fst[i, :DB] = small[i * DB : (i + 1) * DB]
        fst[i, DB:] = high[i * DB : (i + 1) * DB]

    def send_table(other):
        send(fst.at[other], frx.at[b], f_s.at[other], f_r.at[b], dev(other, h))

    over_blk(send_table)
    frx[b] = fst[b]

    g_mid(0, 0)
    g_mid(0, 1)
    g_third(0)
    squares = squares + g_final(0, 3)
    g_second(0, 0)
    g_second(0, 1)
    squares = squares + g_final(0, 2)
    def table_here(other):
        arrived(frx.at[other], f_s.at[other], f_r.at[other])

    over_blk(table_here)
    value = frx[0, :DB].astype(F32)
    for i in range(1, B):
        value = value + frx[i, :DB].astype(F32)
    hrs[h] = value

    def send_small(k, carry):
        other = lax.rem(h + k, H)
        send(hrs.at[h], hrs.at[h], hx_s.at[other], hx_r.at[h], dev(b, other))
        return carry

    lax.fori_loop(1, H, send_small, 0)
    for j in range(G):
        value = frx[j, DB:].astype(F32)
        for i in range(1, S):
            value = value + frx[i * G + j, DB:].astype(F32)
        hrx[h, j] = value
        squares = squares + lanes_of(value)

    def send_places(k, carry):
        other = lax.rem(h + k, H)
        send(hrx.at[h], hrx.at[h], hx_s.at[H + other], hx_r.at[H + h], dev(b, other))
        return carry

    lax.fori_loop(1, H, send_places, 0)

    def small_here(k, carry):
        other = lax.rem(h + k, H)
        arrived(hrs.at[other], hx_s.at[other], hx_r.at[other])
        return carry

    def places_here(k, carry):
        other = lax.rem(h + k, H)
        arrived(hrx.at[other], hx_s.at[H + other], hx_r.at[H + other])
        return carry

    for kind in (0, 1):
        squares = squares + g_final(0, kind)
    lax.fori_loop(1, H, small_here, 0)
    value = hrs[0]
    for i in range(1, H):
        value = value + hrs[i]
    squares = squares + lanes_of(value) * (1.0 / H)
    small_sum = value

    lane_one = lax.broadcasted_iota(jnp.int32, (1, 128), 1)
    packed = jnp.where(lane_one == 0, loss, 0.0) + jnp.where(lane_one == 1, squares, 0.0)
    for i, stat in stats.items():
        packed = packed + jnp.where(lane_one == 2 + i, stat, 0.0)
    scg[B + h] = jnp.broadcast_to(packed, (8, 128))

    def send_heads(k, carry):
        other = lax.rem(h + k, H)
        src = scg.at[B + h]
        send(src, src, sc_s.at[B + other], sc_r.at[B + h], dev(b, other))
        return carry

    lax.fori_loop(1, H, send_heads, 0)

    def heads_here(k, carry):
        other = lax.rem(h + k, H)
        arrived(scg.at[B + other], sc_s.at[B + other], sc_r.at[B + other])
        return carry

    lax.fori_loop(1, H, heads_here, 0)
    out = scg[B]
    for i in range(1, H):
        out = out + scg[B + i]
    scg[b] = out

    def send_scalars(other):
        send(scg.at[b], scg.at[b], sc_s.at[other], sc_r.at[b], dev(other, h))

    over_blk(send_scalars)
    lax.fori_loop(1, H, places_here, 0)
    ge_out[...] = jnp.concatenate(
        [small_sum[:, :VOCAB]] + [hrx[i, j] for j in range(G) for i in range(H)], axis=1
    )
    norm_rows = small_sum.T
    for i in range(2 * L + 1):
        gn_out[i] = norm_rows[NORM_LANE + 2 * i : NORM_LANE + 2 * i + 2]

    def scalars_here(other):
        arrived(scg.at[other], sc_s.at[other], sc_r.at[other])

    over_blk(scalars_here)
    out = scg[0]
    for i in range(1, B):
        out = out + scg[i]
    lane_eight = lax.broadcasted_iota(jnp.int32, (8, 128), 1)
    tokens = lens[0]
    for i in range(1, S):
        tokens = tokens + lens[i]
    roots = jnp.sqrt(jnp.where(lane_eight == 1, out, out / (tokens.astype(F32) * D)))
    out = jnp.where(lane_eight == 0, out, roots)
    out = jnp.where(lane_eight == 2 + 3 * L, weight_sum, out)
    factor = CLIP_NORM / jnp.maximum(out, CLIP_NORM)
    factor = jnp.sum(jnp.where(lane_eight == 1, factor, 0.0), axis=1, keepdims=True)
    scal_out[...] = jnp.where(lane_eight == 3 + 3 * L, factor, out)

    ag_left()
    for copy in waits:
        copy.wait_send()
    for copies in staged.values():
        for copy in copies:
            copy.wait_send()

    def sent(other):
        for src, ssem, rsem in ((idsg.at[other], id_s, id_r), (frx.at[other], f_s, f_r)):
            pltpu.make_async_remote_copy(src, src, ssem.at[other], rsem.at[other], sibling, MESH).wait_send()

    over_blk(sent)

    def heads_sent(k, carry):
        other = lax.rem(h + k, H)
        for src, m in ((hrs.at[other], other), (hrx.at[other], H + other)):
            pltpu.make_async_remote_copy(src, src, hx_s.at[m], hx_r.at[m], sibling, MESH).wait_send()
        src = scg.at[B + other]
        pltpu.make_async_remote_copy(
            src, src, sc_s.at[B + other], sc_r.at[B + other], sibling, MESH
        ).wait_send()
        return carry

    lax.fori_loop(1, H, heads_sent, 0)

    def scalars_sent(other):
        src = scg.at[other]
        pltpu.make_async_remote_copy(
            src, src, sc_s.at[other], sc_r.at[other], sibling, MESH
        ).wait_send()

    over_blk(scalars_sent)


def fused_step(z, token_ids, targets, masked, lengths, family_weight, embed_table, w_qkv, w_out, w_up, w_down, norm_params):
    B, H, S, G, L, D, DB, HC, R, NC, NR, FU, FD, T = (
        z.B, z.H, z.S, z.G, z.L, z.D, z.DB, z.HC, z.R, z.NC, z.NR, z.FU, z.FD, z.T,
    )
    W = 2 * R
    smem = pl.BlockSpec(memory_space=pltpu.SMEM)
    vmem = pl.BlockSpec(memory_space=pltpu.VMEM)
    dma = pltpu.SemaphoreType.DMA
    scratch = [
        pltpu.VMEM((16, R), jnp.int32),
        pltpu.VMEM((L, DB, 3 * HC), BF16),
        pltpu.VMEM((L, DB, HC), BF16),
        pltpu.VMEM((L, G, DB, FU), BF16),
        pltpu.VMEM((L, FD, D), BF16),
        pltpu.VMEM((G, DB, FU), F32),
        pltpu.VMEM((B, 16, R), jnp.int32),
        pltpu.VMEM((D, 128 + T), BF16),
        pltpu.VMEM((L, D, 3 * HC), BF16),
        pltpu.VMEM((L, D, HC), BF16),
        pltpu.VMEM((L, D, FU), BF16),
        pltpu.VMEM((L, FU, D), BF16),
        pltpu.VMEM((L, D, T), BF16),
        pltpu.VMEM((L, D, T), BF16),
        pltpu.VMEM((L, D, T), BF16),
        pltpu.VMEM((L, D, 2 * W), BF16),
        pltpu.VMEM((L, FU, T), BF16),
        pltpu.VMEM((L, FU, T), F32),
        pltpu.VMEM((FU, T), BF16),
        pltpu.VMEM((L, HC, 2 * W), BF16),
        pltpu.VMEM((L, HC, T), BF16),
        pltpu.VMEM((L, HC, T), BF16),
        pltpu.VMEM((L, HC, 2 * W), F32),
        pltpu.VMEM((L, HC, 2 * W), BF16),
        pltpu.VMEM((HC, 2 * W), BF16),
        pltpu.VMEM((L, 8 * (HC // HEAD_DIM), 2 * W), F32),
        pltpu.VMEM((3 * HC, T), BF16),
        pltpu.VMEM((T, 128), F32),
        pltpu.VMEM((2, T, W), F32),
        pltpu.VMEM((2, T, W), BF16),
        pltpu.VMEM((L + 1, D, R), F32),
        pltpu.VMEM((L, D, R), F32),
        pltpu.VMEM((NC, D, R), F32),
        pltpu.VMEM((NC, D, R), BF16),
        pltpu.VMEM((NC, D, R), BF16),
        pltpu.VMEM((4, NC, D, R), BF16),
        pltpu.VMEM((4, NC, D, R), BF16),
        pltpu.VMEM((D, 128), F32),
        pltpu.VMEM((D, 3 * HC), BF16),
        pltpu.VMEM((D, HC), BF16),
        pltpu.VMEM((D, FU), BF16),
        pltpu.VMEM((FU, D), BF16),
        pltpu.VMEM((L, S + 3, DB, 3 * HC), BF16),
        pltpu.VMEM((L, S + 3, DB, HC), BF16),
        pltpu.VMEM((L, S, G * DB, FU), BF16),
        pltpu.VMEM((L, S, FD, D), BF16),
        pltpu.VMEM((L, DB, FU), BF16),
        pltpu.VMEM((3, DB, 3 * HC), BF16),
        pltpu.VMEM((3, DB, HC), BF16),
        pltpu.VMEM((G * DB, FU), BF16),
        pltpu.VMEM((FD, D), BF16),
        pltpu.VMEM((DB, FU), BF16),
        pltpu.VMEM((B, 2 * DB, 128), BF16),
        pltpu.VMEM((B, 2 * DB, 128), BF16),
        pltpu.VMEM((H, DB, 128), F32),
        pltpu.VMEM((H, G, DB, 128), F32),
        pltpu.VMEM((B + H, 8, 128), F32),
        dma((B,)),
        dma((B,)),
        dma((11,)),
        dma((11,)),
        dma((21 * L,)),
        dma((21 * L,)),
        dma((22,)),
        dma((22,)),
        dma((20,)),
        dma((20,)),
        dma((21 * L,)),
        dma((21 * L,)),
        dma((B,)),
        dma((B,)),
        dma((2 * H,)),
        dma((2 * H,)),
        dma((B + H,)),
        dma((B + H,)),
    ]
    outs = (
        jax.ShapeDtypeStruct((8, 128), F32),
        jax.ShapeDtypeStruct((DB, VOCAB + T), F32),
        jax.ShapeDtypeStruct((L, 3, DB, HC), F32),
        jax.ShapeDtypeStruct((L, HC, DB), F32),
        jax.ShapeDtypeStruct((L, DB, S * G * FD), F32),
        jax.ShapeDtypeStruct((L, FD, D), F32),
        jax.ShapeDtypeStruct((2 * L + 1, 2, DB), F32),
    )
    scal, ge, gq, go, gu, gd, gn = pl.pallas_call(
        functools.partial(step_kernel, z),
        out_shape=outs,
        in_specs=[smem, smem] + [vmem] * 9,
        out_specs=[vmem] * 7,
        scratch_shapes=scratch,
        compiler_params=pltpu.CompilerParams(
            collective_id=0, has_side_effects=True, vmem_limit_bytes=62 << 20
        ),
        name="train_step",
    )(
        lengths,
        family_weight,
        token_ids,
        targets,
        masked,
        embed_table.T,
        w_qkv.transpose(0, 2, 1, 3),
        w_out,
        w_up,
        w_down,
        norm_params,
    )
    return scal, (ge, gq, go, gu, gd, gn)


def update_kernel(layers, scal, *refs):
    groups = len(RATES)
    grads, masters, firsts, seconds = (refs[i * groups : (i + 1) * groups] for i in range(4))
    loss, weights, norm, rms = refs[4 * groups : 4 * groups + 4]
    outs = refs[4 * groups + 4 :]
    loss[0] = scal[0, 0]
    norm[0] = scal[0, 1]
    weights[0] = scal[0, 2 + 3 * layers]
    for i in range(layers):
        for j in range(3):
            rms[i, j] = scal[0, 2 + 3 * i + j]
    factor = scal[0, 3 + 3 * layers]
    for i in range(groups):

        def update(at, i=i):
            first, second, weight = adamw_update(
                masters[i][at],
                firsts[i][at],
                seconds[i][at],
                grads[i][at] * factor,
                RATES[i],
                DECAYS[i],
            )
            for ref, value in zip(outs[4 * i : 4 * i + 4], (first, second, weight, weight)):
                ref[at] = value.astype(ref.dtype)

        for k in range(masters[i].shape[0] if len(masters[i].shape) > 2 else 1):
            update(k if len(masters[i].shape) > 2 else slice(None))


def as_stored(groups):
    embed, qkv, out, up, down, norm = groups
    return embed.T, qkv.transpose(0, 2, 1, 3), out, up, down, norm


def fused_update(layers, scal, grads, masters, firsts, seconds):
    arrays = (*grads, *as_stored(masters), *as_stored(firsts), *as_stored(seconds))
    smem = pl.BlockSpec(memory_space=pltpu.SMEM)
    vmem = pl.BlockSpec(memory_space=pltpu.VMEM)
    shapes = [
        jax.ShapeDtypeStruct(master.shape, dtype)
        for master in as_stored(masters)
        for dtype in (F32, F32, F32, BF16)
    ]
    scalars = [jax.ShapeDtypeStruct((1,), F32)] * 3 + [jax.ShapeDtypeStruct((layers, 3), F32)]
    loss, weights, norm, rms, *new = pl.pallas_call(
        functools.partial(update_kernel, layers),
        out_shape=scalars + shapes,
        in_specs=[smem] + [vmem] * len(arrays),
        out_specs=[smem] * 4 + [vmem] * len(shapes),
        compiler_params=pltpu.CompilerParams(vmem_limit_bytes=62 << 20),
        name="adamw",
    )(scal, *arrays)
    by_kind = [as_stored(new[i::4]) for i in range(4)]
    results = [loss[0], weights[0], norm[0], rms]
    for i in range(len(RATES)):
        results += [kind[i] for kind in by_kind]
    return tuple(results)


def local(
    token_ids,
    targets,
    masked,
    lengths,
    family_weight,
    embed_table,
    w_qkv,
    w_out,
    w_up,
    w_down,
    norm_params,
    embed_first,
    qkv_first,
    out_first,
    up_first,
    down_first,
    norm_first,
    embed_second,
    qkv_second,
    out_second,
    up_second,
    down_second,
    norm_second,
):
    z = Sizes(
        lax.axis_size("blk"),
        lax.axis_size("head"),
        token_ids.shape[0],
        token_ids.shape[1],
        w_qkv.shape,
        w_up.shape,
        w_down.shape,
    )
    masters = (embed_table, w_qkv, w_out, w_up, w_down, norm_params)
    firsts = (embed_first, qkv_first, out_first, up_first, down_first, norm_first)
    seconds = (embed_second, qkv_second, out_second, up_second, down_second, norm_second)
    tokens = (token_ids, targets, masked, lengths, family_weight)
    if z.fused(token_ids.shape[1]):
        scal, grads = fused_step(z, *tokens, *masters)
        return fused_update(LAYERS, scal, grads, masters, firsts, seconds)
    loss_sum, weight_sum, grad_norm, squares, grads = plain_step(*tokens, *masters)
    stream_rms = jnp.sqrt(squares.reshape(LAYERS, 3) / (jnp.sum(lengths).astype(jnp.float32) * D))
    factor = CLIP_NORM / jnp.maximum(grad_norm, CLIP_NORM)
    results = [loss_sum, weight_sum, grad_norm, stream_rms]
    for group_idx in range(6):
        first, second, weight = adamw_update(
            masters[group_idx],
            firsts[group_idx],
            seconds[group_idx],
            grads[group_idx] * factor,
            RATES[group_idx],
            DECAYS[group_idx],
        )
        results += [first, second, weight, weight.astype(jnp.bfloat16)]
    return tuple(results)


def solution(mesh):
    return jax.shard_map(
        local,
        mesh=mesh,
        in_specs=(
            P(None, "blk"),
            P(None, "blk"),
            P(None, "blk"),
            P(),
            P(),
            P(None, "blk"),
            P(None, "blk", None, "head"),
            P(None, "head", "blk"),
            P(None, "blk", "head"),
            P(None, ("head", "blk"), None),
            P(None, None, "blk"),
            P(None, "blk"),
            P(None, "blk", None, "head"),
            P(None, "head", "blk"),
            P(None, "blk", "head"),
            P(None, ("head", "blk"), None),
            P(None, None, "blk"),
            P(None, "blk"),
            P(None, "blk", None, "head"),
            P(None, "head", "blk"),
            P(None, "blk", "head"),
            P(None, ("head", "blk"), None),
            P(None, None, "blk"),
        ),
        out_specs=(
            P(),
            P(),
            P(),
            P(),
            P(None, "blk"),
            P(None, "blk"),
            P(None, "blk"),
            P(None, "blk"),
            P(None, "blk", None, "head"),
            P(None, "blk", None, "head"),
            P(None, "blk", None, "head"),
            P(None, "blk", None, "head"),
            P(None, "head", "blk"),
            P(None, "head", "blk"),
            P(None, "head", "blk"),
            P(None, "head", "blk"),
            P(None, "blk", "head"),
            P(None, "blk", "head"),
            P(None, "blk", "head"),
            P(None, "blk", "head"),
            P(None, ("head", "blk"), None),
            P(None, ("head", "blk"), None),
            P(None, ("head", "blk"), None),
            P(None, ("head", "blk"), None),
            P(None, None, "blk"),
            P(None, None, "blk"),
            P(None, None, "blk"),
            P(None, None, "blk"),
        ),
        check_vma=False,
    )
```

```python
import functools

import jax
import jax.numpy as jnp
from jax import lax
from jax.experimental import pallas as pl
from jax.experimental.pallas import tpu as pltpu
from jax.sharding import PartitionSpec as P

VOCAB = 25
D = 640
HEAD_DIM = 32
LAYERS = 2
STEP = 10


NEGATIVE = -1e30
NORM_EPS = 1e-05
CLIP_NORM = 0.01
BETA_FIRST = 0.9
BETA_SECOND = 0.999
ADAM_EPS = 1e-08
RATES = (0.2, 0.1, 0.5, 0.1, 0.03, 0.5)
DECAYS = (0.1, 0.1, 0.1, 0.1, 0.1, 0.0)
HIGHEST = lax.Precision.HIGHEST


def layer_norm(inputs, gain_row, shift_row):
    centred = inputs - jnp.mean(inputs, axis=-1, keepdims=True)
    spread = jnp.mean(centred * centred, axis=-1, keepdims=True)
    return centred * lax.rsqrt(spread + NORM_EPS) * gain_row + shift_row


def gelu_exact(inputs):
    return jax.nn.gelu(inputs, approximate=False)


def adamw_update(weight, first, second, gradient, rate, decay):
    first = BETA_FIRST * first + (1.0 - BETA_FIRST) * gradient
    second = BETA_SECOND * second + (1.0 - BETA_SECOND) * gradient * gradient
    first_hat = first / (1.0 - BETA_FIRST**STEP)
    second_hat = second / (1.0 - BETA_SECOND**STEP)
    weight = weight - rate * (first_hat / (jnp.sqrt(second_hat) + ADAM_EPS) + decay * weight)
    return (first, second, weight)


def slice_head(tensor, head_index):
    return lax.dynamic_slice_in_dim(tensor, head_index * HEAD_DIM, HEAD_DIM, tensor.ndim - 1)


def join_heads(stacked):
    moved = jnp.moveaxis(stacked, 0, 2)
    return moved.reshape(moved.shape[0], moved.shape[1], -1)


def spread_rows(normed):
    return lax.all_gather(normed, "head", axis=0, tiled=True)


def spread_grads(grad_rows):
    return lax.all_gather(grad_rows, "head", axis=0, tiled=True)


def sum_rows(full_rows, weight, row_share):

    def row_term(row_start, row_count):
        return jnp.dot(full_rows, weight, preferred_element_type=jnp.float32)

    return lax.psum_scatter(
        row_term(jnp.int32(0), row_share * lax.axis_size("head")),
        "head",
        scatter_dimension=0,
        tiled=True,
    )


def sum_grads(full_rows, weight, row_share):

    def row_term(row_start, row_count):
        return jnp.einsum("nc,dc->nd", full_rows, weight, preferred_element_type=jnp.float32)

    return lax.psum_scatter(
        row_term(jnp.int32(0), row_share * lax.axis_size("head")).astype(jnp.bfloat16),
        "head",
        scatter_dimension=0,
        tiled=True,
    ).astype(jnp.float32)


def attend(queries, keys_all, values_all, live_keys):
    local_heads = queries.shape[-1] // HEAD_DIM
    score_scale = HEAD_DIM ** (-0.5)
    live_mask = live_keys[:, None, :]

    def one_head(head_index):
        scores = (
            jnp.einsum(
                "ste,sje->stj",
                slice_head(queries, head_index),
                slice_head(keys_all, head_index),
                preferred_element_type=jnp.float32,
            )
            * score_scale
        )
        masked_scores = jnp.where(live_mask, scores, NEGATIVE)
        row_peak = jnp.max(masked_scores, axis=-1, keepdims=True)
        exp_scores = jnp.exp(masked_scores - row_peak)
        row_total = jnp.sum(exp_scores, axis=-1, keepdims=True)
        attn_probs = (exp_scores / row_total).astype(jnp.bfloat16)
        attended = jnp.einsum(
            "stj,sje->ste",
            attn_probs,
            slice_head(values_all, head_index),
            preferred_element_type=jnp.float32,
        )
        return (attended, (row_peak + jnp.log(row_total))[..., 0])

    outputs, log_totals = lax.map(one_head, jnp.arange(local_heads))
    return (join_heads(outputs), log_totals)


def attend_back(queries, keys_all, values_all, grad_heads, log_totals, live_keys):
    local_heads = queries.shape[-1] // HEAD_DIM
    score_scale = HEAD_DIM ** (-0.5)
    live_mask = live_keys[:, None, :]

    def one_head(head_index):
        query_h = slice_head(queries, head_index)
        key_h = slice_head(keys_all, head_index)
        grad_h = slice_head(grad_heads, head_index)
        scores = (
            jnp.einsum("ste,sje->stj", query_h, key_h, preferred_element_type=jnp.float32)
            * score_scale
        )
        masked_scores = jnp.where(live_mask, scores, NEGATIVE)
        attn_probs = jnp.exp(masked_scores - log_totals[head_index][..., None])
        grad_probs = jnp.einsum(
            "ste,sje->stj",
            grad_h,
            slice_head(values_all, head_index),
            preferred_element_type=jnp.float32,
        )
        row_delta = jnp.sum(attn_probs * grad_probs, axis=-1)
        grad_scores = (attn_probs * (grad_probs - row_delta[..., None])).astype(jnp.bfloat16)
        grad_query = (
            jnp.einsum("stj,sje->ste", grad_scores, key_h, preferred_element_type=jnp.float32)
            * score_scale
        )
        grad_key = (
            jnp.einsum("stj,ste->sje", grad_scores, query_h, preferred_element_type=jnp.float32)
            * score_scale
        )
        grad_value = jnp.einsum(
            "stj,ste->sje",
            attn_probs.astype(jnp.bfloat16),
            grad_h,
            preferred_element_type=jnp.float32,
        )
        return (grad_query, grad_key, grad_value)

    grad_query, grad_key, grad_value = lax.map(one_head, jnp.arange(local_heads))
    grad_key, grad_value = (
        lax.psum_scatter(grad_key, "blk", scatter_dimension=2, tiled=True),
        lax.psum_scatter(grad_value, "blk", scatter_dimension=2, tiled=True),
    )
    return (join_heads(grad_query), join_heads(grad_key), join_heads(grad_value))


def layer_forward(stream, layer_weights, norm_rows, live_keys, row_share):
    w_qkv, w_out, w_up, w_down = layer_weights
    seq_count = live_keys.shape[0]
    normed = layer_norm(stream, norm_rows[0, 0], norm_rows[0, 1]).astype(jnp.bfloat16)
    normed_all = spread_rows(normed)
    packed = jnp.dot(
        normed_all, w_qkv.reshape(w_qkv.shape[0], -1), preferred_element_type=jnp.float32
    ).astype(jnp.bfloat16)
    packed = packed.reshape(seq_count, -1, 3, w_qkv.shape[-1])
    queries, keys_local, values_local = (packed[:, :, 0], packed[:, :, 1], packed[:, :, 2])
    keys_all, values_all = (
        lax.all_gather(keys_local, "blk", axis=1, tiled=True),
        lax.all_gather(values_local, "blk", axis=1, tiled=True),
    )
    attended, log_totals = attend(queries, keys_all, values_all, live_keys)
    attended = attended.astype(jnp.bfloat16).reshape(-1, attended.shape[-1])
    attn_out = sum_rows(attended, w_out, row_share)
    middle = stream + attn_out
    normed_two = layer_norm(middle, norm_rows[1, 0], norm_rows[1, 1]).astype(jnp.bfloat16)
    normed_two_all = spread_rows(normed_two)
    hidden_pre = jnp.dot(normed_two_all, w_up, preferred_element_type=jnp.float32)
    hidden_act = gelu_exact(hidden_pre).astype(jnp.bfloat16)
    ffn_out = sum_rows(hidden_act, w_down, row_share)
    kept = (
        stream,
        middle,
        normed_all,
        queries,
        keys_local,
        values_local,
        keys_all,
        values_all,
        log_totals,
        attended,
        normed_two_all,
        hidden_pre,
    )
    return (middle + ffn_out, attn_out, ffn_out, kept)


def layer_backward(grad_stream, kept, layer_weights, norm_rows, live_keys, row_share):
    (
        stream,
        middle,
        normed_all,
        queries,
        keys_local,
        values_local,
        keys_all,
        values_all,
        log_totals,
        attended,
        normed_two_all,
        hidden_pre,
    ) = kept
    w_qkv, w_out, w_up, w_down = layer_weights
    grad_ffn = spread_grads(grad_stream.astype(jnp.bfloat16))
    hidden_act, gelu_back = jax.vjp(gelu_exact, hidden_pre)
    grad_down = jnp.einsum(
        "nf,nd->fd", hidden_act.astype(jnp.bfloat16), grad_ffn, preferred_element_type=jnp.float32
    )
    grad_act = jnp.einsum("nd,fd->nf", grad_ffn, w_down, preferred_element_type=jnp.float32)
    (grad_pre,) = gelu_back(grad_act)
    grad_pre = grad_pre.astype(jnp.bfloat16)
    grad_up = jnp.einsum("nd,nf->df", normed_two_all, grad_pre, preferred_element_type=jnp.float32)
    grad_normed_two = sum_grads(grad_pre, w_up, row_share)
    _, norm_back_two = jax.vjp(layer_norm, middle, norm_rows[1, 0], norm_rows[1, 1])
    grad_mid, gain_two, shift_two = norm_back_two(grad_normed_two)
    grad_middle = grad_stream + grad_mid
    grad_attn = spread_grads(grad_middle.astype(jnp.bfloat16))
    grad_out_w = jnp.einsum("nf,nd->fd", attended, grad_attn, preferred_element_type=jnp.float32)
    grad_heads = (
        jnp.einsum("nd,fd->nf", grad_attn, w_out, preferred_element_type=jnp.float32)
        .astype(jnp.bfloat16)
        .reshape(queries.shape)
    )
    grad_query, grad_key, grad_value = attend_back(
        queries, keys_all, values_all, grad_heads, log_totals, live_keys
    )
    grad_packed = (
        jnp.stack((grad_query, grad_key, grad_value), axis=2)
        .astype(jnp.bfloat16)
        .reshape(normed_all.shape[0], -1)
    )
    grad_qkv = jnp.einsum(
        "nd,nc->dc", normed_all, grad_packed, preferred_element_type=jnp.float32
    ).reshape(w_qkv.shape)
    grad_normed = sum_grads(grad_packed, w_qkv.reshape(w_qkv.shape[0], -1), row_share)
    _, norm_back_one = jax.vjp(layer_norm, stream, norm_rows[0, 0], norm_rows[0, 1])
    grad_input, gain_one, shift_one = norm_back_one(grad_normed)
    norm_grads = jnp.stack((jnp.stack((gain_one, shift_one)), jnp.stack((gain_two, shift_two))))
    return (grad_middle + grad_input, (grad_qkv, grad_out_w, grad_up, grad_down), norm_grads)


def plain_step(
    token_ids,
    targets,
    masked,
    lengths,
    family_weight,
    embed_table,
    w_qkv,
    w_out,
    w_up,
    w_down,
    norm_params,
):
    blk_count = lax.axis_size("blk")
    head_count = lax.axis_size("head")
    seq_count, blk_tokens = token_ids.shape
    row_share = seq_count * blk_tokens // head_count
    row_first = lax.axis_index("head") * row_share
    blk_start = lax.axis_index("blk") * blk_tokens
    table_all, qkv_all, out_all, up_all, down_all, norm_all = (
        lax.all_gather(embed_table.astype(jnp.bfloat16), "blk", axis=1, tiled=True),
        lax.all_gather(w_qkv.astype(jnp.bfloat16), "blk", axis=1, tiled=True),
        lax.all_gather(w_out.astype(jnp.bfloat16), "blk", axis=2, tiled=True),
        lax.all_gather(w_up.astype(jnp.bfloat16), "blk", axis=1, tiled=True),
        lax.all_gather(w_down.astype(jnp.bfloat16), "blk", axis=1, tiled=True),
        lax.all_gather(norm_params.astype(jnp.bfloat16), "blk", axis=2, tiled=True),
    )
    token_table = table_all[:VOCAB]
    place_rows = lax.dynamic_slice_in_dim(table_all, VOCAB + blk_start, blk_tokens, 0)
    norm_rows = norm_all.astype(jnp.float32)
    live_keys = jnp.arange(blk_tokens * blk_count)[None, :] < lengths[:, None]
    positions = blk_start + jnp.arange(blk_tokens)
    live_local = positions[None, :] < lengths[:, None]
    seq_of_row = (row_first + jnp.arange(row_share)) // blk_tokens
    place_of_row = (row_first + jnp.arange(row_share)) % blk_tokens
    seq_hot = (seq_of_row[:, None] == jnp.arange(seq_count)[None, :]).astype(jnp.float32)
    place_hot = place_of_row[:, None] == jnp.arange(blk_tokens)[None, :]
    row_family = jnp.dot(seq_hot, family_weight, precision=HIGHEST)
    row_live = lax.dynamic_slice_in_dim(live_local.reshape(-1), row_first, row_share, 0).astype(
        jnp.float32
    )[:, None]
    row_ids = lax.dynamic_slice_in_dim(token_ids.reshape(-1), row_first, row_share, 0)
    row_targets = lax.dynamic_slice_in_dim(targets.reshape(-1), row_first, row_share, 0)
    row_masked = lax.dynamic_slice_in_dim(masked.reshape(-1), row_first, row_share, 0)
    token_hot = row_ids[:, None] == jnp.arange(VOCAB)[None, :]
    stream = jnp.dot(
        token_hot.astype(jnp.bfloat16), token_table, preferred_element_type=jnp.float32
    ) + jnp.dot(place_hot.astype(jnp.bfloat16), place_rows, preferred_element_type=jnp.float32)
    layer_stats = []
    kept_all = []
    for layer_idx in range(LAYERS):
        layer_weights = (
            qkv_all[layer_idx],
            out_all[layer_idx],
            up_all[layer_idx],
            down_all[layer_idx],
        )
        layer_stats.append(jnp.sum(stream * stream * row_live))
        stream, attn_out, ffn_out, kept = layer_forward(
            stream,
            layer_weights,
            norm_rows[2 * layer_idx : 2 * layer_idx + 2],
            live_keys,
            row_share,
        )
        layer_stats.append(jnp.sum(attn_out * attn_out * row_live))
        layer_stats.append(jnp.sum(ffn_out * ffn_out * row_live))
        kept_all.append(kept)
    final_low = layer_norm(stream, norm_rows[2 * LAYERS, 0], norm_rows[2 * LAYERS, 1]).astype(
        jnp.bfloat16
    )
    logits = jnp.einsum("nd,vd->nv", final_low, token_table, preferred_element_type=jnp.float32)
    shifted = logits - jnp.max(logits, axis=-1, keepdims=True)
    log_probs = shifted - jnp.log(jnp.sum(jnp.exp(shifted), axis=-1, keepdims=True))
    target_hot = (row_targets[:, None] == jnp.arange(VOCAB)[None, :]).astype(jnp.float32)
    token_loss = -jnp.sum(target_hot * log_probs, axis=1)
    token_weight = row_masked.astype(jnp.float32) * row_family
    loss_sum, weight_sum, squares = lax.psum(
        (jnp.sum(token_weight * token_loss), jnp.sum(token_weight), jnp.stack(layer_stats)),
        ("blk", "head"),
    )
    grad_logits = ((token_weight / weight_sum)[:, None] * (jnp.exp(log_probs) - target_hot)).astype(
        jnp.bfloat16
    )
    grad_final = jnp.einsum(
        "nv,vd->nd", grad_logits, token_table, preferred_element_type=jnp.float32
    )
    grad_table = jnp.einsum("nv,nd->vd", grad_logits, final_low, preferred_element_type=jnp.float32)
    _, final_back = jax.vjp(layer_norm, stream, norm_rows[2 * LAYERS, 0], norm_rows[2 * LAYERS, 1])
    grad_stream, gain_last, shift_last = final_back(grad_final)
    layer_grads = []
    norm_grads = []
    for layer_idx in reversed(range(LAYERS)):
        layer_weights = (
            qkv_all[layer_idx],
            out_all[layer_idx],
            up_all[layer_idx],
            down_all[layer_idx],
        )
        grad_stream, grads_now, norms_now = layer_backward(
            grad_stream,
            kept_all[layer_idx],
            layer_weights,
            norm_rows[2 * layer_idx : 2 * layer_idx + 2],
            live_keys,
            row_share,
        )
        layer_grads.insert(0, grads_now)
        norm_grads.insert(0, norms_now)
    grad_table = grad_table + jnp.dot(
        token_hot.astype(jnp.float32).T, grad_stream, precision=HIGHEST
    )
    grad_place = jnp.dot(place_hot.astype(jnp.float32).T, grad_stream, precision=HIGHEST)
    grad_norms = jnp.concatenate(norm_grads + [jnp.stack((gain_last, shift_last))[None]], axis=0)
    stacked = [
        jnp.stack([layer_entry[slot_idx] for layer_entry in layer_grads]) for slot_idx in range(4)
    ]
    table_sum, place_sum, norm_sum = (
        lax.psum(grad_table.astype(jnp.bfloat16), "head").astype(jnp.float32),
        lax.psum(grad_place.astype(jnp.bfloat16), "head").astype(jnp.float32),
        lax.psum(grad_norms.astype(jnp.bfloat16), "head").astype(jnp.float32),
    )
    place_full = lax.dynamic_update_slice_in_dim(
        jnp.zeros((blk_tokens * blk_count, place_sum.shape[1]), jnp.float32),
        place_sum,
        blk_start,
        0,
    )
    full_table = jnp.concatenate((table_sum, place_full), axis=0)
    reduced = (
        lax.psum_scatter(full_table, "blk", scatter_dimension=1, tiled=True),
        lax.psum_scatter(stacked[0], "blk", scatter_dimension=1, tiled=True),
        lax.psum_scatter(stacked[1], "blk", scatter_dimension=2, tiled=True),
        lax.psum_scatter(stacked[2], "blk", scatter_dimension=1, tiled=True),
        lax.psum_scatter(stacked[3], "blk", scatter_dimension=1, tiled=True),
        lax.psum_scatter(norm_sum, "blk", scatter_dimension=2, tiled=True),
    )
    sharded_squares = sum((jnp.sum(grad_part * grad_part) for grad_part in reduced[1:5]))
    shared_squares = (
        jnp.sum(reduced[0] * reduced[0]) + jnp.sum(reduced[5] * reduced[5])
    ) / head_count
    grad_norm = jnp.sqrt(lax.psum(sharded_squares + shared_squares, ("blk", "head")))
    return loss_sum, weight_sum, grad_norm, squares, reduced


BF16 = jnp.bfloat16
F32 = jnp.float32
MESH = pl.DeviceIdType.MESH
LOG2E = 1.4426950408889634
NORM_LANE = 32


def dot(left, right, left_dim, right_dim):
    return lax.dot_general(
        left, right, (((left_dim,), (right_dim,)), ((), ())), preferred_element_type=F32
    )


class Sizes:
    def __init__(self, blk, head, seqs, blk_tokens, w_qkv, w_up, w_down):
        self.B, self.H, self.S = blk, head, seqs
        self.L = w_qkv[0]
        self.DB = w_qkv[1]
        self.D = self.DB * blk
        self.HC = w_qkv[3]
        self.T = blk_tokens * blk
        self.G = blk // seqs if blk % seqs == 0 else 0
        self.FD = w_down[1]
        if self.G:
            self.NR = self.G * head
            self.R = self.T // self.NR
            self.NC = self.NR // 2
            self.FU = w_up[2] // self.G

    def fused(self, blk_tokens):
        if self.G != 2 or self.S != 4 or self.H % 2 or self.R != blk_tokens or self.R != 128:
            return False
        if self.FU != self.FD * self.S or 3 * self.S > 16 or VOCAB > NORM_LANE:
            return False
        if NORM_LANE + 2 * (2 * self.L + 1) > 128:
            return False
        if any(n % 16 for n in (self.DB, self.HC, self.FD)) or self.D % 128 or self.FU % 128:
            return False
        weights = self.L * 2 * (4 * self.D * self.HC + 2 * self.D * self.FU)
        kept = self.L * self.T * (6 * self.D + 6 * self.FU + 14 * self.HC)
        return 3 * weights + kept + 16 * self.T * self.D + 8 * self.T * 256 * 4 < (60 << 20)


def step_kernel(
    z,
    lens,
    fam,
    tok_in,
    tgt_in,
    msk_in,
    emb_in,
    wq_in,
    wo_in,
    wu_in,
    wd_in,
    norm_in,
    scal_out,
    ge_out,
    gq_out,
    go_out,
    gu_out,
    gd_out,
    gn_out,
    ids,
    wq_own,
    wo_own,
    wu_own,
    wd_own,
    gu_sum,
    idsg,
    tg,
    wq,
    wo,
    wu,
    wd,
    h1,
    h2,
    df,
    da,
    act,
    slope,
    du,
    qt,
    kt,
    vt,
    o32,
    ob,
    dob,
    lse,
    dqkv,
    bias,
    sbuf,
    pbuf,
    xs,
    xm,
    keep,
    psrc,
    csrc,
    srecv,
    rrecv,
    sg,
    stq,
    sto,
    stu,
    std,
    rq,
    ro,
    ru,
    rd,
    rc,
    tq,
    to,
    tu,
    td,
    tc,
    fst,
    frx,
    hrs,
    hrx,
    scg,
    id_s,
    id_r,
    tp_s,
    tp_r,
    w_s,
    w_r,
    ag_s,
    ag_r,
    rs_s,
    rs_r,
    g_s,
    g_r,
    f_s,
    f_r,
    hx_s,
    hx_r,
    sc_s,
    sc_r,
):
    B, H, S, G, L, D, DB, HC, R, NC, NR, FU, FD, T = (
        z.B, z.H, z.S, z.G, z.L, z.D, z.DB, z.HC, z.R, z.NC, z.NR, z.FU, z.FD, z.T,
    )
    N_HEADS = HC // HEAD_DIM
    W = 2 * R
    QT = 2
    scale = HEAD_DIM ** (-0.5)
    c2 = scale * LOG2E
    b = lax.axis_index("blk")
    h = lax.axis_index("head")
    s, g = b // G, b % G
    y, c = h // 2, h % 2
    own_row = g * H + h
    s1 = s + 1 - 2 * (s % 2)
    s2 = (s + 2) % S
    s3 = (s1 + 2) % S

    def dev(blk_i, head_i):
        return (blk_i, head_i)

    sibling = dev(b, y * 2 + 1 - c)

    def peer(k):
        return dev(s * G + (g + k // 2) % G, ((y + k % 2) % 2) * 2 + c)

    waits = []

    def send(src, dst, ssem, rsem, device):
        copy = pltpu.make_async_remote_copy(src, dst, ssem, rsem, device, MESH)
        copy.start()
        return copy

    def arrived(dst, ssem, rsem):
        pltpu.make_async_remote_copy(dst, dst, ssem, rsem, sibling, MESH).wait_recv()

    def over_blk(body):
        def one(k, carry):
            body(lax.rem(b + k, B))
            return carry

        lax.fori_loop(1, B, one, 0)

    def rows(i, n):
        return pl.ds(pl.multiple_of(i * n, 16), n)

    barrier = pltpu.get_barrier_semaphore()

    def greet_blk(other):
        pl.semaphore_signal(barrier, inc=1, device_id=dev(other, h), device_id_type=MESH)

    def greet_head(k, carry):
        pl.semaphore_signal(
            barrier, inc=1, device_id=dev(b, lax.rem(h + k, H)), device_id_type=MESH
        )
        return carry

    over_blk(greet_blk)
    lax.fori_loop(1, H, greet_head, 0)

    table = emb_in[...]
    ids[...] = jnp.zeros((16, R), jnp.int32)
    ids[0:S] = tok_in[...]
    ids[S : 2 * S] = tgt_in[...]
    ids[2 * S : 3 * S] = msk_in[...]
    sg[...] = jnp.zeros((D, 128), F32)
    for i in range(2 * L + 1):
        sg[NORM_LANE + 2 * i : NORM_LANE + 2 * i + 2, 0:DB] = norm_in[i]
    lane_small = lax.broadcasted_iota(jnp.int32, (DB, 128), 1)
    token_part = jnp.where(lane_small < VOCAB, table[:, 0:128], sg[0:128, :].T[0:DB]).astype(BF16)
    own_rows = rows(b, DB)
    tg[own_rows, 0:128] = token_part
    tg[own_rows, 128:] = table[:, VOCAB:].astype(BF16)
    pl.semaphore_wait(barrier, B + H - 2)

    def send_ids(other):
        send(ids, idsg.at[b], id_s.at[other], id_r.at[b], dev(other, h))

    over_blk(send_ids)
    idsg[b] = ids[...]

    lanes_in = pl.ds(pl.multiple_of(c * 512, 128), T + 128 - 512)
    lanes_out = pl.ds(pl.multiple_of(c * (T + 128 - 512), 128), 512)
    lanes_back = pl.ds(pl.multiple_of((1 - c) * (T + 128 - 512), 128), 512)

    def t_send(m, at, cut, device):
        block = tg.at[at, cut]
        waits.append(send(block, block, tp_s.at[m], tp_r.at[m], device))

    def t_here(m, at, cut):
        arrived(tg.at[at, cut], tp_s.at[m], tp_r.at[m])

    def plane_rows(plane, column):
        return rows(plane * G + column, DB)

    t_send(0, own_rows, lanes_in, dev(s2 * G + g, h))
    t_send(1, own_rows, lanes_in, dev(s1 * G + g, h))
    t_send(3, own_rows, lanes_in, dev(s * G + 1 - g, h))

    def w_sem(sems, l, kind, m):
        return sems.at[l * 21 + (-1, 6, 14, 17)[kind] + m]

    def w_ref(l, kind, at):
        return (wq, wo, wu, wd)[kind].at[l, at]

    def shard_rows(kind, plane, column=None):
        if kind == 3:
            return rows(plane, FD)
        return rows(plane * G + (g if column is None else column), DB)

    def w_send(l, kind, m, src, at, device):
        waits.append(
            send(src, w_ref(l, kind, at), w_sem(w_s, l, kind, m), w_sem(w_r, l, kind, m), device)
        )

    def w_arrived(l, kind, m, at):
        arrived(w_ref(l, kind, at), w_sem(w_s, l, kind, m), w_sem(w_r, l, kind, m))

    def round_weights(l, kind):
        at = shard_rows(kind, s)
        if kind == 0:
            wq_own[l] = jnp.concatenate([wq_in[l, i] for i in range(3)], axis=1).astype(BF16)
            wq[l, at] = wq_own[l]
        elif kind == 1:
            wo_own[l] = wo_in[l].T.astype(BF16)
            wo[l, at] = wo_own[l]
        elif kind == 2:
            up = wu_in[l]
            for j in range(G):
                parts = [up[:, (i * G + j) * FD : (i * G + j + 1) * FD] for i in range(S)]
                wu_own[l, j] = jnp.concatenate(parts, axis=1).astype(BF16)
            wu[l, at] = wu_own[l, g]
        else:
            wd_own[l] = wd_in[l].astype(BF16)
            wd[l, at] = wd_own[l]

    def plane_block(kind, plane):
        return rows(plane, FD) if kind == 3 else rows(plane, G * DB)

    def send_weights(l, kind):
        round_weights(l, kind)
        at = shard_rows(kind, s)
        if kind == 2:
            w_send(l, 2, 0, wu_own.at[l, 1 - g], at, dev(s * G + 1 - g, h))
            return
        src = (wq_own, wo_own, None, wd_own)[kind].at[l]
        w_send(l, kind, 1, src, at, dev(s2 * G + g, h))
        w_send(l, kind, 2, src, at, dev(s1 * G + g, h))

    def push_weights(l):
        w_arrived(l, 2, 0, shard_rows(2, s, 1 - g))
        at = plane_block(2, s)
        w_send(l, 2, 1, w_ref(l, 2, at), at, dev(s2 * G + g, h))
        w_send(l, 2, 2, w_ref(l, 2, at), at, dev(s1 * G + g, h))

    def relay_weights(l, kind):
        at = shard_rows(kind, s2) if kind < 2 else plane_block(kind, s2)
        w_arrived(l, kind, 1, at)
        w_send(l, kind, 3, w_ref(l, kind, at), at, dev(s1 * G + g, h))

    def cross_weights(l, kind, planes):
        for m, plane, known in ((4, s, True), (5, s2, True), (6, s1, False), (7, s3, False)):
            if m - 4 in planes:
                at = shard_rows(kind, plane)
                if not known:
                    w_arrived(l, kind, m - 4, at)
                w_send(l, kind, m, w_ref(l, kind, at), at, dev(s * G + 1 - g, h))

    def wait_weights(l, kind):
        if kind < 2:
            for m, plane in ((4, s), (5, s2), (6, s1), (7, s3)):
                w_arrived(l, kind, m, shard_rows(kind, plane, 1 - g))
        else:
            w_arrived(l, kind, 2, plane_block(kind, s1))
            w_arrived(l, kind, 3, plane_block(kind, s3))

    send_weights(0, 0)
    cross_weights(0, 0, (0,))
    send_weights(0, 1)
    at = plane_rows(s2, g)
    t_here(0, at, lanes_in)
    t_send(2, at, lanes_in, dev(s1 * G + g, h))
    t_send(4, at, lanes_in, dev(s * G + 1 - g, h))
    send_weights(0, 2)
    for kind in range(2):
        relay_weights(0, kind)
    send_weights(0, 3)
    for m, plane in ((1, s1), (2, s3)):
        at = plane_rows(plane, g)
        t_here(m, at, lanes_in)
        t_send(m + 4, at, lanes_in, dev(s * G + 1 - g, h))
    cross_weights(0, 0, (1, 2, 3))

    half_rows = (slice(0, D // 2), slice(D // 2, D))

    ag_sent = []

    def ag_send(m, src, dst, device):
        ag_sent.append(send(src, dst, ag_s.at[m], ag_r.at[m], device))

    def ag_here(m, dst):
        arrived(dst, ag_s.at[m], ag_r.at[m])

    def ag_left():
        for copy in ag_sent:
            copy.wait_send()
        ag_sent.clear()

    def block(buf, k, half):
        return buf.at[:, k * W + half * R : k * W + half * R + R]

    def block_half(buf, k, half, i):
        return buf.at[half_rows[i], k * W + half * R : k * W + half * R + R]

    def spread(buf, base=0):
        ag_left()
        ag_send(base + 0, block_half(buf, 0, 0, 0), block_half(buf, 1, 0, 0), peer(1))
        ag_send(base + 1, block_half(buf, 0, 0, 1), block_half(buf, 2, 0, 1), peer(2))
        ag_send(base + 2, block_half(buf, 0, 0, 1), block_half(buf, 1, 0, 1), peer(1))
        ag_send(base + 3, block_half(buf, 0, 0, 0), block_half(buf, 2, 0, 0), peer(2))
        ag_send(base + 4, block(buf, 0, 0), block(buf, 0, 1), sibling)

    def relay_near(buf, base=0):
        ag_here(base + 0, block_half(buf, 1, 0, 0))
        ag_send(base + 5, block_half(buf, 1, 0, 0), block_half(buf, 3, 0, 0), peer(2))
        ag_here(base + 1, block_half(buf, 2, 0, 1))
        ag_send(base + 6, block_half(buf, 2, 0, 1), block_half(buf, 3, 0, 1), peer(1))
        ag_here(base + 2, block_half(buf, 1, 0, 1))
        ag_send(base + 7, block(buf, 1, 0), block(buf, 1, 1), sibling)
        ag_here(base + 3, block_half(buf, 2, 0, 0))
        ag_send(base + 8, block(buf, 2, 0), block(buf, 2, 1), sibling)

    def relay_far(buf, base=0):
        for i in range(2):
            ag_here(base + 5 + i, block_half(buf, 3, 0, i))
            ag_send(base + 9 + i, block_half(buf, 3, 0, i), block_half(buf, 3, 1, i), sibling)

    def have(buf, k, base=0):
        if k == 0:
            ag_here(base + 4, block(buf, 0, 1))
        elif k < 3:
            ag_here(base + 6 + k, block(buf, k, 1))
        else:
            for i in range(2):
                ag_here(base + 9 + i, block_half(buf, 3, 1, i))

    def spread_column(buf):
        ag_left()
        ag_send(0, block(buf, 0, 0), block(buf, 1, 0), peer(1))
        ag_send(4, block(buf, 0, 0), block(buf, 0, 1), sibling)

    def relay_column(buf):
        ag_here(0, block(buf, 1, 0))
        ag_send(7, block(buf, 1, 0), block(buf, 1, 1), sibling)

    staged = {}
    summed_pairs = set()
    half_of = (slice(0, D // 2), slice(D // 2, D))

    def stage(ref, key, value):
        for copy in staged.pop(key, ()):
            copy.wait_send()
        ref[...] = value

    def rs_set(use, m):
        return m + 10 * (use % 4 == 3)

    def rs_send(use, m, src, dst, device):
        n = rs_set(use, m)
        return [send(src, dst, rs_s.at[n], rs_r.at[n], device)]

    def rs_here(use, m, dst):
        n = rs_set(use, m)
        arrived(dst, rs_s.at[n], rs_r.at[n])

    def part(use, k, value):
        keep[k] = value[:, :R]
        stage(psrc.at[k], ("p", k), value[:, R:].astype(BF16))
        staged["p", k] = rs_send(use, k, psrc.at[k], srecv.at[use % 4, k], sibling)

    def pair_sum(use, k, at=slice(0, D)):
        if (use, k) not in summed_pairs:
            summed_pairs.add((use, k))
            rs_here(use, k, srecv.at[use % 4, k])
        return keep[k, at] + srecv[use % 4, k, at].astype(F32)

    def pass_half(use, m, k, i, value, slot, device):
        stage(csrc.at[k, half_of[i]], ("c", k, i), value.astype(BF16))
        staged["c", k, i] = rs_send(
            use, m, csrc.at[k, half_of[i]], rrecv.at[use % 4, slot, half_of[i]], device
        )

    def pass_across(use):
        pass_half(use, 4, 3, 0, pair_sum(use, 3, half_of[0]), 0, peer(1))
        pass_half(use, 5, 3, 1, pair_sum(use, 3, half_of[1]), 0, peer(2))

    def pass_near(use):
        pass_half(use, 6, 1, 0, pair_sum(use, 1, half_of[0]), 1, peer(1))
        pass_half(use, 7, 2, 1, pair_sum(use, 2, half_of[1]), 2, peer(2))

    def pass_joined(use):
        for i, k in ((0, 2), (1, 1)):
            rs_here(use, 4 + i, rrecv.at[use % 4, 0, half_of[i]])
            value = pair_sum(use, k, half_of[i]) + rrecv[use % 4, 0, half_of[i]].astype(F32)
            pass_half(use, 8 + i, k, i, value, k, peer(k))

    def total(use):
        out = pair_sum(use, 0)
        for m, k, i in ((6, 1, 0), (7, 2, 1), (8, 2, 0), (9, 1, 1)):
            rs_here(use, m, rrecv.at[use % 4, k, half_of[i]])
        return out + rrecv[use % 4, 1].astype(F32) + rrecv[use % 4, 2].astype(F32)

    def pass_column(use):
        for i in range(2):
            pass_half(use, 6 + 3 * i, 1, i, pair_sum(use, 1, half_of[i]), 1, peer(1))

    def total_column(use):
        out = pair_sum(use, 0)
        for i in range(2):
            rs_here(use, 6 + 3 * i, rrecv.at[use % 4, 1, half_of[i]])
        return out + rrecv[use % 4, 1].astype(F32)

    def g_sem(sems, l, kind, m):
        return sems.at[l * 21 + (0, 7, 14, 18)[kind] + m]

    def g_send(l, kind, m, src, dst, device):
        return send(src, dst, g_sem(g_s, l, kind, m), g_sem(g_r, l, kind, m), device)

    def g_arrived(l, kind, m, dst):
        arrived(dst, g_sem(g_s, l, kind, m), g_sem(g_r, l, kind, m))

    def g_stage(key, ref, value):
        for copy in staged.pop(key, ()):
            copy.wait_send()
        ref[...] = value.astype(BF16)

    def g_first(l, kind, value):
        src, dst = ((stq, rq), (sto, ro), (stu, ru), (std, rd))[kind]
        g_stage(("g", kind), src, value)
        if kind < 2:
            staged["g", kind] = []
            return
        n = G * DB if kind == 2 else FD
        dst[l, 0] = src[rows(s, n)]
        staged["g", kind] = [
            g_send(l, kind, i, src.at[rows(plane, n)], dst.at[l, 1 + i], dev(s1 * G + g, h))
            for i, plane in ((1, s3), (0, s1))
        ]

    def g_cross(l, kind, planes):
        src, dst = ((stq, rq), (sto, ro))[kind]
        for m, plane in planes:
            staged["g", kind].append(
                g_send(
                    l, kind, m, src.at[rows(plane * G + 1 - g, DB)], dst.at[l, m], dev(s * G + 1 - g, h)
                )
            )

    def g_column(l, kind, m, plane):
        src, dst = ((stq, rq), (sto, ro))[kind]
        return src[rows(plane * G + g, DB)].astype(F32) + dst[l, m].astype(F32)

    def g_mid(l, kind):
        src, dst, tmp = ((stq, rq, tq), (sto, ro, to))[kind]
        g_arrived(l, kind, 0, dst.at[l, 0])
        g_stage(("m", kind, 1), tmp.at[1], g_column(l, kind, 0, s3))
        one = g_send(l, kind, 5, tmp.at[1], dst.at[l, S + 1], dev(s1 * G + g, h))
        g_arrived(l, kind, 1, dst.at[l, 1])
        g_stage(("m", kind, 0), tmp.at[0], g_column(l, kind, 1, s1))
        two = g_send(l, kind, 4, tmp.at[0], dst.at[l, S], dev(s1 * G + g, h))
        staged["m", kind, 1] = [one]
        staged["m", kind, 0] = [two]

    def g_second(l, kind):
        if kind < 2:
            src, dst, tmp = ((stq, rq, tq), (sto, ro, to))[kind]
            g_arrived(l, kind, 2, dst.at[l, 2])
            g_arrived(l, kind, 5, dst.at[l, S + 1])
            g_stage(("s", kind), tmp.at[2], g_column(l, kind, 2, s2) + dst[l, S + 1].astype(F32))
            staged["s", kind] = [g_send(l, kind, 6, tmp.at[2], dst.at[l, S + 2], dev(s2 * G + g, h))]
            return
        src, dst, tmp, n = ((stu, ru, tu, G * DB), (std, rd, td, FD))[kind - 2]
        g_arrived(l, kind, 1, dst.at[l, 2])
        g_stage(("s", kind), tmp, src[rows(s2, n)].astype(F32) + dst[l, 2].astype(F32))
        staged["s", kind] = [g_send(l, kind, 2, tmp, dst.at[l, 3], dev(s2 * G + g, h))]

    def g_third(l):
        g_arrived(l, 2, 0, ru.at[l, 1])
        g_arrived(l, 2, 2, ru.at[l, 3])

        def summed(column):
            at = rows(column, DB)
            return sum(ru[l, i, at, :].astype(F32) for i in (0, 1, 3))

        g_stage(("t", 2), tc, summed(1 - g))
        staged["t", 2] = [g_send(l, 2, 3, tc, rc.at[l], dev(s * G + 1 - g, h))]
        gu_sum[g] = summed(g)

    def lanes_of(v):
        folded = jnp.sum(v * v, axis=0, keepdims=True)
        return jnp.sum(folded, axis=1, keepdims=True) + jnp.zeros((1, 128), F32)

    def g_final(l, kind):
        if kind < 2:
            dst, out = ((rq, gq_out), (ro, go_out))[kind]
            g_arrived(l, kind, 3, dst.at[l, 3])
            g_arrived(l, kind, 4, dst.at[l, S])
            g_arrived(l, kind, 6, dst.at[l, S + 2])
            value = g_column(l, kind, 3, s) + dst[l, S].astype(F32) + dst[l, S + 2].astype(F32)
            if kind == 0:
                for i in range(3):
                    out[l, i] = value[:, i * HC : (i + 1) * HC]
            else:
                out[l] = value.T
        elif kind == 2:
            g_arrived(l, 2, 3, rc.at[l])
            value = rc[l].astype(F32)
            gu_sum[1 - g] = value
            parts = [gu_sum[j, :, i * FD : (i + 1) * FD] for i in range(S) for j in range(G)]
            gu_out[l] = jnp.concatenate(parts, axis=1)
            return lanes_of(gu_sum[0]) + lanes_of(gu_sum[1])
        else:
            g_arrived(l, 3, 0, rd.at[l, 1])
            g_arrived(l, 3, 2, rd.at[l, 3])
            value = sum(rd[l, i].astype(F32) for i in (0, 1, 3))
            gd_out[l] = value
        return lanes_of(value)

    squares = jnp.zeros((1, 128), F32)

    length = lens[s]
    for k in range(NC):
        for half in range(2):
            core = c if half == 0 else 1 - c
            block_row = ((g + k // 2) % G) * H + ((y + k % 2) % 2) * 2 + core
            place = block_row * R + lax.broadcasted_iota(jnp.int32, (R, 128), 0)
            bias[k * W + half * R : k * W + half * R + R, :] = jnp.where(place < length, 0.0, NEGATIVE)
    lane_place = own_row * R + lax.broadcasted_iota(jnp.int32, (1, R), 1)
    live = jnp.where(lane_place < length, 1.0, 0.0)
    dqkv[0:HC, QT * W :] = jnp.zeros((HC, T - QT * W), BF16)
    sg[...] = jnp.zeros((D, 128), F32)
    lane = lax.broadcasted_iota(jnp.int32, (D, 128), 1)
    row_of = lax.broadcasted_iota(jnp.int32, (128, R), 0)

    def ids_here(other):
        arrived(idsg.at[other], id_s.at[other], id_r.at[other])

    over_blk(ids_here)
    t_here(3, plane_rows(s, 1 - g), lanes_in)
    t_send(7, plane_rows(s, 1 - g), lanes_out, sibling)
    for m, plane in ((4, s2), (5, s1), (6, s3)):
        t_here(m, plane_rows(plane, 1 - g), lanes_in)
        t_send(m + 4, rows(plane, G * DB), lanes_out, sibling)
    t_here(7, plane_rows(s, 1 - g), lanes_back)
    for m, plane in ((8, s2), (9, s1), (10, s3)):
        t_here(m, rows(plane, G * DB), lanes_back)
    etg = tg.at[:, 0:128]
    target_row = idsg[own_row, pl.ds(S + s, 1), :]
    mask_row = idsg[own_row, pl.ds(2 * S + s, 1), :].astype(F32)
    token_weight = mask_row * fam[s]
    weight_sum = jnp.zeros((1, 1), F32)
    for i in range(S):
        counts = jnp.zeros((1, R), F32)
        for j in range(B):
            counts = counts + idsg[j, 2 * S + i : 2 * S + i + 1, :].astype(F32)
        weight_sum = weight_sum + jnp.sum(counts, axis=1, keepdims=True) * fam[i]

    def gain(i):
        return etg[:, NORM_LANE + 2 * i : NORM_LANE + 2 * i + 1].astype(F32)

    def shift(i):
        return etg[:, NORM_LANE + 2 * i + 1 : NORM_LANE + 2 * i + 2].astype(F32)

    def normalize(v):
        centred = v - jnp.mean(v, axis=0, keepdims=True)
        rstd = lax.rsqrt(jnp.mean(centred * centred, axis=0, keepdims=True) + NORM_EPS)
        return centred * rstd, rstd

    def layer_norm_low(v, i):
        hat, _ = normalize(v)
        return (hat * gain(i) + shift(i)).astype(BF16)

    later = []

    def run_later():
        for work in later:
            work()
        later.clear()

    def norm_grads(grad, hat, i):
        gain_grad = jnp.sum(grad * hat, axis=1, keepdims=True)
        shift_grad = jnp.sum(grad, axis=1, keepdims=True)
        sg[...] += jnp.where(lane == NORM_LANE + 2 * i, gain_grad, 0.0) + jnp.where(
            lane == NORM_LANE + 2 * i + 1, shift_grad, 0.0
        )

    def layer_norm_back(grad, v, i):
        hat, rstd = normalize(v)
        later.append(lambda: norm_grads(grad, hat, i))
        scaled = grad * gain(i)
        mean_one = jnp.mean(scaled, axis=0, keepdims=True)
        mean_two = jnp.mean(scaled * hat, axis=0, keepdims=True)
        return rstd * (scaled - mean_one - hat * mean_two)

    def square_sum(v, l, i):
        later.append(lambda: stats.__setitem__(3 * l + i, squares_of(v)))

    def squares_of(v):
        return jnp.sum(jnp.sum(v * v, axis=0, keepdims=True) * live, axis=1, keepdims=True)

    slots = list(range(NC))
    near = slots[:2]
    stats = {}
    for k in slots:
        for half in range(2):
            core = c if half == 0 else 1 - c
            block_row = ((g + k // 2) % G) * H + ((y + k % 2) % 2) * 2 + core
            hot = jnp.where(row_of == idsg[block_row, pl.ds(s, 1), :], 1.0, 0.0).astype(BF16)
            place = tg[:, pl.ds(pl.multiple_of(128 + block_row * R, 128), R)]
            start = dot(etg[...], hot, 1, 0) + place.astype(F32)
            h1[0, :, k * W + half * R : k * W + half * R + R] = layer_norm_low(start, 0)
            if k == 0 and half == 0:
                xs[0] = start
                token_hot = hot

    def cols(k):
        return slice(k * W, (k + 1) * W)

    for l in range(L):
        x = xs[l]
        square_sum(x, l, 0)
        if l:
            h1[l, :, 0:R] = layer_norm_low(x, 2 * l)
            spread(h1.at[l], 11)
            run_later()
        else:
            push_weights(0)
            cross_weights(0, 1, (0, 1, 2, 3))
        wait_weights(l, 0)

        def project(k):
            if k in near:
                packed = dot(wq[l], h1[l, :, cols(k)], 0, 0).astype(BF16)
                qt[l, :, cols(k)] = packed[0:HC]
                packed = packed[HC:]
            else:
                packed = dot(wq[l, :, :], h1[l, :, cols(k)], 0, 0).astype(BF16)[HC:]
            kt[l, :, cols(k)] = packed[0:HC]
            vt[l, :, cols(k)] = packed[HC:]

        if l:
            have(h1.at[l], 0, 11)
            project(0)
            relay_near(h1.at[l], 11)
            have(h1.at[l], 1, 11)
            project(1)
            relay_far(h1.at[l], 11)
            have(h1.at[l], 2, 11)
            project(2)
            cross_weights(l, 1, (0, 1, 2, 3))
            have(h1.at[l], 3, 11)
            project(3)
        else:
            for k in slots:
                project(k)

        tiles = [(q, i) for q in (1, 0) for i in range(N_HEADS)]
        chunk = W
        peaks, norms, outs = {}, {}, {}

        def head_rows(i):
            return slice(i * HEAD_DIM, (i + 1) * HEAD_DIM)

        def score(n, j):
            q, i = tiles[n]
            keys = slice(j * chunk, (j + 1) * chunk)
            scores = dot(kt[l, head_rows(i), keys], qt[l, head_rows(i), cols(q)], 0, 0)
            scores = scores + jnp.concatenate([bias[keys, :]] * 2, axis=1)
            sbuf[n % 2, keys, :] = scores
            peak = jnp.max(scores, axis=0, keepdims=True)
            peaks[n] = jnp.maximum(peaks[n], peak) if j else peak

        def weigh(n, j):
            keys = slice(j * chunk, (j + 1) * chunk)
            exps = jnp.exp2((sbuf[n % 2, keys, :] - peaks[n]) * c2)
            norm = jnp.sum(exps, axis=0, keepdims=True)
            norms[n] = norms[n] + norm if j else norm
            pbuf[n % 2, keys, :] = exps.astype(BF16)

        def gather_values(n, j):
            q, i = tiles[n]
            keys = slice(j * chunk, (j + 1) * chunk)
            out = dot(vt[l, head_rows(i), keys], pbuf[n % 2, keys, :], 1, 0)
            outs[n] = outs[n] + out if j else out

        def attended(n):
            q, i = tiles[n]
            out = outs[n] * (1.0 / norms[n])
            o32[l, head_rows(i), cols(q)] = out
            ob[l, head_rows(i), cols(q)] = out.astype(BF16)
            lse[l, i * 8 : i * 8 + 8, cols(q)] = jnp.broadcast_to(
                peaks[n] * c2 + jnp.log(norms[n]) * LOG2E, (8, W)
            )

        for j in range(T // chunk):
            score(0, j)
        for n in range(len(tiles) + 1):
            for j in range(T // chunk):
                if n + 1 < len(tiles):
                    score(n + 1, j)
                if n:
                    gather_values(n - 1, j)
                if n < len(tiles):
                    weigh(n, j)
            if n:
                attended(n - 1)
            if n == 1:
                relay_weights(l, 3)
                relay_weights(l, 2)
                if l + 1 < L:
                    for kind in range(3):
                        send_weights(l + 1, kind)
            if n == N_HEADS:
                wait_weights(l, 1)
                part(4 * l, 1, dot(wo[l], ob[l, :, cols(1)], 1, 0))
            if n == N_HEADS + 2:
                pass_column(4 * l)
        part(4 * l, 0, dot(wo[l], ob[l, :, cols(0)], 1, 0))
        attn_out = total_column(4 * l)
        square_sum(attn_out, l, 1)
        middle = xs[l] + attn_out
        xm[l] = middle
        h2[l, :, 0:R] = layer_norm_low(middle, 2 * l + 1)
        spread(h2.at[l])
        run_later()
        wait_weights(l, 2)
        wait_weights(l, 3)

        def feed(k):
            pre = dot(wu[l], h2[l, :, cols(k)], 0, 0)
            cdf = 0.5 * (1.0 + lax.erf(pre * (0.5**0.5)))
            low = (pre * cdf).astype(BF16)
            act[l, :, cols(k)] = low
            slope[l, :, cols(k)] = cdf + pre * (jnp.exp(-0.5 * pre * pre) * 0.3989422804014327)
            part(4 * l + 1, k, dot(wd[l], low, 0, 0))

        have(h2.at[l], 0)
        feed(0)
        relay_near(h2.at[l])
        have(h2.at[l], 1)
        feed(1)
        if l + 1 < L:
            for kind in range(2):
                relay_weights(l + 1, kind)
            cross_weights(l + 1, 0, (0, 1))
            send_weights(l + 1, 3)
            push_weights(l + 1)
        relay_far(h2.at[l])
        have(h2.at[l], 2)
        feed(2)
        pass_near(4 * l + 1)
        have(h2.at[l], 3)
        feed(3)
        pass_across(4 * l + 1)
        pass_joined(4 * l + 1)
        if l + 1 < L:
            cross_weights(l + 1, 0, (2, 3))
        ffn_out = total(4 * l + 1)
        square_sum(ffn_out, l, 2)
        xs[l + 1] = xm[l] + ffn_out

    last = xs[L]
    final_low = layer_norm_low(last, 2 * L)
    logits = dot(etg[...], final_low, 0, 0)[0:NORM_LANE]
    vocab_row = row_of[0:NORM_LANE]
    logits = jnp.where(vocab_row < VOCAB, logits, NEGATIVE)
    shifted = logits - jnp.max(logits, axis=0, keepdims=True)
    log_probs = shifted - jnp.log(jnp.sum(jnp.exp(shifted), axis=0, keepdims=True))
    target_hot = jnp.where(vocab_row == target_row, 1.0, 0.0)
    token_loss = -jnp.sum(target_hot * log_probs, axis=0, keepdims=True)
    loss = jnp.sum(token_weight * token_loss, axis=1, keepdims=True)
    grad_logits = ((token_weight / weight_sum) * (jnp.exp(log_probs) - target_hot)).astype(BF16)
    grad_logits = jnp.concatenate([grad_logits, jnp.zeros((128 - NORM_LANE, R), BF16)], axis=0)
    grad_final = dot(etg[...], grad_logits, 1, 0)
    sg[...] += dot(final_low, grad_logits, 1, 1)
    grad = layer_norm_back(grad_final, last, 2 * L)

    for l in reversed(range(L)):
        df[l, :, 0:R] = grad.astype(BF16)
        xs[l + 1] = grad
        spread(df.at[l])
        run_later()

        def feed_back(k):
            grad_act = dot(wd[l], df[l, :, cols(k)], 1, 0)
            low = (grad_act * slope[l, :, cols(k)]).astype(BF16)
            du[:, cols(k)] = low
            part(4 * l + 2, k, dot(wu[l], low, 1, 0))

        have(df.at[l], 0)
        feed_back(0)
        relay_near(df.at[l])
        if l + 1 < L:
            g_cross(l + 1, 1, ((0, s3), (1, s1)))
            for kind in range(2):
                g_cross(l + 1, kind, ((2, s2), (3, s)))
        have(df.at[l], 1)
        feed_back(1)
        relay_far(df.at[l])
        have(df.at[l], 2)
        feed_back(2)
        pass_near(4 * l + 2)
        have(df.at[l], 3)
        feed_back(3)
        pass_across(4 * l + 2)
        if l + 1 < L:
            g_mid(l + 1, 0)
            g_mid(l + 1, 1)
            g_third(l + 1)
        g_first(l, 3, dot(act[l], df[l], 1, 1))
        pass_joined(4 * l + 2)
        g_first(l, 2, dot(h2[l], du[...], 1, 1))
        grad_middle = xs[l + 1] + layer_norm_back(total(4 * l + 2), xm[l], 2 * l + 1)
        xm[l] = grad_middle

        da[l, :, 0:R] = grad_middle.astype(BF16)
        spread_column(da.at[l])
        run_later()
        if l + 1 < L:
            g_second(l + 1, 0)
            g_second(l + 1, 1)
            for kind in (2, 3):
                squares = squares + g_final(l + 1, kind)

        def out_back(k):
            dob[:, cols(k)] = dot(wo[l], da[l, :, cols(k)], 0, 0).astype(BF16)

        have(da.at[l], 0)
        out_back(0)
        relay_column(da.at[l])
        have(da.at[l], 1)
        out_back(1)

        steps = [(i, q, j) for i in range(N_HEADS) for q in range(QT) for j in range(T // chunk)]
        grad_q, grad_k, grad_v = {}, {}, {}

        def back_scores(n):
            i, q, j = steps[n]
            keys = slice(j * chunk, (j + 1) * chunk)
            sbuf[n % 2, 0:chunk, :] = dot(kt[l, head_rows(i), keys], qt[l, head_rows(i), cols(q)], 0, 0)
            sbuf[n % 2, chunk : 2 * chunk, :] = dot(vt[l, head_rows(i), keys], dob[head_rows(i), cols(q)], 0, 0)

        def back_weigh(n):
            i, q, j = steps[n]
            keys = slice(j * chunk, (j + 1) * chunk)
            delta = jnp.sum(
                dob[head_rows(i), cols(q)].astype(F32) * o32[l, head_rows(i), cols(q)],
                axis=0,
                keepdims=True,
            )
            scores = sbuf[n % 2, 0:chunk, :] + jnp.concatenate([bias[keys, :]] * 2, axis=1)
            probs = jnp.exp2(scores * c2 - lse[l, i * 8 : i * 8 + 1, cols(q)])
            pbuf[n % 2, 0:chunk, :] = probs.astype(BF16)
            pbuf[n % 2, chunk : 2 * chunk, :] = (probs * (sbuf[n % 2, chunk : 2 * chunk, :] - delta)).astype(BF16)

        def back_products(n):
            i, q, j = steps[n]
            keys = slice(j * chunk, (j + 1) * chunk)
            probs = pbuf[n % 2, 0:chunk, :]
            grad_scores = pbuf[n % 2, chunk : 2 * chunk, :]
            term = dot(kt[l, head_rows(i), keys], grad_scores, 1, 0)
            grad_q[i, q] = grad_q[i, q] + term if j else term
            term_k = dot(qt[l, head_rows(i), cols(q)], grad_scores, 1, 1)
            term_v = dot(dob[head_rows(i), cols(q)], probs, 1, 1)
            grad_k[i, j] = grad_k[i, j] + term_k if q else term_k
            grad_v[i, j] = grad_v[i, j] + term_v if q else term_v
            if j == T // chunk - 1:
                dqkv[head_rows(i), cols(q)] = (grad_q[i, q] * scale).astype(BF16)
            if q == QT - 1:
                first = HC + i * HEAD_DIM
                dqkv[first : first + HEAD_DIM, keys] = (grad_k[i, j] * scale).astype(BF16)
                first = 2 * HC + i * HEAD_DIM
                dqkv[first : first + HEAD_DIM, keys] = grad_v[i, j].astype(BF16)

        back_scores(0)
        for n in range(len(steps) + 1):
            if n + 1 < len(steps):
                back_scores(n + 1)
            if n:
                back_products(n - 1)
            if n < len(steps):
                back_weigh(n)
            if n == len(steps) // 2:
                g_second(l, 3)
        def project_back(k):
            part(4 * l + 3, k, dot(wq[l], dqkv[:, cols(k)], 1, 0))

        project_back(3)
        project_back(1)
        pass_across(4 * l + 3)
        project_back(2)
        pass_near(4 * l + 3)
        project_back(0)
        g_second(l, 2)
        if l + 1 < L:
            for kind in range(2):
                squares = squares + g_final(l + 1, kind)
        g_first(l, 0, dot(h1[l], dqkv[...], 1, 1))
        pass_joined(4 * l + 3)
        g_cross(l, 0, ((0, s3), (1, s1)))
        g_first(l, 1, dot(da[l], ob[l], 1, 1))
        if l == 0:
            g_cross(0, 1, ((0, s3), (1, s1)))
            for kind in range(2):
                g_cross(0, kind, ((2, s2), (3, s)))
        grad = xm[l] + layer_norm_back(total(4 * l + 3), xs[l], 2 * l)

    run_later()
    high = grad.astype(BF16)
    low = (grad - high.astype(F32)).astype(BF16)
    small = sg[...] + dot(high, token_hot, 1, 1) + dot(low, token_hot, 1, 1)
    small = small.astype(BF16)
    for i in range(B):
        fst[i, :DB] = small[i * DB : (i + 1) * DB]
        fst[i, DB:] = high[i * DB : (i + 1) * DB]

    def send_table(other):
        send(fst.at[other], frx.at[b], f_s.at[other], f_r.at[b], dev(other, h))

    over_blk(send_table)
    frx[b] = fst[b]

    g_mid(0, 0)
    g_mid(0, 1)
    g_third(0)
    squares = squares + g_final(0, 3)
    g_second(0, 0)
    g_second(0, 1)
    squares = squares + g_final(0, 2)
    def table_here(other):
        arrived(frx.at[other], f_s.at[other], f_r.at[other])

    over_blk(table_here)
    value = frx[0, :DB].astype(F32)
    for i in range(1, B):
        value = value + frx[i, :DB].astype(F32)
    hrs[h] = value

    def send_small(k, carry):
        other = lax.rem(h + k, H)
        send(hrs.at[h], hrs.at[h], hx_s.at[other], hx_r.at[h], dev(b, other))
        return carry

    lax.fori_loop(1, H, send_small, 0)
    for j in range(G):
        value = frx[j, DB:].astype(F32)
        for i in range(1, S):
            value = value + frx[i * G + j, DB:].astype(F32)
        hrx[h, j] = value
        squares = squares + lanes_of(value)

    def send_places(k, carry):
        other = lax.rem(h + k, H)
        send(hrx.at[h], hrx.at[h], hx_s.at[H + other], hx_r.at[H + h], dev(b, other))
        return carry

    lax.fori_loop(1, H, send_places, 0)

    def small_here(k, carry):
        other = lax.rem(h + k, H)
        arrived(hrs.at[other], hx_s.at[other], hx_r.at[other])
        return carry

    def places_here(k, carry):
        other = lax.rem(h + k, H)
        arrived(hrx.at[other], hx_s.at[H + other], hx_r.at[H + other])
        return carry

    for kind in (0, 1):
        squares = squares + g_final(0, kind)
    lax.fori_loop(1, H, small_here, 0)
    value = hrs[0]
    for i in range(1, H):
        value = value + hrs[i]
    squares = squares + lanes_of(value) * (1.0 / H)
    small_sum = value

    lane_one = lax.broadcasted_iota(jnp.int32, (1, 128), 1)
    packed = jnp.where(lane_one == 0, loss, 0.0) + jnp.where(lane_one == 1, squares, 0.0)
    for i, stat in stats.items():
        packed = packed + jnp.where(lane_one == 2 + i, stat, 0.0)
    scg[B + h] = jnp.broadcast_to(packed, (8, 128))

    def send_heads(k, carry):
        other = lax.rem(h + k, H)
        src = scg.at[B + h]
        send(src, src, sc_s.at[B + other], sc_r.at[B + h], dev(b, other))
        return carry

    lax.fori_loop(1, H, send_heads, 0)

    def heads_here(k, carry):
        other = lax.rem(h + k, H)
        arrived(scg.at[B + other], sc_s.at[B + other], sc_r.at[B + other])
        return carry

    lax.fori_loop(1, H, heads_here, 0)
    out = scg[B]
    for i in range(1, H):
        out = out + scg[B + i]
    scg[b] = out

    def send_scalars(other):
        send(scg.at[b], scg.at[b], sc_s.at[other], sc_r.at[b], dev(other, h))

    over_blk(send_scalars)
    lax.fori_loop(1, H, places_here, 0)
    ge_out[...] = jnp.concatenate(
        [small_sum[:, :VOCAB]] + [hrx[i, j] for j in range(G) for i in range(H)], axis=1
    )
    norm_rows = small_sum.T
    for i in range(2 * L + 1):
        gn_out[i] = norm_rows[NORM_LANE + 2 * i : NORM_LANE + 2 * i + 2]

    def scalars_here(other):
        arrived(scg.at[other], sc_s.at[other], sc_r.at[other])

    over_blk(scalars_here)
    out = scg[0]
    for i in range(1, B):
        out = out + scg[i]
    lane_eight = lax.broadcasted_iota(jnp.int32, (8, 128), 1)
    tokens = lens[0]
    for i in range(1, S):
        tokens = tokens + lens[i]
    roots = jnp.sqrt(jnp.where(lane_eight == 1, out, out / (tokens.astype(F32) * D)))
    out = jnp.where(lane_eight == 0, out, roots)
    out = jnp.where(lane_eight == 2 + 3 * L, weight_sum, out)
    factor = CLIP_NORM / jnp.maximum(out, CLIP_NORM)
    factor = jnp.sum(jnp.where(lane_eight == 1, factor, 0.0), axis=1, keepdims=True)
    scal_out[...] = jnp.where(lane_eight == 3 + 3 * L, factor, out)

    ag_left()
    for copy in waits:
        copy.wait_send()
    for copies in staged.values():
        for copy in copies:
            copy.wait_send()

    def sent(other):
        for src, ssem, rsem in ((idsg.at[other], id_s, id_r), (frx.at[other], f_s, f_r)):
            pltpu.make_async_remote_copy(src, src, ssem.at[other], rsem.at[other], sibling, MESH).wait_send()

    over_blk(sent)

    def heads_sent(k, carry):
        other = lax.rem(h + k, H)
        for src, m in ((hrs.at[other], other), (hrx.at[other], H + other)):
            pltpu.make_async_remote_copy(src, src, hx_s.at[m], hx_r.at[m], sibling, MESH).wait_send()
        src = scg.at[B + other]
        pltpu.make_async_remote_copy(
            src, src, sc_s.at[B + other], sc_r.at[B + other], sibling, MESH
        ).wait_send()
        return carry

    lax.fori_loop(1, H, heads_sent, 0)

    def scalars_sent(other):
        src = scg.at[other]
        pltpu.make_async_remote_copy(
            src, src, sc_s.at[other], sc_r.at[other], sibling, MESH
        ).wait_send()

    over_blk(scalars_sent)


def fused_step(z, token_ids, targets, masked, lengths, family_weight, embed_table, w_qkv, w_out, w_up, w_down, norm_params):
    B, H, S, G, L, D, DB, HC, R, NC, NR, FU, FD, T = (
        z.B, z.H, z.S, z.G, z.L, z.D, z.DB, z.HC, z.R, z.NC, z.NR, z.FU, z.FD, z.T,
    )
    W = 2 * R
    smem = pl.BlockSpec(memory_space=pltpu.SMEM)
    vmem = pl.BlockSpec(memory_space=pltpu.VMEM)
    dma = pltpu.SemaphoreType.DMA
    scratch = [
        pltpu.VMEM((16, R), jnp.int32),
        pltpu.VMEM((L, DB, 3 * HC), BF16),
        pltpu.VMEM((L, DB, HC), BF16),
        pltpu.VMEM((L, G, DB, FU), BF16),
        pltpu.VMEM((L, FD, D), BF16),
        pltpu.VMEM((G, DB, FU), F32),
        pltpu.VMEM((B, 16, R), jnp.int32),
        pltpu.VMEM((D, 128 + T), BF16),
        pltpu.VMEM((L, D, 3 * HC), BF16),
        pltpu.VMEM((L, D, HC), BF16),
        pltpu.VMEM((L, D, FU), BF16),
        pltpu.VMEM((L, FU, D), BF16),
        pltpu.VMEM((L, D, T), BF16),
        pltpu.VMEM((L, D, T), BF16),
        pltpu.VMEM((L, D, T), BF16),
        pltpu.VMEM((L, D, 2 * W), BF16),
        pltpu.VMEM((L, FU, T), BF16),
        pltpu.VMEM((L, FU, T), F32),
        pltpu.VMEM((FU, T), BF16),
        pltpu.VMEM((L, HC, 2 * W), BF16),
        pltpu.VMEM((L, HC, T), BF16),
        pltpu.VMEM((L, HC, T), BF16),
        pltpu.VMEM((L, HC, 2 * W), F32),
        pltpu.VMEM((L, HC, 2 * W), BF16),
        pltpu.VMEM((HC, 2 * W), BF16),
        pltpu.VMEM((L, 8 * (HC // HEAD_DIM), 2 * W), F32),
        pltpu.VMEM((3 * HC, T), BF16),
        pltpu.VMEM((T, 128), F32),
        pltpu.VMEM((2, T, W), F32),
        pltpu.VMEM((2, T, W), BF16),
        pltpu.VMEM((L + 1, D, R), F32),
        pltpu.VMEM((L, D, R), F32),
        pltpu.VMEM((NC, D, R), F32),
        pltpu.VMEM((NC, D, R), BF16),
        pltpu.VMEM((NC, D, R), BF16),
        pltpu.VMEM((4, NC, D, R), BF16),
        pltpu.VMEM((4, NC, D, R), BF16),
        pltpu.VMEM((D, 128), F32),
        pltpu.VMEM((D, 3 * HC), BF16),
        pltpu.VMEM((D, HC), BF16),
        pltpu.VMEM((D, FU), BF16),
        pltpu.VMEM((FU, D), BF16),
        pltpu.VMEM((L, S + 3, DB, 3 * HC), BF16),
        pltpu.VMEM((L, S + 3, DB, HC), BF16),
        pltpu.VMEM((L, S, G * DB, FU), BF16),
        pltpu.VMEM((L, S, FD, D), BF16),
        pltpu.VMEM((L, DB, FU), BF16),
        pltpu.VMEM((3, DB, 3 * HC), BF16),
        pltpu.VMEM((3, DB, HC), BF16),
        pltpu.VMEM((G * DB, FU), BF16),
        pltpu.VMEM((FD, D), BF16),
        pltpu.VMEM((DB, FU), BF16),
        pltpu.VMEM((B, 2 * DB, 128), BF16),
        pltpu.VMEM((B, 2 * DB, 128), BF16),
        pltpu.VMEM((H, DB, 128), F32),
        pltpu.VMEM((H, G, DB, 128), F32),
        pltpu.VMEM((B + H, 8, 128), F32),
        dma((B,)),
        dma((B,)),
        dma((11,)),
        dma((11,)),
        dma((21 * L,)),
        dma((21 * L,)),
        dma((22,)),
        dma((22,)),
        dma((20,)),
        dma((20,)),
        dma((21 * L,)),
        dma((21 * L,)),
        dma((B,)),
        dma((B,)),
        dma((2 * H,)),
        dma((2 * H,)),
        dma((B + H,)),
        dma((B + H,)),
    ]
    outs = (
        jax.ShapeDtypeStruct((8, 128), F32),
        jax.ShapeDtypeStruct((DB, VOCAB + T), F32),
        jax.ShapeDtypeStruct((L, 3, DB, HC), F32),
        jax.ShapeDtypeStruct((L, HC, DB), F32),
        jax.ShapeDtypeStruct((L, DB, S * G * FD), F32),
        jax.ShapeDtypeStruct((L, FD, D), F32),
        jax.ShapeDtypeStruct((2 * L + 1, 2, DB), F32),
    )
    scal, ge, gq, go, gu, gd, gn = pl.pallas_call(
        functools.partial(step_kernel, z),
        out_shape=outs,
        in_specs=[smem, smem] + [vmem] * 9,
        out_specs=[vmem] * 7,
        scratch_shapes=scratch,
        compiler_params=pltpu.CompilerParams(
            collective_id=0, has_side_effects=True, vmem_limit_bytes=62 << 20
        ),
        name="train_step",
    )(
        lengths,
        family_weight,
        token_ids,
        targets,
        masked,
        embed_table.T,
        w_qkv.transpose(0, 2, 1, 3),
        w_out,
        w_up,
        w_down,
        norm_params,
    )
    return scal, (ge, gq, go, gu, gd, gn)


def update_kernel(layers, scal, *refs):
    groups = len(RATES)
    grads, masters, firsts, seconds = (refs[i * groups : (i + 1) * groups] for i in range(4))
    loss, weights, norm, rms = refs[4 * groups : 4 * groups + 4]
    outs = refs[4 * groups + 4 :]
    loss[0] = scal[0, 0]
    norm[0] = scal[0, 1]
    weights[0] = scal[0, 2 + 3 * layers]
    for i in range(layers):
        for j in range(3):
            rms[i, j] = scal[0, 2 + 3 * i + j]
    factor = scal[0, 3 + 3 * layers]
    for i in range(groups):

        def update(at, i=i):
            first, second, weight = adamw_update(
                masters[i][at],
                firsts[i][at],
                seconds[i][at],
                grads[i][at] * factor,
                RATES[i],
                DECAYS[i],
            )
            for ref, value in zip(outs[4 * i : 4 * i + 4], (first, second, weight, weight)):
                ref[at] = value.astype(ref.dtype)

        for k in range(masters[i].shape[0] if len(masters[i].shape) > 2 else 1):
            update(k if len(masters[i].shape) > 2 else slice(None))


def as_stored(groups):
    embed, qkv, out, up, down, norm = groups
    return embed.T, qkv.transpose(0, 2, 1, 3), out, up, down, norm


def fused_update(layers, scal, grads, masters, firsts, seconds):
    arrays = (*grads, *as_stored(masters), *as_stored(firsts), *as_stored(seconds))
    smem = pl.BlockSpec(memory_space=pltpu.SMEM)
    vmem = pl.BlockSpec(memory_space=pltpu.VMEM)
    shapes = [
        jax.ShapeDtypeStruct(master.shape, dtype)
        for master in as_stored(masters)
        for dtype in (F32, F32, F32, BF16)
    ]
    scalars = [jax.ShapeDtypeStruct((1,), F32)] * 3 + [jax.ShapeDtypeStruct((layers, 3), F32)]
    loss, weights, norm, rms, *new = pl.pallas_call(
        functools.partial(update_kernel, layers),
        out_shape=scalars + shapes,
        in_specs=[smem] + [vmem] * len(arrays),
        out_specs=[smem] * 4 + [vmem] * len(shapes),
        compiler_params=pltpu.CompilerParams(vmem_limit_bytes=62 << 20),
        name="adamw",
    )(scal, *arrays)
    by_kind = [as_stored(new[i::4]) for i in range(4)]
    results = [loss[0], weights[0], norm[0], rms]
    for i in range(len(RATES)):
        results += [kind[i] for kind in by_kind]
    return tuple(results)


def local(
    token_ids,
    targets,
    masked,
    lengths,
    family_weight,
    embed_table,
    w_qkv,
    w_out,
    w_up,
    w_down,
    norm_params,
    embed_first,
    qkv_first,
    out_first,
    up_first,
    down_first,
    norm_first,
    embed_second,
    qkv_second,
    out_second,
    up_second,
    down_second,
    norm_second,
):
    z = Sizes(
        lax.axis_size("blk"),
        lax.axis_size("head"),
        token_ids.shape[0],
        token_ids.shape[1],
        w_qkv.shape,
        w_up.shape,
        w_down.shape,
    )
    masters = (embed_table, w_qkv, w_out, w_up, w_down, norm_params)
    firsts = (embed_first, qkv_first, out_first, up_first, down_first, norm_first)
    seconds = (embed_second, qkv_second, out_second, up_second, down_second, norm_second)
    tokens = (token_ids, targets, masked, lengths, family_weight)
    if z.fused(token_ids.shape[1]):
        scal, grads = fused_step(z, *tokens, *masters)
        return fused_update(LAYERS, scal, grads, masters, firsts, seconds)
    loss_sum, weight_sum, grad_norm, squares, grads = plain_step(*tokens, *masters)
    stream_rms = jnp.sqrt(squares.reshape(LAYERS, 3) / (jnp.sum(lengths).astype(jnp.float32) * D))
    factor = CLIP_NORM / jnp.maximum(grad_norm, CLIP_NORM)
    results = [loss_sum, weight_sum, grad_norm, stream_rms]
    for group_idx in range(6):
        first, second, weight = adamw_update(
            masters[group_idx],
            firsts[group_idx],
            seconds[group_idx],
            grads[group_idx] * factor,
            RATES[group_idx],
            DECAYS[group_idx],
        )
        results += [first, second, weight, weight.astype(jnp.bfloat16)]
    return tuple(results)


def solution(mesh):
    return jax.shard_map(
        local,
        mesh=mesh,
        in_specs=(
            P(None, "blk"),
            P(None, "blk"),
            P(None, "blk"),
            P(),
            P(),
            P(None, "blk"),
            P(None, "blk", None, "head"),
            P(None, "head", "blk"),
            P(None, "blk", "head"),
            P(None, ("head", "blk"), None),
            P(None, None, "blk"),
            P(None, "blk"),
            P(None, "blk", None, "head"),
            P(None, "head", "blk"),
            P(None, "blk", "head"),
            P(None, ("head", "blk"), None),
            P(None, None, "blk"),
            P(None, "blk"),
            P(None, "blk", None, "head"),
            P(None, "head", "blk"),
            P(None, "blk", "head"),
            P(None, ("head", "blk"), None),
            P(None, None, "blk"),
        ),
        out_specs=(
            P(),
            P(),
            P(),
            P(),
            P(None, "blk"),
            P(None, "blk"),
            P(None, "blk"),
            P(None, "blk"),
            P(None, "blk", None, "head"),
            P(None, "blk", None, "head"),
            P(None, "blk", None, "head"),
            P(None, "blk", None, "head"),
            P(None, "head", "blk"),
            P(None, "head", "blk"),
            P(None, "head", "blk"),
            P(None, "head", "blk"),
            P(None, "blk", "head"),
            P(None, "blk", "head"),
            P(None, "blk", "head"),
            P(None, "blk", "head"),
            P(None, ("head", "blk"), None),
            P(None, ("head", "blk"), None),
            P(None, ("head", "blk"), None),
            P(None, ("head", "blk"), None),
            P(None, None, "blk"),
            P(None, None, "blk"),
            P(None, None, "blk"),
            P(None, None, "blk"),
        ),
        check_vma=False,
    )
```

```python
import functools

import jax
import jax.numpy as jnp
from jax import lax
from jax.experimental import pallas as pl
from jax.experimental.pallas import tpu as pltpu
from jax.sharding import PartitionSpec as P

VOCAB = 25
D = 640
HEAD_DIM = 32
LAYERS = 2
STEP = 10


NEGATIVE = -1e30
NORM_EPS = 1e-05
CLIP_NORM = 0.01
BETA_FIRST = 0.9
BETA_SECOND = 0.999
ADAM_EPS = 1e-08
RATES = (0.2, 0.1, 0.5, 0.1, 0.03, 0.5)
DECAYS = (0.1, 0.1, 0.1, 0.1, 0.1, 0.0)
HIGHEST = lax.Precision.HIGHEST


def layer_norm(inputs, gain_row, shift_row):
    centred = inputs - jnp.mean(inputs, axis=-1, keepdims=True)
    spread = jnp.mean(centred * centred, axis=-1, keepdims=True)
    return centred * lax.rsqrt(spread + NORM_EPS) * gain_row + shift_row


def gelu_exact(inputs):
    return jax.nn.gelu(inputs, approximate=False)


def adamw_update(weight, first, second, gradient, rate, decay):
    first = BETA_FIRST * first + (1.0 - BETA_FIRST) * gradient
    second = BETA_SECOND * second + (1.0 - BETA_SECOND) * gradient * gradient
    first_hat = first / (1.0 - BETA_FIRST**STEP)
    second_hat = second / (1.0 - BETA_SECOND**STEP)
    weight = weight - rate * (first_hat / (jnp.sqrt(second_hat) + ADAM_EPS) + decay * weight)
    return (first, second, weight)


def slice_head(tensor, head_index):
    return lax.dynamic_slice_in_dim(tensor, head_index * HEAD_DIM, HEAD_DIM, tensor.ndim - 1)


def join_heads(stacked):
    moved = jnp.moveaxis(stacked, 0, 2)
    return moved.reshape(moved.shape[0], moved.shape[1], -1)


def spread_rows(normed):
    return lax.all_gather(normed, "head", axis=0, tiled=True)


def spread_grads(grad_rows):
    return lax.all_gather(grad_rows, "head", axis=0, tiled=True)


def sum_rows(full_rows, weight, row_share):

    def row_term(row_start, row_count):
        return jnp.dot(full_rows, weight, preferred_element_type=jnp.float32)

    return lax.psum_scatter(
        row_term(jnp.int32(0), row_share * lax.axis_size("head")),
        "head",
        scatter_dimension=0,
        tiled=True,
    )


def sum_grads(full_rows, weight, row_share):

    def row_term(row_start, row_count):
        return jnp.einsum("nc,dc->nd", full_rows, weight, preferred_element_type=jnp.float32)

    return lax.psum_scatter(
        row_term(jnp.int32(0), row_share * lax.axis_size("head")).astype(jnp.bfloat16),
        "head",
        scatter_dimension=0,
        tiled=True,
    ).astype(jnp.float32)


def attend(queries, keys_all, values_all, live_keys):
    local_heads = queries.shape[-1] // HEAD_DIM
    score_scale = HEAD_DIM ** (-0.5)
    live_mask = live_keys[:, None, :]

    def one_head(head_index):
        scores = (
            jnp.einsum(
                "ste,sje->stj",
                slice_head(queries, head_index),
                slice_head(keys_all, head_index),
                preferred_element_type=jnp.float32,
            )
            * score_scale
        )
        masked_scores = jnp.where(live_mask, scores, NEGATIVE)
        row_peak = jnp.max(masked_scores, axis=-1, keepdims=True)
        exp_scores = jnp.exp(masked_scores - row_peak)
        row_total = jnp.sum(exp_scores, axis=-1, keepdims=True)
        attn_probs = (exp_scores / row_total).astype(jnp.bfloat16)
        attended = jnp.einsum(
            "stj,sje->ste",
            attn_probs,
            slice_head(values_all, head_index),
            preferred_element_type=jnp.float32,
        )
        return (attended, (row_peak + jnp.log(row_total))[..., 0])

    outputs, log_totals = lax.map(one_head, jnp.arange(local_heads))
    return (join_heads(outputs), log_totals)


def attend_back(queries, keys_all, values_all, grad_heads, log_totals, live_keys):
    local_heads = queries.shape[-1] // HEAD_DIM
    score_scale = HEAD_DIM ** (-0.5)
    live_mask = live_keys[:, None, :]

    def one_head(head_index):
        query_h = slice_head(queries, head_index)
        key_h = slice_head(keys_all, head_index)
        grad_h = slice_head(grad_heads, head_index)
        scores = (
            jnp.einsum("ste,sje->stj", query_h, key_h, preferred_element_type=jnp.float32)
            * score_scale
        )
        masked_scores = jnp.where(live_mask, scores, NEGATIVE)
        attn_probs = jnp.exp(masked_scores - log_totals[head_index][..., None])
        grad_probs = jnp.einsum(
            "ste,sje->stj",
            grad_h,
            slice_head(values_all, head_index),
            preferred_element_type=jnp.float32,
        )
        row_delta = jnp.sum(attn_probs * grad_probs, axis=-1)
        grad_scores = (attn_probs * (grad_probs - row_delta[..., None])).astype(jnp.bfloat16)
        grad_query = (
            jnp.einsum("stj,sje->ste", grad_scores, key_h, preferred_element_type=jnp.float32)
            * score_scale
        )
        grad_key = (
            jnp.einsum("stj,ste->sje", grad_scores, query_h, preferred_element_type=jnp.float32)
            * score_scale
        )
        grad_value = jnp.einsum(
            "stj,ste->sje",
            attn_probs.astype(jnp.bfloat16),
            grad_h,
            preferred_element_type=jnp.float32,
        )
        return (grad_query, grad_key, grad_value)

    grad_query, grad_key, grad_value = lax.map(one_head, jnp.arange(local_heads))
    grad_key, grad_value = (
        lax.psum_scatter(grad_key, "blk", scatter_dimension=2, tiled=True),
        lax.psum_scatter(grad_value, "blk", scatter_dimension=2, tiled=True),
    )
    return (join_heads(grad_query), join_heads(grad_key), join_heads(grad_value))


def layer_forward(stream, layer_weights, norm_rows, live_keys, row_share):
    w_qkv, w_out, w_up, w_down = layer_weights
    seq_count = live_keys.shape[0]
    normed = layer_norm(stream, norm_rows[0, 0], norm_rows[0, 1]).astype(jnp.bfloat16)
    normed_all = spread_rows(normed)
    packed = jnp.dot(
        normed_all, w_qkv.reshape(w_qkv.shape[0], -1), preferred_element_type=jnp.float32
    ).astype(jnp.bfloat16)
    packed = packed.reshape(seq_count, -1, 3, w_qkv.shape[-1])
    queries, keys_local, values_local = (packed[:, :, 0], packed[:, :, 1], packed[:, :, 2])
    keys_all, values_all = (
        lax.all_gather(keys_local, "blk", axis=1, tiled=True),
        lax.all_gather(values_local, "blk", axis=1, tiled=True),
    )
    attended, log_totals = attend(queries, keys_all, values_all, live_keys)
    attended = attended.astype(jnp.bfloat16).reshape(-1, attended.shape[-1])
    attn_out = sum_rows(attended, w_out, row_share)
    middle = stream + attn_out
    normed_two = layer_norm(middle, norm_rows[1, 0], norm_rows[1, 1]).astype(jnp.bfloat16)
    normed_two_all = spread_rows(normed_two)
    hidden_pre = jnp.dot(normed_two_all, w_up, preferred_element_type=jnp.float32)
    hidden_act = gelu_exact(hidden_pre).astype(jnp.bfloat16)
    ffn_out = sum_rows(hidden_act, w_down, row_share)
    kept = (
        stream,
        middle,
        normed_all,
        queries,
        keys_local,
        values_local,
        keys_all,
        values_all,
        log_totals,
        attended,
        normed_two_all,
        hidden_pre,
    )
    return (middle + ffn_out, attn_out, ffn_out, kept)


def layer_backward(grad_stream, kept, layer_weights, norm_rows, live_keys, row_share):
    (
        stream,
        middle,
        normed_all,
        queries,
        keys_local,
        values_local,
        keys_all,
        values_all,
        log_totals,
        attended,
        normed_two_all,
        hidden_pre,
    ) = kept
    w_qkv, w_out, w_up, w_down = layer_weights
    grad_ffn = spread_grads(grad_stream.astype(jnp.bfloat16))
    hidden_act, gelu_back = jax.vjp(gelu_exact, hidden_pre)
    grad_down = jnp.einsum(
        "nf,nd->fd", hidden_act.astype(jnp.bfloat16), grad_ffn, preferred_element_type=jnp.float32
    )
    grad_act = jnp.einsum("nd,fd->nf", grad_ffn, w_down, preferred_element_type=jnp.float32)
    (grad_pre,) = gelu_back(grad_act)
    grad_pre = grad_pre.astype(jnp.bfloat16)
    grad_up = jnp.einsum("nd,nf->df", normed_two_all, grad_pre, preferred_element_type=jnp.float32)
    grad_normed_two = sum_grads(grad_pre, w_up, row_share)
    _, norm_back_two = jax.vjp(layer_norm, middle, norm_rows[1, 0], norm_rows[1, 1])
    grad_mid, gain_two, shift_two = norm_back_two(grad_normed_two)
    grad_middle = grad_stream + grad_mid
    grad_attn = spread_grads(grad_middle.astype(jnp.bfloat16))
    grad_out_w = jnp.einsum("nf,nd->fd", attended, grad_attn, preferred_element_type=jnp.float32)
    grad_heads = (
        jnp.einsum("nd,fd->nf", grad_attn, w_out, preferred_element_type=jnp.float32)
        .astype(jnp.bfloat16)
        .reshape(queries.shape)
    )
    grad_query, grad_key, grad_value = attend_back(
        queries, keys_all, values_all, grad_heads, log_totals, live_keys
    )
    grad_packed = (
        jnp.stack((grad_query, grad_key, grad_value), axis=2)
        .astype(jnp.bfloat16)
        .reshape(normed_all.shape[0], -1)
    )
    grad_qkv = jnp.einsum(
        "nd,nc->dc", normed_all, grad_packed, preferred_element_type=jnp.float32
    ).reshape(w_qkv.shape)
    grad_normed = sum_grads(grad_packed, w_qkv.reshape(w_qkv.shape[0], -1), row_share)
    _, norm_back_one = jax.vjp(layer_norm, stream, norm_rows[0, 0], norm_rows[0, 1])
    grad_input, gain_one, shift_one = norm_back_one(grad_normed)
    norm_grads = jnp.stack((jnp.stack((gain_one, shift_one)), jnp.stack((gain_two, shift_two))))
    return (grad_middle + grad_input, (grad_qkv, grad_out_w, grad_up, grad_down), norm_grads)


def plain_step(
    token_ids,
    targets,
    masked,
    lengths,
    family_weight,
    embed_table,
    w_qkv,
    w_out,
    w_up,
    w_down,
    norm_params,
):
    blk_count = lax.axis_size("blk")
    head_count = lax.axis_size("head")
    seq_count, blk_tokens = token_ids.shape
    row_share = seq_count * blk_tokens // head_count
    row_first = lax.axis_index("head") * row_share
    blk_start = lax.axis_index("blk") * blk_tokens
    table_all, qkv_all, out_all, up_all, down_all, norm_all = (
        lax.all_gather(embed_table.astype(jnp.bfloat16), "blk", axis=1, tiled=True),
        lax.all_gather(w_qkv.astype(jnp.bfloat16), "blk", axis=1, tiled=True),
        lax.all_gather(w_out.astype(jnp.bfloat16), "blk", axis=2, tiled=True),
        lax.all_gather(w_up.astype(jnp.bfloat16), "blk", axis=1, tiled=True),
        lax.all_gather(w_down.astype(jnp.bfloat16), "blk", axis=1, tiled=True),
        lax.all_gather(norm_params.astype(jnp.bfloat16), "blk", axis=2, tiled=True),
    )
    token_table = table_all[:VOCAB]
    place_rows = lax.dynamic_slice_in_dim(table_all, VOCAB + blk_start, blk_tokens, 0)
    norm_rows = norm_all.astype(jnp.float32)
    live_keys = jnp.arange(blk_tokens * blk_count)[None, :] < lengths[:, None]
    positions = blk_start + jnp.arange(blk_tokens)
    live_local = positions[None, :] < lengths[:, None]
    seq_of_row = (row_first + jnp.arange(row_share)) // blk_tokens
    place_of_row = (row_first + jnp.arange(row_share)) % blk_tokens
    seq_hot = (seq_of_row[:, None] == jnp.arange(seq_count)[None, :]).astype(jnp.float32)
    place_hot = place_of_row[:, None] == jnp.arange(blk_tokens)[None, :]
    row_family = jnp.dot(seq_hot, family_weight, precision=HIGHEST)
    row_live = lax.dynamic_slice_in_dim(live_local.reshape(-1), row_first, row_share, 0).astype(
        jnp.float32
    )[:, None]
    row_ids = lax.dynamic_slice_in_dim(token_ids.reshape(-1), row_first, row_share, 0)
    row_targets = lax.dynamic_slice_in_dim(targets.reshape(-1), row_first, row_share, 0)
    row_masked = lax.dynamic_slice_in_dim(masked.reshape(-1), row_first, row_share, 0)
    token_hot = row_ids[:, None] == jnp.arange(VOCAB)[None, :]
    stream = jnp.dot(
        token_hot.astype(jnp.bfloat16), token_table, preferred_element_type=jnp.float32
    ) + jnp.dot(place_hot.astype(jnp.bfloat16), place_rows, preferred_element_type=jnp.float32)
    layer_stats = []
    kept_all = []
    for layer_idx in range(LAYERS):
        layer_weights = (
            qkv_all[layer_idx],
            out_all[layer_idx],
            up_all[layer_idx],
            down_all[layer_idx],
        )
        layer_stats.append(jnp.sum(stream * stream * row_live))
        stream, attn_out, ffn_out, kept = layer_forward(
            stream,
            layer_weights,
            norm_rows[2 * layer_idx : 2 * layer_idx + 2],
            live_keys,
            row_share,
        )
        layer_stats.append(jnp.sum(attn_out * attn_out * row_live))
        layer_stats.append(jnp.sum(ffn_out * ffn_out * row_live))
        kept_all.append(kept)
    final_low = layer_norm(stream, norm_rows[2 * LAYERS, 0], norm_rows[2 * LAYERS, 1]).astype(
        jnp.bfloat16
    )
    logits = jnp.einsum("nd,vd->nv", final_low, token_table, preferred_element_type=jnp.float32)
    shifted = logits - jnp.max(logits, axis=-1, keepdims=True)
    log_probs = shifted - jnp.log(jnp.sum(jnp.exp(shifted), axis=-1, keepdims=True))
    target_hot = (row_targets[:, None] == jnp.arange(VOCAB)[None, :]).astype(jnp.float32)
    token_loss = -jnp.sum(target_hot * log_probs, axis=1)
    token_weight = row_masked.astype(jnp.float32) * row_family
    loss_sum, weight_sum, squares = lax.psum(
        (jnp.sum(token_weight * token_loss), jnp.sum(token_weight), jnp.stack(layer_stats)),
        ("blk", "head"),
    )
    grad_logits = ((token_weight / weight_sum)[:, None] * (jnp.exp(log_probs) - target_hot)).astype(
        jnp.bfloat16
    )
    grad_final = jnp.einsum(
        "nv,vd->nd", grad_logits, token_table, preferred_element_type=jnp.float32
    )
    grad_table = jnp.einsum("nv,nd->vd", grad_logits, final_low, preferred_element_type=jnp.float32)
    _, final_back = jax.vjp(layer_norm, stream, norm_rows[2 * LAYERS, 0], norm_rows[2 * LAYERS, 1])
    grad_stream, gain_last, shift_last = final_back(grad_final)
    layer_grads = []
    norm_grads = []
    for layer_idx in reversed(range(LAYERS)):
        layer_weights = (
            qkv_all[layer_idx],
            out_all[layer_idx],
            up_all[layer_idx],
            down_all[layer_idx],
        )
        grad_stream, grads_now, norms_now = layer_backward(
            grad_stream,
            kept_all[layer_idx],
            layer_weights,
            norm_rows[2 * layer_idx : 2 * layer_idx + 2],
            live_keys,
            row_share,
        )
        layer_grads.insert(0, grads_now)
        norm_grads.insert(0, norms_now)
    grad_table = grad_table + jnp.dot(
        token_hot.astype(jnp.float32).T, grad_stream, precision=HIGHEST
    )
    grad_place = jnp.dot(place_hot.astype(jnp.float32).T, grad_stream, precision=HIGHEST)
    grad_norms = jnp.concatenate(norm_grads + [jnp.stack((gain_last, shift_last))[None]], axis=0)
    stacked = [
        jnp.stack([layer_entry[slot_idx] for layer_entry in layer_grads]) for slot_idx in range(4)
    ]
    table_sum, place_sum, norm_sum = (
        lax.psum(grad_table.astype(jnp.bfloat16), "head").astype(jnp.float32),
        lax.psum(grad_place.astype(jnp.bfloat16), "head").astype(jnp.float32),
        lax.psum(grad_norms.astype(jnp.bfloat16), "head").astype(jnp.float32),
    )
    place_full = lax.dynamic_update_slice_in_dim(
        jnp.zeros((blk_tokens * blk_count, place_sum.shape[1]), jnp.float32),
        place_sum,
        blk_start,
        0,
    )
    full_table = jnp.concatenate((table_sum, place_full), axis=0)
    reduced = (
        lax.psum_scatter(full_table, "blk", scatter_dimension=1, tiled=True),
        lax.psum_scatter(stacked[0], "blk", scatter_dimension=1, tiled=True),
        lax.psum_scatter(stacked[1], "blk", scatter_dimension=2, tiled=True),
        lax.psum_scatter(stacked[2], "blk", scatter_dimension=1, tiled=True),
        lax.psum_scatter(stacked[3], "blk", scatter_dimension=1, tiled=True),
        lax.psum_scatter(norm_sum, "blk", scatter_dimension=2, tiled=True),
    )
    sharded_squares = sum((jnp.sum(grad_part * grad_part) for grad_part in reduced[1:5]))
    shared_squares = (
        jnp.sum(reduced[0] * reduced[0]) + jnp.sum(reduced[5] * reduced[5])
    ) / head_count
    grad_norm = jnp.sqrt(lax.psum(sharded_squares + shared_squares, ("blk", "head")))
    return loss_sum, weight_sum, grad_norm, squares, reduced


BF16 = jnp.bfloat16
F32 = jnp.float32
MESH = pl.DeviceIdType.MESH
LOG2E = 1.4426950408889634
NORM_LANE = 32


def dot(left, right, left_dim, right_dim):
    return lax.dot_general(
        left, right, (((left_dim,), (right_dim,)), ((), ())), preferred_element_type=F32
    )


class Sizes:
    def __init__(self, blk, head, seqs, blk_tokens, w_qkv, w_up, w_down):
        self.B, self.H, self.S = blk, head, seqs
        self.L = w_qkv[0]
        self.DB = w_qkv[1]
        self.D = self.DB * blk
        self.HC = w_qkv[3]
        self.T = blk_tokens * blk
        self.G = blk // seqs if blk % seqs == 0 else 0
        self.FD = w_down[1]
        if self.G:
            self.NR = self.G * head
            self.R = self.T // self.NR
            self.NC = self.NR // 2
            self.FU = w_up[2] // self.G

    def fused(self, blk_tokens):
        if self.G != 2 or self.S != 4 or self.H % 2 or self.R != blk_tokens or self.R != 128:
            return False
        if self.FU != self.FD * self.S or 3 * self.S > 16 or VOCAB > NORM_LANE:
            return False
        if NORM_LANE + 2 * (2 * self.L + 1) > 128:
            return False
        if any(n % 16 for n in (self.DB, self.HC, self.FD)) or self.D % 128 or self.FU % 128:
            return False
        weights = self.L * 2 * (4 * self.D * self.HC + 2 * self.D * self.FU)
        kept = self.L * self.T * (6 * self.D + 6 * self.FU + 14 * self.HC)
        return 3 * weights + kept + 16 * self.T * self.D + 8 * self.T * 256 * 4 < (60 << 20)


def step_kernel(
    z,
    lens,
    fam,
    tok_in,
    tgt_in,
    msk_in,
    emb_in,
    wq_in,
    wo_in,
    wu_in,
    wd_in,
    norm_in,
    scal_out,
    ge_out,
    gq_out,
    go_out,
    gu_out,
    gd_out,
    gn_out,
    gq_made,
    go_made,
    gu_made,
    gd_made,
    out_sem,
    ids,
    wq_own,
    wo_own,
    wu_own,
    wd_own,
    gu_sum,
    idsg,
    tg,
    wq,
    wo,
    wu,
    wd,
    h1,
    h2,
    df,
    da,
    act,
    slope,
    du,
    qt,
    kt,
    vt,
    o32,
    ob,
    dob,
    lse,
    dqkv,
    bias,
    sbuf,
    pbuf,
    xs,
    xm,
    keep,
    psrc,
    csrc,
    srecv,
    rrecv,
    sg,
    stq,
    sto,
    stu,
    std,
    rq,
    ro,
    ru,
    rd,
    rc,
    tq,
    to,
    tu,
    td,
    tc,
    fst,
    frx,
    hrs,
    hrx,
    scg,
    id_s,
    id_r,
    tp_s,
    tp_r,
    w_s,
    w_r,
    ag_s,
    ag_r,
    rs_s,
    rs_r,
    g_s,
    g_r,
    f_s,
    f_r,
    hx_s,
    hx_r,
    sc_s,
    sc_r,
):
    B, H, S, G, L, D, DB, HC, R, NC, NR, FU, FD, T = (
        z.B, z.H, z.S, z.G, z.L, z.D, z.DB, z.HC, z.R, z.NC, z.NR, z.FU, z.FD, z.T,
    )
    N_HEADS = HC // HEAD_DIM
    W = 2 * R
    QT = 2
    scale = HEAD_DIM ** (-0.5)
    c2 = scale * LOG2E
    b = lax.axis_index("blk")
    h = lax.axis_index("head")
    s, g = b // G, b % G
    y, c = h // 2, h % 2
    own_row = g * H + h
    s1 = s + 1 - 2 * (s % 2)
    s2 = (s + 2) % S
    s3 = (s1 + 2) % S

    def dev(blk_i, head_i):
        return (blk_i, head_i)

    sibling = dev(b, y * 2 + 1 - c)

    def peer(k):
        return dev(s * G + (g + k // 2) % G, ((y + k % 2) % 2) * 2 + c)

    waits = []

    def send(src, dst, ssem, rsem, device):
        copy = pltpu.make_async_remote_copy(src, dst, ssem, rsem, device, MESH)
        copy.start()
        return copy

    def arrived(dst, ssem, rsem):
        pltpu.make_async_remote_copy(dst, dst, ssem, rsem, sibling, MESH).wait_recv()

    def over_blk(body):
        def one(k, carry):
            body(lax.rem(b + k, B))
            return carry

        lax.fori_loop(1, B, one, 0)

    def rows(i, n):
        return pl.ds(pl.multiple_of(i * n, 16), n)

    barrier = pltpu.get_barrier_semaphore()

    def greet_blk(other):
        pl.semaphore_signal(barrier, inc=1, device_id=dev(other, h), device_id_type=MESH)

    def greet_head(k, carry):
        pl.semaphore_signal(
            barrier, inc=1, device_id=dev(b, lax.rem(h + k, H)), device_id_type=MESH
        )
        return carry

    over_blk(greet_blk)
    lax.fori_loop(1, H, greet_head, 0)

    table = emb_in[...]
    ids[...] = jnp.zeros((16, R), jnp.int32)
    ids[0:S] = tok_in[...]
    ids[S : 2 * S] = tgt_in[...]
    ids[2 * S : 3 * S] = msk_in[...]
    sg[...] = jnp.zeros((D, 128), F32)
    for i in range(2 * L + 1):
        sg[NORM_LANE + 2 * i : NORM_LANE + 2 * i + 2, 0:DB] = norm_in[i]
    lane_small = lax.broadcasted_iota(jnp.int32, (DB, 128), 1)
    token_part = jnp.where(lane_small < VOCAB, table[:, 0:128], sg[0:128, :].T[0:DB]).astype(BF16)
    own_rows = rows(b, DB)
    tg[own_rows, 0:128] = token_part
    tg[own_rows, 128:] = table[:, VOCAB:].astype(BF16)
    pl.semaphore_wait(barrier, B + H - 2)

    def send_ids(other):
        send(ids, idsg.at[b], id_s.at[other], id_r.at[b], dev(other, h))

    over_blk(send_ids)
    idsg[b] = ids[...]

    lanes_in = pl.ds(pl.multiple_of(c * 512, 128), T + 128 - 512)
    lanes_out = pl.ds(pl.multiple_of(c * (T + 128 - 512), 128), 512)
    lanes_back = pl.ds(pl.multiple_of((1 - c) * (T + 128 - 512), 128), 512)

    def t_send(m, at, cut, device):
        block = tg.at[at, cut]
        waits.append(send(block, block, tp_s.at[m], tp_r.at[m], device))

    def t_here(m, at, cut):
        arrived(tg.at[at, cut], tp_s.at[m], tp_r.at[m])

    def plane_rows(plane, column):
        return rows(plane * G + column, DB)

    t_send(0, own_rows, lanes_in, dev(s2 * G + g, h))
    t_send(1, own_rows, lanes_in, dev(s1 * G + g, h))
    t_send(3, own_rows, lanes_in, dev(s * G + 1 - g, h))

    def w_sem(sems, l, kind, m):
        return sems.at[l * 21 + (-1, 6, 14, 17)[kind] + m]

    def w_ref(l, kind, at):
        return (wq, wo, wu, wd)[kind].at[l, at]

    def shard_rows(kind, plane, column=None):
        if kind == 3:
            return rows(plane, FD)
        return rows(plane * G + (g if column is None else column), DB)

    def w_send(l, kind, m, src, at, device):
        waits.append(
            send(src, w_ref(l, kind, at), w_sem(w_s, l, kind, m), w_sem(w_r, l, kind, m), device)
        )

    def w_arrived(l, kind, m, at):
        arrived(w_ref(l, kind, at), w_sem(w_s, l, kind, m), w_sem(w_r, l, kind, m))

    def round_weights(l, kind):
        at = shard_rows(kind, s)
        if kind == 0:
            wq_own[l] = jnp.concatenate([wq_in[l, i] for i in range(3)], axis=1).astype(BF16)
            wq[l, at] = wq_own[l]
        elif kind == 1:
            wo_own[l] = wo_in[l].T.astype(BF16)
            wo[l, at] = wo_own[l]
        elif kind == 2:
            up = wu_in[l]
            for j in range(G):
                parts = [up[:, (i * G + j) * FD : (i * G + j + 1) * FD] for i in range(S)]
                wu_own[l, j] = jnp.concatenate(parts, axis=1).astype(BF16)
            wu[l, at] = wu_own[l, g]
        else:
            wd_own[l] = wd_in[l].astype(BF16)
            wd[l, at] = wd_own[l]

    def plane_block(kind, plane):
        return rows(plane, FD) if kind == 3 else rows(plane, G * DB)

    def send_weights(l, kind):
        round_weights(l, kind)
        at = shard_rows(kind, s)
        if kind == 2:
            w_send(l, 2, 0, wu_own.at[l, 1 - g], at, dev(s * G + 1 - g, h))
            return
        src = (wq_own, wo_own, None, wd_own)[kind].at[l]
        w_send(l, kind, 1, src, at, dev(s2 * G + g, h))
        w_send(l, kind, 2, src, at, dev(s1 * G + g, h))

    def push_weights(l):
        w_arrived(l, 2, 0, shard_rows(2, s, 1 - g))
        at = plane_block(2, s)
        w_send(l, 2, 1, w_ref(l, 2, at), at, dev(s2 * G + g, h))
        w_send(l, 2, 2, w_ref(l, 2, at), at, dev(s1 * G + g, h))

    def relay_weights(l, kind):
        at = shard_rows(kind, s2) if kind < 2 else plane_block(kind, s2)
        w_arrived(l, kind, 1, at)
        w_send(l, kind, 3, w_ref(l, kind, at), at, dev(s1 * G + g, h))

    def cross_weights(l, kind, planes):
        for m, plane, known in ((4, s, True), (5, s2, True), (6, s1, False), (7, s3, False)):
            if m - 4 in planes:
                at = shard_rows(kind, plane)
                if not known:
                    w_arrived(l, kind, m - 4, at)
                w_send(l, kind, m, w_ref(l, kind, at), at, dev(s * G + 1 - g, h))

    def wait_weights(l, kind):
        if kind < 2:
            for m, plane in ((4, s), (5, s2), (6, s1), (7, s3)):
                w_arrived(l, kind, m, shard_rows(kind, plane, 1 - g))
        else:
            w_arrived(l, kind, 2, plane_block(kind, s1))
            w_arrived(l, kind, 3, plane_block(kind, s3))

    send_weights(0, 0)
    cross_weights(0, 0, (0,))
    send_weights(0, 1)
    at = plane_rows(s2, g)
    t_here(0, at, lanes_in)
    t_send(2, at, lanes_in, dev(s1 * G + g, h))
    t_send(4, at, lanes_in, dev(s * G + 1 - g, h))
    send_weights(0, 2)
    for kind in range(2):
        relay_weights(0, kind)
    send_weights(0, 3)
    for m, plane in ((1, s1), (2, s3)):
        at = plane_rows(plane, g)
        t_here(m, at, lanes_in)
        t_send(m + 4, at, lanes_in, dev(s * G + 1 - g, h))
    cross_weights(0, 0, (1, 2, 3))

    half_rows = (slice(0, D // 2), slice(D // 2, D))

    ag_sent = []

    def ag_send(m, src, dst, device):
        ag_sent.append(send(src, dst, ag_s.at[m], ag_r.at[m], device))

    def ag_here(m, dst):
        arrived(dst, ag_s.at[m], ag_r.at[m])

    def ag_left():
        for copy in ag_sent:
            copy.wait_send()
        ag_sent.clear()

    def block(buf, k, half):
        return buf.at[:, k * W + half * R : k * W + half * R + R]

    def block_half(buf, k, half, i):
        return buf.at[half_rows[i], k * W + half * R : k * W + half * R + R]

    def spread(buf, base=0):
        ag_left()
        ag_send(base + 0, block_half(buf, 0, 0, 0), block_half(buf, 1, 0, 0), peer(1))
        ag_send(base + 1, block_half(buf, 0, 0, 1), block_half(buf, 2, 0, 1), peer(2))
        ag_send(base + 2, block_half(buf, 0, 0, 1), block_half(buf, 1, 0, 1), peer(1))
        ag_send(base + 3, block_half(buf, 0, 0, 0), block_half(buf, 2, 0, 0), peer(2))
        ag_send(base + 4, block(buf, 0, 0), block(buf, 0, 1), sibling)

    def relay_near(buf, base=0):
        ag_here(base + 0, block_half(buf, 1, 0, 0))
        ag_send(base + 5, block_half(buf, 1, 0, 0), block_half(buf, 3, 0, 0), peer(2))
        ag_here(base + 1, block_half(buf, 2, 0, 1))
        ag_send(base + 6, block_half(buf, 2, 0, 1), block_half(buf, 3, 0, 1), peer(1))
        ag_here(base + 2, block_half(buf, 1, 0, 1))
        ag_send(base + 7, block(buf, 1, 0), block(buf, 1, 1), sibling)
        ag_here(base + 3, block_half(buf, 2, 0, 0))
        ag_send(base + 8, block(buf, 2, 0), block(buf, 2, 1), sibling)

    def relay_far(buf, base=0):
        for i in range(2):
            ag_here(base + 5 + i, block_half(buf, 3, 0, i))
            ag_send(base + 9 + i, block_half(buf, 3, 0, i), block_half(buf, 3, 1, i), sibling)

    def have(buf, k, base=0):
        if k == 0:
            ag_here(base + 4, block(buf, 0, 1))
        elif k < 3:
            ag_here(base + 6 + k, block(buf, k, 1))
        else:
            for i in range(2):
                ag_here(base + 9 + i, block_half(buf, 3, 1, i))

    def spread_column(buf):
        ag_left()
        ag_send(0, block(buf, 0, 0), block(buf, 1, 0), peer(1))
        ag_send(4, block(buf, 0, 0), block(buf, 0, 1), sibling)

    def relay_column(buf):
        ag_here(0, block(buf, 1, 0))
        ag_send(7, block(buf, 1, 0), block(buf, 1, 1), sibling)

    staged = {}
    summed_pairs = set()
    half_of = (slice(0, D // 2), slice(D // 2, D))

    def stage(ref, key, value):
        for copy in staged.pop(key, ()):
            copy.wait_send()
        ref[...] = value

    def rs_set(use, m):
        return m + 10 * (use % 4 == 3)

    def rs_send(use, m, src, dst, device):
        n = rs_set(use, m)
        return [send(src, dst, rs_s.at[n], rs_r.at[n], device)]

    def rs_here(use, m, dst):
        n = rs_set(use, m)
        arrived(dst, rs_s.at[n], rs_r.at[n])

    def part(use, k, value):
        keep[k] = value[:, :R]
        stage(psrc.at[k], ("p", k), value[:, R:].astype(BF16))
        staged["p", k] = rs_send(use, k, psrc.at[k], srecv.at[use % 4, k], sibling)

    def pair_sum(use, k, at=slice(0, D)):
        if (use, k) not in summed_pairs:
            summed_pairs.add((use, k))
            rs_here(use, k, srecv.at[use % 4, k])
        return keep[k, at] + srecv[use % 4, k, at].astype(F32)

    def pass_half(use, m, k, i, value, slot, device):
        stage(csrc.at[k, half_of[i]], ("c", k, i), value.astype(BF16))
        staged["c", k, i] = rs_send(
            use, m, csrc.at[k, half_of[i]], rrecv.at[use % 4, slot, half_of[i]], device
        )

    def pass_across(use):
        pass_half(use, 4, 3, 0, pair_sum(use, 3, half_of[0]), 0, peer(1))
        pass_half(use, 5, 3, 1, pair_sum(use, 3, half_of[1]), 0, peer(2))

    def pass_near(use):
        pass_half(use, 6, 1, 0, pair_sum(use, 1, half_of[0]), 1, peer(1))
        pass_half(use, 7, 2, 1, pair_sum(use, 2, half_of[1]), 2, peer(2))

    def pass_joined(use):
        for i, k in ((0, 2), (1, 1)):
            rs_here(use, 4 + i, rrecv.at[use % 4, 0, half_of[i]])
            value = pair_sum(use, k, half_of[i]) + rrecv[use % 4, 0, half_of[i]].astype(F32)
            pass_half(use, 8 + i, k, i, value, k, peer(k))

    def total(use):
        out = pair_sum(use, 0)
        for m, k, i in ((6, 1, 0), (7, 2, 1), (8, 2, 0), (9, 1, 1)):
            rs_here(use, m, rrecv.at[use % 4, k, half_of[i]])
        return out + rrecv[use % 4, 1].astype(F32) + rrecv[use % 4, 2].astype(F32)

    def pass_column(use):
        for i in range(2):
            pass_half(use, 6 + 3 * i, 1, i, pair_sum(use, 1, half_of[i]), 1, peer(1))

    def total_column(use):
        out = pair_sum(use, 0)
        for i in range(2):
            rs_here(use, 6 + 3 * i, rrecv.at[use % 4, 1, half_of[i]])
        return out + rrecv[use % 4, 1].astype(F32)

    def g_sem(sems, l, kind, m):
        return sems.at[l * 21 + (0, 7, 14, 18)[kind] + m]

    def g_send(l, kind, m, src, dst, device):
        return send(src, dst, g_sem(g_s, l, kind, m), g_sem(g_r, l, kind, m), device)

    def g_arrived(l, kind, m, dst):
        arrived(dst, g_sem(g_s, l, kind, m), g_sem(g_r, l, kind, m))

    def g_stage(key, ref, value):
        for copy in staged.pop(key, ()):
            copy.wait_send()
        ref[...] = value.astype(BF16)

    def g_first(l, kind, value):
        src, dst = ((stq, rq), (sto, ro), (stu, ru), (std, rd))[kind]
        g_stage(("g", kind), src, value)
        if kind < 2:
            staged["g", kind] = []
            return
        n = G * DB if kind == 2 else FD
        dst[l, 0] = src[rows(s, n)]
        staged["g", kind] = [
            g_send(l, kind, i, src.at[rows(plane, n)], dst.at[l, 1 + i], dev(s1 * G + g, h))
            for i, plane in ((1, s3), (0, s1))
        ]

    def g_cross(l, kind, planes):
        src, dst = ((stq, rq), (sto, ro))[kind]
        for m, plane in planes:
            staged["g", kind].append(
                g_send(
                    l, kind, m, src.at[rows(plane * G + 1 - g, DB)], dst.at[l, m], dev(s * G + 1 - g, h)
                )
            )

    def g_column(l, kind, m, plane):
        src, dst = ((stq, rq), (sto, ro))[kind]
        return src[rows(plane * G + g, DB)].astype(F32) + dst[l, m].astype(F32)

    def g_mid(l, kind):
        src, dst, tmp = ((stq, rq, tq), (sto, ro, to))[kind]
        g_arrived(l, kind, 0, dst.at[l, 0])
        g_stage(("m", kind, 1), tmp.at[1], g_column(l, kind, 0, s3))
        one = g_send(l, kind, 5, tmp.at[1], dst.at[l, S + 1], dev(s1 * G + g, h))
        g_arrived(l, kind, 1, dst.at[l, 1])
        g_stage(("m", kind, 0), tmp.at[0], g_column(l, kind, 1, s1))
        two = g_send(l, kind, 4, tmp.at[0], dst.at[l, S], dev(s1 * G + g, h))
        staged["m", kind, 1] = [one]
        staged["m", kind, 0] = [two]

    def g_second(l, kind):
        if kind < 2:
            src, dst, tmp = ((stq, rq, tq), (sto, ro, to))[kind]
            g_arrived(l, kind, 2, dst.at[l, 2])
            g_arrived(l, kind, 5, dst.at[l, S + 1])
            g_stage(("s", kind), tmp.at[2], g_column(l, kind, 2, s2) + dst[l, S + 1].astype(F32))
            staged["s", kind] = [g_send(l, kind, 6, tmp.at[2], dst.at[l, S + 2], dev(s2 * G + g, h))]
            return
        src, dst, tmp, n = ((stu, ru, tu, G * DB), (std, rd, td, FD))[kind - 2]
        g_arrived(l, kind, 1, dst.at[l, 2])
        g_stage(("s", kind), tmp, src[rows(s2, n)].astype(F32) + dst[l, 2].astype(F32))
        staged["s", kind] = [g_send(l, kind, 2, tmp, dst.at[l, 3], dev(s2 * G + g, h))]

    def g_third(l):
        g_arrived(l, 2, 0, ru.at[l, 1])
        g_arrived(l, 2, 2, ru.at[l, 3])

        def summed(column):
            at = rows(column, DB)
            return sum(ru[l, i, at, :].astype(F32) for i in (0, 1, 3))

        g_stage(("t", 2), tc, summed(1 - g))
        staged["t", 2] = [g_send(l, 2, 3, tc, rc.at[l], dev(s * G + 1 - g, h))]
        gu_sum[g] = summed(g)

    def lanes_of(v):
        folded = jnp.sum(v * v, axis=0, keepdims=True)
        return jnp.sum(folded, axis=1, keepdims=True) + jnp.zeros((1, 128), F32)

    def write_out(l, kind):
        made = (gq_made, go_made, gu_made, gd_made)[kind]
        out = (gq_out, go_out, gu_out, gd_out)[kind]
        return pltpu.make_async_copy(made.at[l], out.at[l], out_sem.at[l * 4 + kind])

    def g_final(l, kind):
        if kind < 2:
            dst, out = ((rq, gq_made), (ro, go_made))[kind]
            g_arrived(l, kind, 3, dst.at[l, 3])
            g_arrived(l, kind, 4, dst.at[l, S])
            g_arrived(l, kind, 6, dst.at[l, S + 2])
            value = g_column(l, kind, 3, s) + dst[l, S].astype(F32) + dst[l, S + 2].astype(F32)
            if kind == 0:
                for i in range(3):
                    out[l, i] = value[:, i * HC : (i + 1) * HC]
            else:
                out[l] = value.T
        elif kind == 2:
            g_arrived(l, 2, 3, rc.at[l])
            value = rc[l].astype(F32)
            gu_sum[1 - g] = value
            parts = [gu_sum[j, :, i * FD : (i + 1) * FD] for i in range(S) for j in range(G)]
            gu_made[l] = jnp.concatenate(parts, axis=1)
            write_out(l, kind).start()
            return lanes_of(gu_sum[0]) + lanes_of(gu_sum[1])
        else:
            g_arrived(l, 3, 0, rd.at[l, 1])
            g_arrived(l, 3, 2, rd.at[l, 3])
            value = sum(rd[l, i].astype(F32) for i in (0, 1, 3))
            gd_made[l] = value
        write_out(l, kind).start()
        return lanes_of(value)

    squares = jnp.zeros((1, 128), F32)

    length = lens[s]
    for k in range(NC):
        for half in range(2):
            core = c if half == 0 else 1 - c
            block_row = ((g + k // 2) % G) * H + ((y + k % 2) % 2) * 2 + core
            place = block_row * R + lax.broadcasted_iota(jnp.int32, (R, 128), 0)
            bias[k * W + half * R : k * W + half * R + R, :] = jnp.where(place < length, 0.0, NEGATIVE)
    lane_place = own_row * R + lax.broadcasted_iota(jnp.int32, (1, R), 1)
    live = jnp.where(lane_place < length, 1.0, 0.0)
    dqkv[0:HC, QT * W :] = jnp.zeros((HC, T - QT * W), BF16)
    sg[...] = jnp.zeros((D, 128), F32)
    lane = lax.broadcasted_iota(jnp.int32, (D, 128), 1)
    row_of = lax.broadcasted_iota(jnp.int32, (128, R), 0)

    def ids_here(other):
        arrived(idsg.at[other], id_s.at[other], id_r.at[other])

    over_blk(ids_here)
    t_here(3, plane_rows(s, 1 - g), lanes_in)
    t_send(7, plane_rows(s, 1 - g), lanes_out, sibling)
    for m, plane in ((4, s2), (5, s1), (6, s3)):
        t_here(m, plane_rows(plane, 1 - g), lanes_in)
        t_send(m + 4, rows(plane, G * DB), lanes_out, sibling)
    t_here(7, plane_rows(s, 1 - g), lanes_back)
    for m, plane in ((8, s2), (9, s1), (10, s3)):
        t_here(m, rows(plane, G * DB), lanes_back)
    etg = tg.at[:, 0:128]
    target_row = idsg[own_row, pl.ds(S + s, 1), :]
    mask_row = idsg[own_row, pl.ds(2 * S + s, 1), :].astype(F32)
    token_weight = mask_row * fam[s]
    weight_sum = jnp.zeros((1, 1), F32)
    for i in range(S):
        counts = jnp.zeros((1, R), F32)
        for j in range(B):
            counts = counts + idsg[j, 2 * S + i : 2 * S + i + 1, :].astype(F32)
        weight_sum = weight_sum + jnp.sum(counts, axis=1, keepdims=True) * fam[i]

    def gain(i):
        return etg[:, NORM_LANE + 2 * i : NORM_LANE + 2 * i + 1].astype(F32)

    def shift(i):
        return etg[:, NORM_LANE + 2 * i + 1 : NORM_LANE + 2 * i + 2].astype(F32)

    def normalize(v):
        centred = v - jnp.mean(v, axis=0, keepdims=True)
        rstd = lax.rsqrt(jnp.mean(centred * centred, axis=0, keepdims=True) + NORM_EPS)
        return centred * rstd, rstd

    def layer_norm_low(v, i):
        hat, _ = normalize(v)
        return (hat * gain(i) + shift(i)).astype(BF16)

    later = []

    def run_later():
        for work in later:
            work()
        later.clear()

    def norm_grads(grad, hat, i):
        gain_grad = jnp.sum(grad * hat, axis=1, keepdims=True)
        shift_grad = jnp.sum(grad, axis=1, keepdims=True)
        sg[...] += jnp.where(lane == NORM_LANE + 2 * i, gain_grad, 0.0) + jnp.where(
            lane == NORM_LANE + 2 * i + 1, shift_grad, 0.0
        )

    def layer_norm_back(grad, v, i):
        hat, rstd = normalize(v)
        later.append(lambda: norm_grads(grad, hat, i))
        scaled = grad * gain(i)
        mean_one = jnp.mean(scaled, axis=0, keepdims=True)
        mean_two = jnp.mean(scaled * hat, axis=0, keepdims=True)
        return rstd * (scaled - mean_one - hat * mean_two)

    def square_sum(v, l, i):
        later.append(lambda: stats.__setitem__(3 * l + i, squares_of(v)))

    def squares_of(v):
        return jnp.sum(jnp.sum(v * v, axis=0, keepdims=True) * live, axis=1, keepdims=True)

    slots = list(range(NC))
    near = slots[:2]
    stats = {}
    for k in slots:
        for half in range(2):
            core = c if half == 0 else 1 - c
            block_row = ((g + k // 2) % G) * H + ((y + k % 2) % 2) * 2 + core
            hot = jnp.where(row_of == idsg[block_row, pl.ds(s, 1), :], 1.0, 0.0).astype(BF16)
            place = tg[:, pl.ds(pl.multiple_of(128 + block_row * R, 128), R)]
            start = dot(etg[...], hot, 1, 0) + place.astype(F32)
            h1[0, :, k * W + half * R : k * W + half * R + R] = layer_norm_low(start, 0)
            if k == 0 and half == 0:
                xs[0] = start
                token_hot = hot

    def cols(k):
        return slice(k * W, (k + 1) * W)

    for l in range(L):
        x = xs[l]
        square_sum(x, l, 0)
        if l:
            h1[l, :, 0:R] = layer_norm_low(x, 2 * l)
            spread(h1.at[l], 11)
            run_later()
        else:
            push_weights(0)
            cross_weights(0, 1, (0, 1, 2, 3))
        wait_weights(l, 0)

        def project(k):
            if k in near:
                packed = dot(wq[l], h1[l, :, cols(k)], 0, 0).astype(BF16)
                qt[l, :, cols(k)] = packed[0:HC]
                packed = packed[HC:]
            else:
                packed = dot(wq[l, :, :], h1[l, :, cols(k)], 0, 0).astype(BF16)[HC:]
            kt[l, :, cols(k)] = packed[0:HC]
            vt[l, :, cols(k)] = packed[HC:]

        if l:
            have(h1.at[l], 0, 11)
            project(0)
            relay_near(h1.at[l], 11)
            have(h1.at[l], 1, 11)
            project(1)
            relay_far(h1.at[l], 11)
            have(h1.at[l], 2, 11)
            project(2)
            cross_weights(l, 1, (0, 1, 2, 3))
            have(h1.at[l], 3, 11)
            project(3)
        else:
            for k in slots:
                project(k)

        tiles = [(q, i) for q in (1, 0) for i in range(N_HEADS)]
        chunk = W
        peaks, norms, outs = {}, {}, {}

        def head_rows(i):
            return slice(i * HEAD_DIM, (i + 1) * HEAD_DIM)

        def score(n, j):
            q, i = tiles[n]
            keys = slice(j * chunk, (j + 1) * chunk)
            scores = dot(kt[l, head_rows(i), keys], qt[l, head_rows(i), cols(q)], 0, 0)
            scores = scores + jnp.concatenate([bias[keys, :]] * 2, axis=1)
            sbuf[n % 2, keys, :] = scores
            peak = jnp.max(scores, axis=0, keepdims=True)
            peaks[n] = jnp.maximum(peaks[n], peak) if j else peak

        def weigh(n, j):
            keys = slice(j * chunk, (j + 1) * chunk)
            exps = jnp.exp2((sbuf[n % 2, keys, :] - peaks[n]) * c2)
            norm = jnp.sum(exps, axis=0, keepdims=True)
            norms[n] = norms[n] + norm if j else norm
            pbuf[n % 2, keys, :] = exps.astype(BF16)

        def gather_values(n, j):
            q, i = tiles[n]
            keys = slice(j * chunk, (j + 1) * chunk)
            out = dot(vt[l, head_rows(i), keys], pbuf[n % 2, keys, :], 1, 0)
            outs[n] = outs[n] + out if j else out

        def attended(n):
            q, i = tiles[n]
            out = outs[n] * (1.0 / norms[n])
            o32[l, head_rows(i), cols(q)] = out
            ob[l, head_rows(i), cols(q)] = out.astype(BF16)
            lse[l, i * 8 : i * 8 + 8, cols(q)] = jnp.broadcast_to(
                peaks[n] * c2 + jnp.log(norms[n]) * LOG2E, (8, W)
            )

        for j in range(T // chunk):
            score(0, j)
        for n in range(len(tiles) + 1):
            for j in range(T // chunk):
                if n + 1 < len(tiles):
                    score(n + 1, j)
                if n:
                    gather_values(n - 1, j)
                if n < len(tiles):
                    weigh(n, j)
            if n:
                attended(n - 1)
            if n == 1:
                relay_weights(l, 3)
                relay_weights(l, 2)
                if l + 1 < L:
                    for kind in range(3):
                        send_weights(l + 1, kind)
            if n == N_HEADS:
                wait_weights(l, 1)
                part(4 * l, 1, dot(wo[l], ob[l, :, cols(1)], 1, 0))
            if n == N_HEADS + 2:
                pass_column(4 * l)
        part(4 * l, 0, dot(wo[l], ob[l, :, cols(0)], 1, 0))
        attn_out = total_column(4 * l)
        square_sum(attn_out, l, 1)
        middle = xs[l] + attn_out
        xm[l] = middle
        h2[l, :, 0:R] = layer_norm_low(middle, 2 * l + 1)
        spread(h2.at[l])
        run_later()
        wait_weights(l, 2)
        wait_weights(l, 3)

        def feed(k):
            pre = dot(wu[l], h2[l, :, cols(k)], 0, 0)
            cdf = 0.5 * (1.0 + lax.erf(pre * (0.5**0.5)))
            low = (pre * cdf).astype(BF16)
            act[l, :, cols(k)] = low
            slope[l, :, cols(k)] = cdf + pre * (jnp.exp(-0.5 * pre * pre) * 0.3989422804014327)
            part(4 * l + 1, k, dot(wd[l], low, 0, 0))

        have(h2.at[l], 0)
        feed(0)
        relay_near(h2.at[l])
        have(h2.at[l], 1)
        feed(1)
        if l + 1 < L:
            for kind in range(2):
                relay_weights(l + 1, kind)
            cross_weights(l + 1, 0, (0, 1))
            send_weights(l + 1, 3)
            push_weights(l + 1)
        relay_far(h2.at[l])
        have(h2.at[l], 2)
        feed(2)
        pass_near(4 * l + 1)
        have(h2.at[l], 3)
        feed(3)
        pass_across(4 * l + 1)
        pass_joined(4 * l + 1)
        if l + 1 < L:
            cross_weights(l + 1, 0, (2, 3))
        ffn_out = total(4 * l + 1)
        square_sum(ffn_out, l, 2)
        xs[l + 1] = xm[l] + ffn_out

    last = xs[L]
    final_low = layer_norm_low(last, 2 * L)
    logits = dot(etg[...], final_low, 0, 0)[0:NORM_LANE]
    vocab_row = row_of[0:NORM_LANE]
    logits = jnp.where(vocab_row < VOCAB, logits, NEGATIVE)
    shifted = logits - jnp.max(logits, axis=0, keepdims=True)
    log_probs = shifted - jnp.log(jnp.sum(jnp.exp(shifted), axis=0, keepdims=True))
    target_hot = jnp.where(vocab_row == target_row, 1.0, 0.0)
    token_loss = -jnp.sum(target_hot * log_probs, axis=0, keepdims=True)
    loss = jnp.sum(token_weight * token_loss, axis=1, keepdims=True)
    grad_logits = ((token_weight / weight_sum) * (jnp.exp(log_probs) - target_hot)).astype(BF16)
    grad_logits = jnp.concatenate([grad_logits, jnp.zeros((128 - NORM_LANE, R), BF16)], axis=0)
    grad_final = dot(etg[...], grad_logits, 1, 0)
    sg[...] += dot(final_low, grad_logits, 1, 1)
    grad = layer_norm_back(grad_final, last, 2 * L)

    for l in reversed(range(L)):
        df[l, :, 0:R] = grad.astype(BF16)
        xs[l + 1] = grad
        spread(df.at[l])
        run_later()

        def feed_back(k):
            grad_act = dot(wd[l], df[l, :, cols(k)], 1, 0)
            low = (grad_act * slope[l, :, cols(k)]).astype(BF16)
            du[:, cols(k)] = low
            part(4 * l + 2, k, dot(wu[l], low, 1, 0))

        have(df.at[l], 0)
        feed_back(0)
        relay_near(df.at[l])
        if l + 1 < L:
            g_cross(l + 1, 1, ((0, s3), (1, s1)))
            for kind in range(2):
                g_cross(l + 1, kind, ((2, s2), (3, s)))
        have(df.at[l], 1)
        feed_back(1)
        relay_far(df.at[l])
        have(df.at[l], 2)
        feed_back(2)
        pass_near(4 * l + 2)
        have(df.at[l], 3)
        feed_back(3)
        pass_across(4 * l + 2)
        if l + 1 < L:
            g_mid(l + 1, 0)
            g_mid(l + 1, 1)
            g_third(l + 1)
        g_first(l, 3, dot(act[l], df[l], 1, 1))
        pass_joined(4 * l + 2)
        g_first(l, 2, dot(h2[l], du[...], 1, 1))
        grad_middle = xs[l + 1] + layer_norm_back(total(4 * l + 2), xm[l], 2 * l + 1)
        xm[l] = grad_middle

        da[l, :, 0:R] = grad_middle.astype(BF16)
        spread_column(da.at[l])
        run_later()
        if l + 1 < L:
            g_second(l + 1, 0)
            g_second(l + 1, 1)
            for kind in (2, 3):
                squares = squares + g_final(l + 1, kind)

        def out_back(k):
            dob[:, cols(k)] = dot(wo[l], da[l, :, cols(k)], 0, 0).astype(BF16)

        have(da.at[l], 0)
        out_back(0)
        relay_column(da.at[l])
        have(da.at[l], 1)
        out_back(1)

        steps = [(i, q, j) for i in range(N_HEADS) for q in range(QT) for j in range(T // chunk)]
        grad_q, grad_k, grad_v = {}, {}, {}

        def back_scores(n):
            i, q, j = steps[n]
            keys = slice(j * chunk, (j + 1) * chunk)
            sbuf[n % 2, 0:chunk, :] = dot(kt[l, head_rows(i), keys], qt[l, head_rows(i), cols(q)], 0, 0)
            sbuf[n % 2, chunk : 2 * chunk, :] = dot(vt[l, head_rows(i), keys], dob[head_rows(i), cols(q)], 0, 0)

        def back_weigh(n):
            i, q, j = steps[n]
            keys = slice(j * chunk, (j + 1) * chunk)
            delta = jnp.sum(
                dob[head_rows(i), cols(q)].astype(F32) * o32[l, head_rows(i), cols(q)],
                axis=0,
                keepdims=True,
            )
            scores = sbuf[n % 2, 0:chunk, :] + jnp.concatenate([bias[keys, :]] * 2, axis=1)
            probs = jnp.exp2(scores * c2 - lse[l, i * 8 : i * 8 + 1, cols(q)])
            pbuf[n % 2, 0:chunk, :] = probs.astype(BF16)
            pbuf[n % 2, chunk : 2 * chunk, :] = (probs * (sbuf[n % 2, chunk : 2 * chunk, :] - delta)).astype(BF16)

        def back_products(n):
            i, q, j = steps[n]
            keys = slice(j * chunk, (j + 1) * chunk)
            probs = pbuf[n % 2, 0:chunk, :]
            grad_scores = pbuf[n % 2, chunk : 2 * chunk, :]
            term = dot(kt[l, head_rows(i), keys], grad_scores, 1, 0)
            grad_q[i, q] = grad_q[i, q] + term if j else term
            term_k = dot(qt[l, head_rows(i), cols(q)], grad_scores, 1, 1)
            term_v = dot(dob[head_rows(i), cols(q)], probs, 1, 1)
            grad_k[i, j] = grad_k[i, j] + term_k if q else term_k
            grad_v[i, j] = grad_v[i, j] + term_v if q else term_v
            if j == T // chunk - 1:
                dqkv[head_rows(i), cols(q)] = (grad_q[i, q] * scale).astype(BF16)
            if q == QT - 1:
                first = HC + i * HEAD_DIM
                dqkv[first : first + HEAD_DIM, keys] = (grad_k[i, j] * scale).astype(BF16)
                first = 2 * HC + i * HEAD_DIM
                dqkv[first : first + HEAD_DIM, keys] = grad_v[i, j].astype(BF16)

        back_scores(0)
        for n in range(len(steps) + 1):
            if n + 1 < len(steps):
                back_scores(n + 1)
            if n:
                back_products(n - 1)
            if n < len(steps):
                back_weigh(n)
            if n == len(steps) // 2:
                g_second(l, 3)
        def project_back(k):
            part(4 * l + 3, k, dot(wq[l], dqkv[:, cols(k)], 1, 0))

        project_back(3)
        project_back(1)
        pass_across(4 * l + 3)
        project_back(2)
        pass_near(4 * l + 3)
        project_back(0)
        g_second(l, 2)
        if l + 1 < L:
            for kind in range(2):
                squares = squares + g_final(l + 1, kind)
        g_first(l, 0, dot(h1[l], dqkv[...], 1, 1))
        pass_joined(4 * l + 3)
        g_cross(l, 0, ((0, s3), (1, s1)))
        g_first(l, 1, dot(da[l], ob[l], 1, 1))
        if l == 0:
            g_cross(0, 1, ((0, s3), (1, s1)))
            for kind in range(2):
                g_cross(0, kind, ((2, s2), (3, s)))
        grad = xm[l] + layer_norm_back(total(4 * l + 3), xs[l], 2 * l)

    run_later()
    high = grad.astype(BF16)
    low = (grad - high.astype(F32)).astype(BF16)
    small = sg[...] + dot(high, token_hot, 1, 1) + dot(low, token_hot, 1, 1)
    small = small.astype(BF16)
    for i in range(B):
        fst[i, :DB] = small[i * DB : (i + 1) * DB]
        fst[i, DB:] = high[i * DB : (i + 1) * DB]

    def send_table(other):
        send(fst.at[other], frx.at[b], f_s.at[other], f_r.at[b], dev(other, h))

    over_blk(send_table)
    frx[b] = fst[b]

    g_mid(0, 0)
    g_mid(0, 1)
    g_third(0)
    squares = squares + g_final(0, 3)

    def table_here(other):
        arrived(frx.at[other], f_s.at[other], f_r.at[other])

    over_blk(table_here)
    value = frx[0, :DB].astype(F32)
    for i in range(1, B):
        value = value + frx[i, :DB].astype(F32)
    hrs[h] = value

    def send_small(k, carry):
        other = lax.rem(h + k, H)
        send(hrs.at[h], hrs.at[h], hx_s.at[other], hx_r.at[h], dev(b, other))
        return carry

    lax.fori_loop(1, H, send_small, 0)
    for j in range(G):
        value = frx[j, DB:].astype(F32)
        for i in range(1, S):
            value = value + frx[i * G + j, DB:].astype(F32)
        hrx[h, j] = value
        squares = squares + lanes_of(value)

    def send_places(k, carry):
        other = lax.rem(h + k, H)
        send(hrx.at[h], hrx.at[h], hx_s.at[H + other], hx_r.at[H + h], dev(b, other))
        return carry

    lax.fori_loop(1, H, send_places, 0)

    def small_here(k, carry):
        other = lax.rem(h + k, H)
        arrived(hrs.at[other], hx_s.at[other], hx_r.at[other])
        return carry

    def places_here(k, carry):
        other = lax.rem(h + k, H)
        arrived(hrx.at[other], hx_s.at[H + other], hx_r.at[H + other])
        return carry

    g_second(0, 0)
    g_second(0, 1)
    lax.fori_loop(1, H, small_here, 0)
    value = hrs[0]
    for i in range(1, H):
        value = value + hrs[i]
    squares = squares + lanes_of(value) * (1.0 / H)
    small_sum = value
    for kind in (2, 0, 1):
        squares = squares + g_final(0, kind)

    lane_one = lax.broadcasted_iota(jnp.int32, (1, 128), 1)
    packed = jnp.where(lane_one == 0, loss, 0.0) + jnp.where(lane_one == 1, squares, 0.0)
    for i, stat in stats.items():
        packed = packed + jnp.where(lane_one == 2 + i, stat, 0.0)
    scg[B + h] = jnp.broadcast_to(packed, (8, 128))

    def send_heads(k, carry):
        other = lax.rem(h + k, H)
        src = scg.at[B + h]
        send(src, src, sc_s.at[B + other], sc_r.at[B + h], dev(b, other))
        return carry

    lax.fori_loop(1, H, send_heads, 0)

    def heads_here(k, carry):
        other = lax.rem(h + k, H)
        arrived(scg.at[B + other], sc_s.at[B + other], sc_r.at[B + other])
        return carry

    lax.fori_loop(1, H, heads_here, 0)
    out = scg[B]
    for i in range(1, H):
        out = out + scg[B + i]
    scg[b] = out

    def send_scalars(other):
        send(scg.at[b], scg.at[b], sc_s.at[other], sc_r.at[b], dev(other, h))

    over_blk(send_scalars)
    lax.fori_loop(1, H, places_here, 0)
    ge_out[...] = jnp.concatenate(
        [small_sum[:, :VOCAB]] + [hrx[i, j] for j in range(G) for i in range(H)], axis=1
    )
    norm_rows = small_sum.T
    for i in range(2 * L + 1):
        gn_out[i] = norm_rows[NORM_LANE + 2 * i : NORM_LANE + 2 * i + 2]

    def scalars_here(other):
        arrived(scg.at[other], sc_s.at[other], sc_r.at[other])

    over_blk(scalars_here)
    out = scg[0]
    for i in range(1, B):
        out = out + scg[i]
    lane_eight = lax.broadcasted_iota(jnp.int32, (8, 128), 1)
    tokens = lens[0]
    for i in range(1, S):
        tokens = tokens + lens[i]
    roots = jnp.sqrt(jnp.where(lane_eight == 1, out, out / (tokens.astype(F32) * D)))
    out = jnp.where(lane_eight == 0, out, roots)
    out = jnp.where(lane_eight == 2 + 3 * L, weight_sum, out)
    factor = CLIP_NORM / jnp.maximum(out, CLIP_NORM)
    factor = jnp.sum(jnp.where(lane_eight == 1, factor, 0.0), axis=1, keepdims=True)
    scal_out[...] = jnp.where(lane_eight == 3 + 3 * L, factor, out)

    for l in range(L):
        for kind in range(4):
            write_out(l, kind).wait()
    ag_left()
    for copy in waits:
        copy.wait_send()
    for copies in staged.values():
        for copy in copies:
            copy.wait_send()

    def sent(other):
        for src, ssem, rsem in ((idsg.at[other], id_s, id_r), (frx.at[other], f_s, f_r)):
            pltpu.make_async_remote_copy(src, src, ssem.at[other], rsem.at[other], sibling, MESH).wait_send()

    over_blk(sent)

    def heads_sent(k, carry):
        other = lax.rem(h + k, H)
        for src, m in ((hrs.at[other], other), (hrx.at[other], H + other)):
            pltpu.make_async_remote_copy(src, src, hx_s.at[m], hx_r.at[m], sibling, MESH).wait_send()
        src = scg.at[B + other]
        pltpu.make_async_remote_copy(
            src, src, sc_s.at[B + other], sc_r.at[B + other], sibling, MESH
        ).wait_send()
        return carry

    lax.fori_loop(1, H, heads_sent, 0)

    def scalars_sent(other):
        src = scg.at[other]
        pltpu.make_async_remote_copy(
            src, src, sc_s.at[other], sc_r.at[other], sibling, MESH
        ).wait_send()

    over_blk(scalars_sent)


def fused_step(z, token_ids, targets, masked, lengths, family_weight, embed_table, w_qkv, w_out, w_up, w_down, norm_params):
    B, H, S, G, L, D, DB, HC, R, NC, NR, FU, FD, T = (
        z.B, z.H, z.S, z.G, z.L, z.D, z.DB, z.HC, z.R, z.NC, z.NR, z.FU, z.FD, z.T,
    )
    W = 2 * R
    smem = pl.BlockSpec(memory_space=pltpu.SMEM)
    vmem = pl.BlockSpec(memory_space=pltpu.VMEM)
    dma = pltpu.SemaphoreType.DMA
    scratch = [
        pltpu.VMEM((L, 3, DB, HC), F32),
        pltpu.VMEM((L, HC, DB), F32),
        pltpu.VMEM((L, DB, S * G * FD), F32),
        pltpu.VMEM((L, FD, D), F32),
        dma((4 * L,)),
        pltpu.VMEM((16, R), jnp.int32),
        pltpu.VMEM((L, DB, 3 * HC), BF16),
        pltpu.VMEM((L, DB, HC), BF16),
        pltpu.VMEM((L, G, DB, FU), BF16),
        pltpu.VMEM((L, FD, D), BF16),
        pltpu.VMEM((G, DB, FU), F32),
        pltpu.VMEM((B, 16, R), jnp.int32),
        pltpu.VMEM((D, 128 + T), BF16),
        pltpu.VMEM((L, D, 3 * HC), BF16),
        pltpu.VMEM((L, D, HC), BF16),
        pltpu.VMEM((L, D, FU), BF16),
        pltpu.VMEM((L, FU, D), BF16),
        pltpu.VMEM((L, D, T), BF16),
        pltpu.VMEM((L, D, T), BF16),
        pltpu.VMEM((L, D, T), BF16),
        pltpu.VMEM((L, D, 2 * W), BF16),
        pltpu.VMEM((L, FU, T), BF16),
        pltpu.VMEM((L, FU, T), F32),
        pltpu.VMEM((FU, T), BF16),
        pltpu.VMEM((L, HC, 2 * W), BF16),
        pltpu.VMEM((L, HC, T), BF16),
        pltpu.VMEM((L, HC, T), BF16),
        pltpu.VMEM((L, HC, 2 * W), F32),
        pltpu.VMEM((L, HC, 2 * W), BF16),
        pltpu.VMEM((HC, 2 * W), BF16),
        pltpu.VMEM((L, 8 * (HC // HEAD_DIM), 2 * W), F32),
        pltpu.VMEM((3 * HC, T), BF16),
        pltpu.VMEM((T, 128), F32),
        pltpu.VMEM((2, T, W), F32),
        pltpu.VMEM((2, T, W), BF16),
        pltpu.VMEM((L + 1, D, R), F32),
        pltpu.VMEM((L, D, R), F32),
        pltpu.VMEM((NC, D, R), F32),
        pltpu.VMEM((NC, D, R), BF16),
        pltpu.VMEM((NC, D, R), BF16),
        pltpu.VMEM((4, NC, D, R), BF16),
        pltpu.VMEM((4, NC, D, R), BF16),
        pltpu.VMEM((D, 128), F32),
        pltpu.VMEM((D, 3 * HC), BF16),
        pltpu.VMEM((D, HC), BF16),
        pltpu.VMEM((D, FU), BF16),
        pltpu.VMEM((FU, D), BF16),
        pltpu.VMEM((L, S + 3, DB, 3 * HC), BF16),
        pltpu.VMEM((L, S + 3, DB, HC), BF16),
        pltpu.VMEM((L, S, G * DB, FU), BF16),
        pltpu.VMEM((L, S, FD, D), BF16),
        pltpu.VMEM((L, DB, FU), BF16),
        pltpu.VMEM((3, DB, 3 * HC), BF16),
        pltpu.VMEM((3, DB, HC), BF16),
        pltpu.VMEM((G * DB, FU), BF16),
        pltpu.VMEM((FD, D), BF16),
        pltpu.VMEM((DB, FU), BF16),
        pltpu.VMEM((B, 2 * DB, 128), BF16),
        pltpu.VMEM((B, 2 * DB, 128), BF16),
        pltpu.VMEM((H, DB, 128), F32),
        pltpu.VMEM((H, G, DB, 128), F32),
        pltpu.VMEM((B + H, 8, 128), F32),
        dma((B,)),
        dma((B,)),
        dma((11,)),
        dma((11,)),
        dma((21 * L,)),
        dma((21 * L,)),
        dma((22,)),
        dma((22,)),
        dma((20,)),
        dma((20,)),
        dma((21 * L,)),
        dma((21 * L,)),
        dma((B,)),
        dma((B,)),
        dma((2 * H,)),
        dma((2 * H,)),
        dma((B + H,)),
        dma((B + H,)),
    ]
    outs = (
        jax.ShapeDtypeStruct((8, 128), F32),
        jax.ShapeDtypeStruct((DB, VOCAB + T), F32),
        jax.ShapeDtypeStruct((L, 3, DB, HC), F32),
        jax.ShapeDtypeStruct((L, HC, DB), F32),
        jax.ShapeDtypeStruct((L, DB, S * G * FD), F32),
        jax.ShapeDtypeStruct((L, FD, D), F32),
        jax.ShapeDtypeStruct((2 * L + 1, 2, DB), F32),
    )
    scal, ge, gq, go, gu, gd, gn = pl.pallas_call(
        functools.partial(step_kernel, z),
        out_shape=outs,
        in_specs=[smem, smem] + [vmem] * 9,
        out_specs=[vmem] * 2 + [pl.BlockSpec(memory_space=pl.ANY)] * 4 + [vmem],
        scratch_shapes=scratch,
        compiler_params=pltpu.CompilerParams(
            collective_id=0, has_side_effects=True, vmem_limit_bytes=62 << 20
        ),
        name="train_step",
    )(
        lengths,
        family_weight,
        token_ids,
        targets,
        masked,
        embed_table.T,
        w_qkv.transpose(0, 2, 1, 3),
        w_out,
        w_up,
        w_down,
        norm_params,
    )
    return scal, (ge, gq, go, gu, gd, gn)


def update_kernel(layers, scal, *refs):
    groups = len(RATES)
    grads, masters, firsts, seconds = (refs[i * groups : (i + 1) * groups] for i in range(4))
    loss, weights, norm, rms = refs[4 * groups : 4 * groups + 4]
    outs = refs[4 * groups + 4 :]
    loss[0] = scal[0, 0]
    norm[0] = scal[0, 1]
    weights[0] = scal[0, 2 + 3 * layers]
    for i in range(layers):
        for j in range(3):
            rms[i, j] = scal[0, 2 + 3 * i + j]
    factor = scal[0, 3 + 3 * layers]
    for i in range(groups):

        def update(at, i=i):
            first, second, weight = adamw_update(
                masters[i][at],
                firsts[i][at],
                seconds[i][at],
                grads[i][at] * factor,
                RATES[i],
                DECAYS[i],
            )
            for ref, value in zip(outs[4 * i : 4 * i + 4], (first, second, weight, weight)):
                ref[at] = value.astype(ref.dtype)

        for k in range(masters[i].shape[0] if len(masters[i].shape) > 2 else 1):
            update(k if len(masters[i].shape) > 2 else slice(None))


def as_stored(groups):
    embed, qkv, out, up, down, norm = groups
    return embed.T, qkv.transpose(0, 2, 1, 3), out, up, down, norm


def fused_update(layers, scal, grads, masters, firsts, seconds):
    arrays = (*grads, *as_stored(masters), *as_stored(firsts), *as_stored(seconds))
    smem = pl.BlockSpec(memory_space=pltpu.SMEM)
    vmem = pl.BlockSpec(memory_space=pltpu.VMEM)
    shapes = [
        jax.ShapeDtypeStruct(master.shape, dtype)
        for master in as_stored(masters)
        for dtype in (F32, F32, F32, BF16)
    ]
    scalars = [jax.ShapeDtypeStruct((1,), F32)] * 3 + [jax.ShapeDtypeStruct((layers, 3), F32)]
    loss, weights, norm, rms, *new = pl.pallas_call(
        functools.partial(update_kernel, layers),
        out_shape=scalars + shapes,
        in_specs=[smem] + [vmem] * len(arrays),
        out_specs=[smem] * 4 + [vmem] * len(shapes),
        compiler_params=pltpu.CompilerParams(vmem_limit_bytes=62 << 20),
        name="adamw",
    )(scal, *arrays)
    by_kind = [as_stored(new[i::4]) for i in range(4)]
    results = [loss[0], weights[0], norm[0], rms]
    for i in range(len(RATES)):
        results += [kind[i] for kind in by_kind]
    return tuple(results)


def local(
    token_ids,
    targets,
    masked,
    lengths,
    family_weight,
    embed_table,
    w_qkv,
    w_out,
    w_up,
    w_down,
    norm_params,
    embed_first,
    qkv_first,
    out_first,
    up_first,
    down_first,
    norm_first,
    embed_second,
    qkv_second,
    out_second,
    up_second,
    down_second,
    norm_second,
):
    z = Sizes(
        lax.axis_size("blk"),
        lax.axis_size("head"),
        token_ids.shape[0],
        token_ids.shape[1],
        w_qkv.shape,
        w_up.shape,
        w_down.shape,
    )
    masters = (embed_table, w_qkv, w_out, w_up, w_down, norm_params)
    firsts = (embed_first, qkv_first, out_first, up_first, down_first, norm_first)
    seconds = (embed_second, qkv_second, out_second, up_second, down_second, norm_second)
    tokens = (token_ids, targets, masked, lengths, family_weight)
    if z.fused(token_ids.shape[1]):
        scal, grads = fused_step(z, *tokens, *masters)
        return fused_update(LAYERS, scal, grads, masters, firsts, seconds)
    loss_sum, weight_sum, grad_norm, squares, grads = plain_step(*tokens, *masters)
    stream_rms = jnp.sqrt(squares.reshape(LAYERS, 3) / (jnp.sum(lengths).astype(jnp.float32) * D))
    factor = CLIP_NORM / jnp.maximum(grad_norm, CLIP_NORM)
    results = [loss_sum, weight_sum, grad_norm, stream_rms]
    for group_idx in range(6):
        first, second, weight = adamw_update(
            masters[group_idx],
            firsts[group_idx],
            seconds[group_idx],
            grads[group_idx] * factor,
            RATES[group_idx],
            DECAYS[group_idx],
        )
        results += [first, second, weight, weight.astype(jnp.bfloat16)]
    return tuple(results)


def solution(mesh):
    return jax.shard_map(
        local,
        mesh=mesh,
        in_specs=(
            P(None, "blk"),
            P(None, "blk"),
            P(None, "blk"),
            P(),
            P(),
            P(None, "blk"),
            P(None, "blk", None, "head"),
            P(None, "head", "blk"),
            P(None, "blk", "head"),
            P(None, ("head", "blk"), None),
            P(None, None, "blk"),
            P(None, "blk"),
            P(None, "blk", None, "head"),
            P(None, "head", "blk"),
            P(None, "blk", "head"),
            P(None, ("head", "blk"), None),
            P(None, None, "blk"),
            P(None, "blk"),
            P(None, "blk", None, "head"),
            P(None, "head", "blk"),
            P(None, "blk", "head"),
            P(None, ("head", "blk"), None),
            P(None, None, "blk"),
        ),
        out_specs=(
            P(),
            P(),
            P(),
            P(),
            P(None, "blk"),
            P(None, "blk"),
            P(None, "blk"),
            P(None, "blk"),
            P(None, "blk", None, "head"),
            P(None, "blk", None, "head"),
            P(None, "blk", None, "head"),
            P(None, "blk", None, "head"),
            P(None, "head", "blk"),
            P(None, "head", "blk"),
            P(None, "head", "blk"),
            P(None, "head", "blk"),
            P(None, "blk", "head"),
            P(None, "blk", "head"),
            P(None, "blk", "head"),
            P(None, "blk", "head"),
            P(None, ("head", "blk"), None),
            P(None, ("head", "blk"), None),
            P(None, ("head", "blk"), None),
            P(None, ("head", "blk"), None),
            P(None, None, "blk"),
            P(None, None, "blk"),
            P(None, None, "blk"),
            P(None, None, "blk"),
        ),
        check_vma=False,
    )
```

```python
import functools

import jax
import jax.numpy as jnp
from jax import lax
from jax.experimental import pallas as pl
from jax.experimental.pallas import tpu as pltpu
from jax.sharding import PartitionSpec as P

VOCAB = 25
D = 640
HEAD_DIM = 32
LAYERS = 2
STEP = 10


NEGATIVE = -1e30
NORM_EPS = 1e-05
CLIP_NORM = 0.01
BETA_FIRST = 0.9
BETA_SECOND = 0.999
ADAM_EPS = 1e-08
RATES = (0.2, 0.1, 0.5, 0.1, 0.03, 0.5)
DECAYS = (0.1, 0.1, 0.1, 0.1, 0.1, 0.0)
HIGHEST = lax.Precision.HIGHEST


def layer_norm(inputs, gain_row, shift_row):
    centred = inputs - jnp.mean(inputs, axis=-1, keepdims=True)
    spread = jnp.mean(centred * centred, axis=-1, keepdims=True)
    return centred * lax.rsqrt(spread + NORM_EPS) * gain_row + shift_row


def gelu_exact(inputs):
    return jax.nn.gelu(inputs, approximate=False)


def adamw_update(weight, first, second, gradient, rate, decay):
    first = BETA_FIRST * first + (1.0 - BETA_FIRST) * gradient
    second = BETA_SECOND * second + (1.0 - BETA_SECOND) * gradient * gradient
    first_hat = first / (1.0 - BETA_FIRST**STEP)
    second_hat = second / (1.0 - BETA_SECOND**STEP)
    weight = weight - rate * (first_hat / (jnp.sqrt(second_hat) + ADAM_EPS) + decay * weight)
    return (first, second, weight)


def slice_head(tensor, head_index):
    return lax.dynamic_slice_in_dim(tensor, head_index * HEAD_DIM, HEAD_DIM, tensor.ndim - 1)


def join_heads(stacked):
    moved = jnp.moveaxis(stacked, 0, 2)
    return moved.reshape(moved.shape[0], moved.shape[1], -1)


def spread_rows(normed):
    return lax.all_gather(normed, "head", axis=0, tiled=True)


def spread_grads(grad_rows):
    return lax.all_gather(grad_rows, "head", axis=0, tiled=True)


def sum_rows(full_rows, weight, row_share):

    def row_term(row_start, row_count):
        return jnp.dot(full_rows, weight, preferred_element_type=jnp.float32)

    return lax.psum_scatter(
        row_term(jnp.int32(0), row_share * lax.axis_size("head")),
        "head",
        scatter_dimension=0,
        tiled=True,
    )


def sum_grads(full_rows, weight, row_share):

    def row_term(row_start, row_count):
        return jnp.einsum("nc,dc->nd", full_rows, weight, preferred_element_type=jnp.float32)

    return lax.psum_scatter(
        row_term(jnp.int32(0), row_share * lax.axis_size("head")).astype(jnp.bfloat16),
        "head",
        scatter_dimension=0,
        tiled=True,
    ).astype(jnp.float32)


def attend(queries, keys_all, values_all, live_keys):
    local_heads = queries.shape[-1] // HEAD_DIM
    score_scale = HEAD_DIM ** (-0.5)
    live_mask = live_keys[:, None, :]

    def one_head(head_index):
        scores = (
            jnp.einsum(
                "ste,sje->stj",
                slice_head(queries, head_index),
                slice_head(keys_all, head_index),
                preferred_element_type=jnp.float32,
            )
            * score_scale
        )
        masked_scores = jnp.where(live_mask, scores, NEGATIVE)
        row_peak = jnp.max(masked_scores, axis=-1, keepdims=True)
        exp_scores = jnp.exp(masked_scores - row_peak)
        row_total = jnp.sum(exp_scores, axis=-1, keepdims=True)
        attn_probs = (exp_scores / row_total).astype(jnp.bfloat16)
        attended = jnp.einsum(
            "stj,sje->ste",
            attn_probs,
            slice_head(values_all, head_index),
            preferred_element_type=jnp.float32,
        )
        return (attended, (row_peak + jnp.log(row_total))[..., 0])

    outputs, log_totals = lax.map(one_head, jnp.arange(local_heads))
    return (join_heads(outputs), log_totals)


def attend_back(queries, keys_all, values_all, grad_heads, log_totals, live_keys):
    local_heads = queries.shape[-1] // HEAD_DIM
    score_scale = HEAD_DIM ** (-0.5)
    live_mask = live_keys[:, None, :]

    def one_head(head_index):
        query_h = slice_head(queries, head_index)
        key_h = slice_head(keys_all, head_index)
        grad_h = slice_head(grad_heads, head_index)
        scores = (
            jnp.einsum("ste,sje->stj", query_h, key_h, preferred_element_type=jnp.float32)
            * score_scale
        )
        masked_scores = jnp.where(live_mask, scores, NEGATIVE)
        attn_probs = jnp.exp(masked_scores - log_totals[head_index][..., None])
        grad_probs = jnp.einsum(
            "ste,sje->stj",
            grad_h,
            slice_head(values_all, head_index),
            preferred_element_type=jnp.float32,
        )
        row_delta = jnp.sum(attn_probs * grad_probs, axis=-1)
        grad_scores = (attn_probs * (grad_probs - row_delta[..., None])).astype(jnp.bfloat16)
        grad_query = (
            jnp.einsum("stj,sje->ste", grad_scores, key_h, preferred_element_type=jnp.float32)
            * score_scale
        )
        grad_key = (
            jnp.einsum("stj,ste->sje", grad_scores, query_h, preferred_element_type=jnp.float32)
            * score_scale
        )
        grad_value = jnp.einsum(
            "stj,ste->sje",
            attn_probs.astype(jnp.bfloat16),
            grad_h,
            preferred_element_type=jnp.float32,
        )
        return (grad_query, grad_key, grad_value)

    grad_query, grad_key, grad_value = lax.map(one_head, jnp.arange(local_heads))
    grad_key, grad_value = (
        lax.psum_scatter(grad_key, "blk", scatter_dimension=2, tiled=True),
        lax.psum_scatter(grad_value, "blk", scatter_dimension=2, tiled=True),
    )
    return (join_heads(grad_query), join_heads(grad_key), join_heads(grad_value))


def layer_forward(stream, layer_weights, norm_rows, live_keys, row_share):
    w_qkv, w_out, w_up, w_down = layer_weights
    seq_count = live_keys.shape[0]
    normed = layer_norm(stream, norm_rows[0, 0], norm_rows[0, 1]).astype(jnp.bfloat16)
    normed_all = spread_rows(normed)
    packed = jnp.dot(
        normed_all, w_qkv.reshape(w_qkv.shape[0], -1), preferred_element_type=jnp.float32
    ).astype(jnp.bfloat16)
    packed = packed.reshape(seq_count, -1, 3, w_qkv.shape[-1])
    queries, keys_local, values_local = (packed[:, :, 0], packed[:, :, 1], packed[:, :, 2])
    keys_all, values_all = (
        lax.all_gather(keys_local, "blk", axis=1, tiled=True),
        lax.all_gather(values_local, "blk", axis=1, tiled=True),
    )
    attended, log_totals = attend(queries, keys_all, values_all, live_keys)
    attended = attended.astype(jnp.bfloat16).reshape(-1, attended.shape[-1])
    attn_out = sum_rows(attended, w_out, row_share)
    middle = stream + attn_out
    normed_two = layer_norm(middle, norm_rows[1, 0], norm_rows[1, 1]).astype(jnp.bfloat16)
    normed_two_all = spread_rows(normed_two)
    hidden_pre = jnp.dot(normed_two_all, w_up, preferred_element_type=jnp.float32)
    hidden_act = gelu_exact(hidden_pre).astype(jnp.bfloat16)
    ffn_out = sum_rows(hidden_act, w_down, row_share)
    kept = (
        stream,
        middle,
        normed_all,
        queries,
        keys_local,
        values_local,
        keys_all,
        values_all,
        log_totals,
        attended,
        normed_two_all,
        hidden_pre,
    )
    return (middle + ffn_out, attn_out, ffn_out, kept)


def layer_backward(grad_stream, kept, layer_weights, norm_rows, live_keys, row_share):
    (
        stream,
        middle,
        normed_all,
        queries,
        keys_local,
        values_local,
        keys_all,
        values_all,
        log_totals,
        attended,
        normed_two_all,
        hidden_pre,
    ) = kept
    w_qkv, w_out, w_up, w_down = layer_weights
    grad_ffn = spread_grads(grad_stream.astype(jnp.bfloat16))
    hidden_act, gelu_back = jax.vjp(gelu_exact, hidden_pre)
    grad_down = jnp.einsum(
        "nf,nd->fd", hidden_act.astype(jnp.bfloat16), grad_ffn, preferred_element_type=jnp.float32
    )
    grad_act = jnp.einsum("nd,fd->nf", grad_ffn, w_down, preferred_element_type=jnp.float32)
    (grad_pre,) = gelu_back(grad_act)
    grad_pre = grad_pre.astype(jnp.bfloat16)
    grad_up = jnp.einsum("nd,nf->df", normed_two_all, grad_pre, preferred_element_type=jnp.float32)
    grad_normed_two = sum_grads(grad_pre, w_up, row_share)
    _, norm_back_two = jax.vjp(layer_norm, middle, norm_rows[1, 0], norm_rows[1, 1])
    grad_mid, gain_two, shift_two = norm_back_two(grad_normed_two)
    grad_middle = grad_stream + grad_mid
    grad_attn = spread_grads(grad_middle.astype(jnp.bfloat16))
    grad_out_w = jnp.einsum("nf,nd->fd", attended, grad_attn, preferred_element_type=jnp.float32)
    grad_heads = (
        jnp.einsum("nd,fd->nf", grad_attn, w_out, preferred_element_type=jnp.float32)
        .astype(jnp.bfloat16)
        .reshape(queries.shape)
    )
    grad_query, grad_key, grad_value = attend_back(
        queries, keys_all, values_all, grad_heads, log_totals, live_keys
    )
    grad_packed = (
        jnp.stack((grad_query, grad_key, grad_value), axis=2)
        .astype(jnp.bfloat16)
        .reshape(normed_all.shape[0], -1)
    )
    grad_qkv = jnp.einsum(
        "nd,nc->dc", normed_all, grad_packed, preferred_element_type=jnp.float32
    ).reshape(w_qkv.shape)
    grad_normed = sum_grads(grad_packed, w_qkv.reshape(w_qkv.shape[0], -1), row_share)
    _, norm_back_one = jax.vjp(layer_norm, stream, norm_rows[0, 0], norm_rows[0, 1])
    grad_input, gain_one, shift_one = norm_back_one(grad_normed)
    norm_grads = jnp.stack((jnp.stack((gain_one, shift_one)), jnp.stack((gain_two, shift_two))))
    return (grad_middle + grad_input, (grad_qkv, grad_out_w, grad_up, grad_down), norm_grads)


def plain_step(
    token_ids,
    targets,
    masked,
    lengths,
    family_weight,
    embed_table,
    w_qkv,
    w_out,
    w_up,
    w_down,
    norm_params,
):
    blk_count = lax.axis_size("blk")
    head_count = lax.axis_size("head")
    seq_count, blk_tokens = token_ids.shape
    row_share = seq_count * blk_tokens // head_count
    row_first = lax.axis_index("head") * row_share
    blk_start = lax.axis_index("blk") * blk_tokens
    table_all, qkv_all, out_all, up_all, down_all, norm_all = (
        lax.all_gather(embed_table.astype(jnp.bfloat16), "blk", axis=1, tiled=True),
        lax.all_gather(w_qkv.astype(jnp.bfloat16), "blk", axis=1, tiled=True),
        lax.all_gather(w_out.astype(jnp.bfloat16), "blk", axis=2, tiled=True),
        lax.all_gather(w_up.astype(jnp.bfloat16), "blk", axis=1, tiled=True),
        lax.all_gather(w_down.astype(jnp.bfloat16), "blk", axis=1, tiled=True),
        lax.all_gather(norm_params.astype(jnp.bfloat16), "blk", axis=2, tiled=True),
    )
    token_table = table_all[:VOCAB]
    place_rows = lax.dynamic_slice_in_dim(table_all, VOCAB + blk_start, blk_tokens, 0)
    norm_rows = norm_all.astype(jnp.float32)
    live_keys = jnp.arange(blk_tokens * blk_count)[None, :] < lengths[:, None]
    positions = blk_start + jnp.arange(blk_tokens)
    live_local = positions[None, :] < lengths[:, None]
    seq_of_row = (row_first + jnp.arange(row_share)) // blk_tokens
    place_of_row = (row_first + jnp.arange(row_share)) % blk_tokens
    seq_hot = (seq_of_row[:, None] == jnp.arange(seq_count)[None, :]).astype(jnp.float32)
    place_hot = place_of_row[:, None] == jnp.arange(blk_tokens)[None, :]
    row_family = jnp.dot(seq_hot, family_weight, precision=HIGHEST)
    row_live = lax.dynamic_slice_in_dim(live_local.reshape(-1), row_first, row_share, 0).astype(
        jnp.float32
    )[:, None]
    row_ids = lax.dynamic_slice_in_dim(token_ids.reshape(-1), row_first, row_share, 0)
    row_targets = lax.dynamic_slice_in_dim(targets.reshape(-1), row_first, row_share, 0)
    row_masked = lax.dynamic_slice_in_dim(masked.reshape(-1), row_first, row_share, 0)
    token_hot = row_ids[:, None] == jnp.arange(VOCAB)[None, :]
    stream = jnp.dot(
        token_hot.astype(jnp.bfloat16), token_table, preferred_element_type=jnp.float32
    ) + jnp.dot(place_hot.astype(jnp.bfloat16), place_rows, preferred_element_type=jnp.float32)
    layer_stats = []
    kept_all = []
    for layer_idx in range(LAYERS):
        layer_weights = (
            qkv_all[layer_idx],
            out_all[layer_idx],
            up_all[layer_idx],
            down_all[layer_idx],
        )
        layer_stats.append(jnp.sum(stream * stream * row_live))
        stream, attn_out, ffn_out, kept = layer_forward(
            stream,
            layer_weights,
            norm_rows[2 * layer_idx : 2 * layer_idx + 2],
            live_keys,
            row_share,
        )
        layer_stats.append(jnp.sum(attn_out * attn_out * row_live))
        layer_stats.append(jnp.sum(ffn_out * ffn_out * row_live))
        kept_all.append(kept)
    final_low = layer_norm(stream, norm_rows[2 * LAYERS, 0], norm_rows[2 * LAYERS, 1]).astype(
        jnp.bfloat16
    )
    logits = jnp.einsum("nd,vd->nv", final_low, token_table, preferred_element_type=jnp.float32)
    shifted = logits - jnp.max(logits, axis=-1, keepdims=True)
    log_probs = shifted - jnp.log(jnp.sum(jnp.exp(shifted), axis=-1, keepdims=True))
    target_hot = (row_targets[:, None] == jnp.arange(VOCAB)[None, :]).astype(jnp.float32)
    token_loss = -jnp.sum(target_hot * log_probs, axis=1)
    token_weight = row_masked.astype(jnp.float32) * row_family
    loss_sum, weight_sum, squares = lax.psum(
        (jnp.sum(token_weight * token_loss), jnp.sum(token_weight), jnp.stack(layer_stats)),
        ("blk", "head"),
    )
    grad_logits = ((token_weight / weight_sum)[:, None] * (jnp.exp(log_probs) - target_hot)).astype(
        jnp.bfloat16
    )
    grad_final = jnp.einsum(
        "nv,vd->nd", grad_logits, token_table, preferred_element_type=jnp.float32
    )
    grad_table = jnp.einsum("nv,nd->vd", grad_logits, final_low, preferred_element_type=jnp.float32)
    _, final_back = jax.vjp(layer_norm, stream, norm_rows[2 * LAYERS, 0], norm_rows[2 * LAYERS, 1])
    grad_stream, gain_last, shift_last = final_back(grad_final)
    layer_grads = []
    norm_grads = []
    for layer_idx in reversed(range(LAYERS)):
        layer_weights = (
            qkv_all[layer_idx],
            out_all[layer_idx],
            up_all[layer_idx],
            down_all[layer_idx],
        )
        grad_stream, grads_now, norms_now = layer_backward(
            grad_stream,
            kept_all[layer_idx],
            layer_weights,
            norm_rows[2 * layer_idx : 2 * layer_idx + 2],
            live_keys,
            row_share,
        )
        layer_grads.insert(0, grads_now)
        norm_grads.insert(0, norms_now)
    grad_table = grad_table + jnp.dot(
        token_hot.astype(jnp.float32).T, grad_stream, precision=HIGHEST
    )
    grad_place = jnp.dot(place_hot.astype(jnp.float32).T, grad_stream, precision=HIGHEST)
    grad_norms = jnp.concatenate(norm_grads + [jnp.stack((gain_last, shift_last))[None]], axis=0)
    stacked = [
        jnp.stack([layer_entry[slot_idx] for layer_entry in layer_grads]) for slot_idx in range(4)
    ]
    table_sum, place_sum, norm_sum = (
        lax.psum(grad_table.astype(jnp.bfloat16), "head").astype(jnp.float32),
        lax.psum(grad_place.astype(jnp.bfloat16), "head").astype(jnp.float32),
        lax.psum(grad_norms.astype(jnp.bfloat16), "head").astype(jnp.float32),
    )
    place_full = lax.dynamic_update_slice_in_dim(
        jnp.zeros((blk_tokens * blk_count, place_sum.shape[1]), jnp.float32),
        place_sum,
        blk_start,
        0,
    )
    full_table = jnp.concatenate((table_sum, place_full), axis=0)
    reduced = (
        lax.psum_scatter(full_table, "blk", scatter_dimension=1, tiled=True),
        lax.psum_scatter(stacked[0], "blk", scatter_dimension=1, tiled=True),
        lax.psum_scatter(stacked[1], "blk", scatter_dimension=2, tiled=True),
        lax.psum_scatter(stacked[2], "blk", scatter_dimension=1, tiled=True),
        lax.psum_scatter(stacked[3], "blk", scatter_dimension=1, tiled=True),
        lax.psum_scatter(norm_sum, "blk", scatter_dimension=2, tiled=True),
    )
    sharded_squares = sum((jnp.sum(grad_part * grad_part) for grad_part in reduced[1:5]))
    shared_squares = (
        jnp.sum(reduced[0] * reduced[0]) + jnp.sum(reduced[5] * reduced[5])
    ) / head_count
    grad_norm = jnp.sqrt(lax.psum(sharded_squares + shared_squares, ("blk", "head")))
    return loss_sum, weight_sum, grad_norm, squares, reduced


BF16 = jnp.bfloat16
F32 = jnp.float32
MESH = pl.DeviceIdType.MESH
LOG2E = 1.4426950408889634
NORM_LANE = 32


def dot(left, right, left_dim, right_dim):
    return lax.dot_general(
        left, right, (((left_dim,), (right_dim,)), ((), ())), preferred_element_type=F32
    )


class Sizes:
    def __init__(self, blk, head, seqs, blk_tokens, w_qkv, w_up, w_down):
        self.B, self.H, self.S = blk, head, seqs
        self.L = w_qkv[0]
        self.DB = w_qkv[1]
        self.D = self.DB * blk
        self.HC = w_qkv[3]
        self.T = blk_tokens * blk
        self.G = blk // seqs if blk % seqs == 0 else 0
        self.FD = w_down[1]
        if self.G:
            self.NR = self.G * head
            self.R = self.T // self.NR
            self.NC = self.NR // 2
            self.FU = w_up[2] // self.G

    def fused(self, blk_tokens):
        if self.G != 2 or self.S != 4 or self.H % 2 or self.R != blk_tokens or self.R != 128:
            return False
        if self.FU != self.FD * self.S or 3 * self.S > 16 or VOCAB > NORM_LANE:
            return False
        if NORM_LANE + 2 * (2 * self.L + 1) > 128:
            return False
        if any(n % 16 for n in (self.DB, self.HC, self.FD)) or self.D % 128 or self.FU % 128:
            return False
        weights = self.L * 2 * (4 * self.D * self.HC + 2 * self.D * self.FU)
        kept = self.L * self.T * (6 * self.D + 6 * self.FU + 14 * self.HC)
        return 3 * weights + kept + 16 * self.T * self.D + 8 * self.T * 256 * 4 < (60 << 20)


def step_kernel(
    z,
    lens,
    fam,
    tok_in,
    tgt_in,
    msk_in,
    emb_in,
    wq_in,
    wo_in,
    wu_hbm,
    wd_hbm,
    norm_in,
    scal_out,
    ge_out,
    gq_out,
    go_out,
    gu_out,
    gd_out,
    gn_out,
    wu_in,
    wd_in,
    in_sem,
    ge_made,
    gq_made,
    go_made,
    gu_made,
    gd_made,
    out_sem,
    ids,
    wq_own,
    wo_own,
    wu_own,
    wd_own,
    gu_sum,
    idsg,
    tg,
    wq,
    wo,
    wu,
    wd,
    h1,
    h2,
    df,
    da,
    act,
    slope,
    du,
    qt,
    kt,
    vt,
    o32,
    ob,
    dob,
    lse,
    dqkv,
    bias,
    sbuf,
    pbuf,
    xs,
    xm,
    keep,
    psrc,
    csrc,
    srecv,
    rrecv,
    sg,
    stq,
    sto,
    stu,
    std,
    rq,
    ro,
    ru,
    rd,
    rc,
    tq,
    to,
    tu,
    td,
    tc,
    fst,
    frx,
    hrs,
    hrx,
    scg,
    id_s,
    id_r,
    tp_s,
    tp_r,
    w_s,
    w_r,
    ag_s,
    ag_r,
    rs_s,
    rs_r,
    g_s,
    g_r,
    f_s,
    f_r,
    hx_s,
    hx_r,
    sc_s,
    sc_r,
):
    B, H, S, G, L, D, DB, HC, R, NC, NR, FU, FD, T = (
        z.B, z.H, z.S, z.G, z.L, z.D, z.DB, z.HC, z.R, z.NC, z.NR, z.FU, z.FD, z.T,
    )
    N_HEADS = HC // HEAD_DIM
    W = 2 * R
    QT = 2
    scale = HEAD_DIM ** (-0.5)
    c2 = scale * LOG2E
    b = lax.axis_index("blk")
    h = lax.axis_index("head")
    s, g = b // G, b % G
    y, c = h // 2, h % 2
    own_row = g * H + h
    s1 = s + 1 - 2 * (s % 2)
    s2 = (s + 2) % S
    s3 = (s1 + 2) % S

    def dev(blk_i, head_i):
        return (blk_i, head_i)

    sibling = dev(b, y * 2 + 1 - c)

    def peer(k):
        return dev(s * G + (g + k // 2) % G, ((y + k % 2) % 2) * 2 + c)

    waits = []

    def send(src, dst, ssem, rsem, device):
        copy = pltpu.make_async_remote_copy(src, dst, ssem, rsem, device, MESH)
        copy.start()
        return copy

    def arrived(dst, ssem, rsem):
        pltpu.make_async_remote_copy(dst, dst, ssem, rsem, sibling, MESH).wait_recv()

    def over_blk(body):
        def one(k, carry):
            body(lax.rem(b + k, B))
            return carry

        lax.fori_loop(1, B, one, 0)

    def rows(i, n):
        return pl.ds(pl.multiple_of(i * n, 16), n)

    inputs = [
        pltpu.make_async_copy(wu_hbm, wu_in, in_sem.at[0]),
        pltpu.make_async_copy(wd_hbm, wd_in, in_sem.at[1]),
    ]
    for copy in inputs:
        copy.start()

    barrier = pltpu.get_barrier_semaphore()

    def greet_blk(other):
        pl.semaphore_signal(barrier, inc=1, device_id=dev(other, h), device_id_type=MESH)

    def greet_head(k, carry):
        pl.semaphore_signal(
            barrier, inc=1, device_id=dev(b, lax.rem(h + k, H)), device_id_type=MESH
        )
        return carry

    over_blk(greet_blk)
    lax.fori_loop(1, H, greet_head, 0)

    table = emb_in[...]
    ids[...] = jnp.zeros((16, R), jnp.int32)
    ids[0:S] = tok_in[...]
    ids[S : 2 * S] = tgt_in[...]
    ids[2 * S : 3 * S] = msk_in[...]
    sg[...] = jnp.zeros((D, 128), F32)
    for i in range(2 * L + 1):
        sg[NORM_LANE + 2 * i : NORM_LANE + 2 * i + 2, 0:DB] = norm_in[i]
    lane_small = lax.broadcasted_iota(jnp.int32, (DB, 128), 1)
    token_part = jnp.where(lane_small < VOCAB, table[:, 0:128], sg[0:128, :].T[0:DB]).astype(BF16)
    own_rows = rows(b, DB)
    tg[own_rows, 0:128] = token_part
    tg[own_rows, 128:] = table[:, VOCAB:].astype(BF16)
    pl.semaphore_wait(barrier, B + H - 2)

    def send_ids(other):
        send(ids, idsg.at[b], id_s.at[other], id_r.at[b], dev(other, h))

    over_blk(send_ids)
    idsg[b] = ids[...]

    lanes_in = pl.ds(pl.multiple_of(c * 512, 128), T + 128 - 512)
    lanes_out = pl.ds(pl.multiple_of(c * (T + 128 - 512), 128), 512)
    lanes_back = pl.ds(pl.multiple_of((1 - c) * (T + 128 - 512), 128), 512)

    def t_send(m, at, cut, device):
        block = tg.at[at, cut]
        waits.append(send(block, block, tp_s.at[m], tp_r.at[m], device))

    def t_here(m, at, cut):
        arrived(tg.at[at, cut], tp_s.at[m], tp_r.at[m])

    def plane_rows(plane, column):
        return rows(plane * G + column, DB)

    t_send(0, own_rows, lanes_in, dev(s2 * G + g, h))
    t_send(1, own_rows, lanes_in, dev(s1 * G + g, h))
    t_send(3, own_rows, lanes_in, dev(s * G + 1 - g, h))

    def w_sem(sems, l, kind, m):
        return sems.at[l * 21 + (-1, 6, 14, 17)[kind] + m]

    def w_ref(l, kind, at):
        return (wq, wo, wu, wd)[kind].at[l, at]

    def shard_rows(kind, plane, column=None):
        if kind == 3:
            return rows(plane, FD)
        return rows(plane * G + (g if column is None else column), DB)

    def w_send(l, kind, m, src, at, device):
        waits.append(
            send(src, w_ref(l, kind, at), w_sem(w_s, l, kind, m), w_sem(w_r, l, kind, m), device)
        )

    def w_arrived(l, kind, m, at):
        arrived(w_ref(l, kind, at), w_sem(w_s, l, kind, m), w_sem(w_r, l, kind, m))

    rounded = set()

    def round_weights(l, kind):
        if (l, kind) in rounded:
            return
        rounded.add((l, kind))
        at = shard_rows(kind, s)
        if kind == 0:
            wq_own[l] = jnp.concatenate([wq_in[l, i] for i in range(3)], axis=1).astype(BF16)
            wq[l, at] = wq_own[l]
        elif kind == 1:
            wo_own[l] = wo_in[l].T.astype(BF16)
            wo[l, at] = wo_own[l]
        elif kind == 2:
            up = wu_in[l]
            for j in range(G):
                parts = [up[:, (i * G + j) * FD : (i * G + j + 1) * FD] for i in range(S)]
                wu_own[l, j] = jnp.concatenate(parts, axis=1).astype(BF16)
            wu[l, at] = wu_own[l, g]
        else:
            wd_own[l] = wd_in[l].astype(BF16)
            wd[l, at] = wd_own[l]

    def plane_block(kind, plane):
        return rows(plane, FD) if kind == 3 else rows(plane, G * DB)

    def send_weights(l, kind):
        round_weights(l, kind)
        at = shard_rows(kind, s)
        if kind == 2:
            w_send(l, 2, 0, wu_own.at[l, 1 - g], at, dev(s * G + 1 - g, h))
            return
        src = (wq_own, wo_own, None, wd_own)[kind].at[l]
        w_send(l, kind, 1, src, at, dev(s2 * G + g, h))
        w_send(l, kind, 2, src, at, dev(s1 * G + g, h))

    def push_weights(l):
        w_arrived(l, 2, 0, shard_rows(2, s, 1 - g))
        at = plane_block(2, s)
        w_send(l, 2, 1, w_ref(l, 2, at), at, dev(s2 * G + g, h))
        w_send(l, 2, 2, w_ref(l, 2, at), at, dev(s1 * G + g, h))

    def relay_weights(l, kind):
        at = shard_rows(kind, s2) if kind < 2 else plane_block(kind, s2)
        w_arrived(l, kind, 1, at)
        w_send(l, kind, 3, w_ref(l, kind, at), at, dev(s1 * G + g, h))

    def cross_weights(l, kind, planes):
        for m, plane, known in ((4, s, True), (5, s2, True), (6, s1, False), (7, s3, False)):
            if m - 4 in planes:
                at = shard_rows(kind, plane)
                if not known:
                    w_arrived(l, kind, m - 4, at)
                w_send(l, kind, m, w_ref(l, kind, at), at, dev(s * G + 1 - g, h))

    def wait_weights(l, kind):
        if kind < 2:
            for m, plane in ((4, s), (5, s2), (6, s1), (7, s3)):
                w_arrived(l, kind, m, shard_rows(kind, plane, 1 - g))
        else:
            w_arrived(l, kind, 2, plane_block(kind, s1))
            w_arrived(l, kind, 3, plane_block(kind, s3))

    send_weights(0, 0)
    cross_weights(0, 0, (0,))
    send_weights(0, 1)
    at = plane_rows(s2, g)
    t_here(0, at, lanes_in)
    t_send(2, at, lanes_in, dev(s1 * G + g, h))
    t_send(4, at, lanes_in, dev(s * G + 1 - g, h))
    for copy in inputs:
        copy.wait()
    send_weights(0, 2)
    for kind in range(2):
        relay_weights(0, kind)
    send_weights(0, 3)
    for later_layer in range(1, L):
        for kind in range(4):
            round_weights(later_layer, kind)
    for m, plane in ((1, s1), (2, s3)):
        at = plane_rows(plane, g)
        t_here(m, at, lanes_in)
        t_send(m + 4, at, lanes_in, dev(s * G + 1 - g, h))
    cross_weights(0, 0, (1, 2, 3))

    half_rows = (slice(0, D // 2), slice(D // 2, D))

    ag_sent = []

    def ag_send(m, src, dst, device):
        ag_sent.append(send(src, dst, ag_s.at[m], ag_r.at[m], device))

    def ag_here(m, dst):
        arrived(dst, ag_s.at[m], ag_r.at[m])

    def ag_left():
        for copy in ag_sent:
            copy.wait_send()
        ag_sent.clear()

    def block(buf, k, half):
        return buf.at[:, k * W + half * R : k * W + half * R + R]

    def block_half(buf, k, half, i):
        return buf.at[half_rows[i], k * W + half * R : k * W + half * R + R]

    def spread(buf, base=0):
        ag_left()
        ag_send(base + 0, block_half(buf, 0, 0, 0), block_half(buf, 1, 0, 0), peer(1))
        ag_send(base + 1, block_half(buf, 0, 0, 1), block_half(buf, 2, 0, 1), peer(2))
        ag_send(base + 2, block_half(buf, 0, 0, 1), block_half(buf, 1, 0, 1), peer(1))
        ag_send(base + 3, block_half(buf, 0, 0, 0), block_half(buf, 2, 0, 0), peer(2))
        ag_send(base + 4, block(buf, 0, 0), block(buf, 0, 1), sibling)

    def relay_near(buf, base=0):
        ag_here(base + 0, block_half(buf, 1, 0, 0))
        ag_send(base + 5, block_half(buf, 1, 0, 0), block_half(buf, 3, 0, 0), peer(2))
        ag_here(base + 1, block_half(buf, 2, 0, 1))
        ag_send(base + 6, block_half(buf, 2, 0, 1), block_half(buf, 3, 0, 1), peer(1))
        ag_here(base + 2, block_half(buf, 1, 0, 1))
        ag_send(base + 7, block(buf, 1, 0), block(buf, 1, 1), sibling)
        ag_here(base + 3, block_half(buf, 2, 0, 0))
        ag_send(base + 8, block(buf, 2, 0), block(buf, 2, 1), sibling)

    def relay_far(buf, base=0):
        for i in range(2):
            ag_here(base + 5 + i, block_half(buf, 3, 0, i))
            ag_send(base + 9 + i, block_half(buf, 3, 0, i), block_half(buf, 3, 1, i), sibling)

    def have(buf, k, base=0):
        if k == 0:
            ag_here(base + 4, block(buf, 0, 1))
        elif k < 3:
            ag_here(base + 6 + k, block(buf, k, 1))
        else:
            for i in range(2):
                ag_here(base + 9 + i, block_half(buf, 3, 1, i))

    def spread_column(buf):
        ag_left()
        ag_send(0, block(buf, 0, 0), block(buf, 1, 0), peer(1))
        ag_send(4, block(buf, 0, 0), block(buf, 0, 1), sibling)

    def relay_column(buf):
        ag_here(0, block(buf, 1, 0))
        ag_send(7, block(buf, 1, 0), block(buf, 1, 1), sibling)

    staged = {}
    summed_pairs = set()
    half_of = (slice(0, D // 2), slice(D // 2, D))

    def stage(ref, key, value):
        for copy in staged.pop(key, ()):
            copy.wait_send()
        ref[...] = value

    def rs_set(use, m):
        return m + 10 * (use % 4 == 3)

    def rs_send(use, m, src, dst, device):
        n = rs_set(use, m)
        return [send(src, dst, rs_s.at[n], rs_r.at[n], device)]

    def rs_here(use, m, dst):
        n = rs_set(use, m)
        arrived(dst, rs_s.at[n], rs_r.at[n])

    def part(use, k, value):
        keep[k] = value[:, :R]
        stage(psrc.at[k], ("p", k), value[:, R:].astype(BF16))
        staged["p", k] = rs_send(use, k, psrc.at[k], srecv.at[use % 4, k], sibling)

    def pair_sum(use, k, at=slice(0, D)):
        if (use, k) not in summed_pairs:
            summed_pairs.add((use, k))
            rs_here(use, k, srecv.at[use % 4, k])
        return keep[k, at] + srecv[use % 4, k, at].astype(F32)

    def pass_half(use, m, k, i, value, slot, device):
        stage(csrc.at[k, half_of[i]], ("c", k, i), value.astype(BF16))
        staged["c", k, i] = rs_send(
            use, m, csrc.at[k, half_of[i]], rrecv.at[use % 4, slot, half_of[i]], device
        )

    def pass_across(use):
        pass_half(use, 4, 3, 0, pair_sum(use, 3, half_of[0]), 0, peer(1))
        pass_half(use, 5, 3, 1, pair_sum(use, 3, half_of[1]), 0, peer(2))

    def pass_near(use):
        pass_half(use, 6, 1, 0, pair_sum(use, 1, half_of[0]), 1, peer(1))
        pass_half(use, 7, 2, 1, pair_sum(use, 2, half_of[1]), 2, peer(2))

    def pass_joined(use):
        for i, k in ((0, 2), (1, 1)):
            rs_here(use, 4 + i, rrecv.at[use % 4, 0, half_of[i]])
            value = pair_sum(use, k, half_of[i]) + rrecv[use % 4, 0, half_of[i]].astype(F32)
            pass_half(use, 8 + i, k, i, value, k, peer(k))

    def total(use):
        out = pair_sum(use, 0)
        for m, k, i in ((6, 1, 0), (7, 2, 1), (8, 2, 0), (9, 1, 1)):
            rs_here(use, m, rrecv.at[use % 4, k, half_of[i]])
        return out + rrecv[use % 4, 1].astype(F32) + rrecv[use % 4, 2].astype(F32)

    def pass_column(use):
        for i in range(2):
            pass_half(use, 6 + 3 * i, 1, i, pair_sum(use, 1, half_of[i]), 1, peer(1))

    def total_column(use):
        out = pair_sum(use, 0)
        for i in range(2):
            rs_here(use, 6 + 3 * i, rrecv.at[use % 4, 1, half_of[i]])
        return out + rrecv[use % 4, 1].astype(F32)

    def g_sem(sems, l, kind, m):
        return sems.at[l * 21 + (0, 7, 14, 18)[kind] + m]

    def g_send(l, kind, m, src, dst, device):
        return send(src, dst, g_sem(g_s, l, kind, m), g_sem(g_r, l, kind, m), device)

    def g_arrived(l, kind, m, dst):
        arrived(dst, g_sem(g_s, l, kind, m), g_sem(g_r, l, kind, m))

    def g_stage(key, ref, value):
        for copy in staged.pop(key, ()):
            copy.wait_send()
        ref[...] = value.astype(BF16)

    def g_first(l, kind, value):
        src, dst = ((stq, rq), (sto, ro), (stu, ru), (std, rd))[kind]
        g_stage(("g", kind), src, value)
        if kind < 2:
            staged["g", kind] = []
            return
        n = G * DB if kind == 2 else FD
        dst[l, 0] = src[rows(s, n)]
        staged["g", kind] = [
            g_send(l, kind, i, src.at[rows(plane, n)], dst.at[l, 1 + i], dev(s1 * G + g, h))
            for i, plane in ((1, s3), (0, s1))
        ]

    def g_cross(l, kind, planes):
        src, dst = ((stq, rq), (sto, ro))[kind]
        for m, plane in planes:
            staged["g", kind].append(
                g_send(
                    l, kind, m, src.at[rows(plane * G + 1 - g, DB)], dst.at[l, m], dev(s * G + 1 - g, h)
                )
            )

    def g_column(l, kind, m, plane):
        src, dst = ((stq, rq), (sto, ro))[kind]
        return src[rows(plane * G + g, DB)].astype(F32) + dst[l, m].astype(F32)

    def g_mid(l, kind):
        src, dst, tmp = ((stq, rq, tq), (sto, ro, to))[kind]
        g_arrived(l, kind, 0, dst.at[l, 0])
        g_stage(("m", kind, 1), tmp.at[1], g_column(l, kind, 0, s3))
        one = g_send(l, kind, 5, tmp.at[1], dst.at[l, S + 1], dev(s1 * G + g, h))
        g_arrived(l, kind, 1, dst.at[l, 1])
        g_stage(("m", kind, 0), tmp.at[0], g_column(l, kind, 1, s1))
        two = g_send(l, kind, 4, tmp.at[0], dst.at[l, S], dev(s1 * G + g, h))
        staged["m", kind, 1] = [one]
        staged["m", kind, 0] = [two]

    def g_second(l, kind):
        if kind < 2:
            src, dst, tmp = ((stq, rq, tq), (sto, ro, to))[kind]
            g_arrived(l, kind, 2, dst.at[l, 2])
            g_arrived(l, kind, 5, dst.at[l, S + 1])
            g_stage(("s", kind), tmp.at[2], g_column(l, kind, 2, s2) + dst[l, S + 1].astype(F32))
            staged["s", kind] = [g_send(l, kind, 6, tmp.at[2], dst.at[l, S + 2], dev(s2 * G + g, h))]
            return
        src, dst, tmp, n = ((stu, ru, tu, G * DB), (std, rd, td, FD))[kind - 2]
        g_arrived(l, kind, 1, dst.at[l, 2])
        g_stage(("s", kind), tmp, src[rows(s2, n)].astype(F32) + dst[l, 2].astype(F32))
        staged["s", kind] = [g_send(l, kind, 2, tmp, dst.at[l, 3], dev(s2 * G + g, h))]

    def g_third(l):
        g_arrived(l, 2, 0, ru.at[l, 1])
        g_arrived(l, 2, 2, ru.at[l, 3])

        def summed(column):
            at = rows(column, DB)
            return sum(ru[l, i, at, :].astype(F32) for i in (0, 1, 3))

        g_stage(("t", 2), tc, summed(1 - g))
        staged["t", 2] = [g_send(l, 2, 3, tc, rc.at[l], dev(s * G + 1 - g, h))]
        gu_sum[g] = summed(g)

    def lanes_of(v):
        folded = jnp.sum(v * v, axis=0, keepdims=True)
        return jnp.sum(folded, axis=1, keepdims=True) + jnp.zeros((1, 128), F32)

    def write_out(l, kind):
        made = (gq_made, go_made, gu_made, gd_made)[kind]
        out = (gq_out, go_out, gu_out, gd_out)[kind]
        return pltpu.make_async_copy(made.at[l], out.at[l], out_sem.at[l * 4 + kind])

    def g_final(l, kind):
        if kind < 2:
            dst, out = ((rq, gq_made), (ro, go_made))[kind]
            g_arrived(l, kind, 3, dst.at[l, 3])
            g_arrived(l, kind, 4, dst.at[l, S])
            g_arrived(l, kind, 6, dst.at[l, S + 2])
            value = g_column(l, kind, 3, s) + dst[l, S].astype(F32) + dst[l, S + 2].astype(F32)
            if kind == 0:
                for i in range(3):
                    out[l, i] = value[:, i * HC : (i + 1) * HC]
            else:
                out[l] = value.T
        elif kind == 2:
            g_arrived(l, 2, 3, rc.at[l])
            value = rc[l].astype(F32)
            gu_sum[1 - g] = value
            parts = [gu_sum[j, :, i * FD : (i + 1) * FD] for i in range(S) for j in range(G)]
            gu_made[l] = jnp.concatenate(parts, axis=1)
            write_out(l, kind).start()
            return lanes_of(gu_sum[0]) + lanes_of(gu_sum[1])
        else:
            g_arrived(l, 3, 0, rd.at[l, 1])
            g_arrived(l, 3, 2, rd.at[l, 3])
            value = sum(rd[l, i].astype(F32) for i in (0, 1, 3))
            gd_made[l] = value
        write_out(l, kind).start()
        return lanes_of(value)

    squares = jnp.zeros((1, 128), F32)

    length = lens[s]
    for k in range(NC):
        for half in range(2):
            core = c if half == 0 else 1 - c
            block_row = ((g + k // 2) % G) * H + ((y + k % 2) % 2) * 2 + core
            place = block_row * R + lax.broadcasted_iota(jnp.int32, (R, 128), 0)
            bias[k * W + half * R : k * W + half * R + R, :] = jnp.where(place < length, 0.0, NEGATIVE)
    lane_place = own_row * R + lax.broadcasted_iota(jnp.int32, (1, R), 1)
    live = jnp.where(lane_place < length, 1.0, 0.0)
    dqkv[0:HC, QT * W :] = jnp.zeros((HC, T - QT * W), BF16)
    sg[...] = jnp.zeros((D, 128), F32)
    lane = lax.broadcasted_iota(jnp.int32, (D, 128), 1)
    row_of = lax.broadcasted_iota(jnp.int32, (128, R), 0)

    def ids_here(other):
        arrived(idsg.at[other], id_s.at[other], id_r.at[other])

    over_blk(ids_here)
    t_here(3, plane_rows(s, 1 - g), lanes_in)
    t_send(7, plane_rows(s, 1 - g), lanes_out, sibling)
    for m, plane in ((4, s2), (5, s1), (6, s3)):
        t_here(m, plane_rows(plane, 1 - g), lanes_in)
        t_send(m + 4, rows(plane, G * DB), lanes_out, sibling)
    t_here(7, plane_rows(s, 1 - g), lanes_back)
    for m, plane in ((8, s2), (9, s1), (10, s3)):
        t_here(m, rows(plane, G * DB), lanes_back)
    etg = tg.at[:, 0:128]
    target_row = idsg[own_row, pl.ds(S + s, 1), :]
    mask_row = idsg[own_row, pl.ds(2 * S + s, 1), :].astype(F32)
    token_weight = mask_row * fam[s]
    weight_sum = jnp.zeros((1, 1), F32)
    for i in range(S):
        counts = jnp.zeros((1, R), F32)
        for j in range(B):
            counts = counts + idsg[j, 2 * S + i : 2 * S + i + 1, :].astype(F32)
        weight_sum = weight_sum + jnp.sum(counts, axis=1, keepdims=True) * fam[i]

    def gain(i):
        return etg[:, NORM_LANE + 2 * i : NORM_LANE + 2 * i + 1].astype(F32)

    def shift(i):
        return etg[:, NORM_LANE + 2 * i + 1 : NORM_LANE + 2 * i + 2].astype(F32)

    def normalize(v):
        centred = v - jnp.mean(v, axis=0, keepdims=True)
        rstd = lax.rsqrt(jnp.mean(centred * centred, axis=0, keepdims=True) + NORM_EPS)
        return centred * rstd, rstd

    def layer_norm_low(v, i):
        hat, _ = normalize(v)
        return (hat * gain(i) + shift(i)).astype(BF16)

    later = []

    def run_later():
        for work in later:
            work()
        later.clear()

    def norm_grads(grad, hat, i):
        gain_grad = jnp.sum(grad * hat, axis=1, keepdims=True)
        shift_grad = jnp.sum(grad, axis=1, keepdims=True)
        sg[...] += jnp.where(lane == NORM_LANE + 2 * i, gain_grad, 0.0) + jnp.where(
            lane == NORM_LANE + 2 * i + 1, shift_grad, 0.0
        )

    def layer_norm_back(grad, v, i):
        hat, rstd = normalize(v)
        later.append(lambda: norm_grads(grad, hat, i))
        scaled = grad * gain(i)
        mean_one = jnp.mean(scaled, axis=0, keepdims=True)
        mean_two = jnp.mean(scaled * hat, axis=0, keepdims=True)
        return rstd * (scaled - mean_one - hat * mean_two)

    def square_sum(v, l, i):
        later.append(lambda: stats.__setitem__(3 * l + i, squares_of(v)))

    def squares_of(v):
        return jnp.sum(jnp.sum(v * v, axis=0, keepdims=True) * live, axis=1, keepdims=True)

    slots = list(range(NC))
    near = slots[:2]
    stats = {}
    for k in slots:
        for half in range(2):
            core = c if half == 0 else 1 - c
            block_row = ((g + k // 2) % G) * H + ((y + k % 2) % 2) * 2 + core
            hot = jnp.where(row_of == idsg[block_row, pl.ds(s, 1), :], 1.0, 0.0).astype(BF16)
            place = tg[:, pl.ds(pl.multiple_of(128 + block_row * R, 128), R)]
            start = dot(etg[...], hot, 1, 0) + place.astype(F32)
            h1[0, :, k * W + half * R : k * W + half * R + R] = layer_norm_low(start, 0)
            if k == 0 and half == 0:
                xs[0] = start
                token_hot = hot

    def cols(k):
        return slice(k * W, (k + 1) * W)

    for l in range(L):
        x = xs[l]
        square_sum(x, l, 0)
        if l:
            h1[l, :, 0:R] = layer_norm_low(x, 2 * l)
            spread(h1.at[l], 11)
            run_later()
        else:
            push_weights(0)
            cross_weights(0, 1, (0, 1, 2, 3))
        wait_weights(l, 0)

        def project(k):
            if k in near:
                packed = dot(wq[l], h1[l, :, cols(k)], 0, 0).astype(BF16)
                qt[l, :, cols(k)] = packed[0:HC]
                packed = packed[HC:]
            else:
                packed = dot(wq[l, :, :], h1[l, :, cols(k)], 0, 0).astype(BF16)[HC:]
            kt[l, :, cols(k)] = packed[0:HC]
            vt[l, :, cols(k)] = packed[HC:]

        if l:
            have(h1.at[l], 0, 11)
            project(0)
            relay_near(h1.at[l], 11)
            have(h1.at[l], 1, 11)
            project(1)
            relay_far(h1.at[l], 11)
            have(h1.at[l], 2, 11)
            project(2)
            cross_weights(l, 1, (0, 1, 2, 3))
            have(h1.at[l], 3, 11)
            project(3)
        else:
            for k in slots:
                project(k)

        tiles = [(q, i) for q in (1, 0) for i in range(N_HEADS)]
        chunk = W
        peaks, norms, outs = {}, {}, {}

        def head_rows(i):
            return slice(i * HEAD_DIM, (i + 1) * HEAD_DIM)

        def score(n, j):
            q, i = tiles[n]
            keys = slice(j * chunk, (j + 1) * chunk)
            scores = dot(kt[l, head_rows(i), keys], qt[l, head_rows(i), cols(q)], 0, 0)
            scores = scores + jnp.concatenate([bias[keys, :]] * 2, axis=1)
            sbuf[n % 2, keys, :] = scores
            peak = jnp.max(scores, axis=0, keepdims=True)
            peaks[n] = jnp.maximum(peaks[n], peak) if j else peak

        def weigh(n, j):
            keys = slice(j * chunk, (j + 1) * chunk)
            exps = jnp.exp2((sbuf[n % 2, keys, :] - peaks[n]) * c2)
            norm = jnp.sum(exps, axis=0, keepdims=True)
            norms[n] = norms[n] + norm if j else norm
            pbuf[n % 2, keys, :] = exps.astype(BF16)

        def gather_values(n, j):
            q, i = tiles[n]
            keys = slice(j * chunk, (j + 1) * chunk)
            out = dot(vt[l, head_rows(i), keys], pbuf[n % 2, keys, :], 1, 0)
            outs[n] = outs[n] + out if j else out

        def attended(n):
            q, i = tiles[n]
            out = outs[n] * (1.0 / norms[n])
            o32[l, head_rows(i), cols(q)] = out
            ob[l, head_rows(i), cols(q)] = out.astype(BF16)
            lse[l, i * 8 : i * 8 + 8, cols(q)] = jnp.broadcast_to(
                peaks[n] * c2 + jnp.log(norms[n]) * LOG2E, (8, W)
            )

        for j in range(T // chunk):
            score(0, j)
        for n in range(len(tiles) + 1):
            for j in range(T // chunk):
                if n + 1 < len(tiles):
                    score(n + 1, j)
                if n:
                    gather_values(n - 1, j)
                if n < len(tiles):
                    weigh(n, j)
            if n:
                attended(n - 1)
            if n == 1:
                relay_weights(l, 3)
                relay_weights(l, 2)
                if l + 1 < L:
                    for kind in range(3):
                        send_weights(l + 1, kind)
            if n == N_HEADS:
                wait_weights(l, 1)
                part(4 * l, 1, dot(wo[l], ob[l, :, cols(1)], 1, 0))
            if n == N_HEADS + 2:
                pass_column(4 * l)
        part(4 * l, 0, dot(wo[l], ob[l, :, cols(0)], 1, 0))
        attn_out = total_column(4 * l)
        square_sum(attn_out, l, 1)
        middle = xs[l] + attn_out
        xm[l] = middle
        h2[l, :, 0:R] = layer_norm_low(middle, 2 * l + 1)
        spread(h2.at[l])
        run_later()
        wait_weights(l, 2)
        wait_weights(l, 3)

        def feed(k):
            pre = dot(wu[l], h2[l, :, cols(k)], 0, 0)
            cdf = 0.5 * (1.0 + lax.erf(pre * (0.5**0.5)))
            low = (pre * cdf).astype(BF16)
            act[l, :, cols(k)] = low
            slope[l, :, cols(k)] = cdf + pre * (jnp.exp(-0.5 * pre * pre) * 0.3989422804014327)
            part(4 * l + 1, k, dot(wd[l], low, 0, 0))

        have(h2.at[l], 0)
        feed(0)
        relay_near(h2.at[l])
        have(h2.at[l], 1)
        feed(1)
        if l + 1 < L:
            for kind in range(2):
                relay_weights(l + 1, kind)
            cross_weights(l + 1, 0, (0, 1))
            send_weights(l + 1, 3)
            push_weights(l + 1)
        relay_far(h2.at[l])
        have(h2.at[l], 2)
        feed(2)
        pass_near(4 * l + 1)
        have(h2.at[l], 3)
        feed(3)
        pass_across(4 * l + 1)
        pass_joined(4 * l + 1)
        if l + 1 < L:
            cross_weights(l + 1, 0, (2, 3))
        ffn_out = total(4 * l + 1)
        square_sum(ffn_out, l, 2)
        xs[l + 1] = xm[l] + ffn_out

    last = xs[L]
    final_low = layer_norm_low(last, 2 * L)
    logits = dot(etg[...], final_low, 0, 0)[0:NORM_LANE]
    vocab_row = row_of[0:NORM_LANE]
    logits = jnp.where(vocab_row < VOCAB, logits, NEGATIVE)
    shifted = logits - jnp.max(logits, axis=0, keepdims=True)
    log_probs = shifted - jnp.log(jnp.sum(jnp.exp(shifted), axis=0, keepdims=True))
    target_hot = jnp.where(vocab_row == target_row, 1.0, 0.0)
    token_loss = -jnp.sum(target_hot * log_probs, axis=0, keepdims=True)
    loss = jnp.sum(token_weight * token_loss, axis=1, keepdims=True)
    grad_logits = ((token_weight / weight_sum) * (jnp.exp(log_probs) - target_hot)).astype(BF16)
    grad_logits = jnp.concatenate([grad_logits, jnp.zeros((128 - NORM_LANE, R), BF16)], axis=0)
    grad_final = dot(etg[...], grad_logits, 1, 0)
    sg[...] += dot(final_low, grad_logits, 1, 1)
    grad = layer_norm_back(grad_final, last, 2 * L)

    for l in reversed(range(L)):
        df[l, :, 0:R] = grad.astype(BF16)
        xs[l + 1] = grad
        spread(df.at[l])
        run_later()
        if l + 1 == L:
            for copy in waits:
                copy.wait_send()
            waits.clear()

        def feed_back(k):
            grad_act = dot(wd[l], df[l, :, cols(k)], 1, 0)
            low = (grad_act * slope[l, :, cols(k)]).astype(BF16)
            du[:, cols(k)] = low
            part(4 * l + 2, k, dot(wu[l], low, 1, 0))

        have(df.at[l], 0)
        feed_back(0)
        relay_near(df.at[l])
        if l + 1 < L:
            g_cross(l + 1, 1, ((0, s3), (1, s1)))
            for kind in range(2):
                g_cross(l + 1, kind, ((2, s2), (3, s)))
        have(df.at[l], 1)
        feed_back(1)
        relay_far(df.at[l])
        have(df.at[l], 2)
        feed_back(2)
        pass_near(4 * l + 2)
        have(df.at[l], 3)
        feed_back(3)
        pass_across(4 * l + 2)
        if l + 1 < L:
            g_mid(l + 1, 0)
            g_mid(l + 1, 1)
            g_third(l + 1)
        g_first(l, 3, dot(act[l], df[l], 1, 1))
        pass_joined(4 * l + 2)
        g_first(l, 2, dot(h2[l], du[...], 1, 1))
        grad_middle = xs[l + 1] + layer_norm_back(total(4 * l + 2), xm[l], 2 * l + 1)
        xm[l] = grad_middle

        da[l, :, 0:R] = grad_middle.astype(BF16)
        spread_column(da.at[l])
        run_later()
        if l + 1 < L:
            g_second(l + 1, 0)
            g_second(l + 1, 1)
            for kind in (2, 3):
                squares = squares + g_final(l + 1, kind)

        def out_back(k):
            dob[:, cols(k)] = dot(wo[l], da[l, :, cols(k)], 0, 0).astype(BF16)

        have(da.at[l], 0)
        out_back(0)
        relay_column(da.at[l])
        have(da.at[l], 1)
        out_back(1)

        steps = [(i, q, j) for i in range(N_HEADS) for q in range(QT) for j in range(T // chunk)]
        grad_q, grad_k, grad_v = {}, {}, {}

        def back_scores(n):
            i, q, j = steps[n]
            keys = slice(j * chunk, (j + 1) * chunk)
            sbuf[n % 2, 0:chunk, :] = dot(kt[l, head_rows(i), keys], qt[l, head_rows(i), cols(q)], 0, 0)
            sbuf[n % 2, chunk : 2 * chunk, :] = dot(vt[l, head_rows(i), keys], dob[head_rows(i), cols(q)], 0, 0)

        def back_weigh(n):
            i, q, j = steps[n]
            keys = slice(j * chunk, (j + 1) * chunk)
            delta = jnp.sum(
                dob[head_rows(i), cols(q)].astype(F32) * o32[l, head_rows(i), cols(q)],
                axis=0,
                keepdims=True,
            )
            scores = sbuf[n % 2, 0:chunk, :] + jnp.concatenate([bias[keys, :]] * 2, axis=1)
            probs = jnp.exp2(scores * c2 - lse[l, i * 8 : i * 8 + 1, cols(q)])
            pbuf[n % 2, 0:chunk, :] = probs.astype(BF16)
            pbuf[n % 2, chunk : 2 * chunk, :] = (probs * (sbuf[n % 2, chunk : 2 * chunk, :] - delta)).astype(BF16)

        def back_products(n):
            i, q, j = steps[n]
            keys = slice(j * chunk, (j + 1) * chunk)
            probs = pbuf[n % 2, 0:chunk, :]
            grad_scores = pbuf[n % 2, chunk : 2 * chunk, :]
            term = dot(kt[l, head_rows(i), keys], grad_scores, 1, 0)
            grad_q[i, q] = grad_q[i, q] + term if j else term
            term_k = dot(qt[l, head_rows(i), cols(q)], grad_scores, 1, 1)
            term_v = dot(dob[head_rows(i), cols(q)], probs, 1, 1)
            grad_k[i, j] = grad_k[i, j] + term_k if q else term_k
            grad_v[i, j] = grad_v[i, j] + term_v if q else term_v
            if j == T // chunk - 1:
                dqkv[head_rows(i), cols(q)] = (grad_q[i, q] * scale).astype(BF16)
            if q == QT - 1:
                first = HC + i * HEAD_DIM
                dqkv[first : first + HEAD_DIM, keys] = (grad_k[i, j] * scale).astype(BF16)
                first = 2 * HC + i * HEAD_DIM
                dqkv[first : first + HEAD_DIM, keys] = grad_v[i, j].astype(BF16)

        back_scores(0)
        for n in range(len(steps) + 1):
            if n + 1 < len(steps):
                back_scores(n + 1)
            if n:
                back_products(n - 1)
            if n < len(steps):
                back_weigh(n)
            if n == len(steps) // 2:
                g_second(l, 3)
        def project_back(k):
            part(4 * l + 3, k, dot(wq[l], dqkv[:, cols(k)], 1, 0))

        project_back(3)
        project_back(1)
        pass_across(4 * l + 3)
        project_back(2)
        pass_near(4 * l + 3)
        project_back(0)
        g_second(l, 2)
        if l + 1 < L:
            for kind in range(2):
                squares = squares + g_final(l + 1, kind)
        g_first(l, 0, dot(h1[l], dqkv[...], 1, 1))
        pass_joined(4 * l + 3)
        g_cross(l, 0, ((0, s3), (1, s1)))
        g_first(l, 1, dot(da[l], ob[l], 1, 1))
        if l == 0:
            g_cross(0, 1, ((0, s3), (1, s1)))
            for kind in range(2):
                g_cross(0, kind, ((2, s2), (3, s)))
        grad = xm[l] + layer_norm_back(total(4 * l + 3), xs[l], 2 * l)

    run_later()
    high = grad.astype(BF16)
    low = (grad - high.astype(F32)).astype(BF16)
    small = sg[...] + dot(high, token_hot, 1, 1) + dot(low, token_hot, 1, 1)
    small = small.astype(BF16)
    for i in range(B):
        fst[i, :DB] = small[i * DB : (i + 1) * DB]
        fst[i, DB:] = high[i * DB : (i + 1) * DB]

    def send_table(other):
        send(fst.at[other], frx.at[b], f_s.at[other], f_r.at[b], dev(other, h))

    over_blk(send_table)
    frx[b] = fst[b]

    g_mid(0, 0)
    g_mid(0, 1)
    g_third(0)
    squares = squares + g_final(0, 3)

    def table_here(other):
        arrived(frx.at[other], f_s.at[other], f_r.at[other])

    over_blk(table_here)
    value = frx[0, :DB].astype(F32)
    for i in range(1, B):
        value = value + frx[i, :DB].astype(F32)
    hrs[h] = value

    def send_small(k, carry):
        other = lax.rem(h + k, H)
        send(hrs.at[h], hrs.at[h], hx_s.at[other], hx_r.at[h], dev(b, other))
        return carry

    lax.fori_loop(1, H, send_small, 0)
    for j in range(G):
        value = frx[j, DB:].astype(F32)
        for i in range(1, S):
            value = value + frx[i * G + j, DB:].astype(F32)
        hrx[h, j] = value
        squares = squares + lanes_of(value)

    def send_places(k, carry):
        other = lax.rem(h + k, H)
        send(hrx.at[h], hrx.at[h], hx_s.at[H + other], hx_r.at[H + h], dev(b, other))
        return carry

    lax.fori_loop(1, H, send_places, 0)

    def small_here(k, carry):
        other = lax.rem(h + k, H)
        arrived(hrs.at[other], hx_s.at[other], hx_r.at[other])
        return carry

    def places_here(k, carry):
        other = lax.rem(h + k, H)
        arrived(hrx.at[other], hx_s.at[H + other], hx_r.at[H + other])
        return carry

    g_second(0, 0)
    g_second(0, 1)
    lax.fori_loop(1, H, small_here, 0)
    value = hrs[0]
    for i in range(1, H):
        value = value + hrs[i]
    squares = squares + lanes_of(value) * (1.0 / H)
    small_sum = value
    for kind in (2, 0, 1):
        squares = squares + g_final(0, kind)

    lane_one = lax.broadcasted_iota(jnp.int32, (1, 128), 1)
    packed = jnp.where(lane_one == 0, loss, 0.0) + jnp.where(lane_one == 1, squares, 0.0)
    for i, stat in stats.items():
        packed = packed + jnp.where(lane_one == 2 + i, stat, 0.0)
    scg[B + h] = jnp.broadcast_to(packed, (8, 128))

    def send_heads(k, carry):
        other = lax.rem(h + k, H)
        src = scg.at[B + h]
        send(src, src, sc_s.at[B + other], sc_r.at[B + h], dev(b, other))
        return carry

    lax.fori_loop(1, H, send_heads, 0)

    def heads_here(k, carry):
        other = lax.rem(h + k, H)
        arrived(scg.at[B + other], sc_s.at[B + other], sc_r.at[B + other])
        return carry

    lax.fori_loop(1, H, heads_here, 0)
    out = scg[B]
    for i in range(1, H):
        out = out + scg[B + i]
    scg[b] = out

    def send_scalars(other):
        send(scg.at[b], scg.at[b], sc_s.at[other], sc_r.at[b], dev(other, h))

    over_blk(send_scalars)
    lax.fori_loop(1, H, places_here, 0)
    ge_made[...] = jnp.concatenate(
        [small_sum[:, :VOCAB]] + [hrx[i, j] for j in range(G) for i in range(H)], axis=1
    )
    norm_rows = small_sum.T
    for i in range(2 * L + 1):
        gn_out[i] = norm_rows[NORM_LANE + 2 * i : NORM_LANE + 2 * i + 2]

    table_out = pltpu.make_async_copy(ge_made, ge_out, out_sem.at[4 * L])
    table_out.start()

    for l in range(L):
        for kind in range(4):
            write_out(l, kind).wait()
    ag_left()
    for copy in waits:
        copy.wait_send()
    for copies in staged.values():
        for copy in copies:
            copy.wait_send()

    def sent(other):
        for src, ssem, rsem in ((idsg.at[other], id_s, id_r), (frx.at[other], f_s, f_r)):
            pltpu.make_async_remote_copy(src, src, ssem.at[other], rsem.at[other], sibling, MESH).wait_send()

    over_blk(sent)

    def heads_sent(k, carry):
        other = lax.rem(h + k, H)
        for src, m in ((hrs.at[other], other), (hrx.at[other], H + other)):
            pltpu.make_async_remote_copy(src, src, hx_s.at[m], hx_r.at[m], sibling, MESH).wait_send()
        src = scg.at[B + other]
        pltpu.make_async_remote_copy(
            src, src, sc_s.at[B + other], sc_r.at[B + other], sibling, MESH
        ).wait_send()
        return carry

    lax.fori_loop(1, H, heads_sent, 0)

    def scalars_here(other):
        arrived(scg.at[other], sc_s.at[other], sc_r.at[other])

    over_blk(scalars_here)
    out = scg[0]
    for i in range(1, B):
        out = out + scg[i]
    lane_eight = lax.broadcasted_iota(jnp.int32, (8, 128), 1)
    tokens = lens[0]
    for i in range(1, S):
        tokens = tokens + lens[i]
    roots = jnp.sqrt(jnp.where(lane_eight == 1, out, out / (tokens.astype(F32) * D)))
    out = jnp.where(lane_eight == 0, out, roots)
    out = jnp.where(lane_eight == 2 + 3 * L, weight_sum, out)
    factor = CLIP_NORM / jnp.maximum(out, CLIP_NORM)
    factor = jnp.sum(jnp.where(lane_eight == 1, factor, 0.0), axis=1, keepdims=True)
    scal_out[...] = jnp.where(lane_eight == 3 + 3 * L, factor, out)

    table_out.wait()

    def scalars_sent(other):
        src = scg.at[other]
        pltpu.make_async_remote_copy(
            src, src, sc_s.at[other], sc_r.at[other], sibling, MESH
        ).wait_send()

    over_blk(scalars_sent)


def fused_step(z, token_ids, targets, masked, lengths, family_weight, embed_table, w_qkv, w_out, w_up, w_down, norm_params):
    B, H, S, G, L, D, DB, HC, R, NC, NR, FU, FD, T = (
        z.B, z.H, z.S, z.G, z.L, z.D, z.DB, z.HC, z.R, z.NC, z.NR, z.FU, z.FD, z.T,
    )
    W = 2 * R
    smem = pl.BlockSpec(memory_space=pltpu.SMEM)
    vmem = pl.BlockSpec(memory_space=pltpu.VMEM)
    dma = pltpu.SemaphoreType.DMA
    scratch = [
        pltpu.VMEM((L, DB, S * G * FD), F32),
        pltpu.VMEM((L, FD, D), F32),
        dma((2,)),
        pltpu.VMEM((DB, VOCAB + T), F32),
        pltpu.VMEM((L, 3, DB, HC), F32),
        pltpu.VMEM((L, HC, DB), F32),
        pltpu.VMEM((L, DB, S * G * FD), F32),
        pltpu.VMEM((L, FD, D), F32),
        dma((4 * L + 1,)),
        pltpu.VMEM((16, R), jnp.int32),
        pltpu.VMEM((L, DB, 3 * HC), BF16),
        pltpu.VMEM((L, DB, HC), BF16),
        pltpu.VMEM((L, G, DB, FU), BF16),
        pltpu.VMEM((L, FD, D), BF16),
        pltpu.VMEM((G, DB, FU), F32),
        pltpu.VMEM((B, 16, R), jnp.int32),
        pltpu.VMEM((D, 128 + T), BF16),
        pltpu.VMEM((L, D, 3 * HC), BF16),
        pltpu.VMEM((L, D, HC), BF16),
        pltpu.VMEM((L, D, FU), BF16),
        pltpu.VMEM((L, FU, D), BF16),
        pltpu.VMEM((L, D, T), BF16),
        pltpu.VMEM((L, D, T), BF16),
        pltpu.VMEM((L, D, T), BF16),
        pltpu.VMEM((L, D, 2 * W), BF16),
        pltpu.VMEM((L, FU, T), BF16),
        pltpu.VMEM((L, FU, T), F32),
        pltpu.VMEM((FU, T), BF16),
        pltpu.VMEM((L, HC, 2 * W), BF16),
        pltpu.VMEM((L, HC, T), BF16),
        pltpu.VMEM((L, HC, T), BF16),
        pltpu.VMEM((L, HC, 2 * W), F32),
        pltpu.VMEM((L, HC, 2 * W), BF16),
        pltpu.VMEM((HC, 2 * W), BF16),
        pltpu.VMEM((L, 8 * (HC // HEAD_DIM), 2 * W), F32),
        pltpu.VMEM((3 * HC, T), BF16),
        pltpu.VMEM((T, 128), F32),
        pltpu.VMEM((2, T, W), F32),
        pltpu.VMEM((2, T, W), BF16),
        pltpu.VMEM((L + 1, D, R), F32),
        pltpu.VMEM((L, D, R), F32),
        pltpu.VMEM((NC, D, R), F32),
        pltpu.VMEM((NC, D, R), BF16),
        pltpu.VMEM((NC, D, R), BF16),
        pltpu.VMEM((4, NC, D, R), BF16),
        pltpu.VMEM((4, NC, D, R), BF16),
        pltpu.VMEM((D, 128), F32),
        pltpu.VMEM((D, 3 * HC), BF16),
        pltpu.VMEM((D, HC), BF16),
        pltpu.VMEM((D, FU), BF16),
        pltpu.VMEM((FU, D), BF16),
        pltpu.VMEM((L, S + 3, DB, 3 * HC), BF16),
        pltpu.VMEM((L, S + 3, DB, HC), BF16),
        pltpu.VMEM((L, S, G * DB, FU), BF16),
        pltpu.VMEM((L, S, FD, D), BF16),
        pltpu.VMEM((L, DB, FU), BF16),
        pltpu.VMEM((3, DB, 3 * HC), BF16),
        pltpu.VMEM((3, DB, HC), BF16),
        pltpu.VMEM((G * DB, FU), BF16),
        pltpu.VMEM((FD, D), BF16),
        pltpu.VMEM((DB, FU), BF16),
        pltpu.VMEM((B, 2 * DB, 128), BF16),
        pltpu.VMEM((B, 2 * DB, 128), BF16),
        pltpu.VMEM((H, DB, 128), F32),
        pltpu.VMEM((H, G, DB, 128), F32),
        pltpu.VMEM((B + H, 8, 128), F32),
        dma((B,)),
        dma((B,)),
        dma((11,)),
        dma((11,)),
        dma((21 * L,)),
        dma((21 * L,)),
        dma((22,)),
        dma((22,)),
        dma((20,)),
        dma((20,)),
        dma((21 * L,)),
        dma((21 * L,)),
        dma((B,)),
        dma((B,)),
        dma((2 * H,)),
        dma((2 * H,)),
        dma((B + H,)),
        dma((B + H,)),
    ]
    outs = (
        jax.ShapeDtypeStruct((8, 128), F32),
        jax.ShapeDtypeStruct((DB, VOCAB + T), F32),
        jax.ShapeDtypeStruct((L, 3, DB, HC), F32),
        jax.ShapeDtypeStruct((L, HC, DB), F32),
        jax.ShapeDtypeStruct((L, DB, S * G * FD), F32),
        jax.ShapeDtypeStruct((L, FD, D), F32),
        jax.ShapeDtypeStruct((2 * L + 1, 2, DB), F32),
    )
    scal, ge, gq, go, gu, gd, gn = pl.pallas_call(
        functools.partial(step_kernel, z),
        out_shape=outs,
        in_specs=[smem, smem] + [vmem] * 6 + [pl.BlockSpec(memory_space=pl.ANY)] * 2 + [vmem],
        out_specs=[vmem] + [pl.BlockSpec(memory_space=pl.ANY)] * 5 + [vmem],
        scratch_shapes=scratch,
        compiler_params=pltpu.CompilerParams(
            collective_id=0, has_side_effects=True, vmem_limit_bytes=62 << 20
        ),
        name="train_step",
    )(
        lengths,
        family_weight,
        token_ids,
        targets,
        masked,
        embed_table.T,
        w_qkv.transpose(0, 2, 1, 3),
        w_out,
        w_up,
        w_down,
        norm_params,
    )
    return scal, (ge, gq, go, gu, gd, gn)


def update_kernel(layers, scal, *refs):
    groups = len(RATES)
    grads, masters, firsts, seconds = (refs[i * groups : (i + 1) * groups] for i in range(4))
    loss, weights, norm, rms = refs[4 * groups : 4 * groups + 4]
    outs = refs[4 * groups + 4 :]
    loss[0] = scal[0, 0]
    norm[0] = scal[0, 1]
    weights[0] = scal[0, 2 + 3 * layers]
    for i in range(layers):
        for j in range(3):
            rms[i, j] = scal[0, 2 + 3 * i + j]
    factor = scal[0, 3 + 3 * layers]
    for i in range(groups):

        def update(at, i=i):
            first, second, weight = adamw_update(
                masters[i][at],
                firsts[i][at],
                seconds[i][at],
                grads[i][at] * factor,
                RATES[i],
                DECAYS[i],
            )
            for ref, value in zip(outs[4 * i : 4 * i + 4], (first, second, weight, weight)):
                ref[at] = value.astype(ref.dtype)

        for k in range(masters[i].shape[0] if len(masters[i].shape) > 2 else 1):
            update(k if len(masters[i].shape) > 2 else slice(None))


def as_stored(groups):
    embed, qkv, out, up, down, norm = groups
    return embed.T, qkv.transpose(0, 2, 1, 3), out, up, down, norm


def fused_update(layers, scal, grads, masters, firsts, seconds):
    arrays = (*grads, *as_stored(masters), *as_stored(firsts), *as_stored(seconds))
    smem = pl.BlockSpec(memory_space=pltpu.SMEM)
    vmem = pl.BlockSpec(memory_space=pltpu.VMEM)
    shapes = [
        jax.ShapeDtypeStruct(master.shape, dtype)
        for master in as_stored(masters)
        for dtype in (F32, F32, F32, BF16)
    ]
    scalars = [jax.ShapeDtypeStruct((1,), F32)] * 3 + [jax.ShapeDtypeStruct((layers, 3), F32)]
    loss, weights, norm, rms, *new = pl.pallas_call(
        functools.partial(update_kernel, layers),
        out_shape=scalars + shapes,
        in_specs=[smem] + [vmem] * len(arrays),
        out_specs=[smem] * 4 + [vmem] * len(shapes),
        compiler_params=pltpu.CompilerParams(vmem_limit_bytes=62 << 20),
        name="adamw",
    )(scal, *arrays)
    by_kind = [as_stored(new[i::4]) for i in range(4)]
    results = [loss[0], weights[0], norm[0], rms]
    for i in range(len(RATES)):
        results += [kind[i] for kind in by_kind]
    return tuple(results)


def local(
    token_ids,
    targets,
    masked,
    lengths,
    family_weight,
    embed_table,
    w_qkv,
    w_out,
    w_up,
    w_down,
    norm_params,
    embed_first,
    qkv_first,
    out_first,
    up_first,
    down_first,
    norm_first,
    embed_second,
    qkv_second,
    out_second,
    up_second,
    down_second,
    norm_second,
):
    z = Sizes(
        lax.axis_size("blk"),
        lax.axis_size("head"),
        token_ids.shape[0],
        token_ids.shape[1],
        w_qkv.shape,
        w_up.shape,
        w_down.shape,
    )
    masters = (embed_table, w_qkv, w_out, w_up, w_down, norm_params)
    firsts = (embed_first, qkv_first, out_first, up_first, down_first, norm_first)
    seconds = (embed_second, qkv_second, out_second, up_second, down_second, norm_second)
    tokens = (token_ids, targets, masked, lengths, family_weight)
    if z.fused(token_ids.shape[1]):
        scal, grads = fused_step(z, *tokens, *masters)
        return fused_update(LAYERS, scal, grads, masters, firsts, seconds)
    loss_sum, weight_sum, grad_norm, squares, grads = plain_step(*tokens, *masters)
    stream_rms = jnp.sqrt(squares.reshape(LAYERS, 3) / (jnp.sum(lengths).astype(jnp.float32) * D))
    factor = CLIP_NORM / jnp.maximum(grad_norm, CLIP_NORM)
    results = [loss_sum, weight_sum, grad_norm, stream_rms]
    for group_idx in range(6):
        first, second, weight = adamw_update(
            masters[group_idx],
            firsts[group_idx],
            seconds[group_idx],
            grads[group_idx] * factor,
            RATES[group_idx],
            DECAYS[group_idx],
        )
        results += [first, second, weight, weight.astype(jnp.bfloat16)]
    return tuple(results)


def solution(mesh):
    return jax.shard_map(
        local,
        mesh=mesh,
        in_specs=(
            P(None, "blk"),
            P(None, "blk"),
            P(None, "blk"),
            P(),
            P(),
            P(None, "blk"),
            P(None, "blk", None, "head"),
            P(None, "head", "blk"),
            P(None, "blk", "head"),
            P(None, ("head", "blk"), None),
            P(None, None, "blk"),
            P(None, "blk"),
            P(None, "blk", None, "head"),
            P(None, "head", "blk"),
            P(None, "blk", "head"),
            P(None, ("head", "blk"), None),
            P(None, None, "blk"),
            P(None, "blk"),
            P(None, "blk", None, "head"),
            P(None, "head", "blk"),
            P(None, "blk", "head"),
            P(None, ("head", "blk"), None),
            P(None, None, "blk"),
        ),
        out_specs=(
            P(),
            P(),
            P(),
            P(),
            P(None, "blk"),
            P(None, "blk"),
            P(None, "blk"),
            P(None, "blk"),
            P(None, "blk", None, "head"),
            P(None, "blk", None, "head"),
            P(None, "blk", None, "head"),
            P(None, "blk", None, "head"),
            P(None, "head", "blk"),
            P(None, "head", "blk"),
            P(None, "head", "blk"),
            P(None, "head", "blk"),
            P(None, "blk", "head"),
            P(None, "blk", "head"),
            P(None, "blk", "head"),
            P(None, "blk", "head"),
            P(None, ("head", "blk"), None),
            P(None, ("head", "blk"), None),
            P(None, ("head", "blk"), None),
            P(None, ("head", "blk"), None),
            P(None, None, "blk"),
            P(None, None, "blk"),
            P(None, None, "blk"),
            P(None, None, "blk"),
        ),
        check_vma=False,
    )
```
